256 devices in a mesh: patch: 2 (over core), lat: 8 (over z), lon: 16 (over y, x).
Axes of the slice: x: 4, y: 4, z: 8, core: 2. Of those that a mesh axis runs over, the one named last changes fastest.
Arguments:
- flow_vector: float32 [3, 2, 2, 1024, 2048], P(None, 'patch', None, 'lat', 'lon'), may hold values from -6 to 6
- normal_stress: float32 [2, 2, 1024, 2048], P('patch', None, 'lat', 'lon'), may hold values from -6 to 6
- thermal_field: float32 [2, 2, 1024, 2048], P('patch', None, 'lat', 'lon'), may hold values from 0 to 1
- shear_resistance: float32 [2, 2, 1024, 2048], P('patch', None, 'lat', 'lon'), may hold values from 0.1 to 10
- departing_bands: int32 [2, 8, 16, 1], P('patch', 'lat', 'lon'), may hold values from 0 to 127, as said below
- receiving_processor: int32 [2, 8, 16, 1], P('patch', 'lat', 'lon'), may hold values from -1 to 127, as said below
- shift_filled_by_lane: int32 [2, 8, 16, 128], P('patch', 'lat', 'lon'), may hold values from 0 to 8, as said below
- blending_factors: float32 [2, 8, 16, 8, 128, 128], P('patch', 'lat', 'lon'), may hold values from -2 to 2, as said below
Outputs:
- velocity_out: float32 [3, 2, 2, 1024, 2048], P(None, 'patch', None, 'lat', 'lon')
- pressure_out: float32 [2, 2, 1024, 2048], P('patch', None, 'lat', 'lon')
- temperature_out: float32 [2, 2, 1024, 2048], P('patch', None, 'lat', 'lon')
The draws below stay inside these ranges and needn't reach their ends.
Inputs may be any that keep to these rules, and one draw needn't show every extreme that they name: `departing_bands`: A row of the sending device's own 128 rows. `receiving_processor`: the flat number a * 16 + b of the device of the other patch that receives the slot, or -1 for an unused slot. A device uses at most 1 slots; some device uses all of them. Consistent with shift_filled_by_lane. `shift_filled_by_lane`: entry q + s of device d names the offset side * 2 + t that slot s of device q of the other patch fills at d, or 8 if that slot fills nothing at d. Sides 0, 1, 2, 3 are the ghost row before the first row, after the last row, the ghost column before the first column and after the last column. A side is filled exactly where it lies on the patch's edge, and then each of its 2 offsets is named by exactly one entry. `blending_factors`: dense interpolation weights, a matrix of 128 by 128 for each offset.
All inputs are finite; a program needn't handle non-finite values.
Results may differ from the reference program's by a relative error of at most 0.0001.
Values sent between devices are 32-bit elements; how exact they have to be, the bound alone decides.
No kernel may reach another device: no remote copies, remote signals or barrier semaphores. Data moves between devices by JAX's collectives and lax.ppermute only.
A program may use at most 64 MiB of HBM per device.

```python
import math
import jax
import jax.numpy as jnp
from jax import lax

DEPTH_SHELLS = 2
CELLS = 128
SWEEPS = 4
TERMS = 2
SIDES = 4
POLAR_ANGLE_BANDS = 1024
AZIMUTH_STRIPS = 2048
SEND_MOST = 1
N_LAT = 8
N_LON = 16


def force_entry(order, position, value):
    where = jnp.argmax(order == value).astype(jnp.int32)
    moved = order[position]
    order = order.at[where].set(moved)
    return order.at[position].set(value)


def intersection_plan(key):
    devices = N_LAT * N_LON
    segments = 2 * N_LON + 2 * N_LAT
    block_count = segments * TERMS
    offset_none = SIDES * TERMS
    rows_all = jnp.zeros((2, devices, SEND_MOST), jnp.int32)
    peers_all = jnp.full((2, devices, SEND_MOST), -1, jnp.int32)
    slots_all = jnp.full((2, devices, devices * SEND_MOST), offset_none, jnp.int32)
    index = jnp.arange(block_count, dtype=jnp.int32)
    segment = index // TERMS
    term_ids = index % TERMS
    first_b = segment < N_LON
    second_b = segment < 2 * N_LON
    third_b = segment < 2 * N_LON + N_LAT
    dest_lat = jnp.where(first_b, 0, jnp.where(second_b, N_LAT - 1, jnp.where(third_b, segment - 2 * N_LON, segment - 2 * N_LON - N_LAT)))
    dest_lon = jnp.where(first_b, segment, jnp.where(second_b, segment - N_LON, jnp.where(third_b, 0, N_LON - 1)))
    side_ids = jnp.where(first_b, 0, jnp.where(second_b, 1, jnp.where(third_b, 2, 3)))
    dest = (dest_lat * N_LON + dest_lon).astype(jnp.int32)
    offset = (side_ids * TERMS + term_ids).astype(jnp.int32)
    slot_pos = index // devices
    for source in range(2):
        subkey = jax.random.fold_in(key, 11 + source)
        order = jax.random.permutation(subkey, devices).astype(jnp.int32)
        order = force_entry(order, 0, devices // 2)
        order = force_entry(order, 1, 1)
        picked = jax.random.randint(jax.random.fold_in(subkey, 5), (block_count,), 0, CELLS, dtype=jnp.int32)
        spare = jax.random.randint(jax.random.fold_in(subkey, 7), (devices, SEND_MOST), 0, CELLS, dtype=jnp.int32)
        sender = order[index % devices]
        rows_all = rows_all.at[source].set(spare.at[sender, slot_pos].set(picked))
        peers_all = peers_all.at[source, sender, slot_pos].set(dest)
        slots_all = slots_all.at[1 - source, dest, sender * SEND_MOST + slot_pos].set(offset)
    return (rows_all.reshape(2, N_LAT, N_LON, SEND_MOST), peers_all.reshape(2, N_LAT, N_LON, SEND_MOST), slots_all.reshape(2, N_LAT, N_LON, devices * SEND_MOST))


def draw_departing_bands(key, part):
    plan = intersection_plan(key)
    return plan[0]


def draw_receiving_processor(key, part):
    plan = intersection_plan(key)
    return plan[1]


def draw_shift_filled_by_lane(key, part):
    plan = intersection_plan(key)
    return plan[2]


def draw_blending_factors(key, part):
    key = jax.random.fold_in(key, 4)
    shape = (2, N_LAT, N_LON, SIDES * TERMS, CELLS, CELLS)
    spread = 0.5 / CELLS ** 0.5
    noise = jax.random.truncated_normal(key, -4.0, 4.0, shape, jnp.float32) * spread
    centre = 0.5
    identity = jnp.eye(CELLS, dtype=jnp.float32)
    return (noise + centre * identity).astype(jnp.float32)


def shard_levels(key, dims, split, least, top_value):
    def one(dim, blocks):
        heights = jax.random.uniform(jax.random.fold_in(jax.random.fold_in(key, 6), dim), (blocks,), jnp.float32, least / len(split), top_value / len(split))
        return jnp.repeat(jnp.exp(heights), dims[dim] // blocks).reshape((-1,) + (1,) * (len(dims) - dim - 1))

    loudness = one(*split[0])
    for cut in split[1:]:
        loudness = loudness * one(*cut)
    return loudness


def bell_draw(key, dims, scale, most, split=(), held_as=jnp.bfloat16):
    entries = scale * jax.random.normal(key, dims, jnp.float32)
    if split:
        entries = entries * shard_levels(key, dims, split, -0.22, 0.18)
    return jnp.clip(entries, -most, most).astype(held_as)


def setup_inputs(seed: int = 0) -> dict:
    streams_of = jax.random.split(jax.random.key(seed), 9)
    flow_vector = bell_draw(streams_of[0], (3, 2, DEPTH_SHELLS, POLAR_ANGLE_BANDS, AZIMUTH_STRIPS), 1.0, 6.0, ((1, 2), (3, 8), (4, 16)), jnp.float32)
    normal_stress = bell_draw(streams_of[1], (2, DEPTH_SHELLS, POLAR_ANGLE_BANDS, AZIMUTH_STRIPS), 1.0, 6.0, ((0, 2), (2, 8), (3, 16)), jnp.float32)
    thermal_field = jnp.clip(1.0 * jax.random.uniform(streams_of[2], (2, DEPTH_SHELLS, POLAR_ANGLE_BANDS, AZIMUTH_STRIPS), jnp.float32) ** shard_levels(streams_of[2], (2, DEPTH_SHELLS, POLAR_ANGLE_BANDS, AZIMUTH_STRIPS), ((0, 2), (2, 8), (3, 16)), -0.2, 0.2), 0.0, 1.0)
    shear_resistance = jnp.clip(jnp.exp(math.log(10.0) - 4.6051702 * jax.random.uniform(streams_of[3], (2, DEPTH_SHELLS, POLAR_ANGLE_BANDS, AZIMUTH_STRIPS), jnp.float32) ** shard_levels(streams_of[3], (2, DEPTH_SHELLS, POLAR_ANGLE_BANDS, AZIMUTH_STRIPS), ((0, 2), (2, 8), (3, 16)), -0.2, 0.2)), 0.1, 10.0)
    departing_bands = draw_departing_bands(jax.random.fold_in(streams_of[8], 71), 0)
    receiving_processor = draw_receiving_processor(jax.random.fold_in(streams_of[8], 71), 0)
    shift_filled_by_lane = draw_shift_filled_by_lane(jax.random.fold_in(streams_of[8], 71), 0)
    blending_factors = draw_blending_factors(jax.random.fold_in(streams_of[8], 71), 0)
    return {"flow_vector": flow_vector, "normal_stress": normal_stress, "thermal_field": thermal_field, "shear_resistance": shear_resistance, "departing_bands": departing_bands, "receiving_processor": receiving_processor, "shift_filled_by_lane": shift_filled_by_lane, "blending_factors": blending_factors}


PRECISE = lax.Precision.HIGHEST


def neighbours(bordered_mesh):
    return (bordered_mesh[..., 2:, 1:-1, 1:-1], bordered_mesh[..., :-2, 1:-1, 1:-1],
            bordered_mesh[..., 1:-1, 2:, 1:-1], bordered_mesh[..., 1:-1, :-2, 1:-1],
            bordered_mesh[..., 1:-1, 1:-1, 2:], bordered_mesh[..., 1:-1, 1:-1, :-2])


def cycle_cells(stack, departing_bands, receiving_processor, shift_filled_by_lane, blending_factors):
    field_count = stack.shape[0]
    devices = N_LAT * N_LON
    offset_count = SIDES * TERMS
    tiles = stack.reshape(field_count, 2, DEPTH_SHELLS, N_LAT, CELLS, N_LON, CELLS)
    tiles = tiles.transpose(0, 1, 2, 3, 5, 4, 6).reshape(field_count, 2, DEPTH_SHELLS, devices, CELLS, CELLS)
    row_ids = departing_bands.reshape(1, 2, 1, devices, SEND_MOST, 1).astype(jnp.int32)
    row_ids = jnp.broadcast_to(row_ids, (field_count, 2, DEPTH_SHELLS, devices, SEND_MOST, CELLS))
    blocks = jnp.take_along_axis(tiles, row_ids, axis=4)
    blocks = blocks.reshape(field_count, 2, DEPTH_SHELLS, devices * SEND_MOST, CELLS)
    slot_ids = shift_filled_by_lane.reshape(2, devices, devices * SEND_MOST)
    dest_ids = receiving_processor.reshape(2, devices * SEND_MOST).astype(jnp.int32)
    device_ids = jnp.arange(devices, dtype=jnp.int32)
    pieces = []
    for patch in range(2):
        reach = dest_ids[1 - patch][None, :] == device_ids[:, None]
        matches = (slot_ids[patch][:, :, None] == jnp.arange(offset_count, dtype=jnp.int32)[None, None, :]) & reach[:, :, None]
        source_pos = jnp.argmax(matches, axis=1).astype(jnp.int32)
        live = jnp.any(matches, axis=1).astype(stack.dtype)
        other = blocks[:, 1 - patch]
        taken = other[:, :, source_pos.reshape(-1), :]
        taken = taken.reshape(field_count, DEPTH_SHELLS, devices, offset_count, CELLS)
        pieces.append(taken * live[None, None, :, :, None])
    chosen = jnp.stack(pieces, axis=1)
    weights = blending_factors.reshape(2, devices, offset_count, CELLS, CELLS)
    cycle_vals = jnp.einsum("pdojc,fpkdoc->fpkdoj", weights, chosen, precision=PRECISE)
    cycle_vals = cycle_vals.reshape(field_count, 2, DEPTH_SHELLS, N_LAT, N_LON, SIDES, TERMS, CELLS).sum(axis=6)
    return cycle_vals


def widen_sector(stack, departing_bands, receiving_processor, shift_filled_by_lane, blending_factors):
    field_count = stack.shape[0]
    cycle_vals = cycle_cells(stack, departing_bands, receiving_processor, shift_filled_by_lane, blending_factors)
    bordered_mesh = jnp.pad(stack, ((0, 0), (0, 0), (1, 1), (1, 1), (1, 1)))
    upper = cycle_vals[:, :, :, 0, :, 0, :].reshape(field_count, 2, DEPTH_SHELLS, AZIMUTH_STRIPS)
    lower = cycle_vals[:, :, :, N_LAT - 1, :, 1, :].reshape(field_count, 2, DEPTH_SHELLS, AZIMUTH_STRIPS)
    before = cycle_vals[:, :, :, :, 0, 2, :].reshape(field_count, 2, DEPTH_SHELLS, POLAR_ANGLE_BANDS)
    after = cycle_vals[:, :, :, :, N_LON - 1, 3, :].reshape(field_count, 2, DEPTH_SHELLS, POLAR_ANGLE_BANDS)
    bordered_mesh = bordered_mesh.at[:, :, 1:-1, 0, 1:-1].add(upper)
    bordered_mesh = bordered_mesh.at[:, :, 1:-1, -1, 1:-1].add(lower)
    bordered_mesh = bordered_mesh.at[:, :, 1:-1, 1:-1, 0].add(before)
    bordered_mesh = bordered_mesh.at[:, :, 1:-1, 1:-1, -1].add(after)
    return bordered_mesh


def creeping_flow_relaxation(bordered_mesh, earth_interior_fields, thermal_mesh, resistive_friction, boundary_entries, main_coefficient):
    adjacent_neighbour_entry = neighbours(bordered_mesh)
    second_derivative_sum = sum(face * (other - earth_interior_fields) for face, other in zip(boundary_entries, adjacent_neighbour_entry))
    middle_entry = [(adjacent_neighbour_entry[2 * axis_extent] - adjacent_neighbour_entry[2 * axis_extent + 1]) * 0.5 for axis_extent in range(3)]
    divergence = middle_entry[0][0] + middle_entry[1][1] + middle_entry[2][2]
    depthwise = earth_interior_fields[0] + 0.8 * (1.0 * thermal_mesh + second_derivative_sum[0] - middle_entry[0][3]) / main_coefficient
    colat = earth_interior_fields[1] + 0.8 * (second_derivative_sum[1] - middle_entry[1][3]) / main_coefficient
    longit = earth_interior_fields[2] + 0.8 * (second_derivative_sum[2] - middle_entry[2][3]) / main_coefficient
    pressure_new = earth_interior_fields[3] - 0.25 * resistive_friction * divergence
    return jnp.stack([depthwise, colat, longit, pressure_new])


def heat_update(bordered_mesh, thermal_mesh, carried_along):
    adjacent_neighbour_entry = neighbours(bordered_mesh)
    transport_flow = jnp.zeros_like(thermal_mesh)
    for axis_extent in range(3):
        flow_magnitude = carried_along[axis_extent]
        transport_flow = transport_flow + jnp.maximum(flow_magnitude, 0.0) * (thermal_mesh - adjacent_neighbour_entry[2 * axis_extent + 1])
        transport_flow = transport_flow + jnp.minimum(flow_magnitude, 0.0) * (adjacent_neighbour_entry[2 * axis_extent] - thermal_mesh)
    second_derivative_sum = sum(adjacent_neighbour_entry) - 6.0 * thermal_mesh
    return thermal_mesh + 0.1 * (1.0 * second_derivative_sum - transport_flow)


def reference(flow_vector, normal_stress, thermal_field, shear_resistance, departing_bands, receiving_processor, shift_filled_by_lane, blending_factors):
    rim = jnp.pad(shear_resistance, ((0, 0), (1, 1), (1, 1), (1, 1)), mode="edge")
    boundary_entries = tuple(0.5 * (shear_resistance + other) for other in neighbours(rim))
    main_coefficient = sum(boundary_entries)
    earth_interior_fields = jnp.concatenate([flow_vector, normal_stress[None]], axis=0)
    for sweep in range(SWEEPS):
        bordered_mesh = widen_sector(earth_interior_fields, departing_bands, receiving_processor, shift_filled_by_lane, blending_factors)
        earth_interior_fields = creeping_flow_relaxation(bordered_mesh, earth_interior_fields, thermal_field, shear_resistance, boundary_entries, main_coefficient)
    bordered_heat = widen_sector(thermal_field[None], departing_bands, receiving_processor, shift_filled_by_lane, blending_factors)[0]
    bordered_heat = bordered_heat.at[..., 0, :, :].set(1.0)
    thermal_following = heat_update(bordered_heat, thermal_field, earth_interior_fields[:3])
    return earth_interior_fields[:3], earth_interior_fields[3], thermal_following
```

```python
import functools

import jax
import jax.numpy as jnp
from jax import lax
from jax.experimental import pallas as pl
from jax.experimental.pallas import tpu as pltpu
from jax.sharding import PartitionSpec as P

SWEEPS = 4
CELLS = 128
BLOCKS = 16
F32 = jnp.float32
VMEM = pl.BlockSpec(memory_space=pltpu.VMEM)
SMEM = pl.BlockSpec(memory_space=pltpu.SMEM)
PARAMS = pltpu.CompilerParams(vmem_limit_bytes=32 * 1024 * 1024)


def west_lane(f):
    return 2 * f


def east_lane(f):
    return (2 * f - 1) % CELLS


def lanes():
    return lax.broadcasted_iota(jnp.int32, (8, CELLS), 1)


def sublanes():
    return lax.broadcasted_iota(jnp.int32, (8, CELLS), 0)


def roll_lanes(x, shift):
    shift = shift % CELLS
    return x if shift == 0 else pltpu.roll(x, shift, 1)


def ghost_columns(west, east, count, rows_ref, cols_ref):
    for f in range(count):
        rows_ref[west_lane(f), :] = west[f, :]
        rows_ref[east_lane(f), :] = east[f, :]
    cols_ref[...] = rows_ref[...].T


def collect_edges(planes, count, rows_ref, cols_ref, north, south, west, east):
    lane = lanes()
    for b in range(BLOCKS):
        gathered = jnp.zeros((8, CELLS), F32)
        for f in range(count):
            here = planes(f)[8 * b : 8 * b + 8, :]
            mine = (lane == west_lane(f)) | (lane == east_lane(f))
            gathered = jnp.where(mine, roll_lanes(here, 2 * f), gathered)
        cols_ref[8 * b : 8 * b + 8, :] = gathered
    rows_ref[...] = cols_ref[...].T
    for f in range(count):
        west[f, :] = rows_ref[west_lane(f), :]
        east[f, :] = rows_ref[east_lane(f), :]
        north[f, :] = planes(f)[0, :]
        south[f, :] = planes(f)[CELLS - 1, :]


def around(ref, b, north, south, column, f):
    lo = 8 * b
    here = ref[lo : lo + 8, :]
    sub, lane = sublanes(), lanes()
    if b == 0:
        up = jnp.where(sub == 0, north, pltpu.roll(here, 1, 0))
    else:
        up = ref[lo - 1 : lo + 7, :]
    if b == BLOCKS - 1:
        down = jnp.where(sub == 7, south, pltpu.roll(here, 7, 0))
    else:
        down = ref[lo + 1 : lo + 9, :]
    turned = roll_lanes(column, -2 * f)
    left = jnp.where(lane == 0, turned, pltpu.roll(here, 1, 1))
    right = jnp.where(lane == CELLS - 1, turned, pltpu.roll(here, CELLS - 1, 1))
    return here, up, down, left, right


def start_kernel(meta, flow, pressure, heat, friction, row, north, south, west, east, rows_s, cols_s):
    def planes(f):
        if f < 6:
            return flow.at[f]
        if f < 8:
            return pressure.at[f - 6]
        if f < 10:
            return heat.at[f - 8]
        return friction.at[f - 10]

    at = meta[0]
    for f in range(10):
        row[f, :] = planes(f)[pl.ds(at, 1), :][0]
    collect_edges(planes, 12, rows_s, cols_s, north, south, west, east)


def coefficient_kernel(meta, friction, heat, north, south, west, east, out, rows_s, cols_s):
    lane = lanes()
    sub = sublanes()
    for k in range(2):
        rows_s[west_lane(k), :] = west[10 + k, :]
        rows_s[east_lane(k), :] = east[10 + k, :]
    cols_s[...] = rows_s[...].T
    at_north, at_south = meta[9] > 0, meta[10] > 0
    at_west, at_east = meta[11] > 0, meta[12] > 0
    for b in range(BLOCKS):
        lo = 8 * b
        centre = [friction[k, lo : lo + 8, :] for k in range(2)]
        for k in range(2):
            here, up, down, left, right = around(
                friction.at[k],
                b,
                north[10 + k : 11 + k, :],
                south[10 + k : 11 + k, :],
                cols_s[lo : lo + 8, :],
                k,
            )
            if b == 0:
                up = jnp.where((sub == 0) & at_north, here, up)
            if b == BLOCKS - 1:
                down = jnp.where((sub == 7) & at_south, here, down)
            left = jnp.where((lane == 0) & at_west, here, left)
            right = jnp.where((lane == CELLS - 1) & at_east, here, right)
            faces = [0.5 * (here + other) for other in (up, down, left, right)]
            between = 0.5 * (centre[0] + centre[1])
            diagonal = (faces[0] + faces[1]) + (faces[2] + faces[3]) + (between + here)
            inverse = 0.8 / diagonal
            for n, face in enumerate(faces):
                out[n, k, lo : lo + 8, :] = inverse * face
            out[4, k, lo : lo + 8, :] = inverse * between
            out[5, k, lo : lo + 8, :] = 0.5 * inverse
            out[6, k, lo : lo + 8, :] = inverse * heat[k, lo : lo + 8, :]
            out[7, k, lo : lo + 8, :] = 0.125 * here


def split(x):
    high = x.astype(jnp.bfloat16)
    return high, (x - high.astype(F32)).astype(jnp.bfloat16)


def blended(block, weights):
    dims = (((1,), (1,)), ((), ()))
    b_high, b_low = split(block)
    w_high, w_low = split(weights)
    out = lax.dot_general(b_high, w_low, dims, preferred_element_type=F32)
    out = out + lax.dot_general(b_low, w_high, dims, preferred_element_type=F32)
    return out + lax.dot_general(b_high, w_high, dims, preferred_element_type=F32)


def fill_ghosts(meta, halos, arrived, weights, ghosts, count):
    for side in range(4):
        ghosts[side, :count, :] = halos[side][:count, :]

        @pl.when(meta[9 + side] > 0)
        def _():
            total = ghosts[side, :count, :]
            for term in range(2):
                offset = 2 * side + term
                total = total + blended(arrived[meta[1 + offset]], weights[offset])
            ghosts[side, :count, :] = total


def relaxed_block(coef, flow, pressure, ghosts, column, b):
    lo = 8 * b
    half = [coef[5, k, lo : lo + 8, :] for k in range(2)]
    turn = {}
    for f in range(8):
        ref = flow.at[f] if f < 6 else pressure.at[f - 6]
        turn[f] = around(ref, b, ghosts[0, f : f + 1, :], ghosts[1, f : f + 1, :], column, f)
    new = []
    for component in range(3):
        for k in range(2):
            here, up, down, left, right = turn[2 * component + k]
            vertical = turn[2 * component + 1 - k][0]
            value = 0.2 * here
            value = value + coef[0, k, lo : lo + 8, :] * up
            value = value + coef[1, k, lo : lo + 8, :] * down
            value = value + coef[2, k, lo : lo + 8, :] * left
            value = value + coef[3, k, lo : lo + 8, :] * right
            value = value + coef[4, k, lo : lo + 8, :] * vertical
            if component == 0:
                value = value + coef[6, k, lo : lo + 8, :]
                other = turn[6 + 1 - k][0]
                value = value - half[k] * other if k == 0 else value + half[k] * other
            elif component == 1:
                value = value - half[k] * (turn[6 + k][2] - turn[6 + k][1])
            else:
                value = value - half[k] * (turn[6 + k][4] - turn[6 + k][3])
            new.append(value)
    for k in range(2):
        other = turn[1 - k][0]
        divergence = (turn[2 + k][2] - turn[2 + k][1]) + (turn[4 + k][4] - turn[4 + k][3])
        divergence = divergence + other if k == 0 else divergence - other
        new.append(turn[6 + k][0] - coef[7, k, lo : lo + 8, :] * divergence)
    return new


def sweep_kernel(
    count, meta, flow, pressure, coef, north, south, west, east, arrived, weights, *rest
):
    if count > 8:
        (flow_out, pressure_out, row, n_out, s_out, w_out, e_out, heat_out) = rest[:8]
    else:
        (flow_out, pressure_out, row, n_out, s_out, w_out, e_out) = rest[:7]
    ghosts, rows_s, cols_s, edge_s = rest[-4:]
    fill_ghosts(meta, (north, south, west, east), arrived, weights, ghosts, count)
    ghost_columns(ghosts.at[2], ghosts.at[3], 8, rows_s, cols_s)
    lane = lanes()
    for b in range(BLOCKS):
        lo = 8 * b
        new = relaxed_block(coef, flow, pressure, ghosts, cols_s[lo : lo + 8, :], b)
        gathered = jnp.zeros((8, CELLS), F32)
        for f in range(8):
            if f < 6:
                flow_out[f, lo : lo + 8, :] = new[f]
            else:
                pressure_out[f - 6, lo : lo + 8, :] = new[f]
            mine = (lane == west_lane(f)) | (lane == east_lane(f))
            gathered = jnp.where(mine, roll_lanes(new[f], 2 * f), gathered)
            if b == 0:
                n_out[f : f + 1, :] = new[f][0:1, :]
            if b == BLOCKS - 1:
                s_out[f : f + 1, :] = new[f][7:8, :]
        edge_s[lo : lo + 8, :] = gathered
    at = meta[0]
    for f in range(8):
        ref = flow_out.at[f] if f < 6 else pressure_out.at[f - 6]
        row[f, :] = ref[pl.ds(at, 1), :][0]
    rows_s[...] = edge_s[...].T
    for f in range(8):
        w_out[f, :] = rows_s[west_lane(f), :]
        e_out[f, :] = rows_s[east_lane(f), :]
    if count > 8:
        for side in range(4):
            heat_out[side, :, :] = ghosts[side, 8:10, :]


def final_kernel(
    meta, flow, pressure, coef, north, south, west, east, arrived, weights, heat, heat_ghosts,
    flow_out, pressure_out, heat_out, ghosts, rows_s, cols_s, heat_cols_s,
):
    ghost_columns(heat_ghosts.at[2], heat_ghosts.at[3], 2, rows_s, heat_cols_s)
    fill_ghosts(meta, (north, south, west, east), arrived, weights, ghosts, 8)
    ghost_columns(ghosts.at[2], ghosts.at[3], 8, rows_s, cols_s)
    for b in range(BLOCKS):
        lo = 8 * b
        new = relaxed_block(coef, flow, pressure, ghosts, cols_s[lo : lo + 8, :], b)
        for f in range(8):
            if f < 6:
                flow_out[f, lo : lo + 8, :] = new[f]
            else:
                pressure_out[f - 6, lo : lo + 8, :] = new[f]
        layers = [
            around(
                heat.at[k],
                b,
                heat_ghosts[0, k : k + 1, :],
                heat_ghosts[1, k : k + 1, :],
                heat_cols_s[lo : lo + 8, :],
                k,
            )
            for k in range(2)
        ]
        for k in range(2):
            here, up, down, left, right = layers[k]
            below = jnp.ones((8, CELLS), F32) if k == 0 else layers[0][0]
            above = layers[1][0] if k == 0 else jnp.zeros((8, CELLS), F32)
            advect = jnp.zeros((8, CELLS), F32)
            for component, minus, plus in ((0, below, above), (1, up, down), (2, left, right)):
                speed = new[2 * component + k]
                advect = advect + jnp.maximum(speed, 0.0) * (here - minus)
                advect = advect + jnp.minimum(speed, 0.0) * (plus - here)
            spread = (up + down) + (left + right) + (below + above) - 6.0 * here
            heat_out[k, lo : lo + 8, :] = here + 0.1 * (spread - advect)


def shape(*dims):
    return jax.ShapeDtypeStruct(dims, F32)


def square(*lead):
    return pltpu.VMEM((*lead, CELLS, CELLS), F32)


def call(kernel, outs, ins, scratch):
    return pl.pallas_call(
        kernel,
        out_shape=outs,
        in_specs=[SMEM] + [VMEM] * (len(ins) - 1),
        out_specs=[VMEM] * len(outs),
        scratch_shapes=scratch,
        compiler_params=PARAMS,
    )(*ins)


def shards(
    flow_vector,
    normal_stress,
    thermal_field,
    shear_resistance,
    departing_bands,
    receiving_processor,
    shift_filled_by_lane,
    blending_factors,
):
    flow = flow_vector.reshape(6, CELLS, CELLS)
    pressure = normal_stress[0]
    heat = thermal_field[0]
    friction = shear_resistance[0]
    weights = blending_factors.reshape(8, CELLS, CELLS)
    slots = shift_filled_by_lane.reshape(CELLS)
    lat, lon = lax.axis_index("lat"), lax.axis_index("lon")
    n_lat, n_lon = lax.axis_size("lat"), lax.axis_size("lon")

    named = slots[None, :] == jnp.arange(8, dtype=jnp.int32)[:, None]
    position = jnp.sum(jnp.where(named, jnp.arange(CELLS, dtype=jnp.int32)[None, :], 0), axis=1)
    on_edge = jnp.stack([lat == 0, lat == n_lat - 1, lon == 0, lon == n_lon - 1]).astype(jnp.int32)
    own_row = departing_bands.reshape(1)
    meta = jnp.concatenate([own_row, position, on_edge])

    def swap(x):
        return lax.ppermute(x, "patch", [(0, 1), (1, 0)])

    target = swap(receiving_processor.reshape(1).astype(F32))
    chosen = jnp.arange(n_lat * n_lon, dtype=jnp.int32).astype(F32) == target

    def deliver(row):
        crossed = swap(row)
        sent = jnp.where(chosen[:, None, None], crossed[None], 0.0)
        return lax.all_to_all(sent, ("lat", "lon"), 0, 0, tiled=True)

    def exchange(north, south, west, east):
        up = [(i + 1, i) for i in range(n_lat - 1)]
        down = [(i, i + 1) for i in range(n_lat - 1)]
        left = [(i + 1, i) for i in range(n_lon - 1)]
        right = [(i, i + 1) for i in range(n_lon - 1)]
        return (
            lax.ppermute(south, "lat", down),
            lax.ppermute(north, "lat", up),
            lax.ppermute(east, "lon", right),
            lax.ppermute(west, "lon", left),
        )

    edges = [shape(12, CELLS)] * 4
    row, *sides = call(
        start_kernel,
        [shape(10, CELLS)] + edges,
        (meta[:1], flow, pressure, heat, friction),
        [square(), square()],
    )
    arrived = deliver(row)
    halos = exchange(*sides)
    (coef,) = call(
        coefficient_kernel,
        [shape(8, 2, CELLS, CELLS)],
        (meta, friction, heat, *halos),
        [square(), square()],
    )
    state = [shape(6, CELLS, CELLS), shape(2, CELLS, CELLS)]
    heat_ghosts = None
    for sweep in range(SWEEPS - 1):
        count = 10 if sweep == 0 else 8
        outs = state + [shape(8, CELLS)] * 5 + ([shape(4, 2, CELLS)] if sweep == 0 else [])
        got = call(
            functools.partial(sweep_kernel, count),
            outs,
            (meta, flow, pressure, coef, *halos, arrived, weights),
            [pltpu.VMEM((4, count, CELLS), F32), square(), square(), square()],
        )
        flow, pressure, row = got[:3]
        if sweep == 0:
            heat_ghosts = got[7]
        arrived = deliver(row)
        halos = exchange(*got[3:7])
    flow, pressure, heat = call(
        final_kernel,
        state + [shape(2, CELLS, CELLS)],
        (meta, flow, pressure, coef, *halos, arrived, weights, heat, heat_ghosts),
        [pltpu.VMEM((4, 8, CELLS), F32), square(), square(), square()],
    )
    return flow.reshape(3, 1, 2, CELLS, CELLS), pressure[None], heat[None]


def solution(mesh):
    placed = (
        P(None, "patch", None, "lat", "lon"),
        P("patch", None, "lat", "lon"),
        P("patch", None, "lat", "lon"),
        P("patch", None, "lat", "lon"),
        P("patch", "lat", "lon", None),
        P("patch", "lat", "lon", None),
        P("patch", "lat", "lon", None),
        P("patch", "lat", "lon", None, None, None),
    )
    return jax.shard_map(
        shards,
        mesh=mesh,
        in_specs=placed,
        out_specs=(
            P(None, "patch", None, "lat", "lon"),
            P("patch", None, "lat", "lon"),
            P("patch", None, "lat", "lon"),
        ),
        check_vma=False,
    )
```

```python
import jax
import jax.numpy as jnp
from jax import lax
from jax.experimental import pallas as pl
from jax.experimental.pallas import tpu as pltpu
from jax.sharding import PartitionSpec as P

SWEEPS = 4
CELLS = 128
TILES = 16
ROWS = CELLS + 16
LANES = 2 * CELLS
HALO = 4
PLANES = 12
F32 = jnp.float32
VMEM = pl.BlockSpec(memory_space=pltpu.VMEM)
SMEM = pl.BlockSpec(memory_space=pltpu.SMEM)
ANY = pl.BlockSpec(memory_space=pl.ANY)
NORTH, SOUTH, WEST, EAST = 1, 2, 3, 4
PLACES = 5
LAT_BASE, LON_BASE = 17, 18


def lanes():
    return lax.broadcasted_iota(jnp.int32, (8, CELLS), 1)


def sublanes():
    return lax.broadcasted_iota(jnp.int32, (8, CELLS), 0)


def turn(x, shift):
    shift = shift % CELLS
    return x if shift == 0 else pltpu.roll(x, shift, 1)


def tile(b):
    return pl.ds(8 * b, 8)


def plane_of(flow, pressure, heat, friction, f):
    if f < 6:
        return flow.at[f]
    if f < 8:
        return pressure.at[f - 6]
    if f < 10:
        return heat.at[f - 8]
    return friction.at[f - 10]


def start_kernel(at, slots, flow, pressure, heat, friction, weights, row, top, bottom, near, sems):
    start = pl.multiple_of((at[0] // 8) * 8, 8)
    copies = []

    def fetch(source, target):
        copy = pltpu.make_async_copy(source, target, sems.at[len(copies)])
        copy.start()
        copies.append(copy)

    fetch(flow.at[:, pl.ds(start, 8), :], near.at[0:6])
    fetch(pressure.at[:, pl.ds(start, 8), :], near.at[6:8])
    fetch(heat.at[:, pl.ds(start, 8), :], near.at[8:10])
    for out, lo in ((top, 0), (bottom, CELLS - 8)):
        fetch(flow.at[:, lo : lo + 8, :], out.at[0:6])
        fetch(pressure.at[:, lo : lo + 8, :], out.at[6:8])
        fetch(heat.at[:, lo : lo + 8, :], out.at[8:10])
        fetch(friction.at[:, lo : lo + 8, :], out.at[10:12])
        fetch(weights.at[4:8, lo : lo + 8, :], out.at[12:16])
    named = jnp.broadcast_to(slots[...], (8, CELLS)) == sublanes()
    place = jnp.sum(jnp.where(named, lanes(), 0).astype(F32), axis=1, keepdims=True)
    top[16] = jnp.broadcast_to(place, (8, CELLS))
    bottom[16] = jnp.broadcast_to(place, (8, CELLS))
    row[...] = jnp.zeros((16, CELLS), F32)
    for copy in copies:
        copy.wait()
    inside = at[0] - start
    for f in range(10):
        row[f : f + 1, :] = near[f, pl.ds(inside, 1), :]


def fill_kernel(chunks, row, out):
    out[...] = jnp.zeros((CELLS, 8, CELLS), F32)
    for n in range(5):
        out[chunks[n]] = row[0:8, :]
    out[chunks[5]] = row[8:16, :]


def refill_kernel(chunks, row, old, out):
    del old
    for n in range(5):
        out[chunks[n]] = row[...]


def columns_kernel(flow, pressure, heat, friction, weights, north, south, to_west, to_east, cols_s, rows_s):
    lane = lanes()

    def pack(block):
        gathered = jnp.zeros((8, CELLS), F32)
        for f in range(PLANES):
            gathered = jnp.where(lane // 8 == f, turn(block(f), 8 * f + HALO), gathered)
        return gathered

    def unload(first):
        rows_s[...] = cols_s[...].T
        for f in range(PLANES):
            lo = first + HALO * f
            to_east[lo : lo + HALO, :] = rows_s[8 * f : 8 * f + HALO, :]
            to_west[lo : lo + HALO, :] = rows_s[8 * f + HALO : 8 * f + 8, :]

    for b in range(TILES):
        cols_s[tile(b), :] = pack(lambda f: plane_of(flow, pressure, heat, friction, f)[tile(b), :])
    unload(0)
    cols_s[tile(TILES - 1), :] = pack(lambda f: north[f])
    cols_s[tile(0), :] = pack(lambda f: south[f])
    unload(HALO * PLANES)
    for n in range(4):
        lo = 2 * HALO * PLANES + 8 * n
        to_west[lo : lo + 8, :] = weights[n, 0:8, :]
        to_east[lo : lo + 8, :] = weights[n, CELLS - 8 : CELLS, :]


def sideways(first, second):
    lane = lanes()
    f_up, s_up = pltpu.roll(first, 1, 1), pltpu.roll(second, 1, 1)
    f_down, s_down = pltpu.roll(first, CELLS - 1, 1), pltpu.roll(second, CELLS - 1, 1)
    lefts = (jnp.where(lane == 0, s_up, f_up), jnp.where(lane == 0, f_up, s_up))
    rights = (
        jnp.where(lane == CELLS - 1, s_down, f_down),
        jnp.where(lane == CELLS - 1, f_down, s_down),
    )
    return lefts, rights


def around(ref, b, halves):
    both = [ref[half, tile(b), :] for half in range(2)]
    lefts, rights = sideways(*both)
    found = []
    for half in range(halves):
        up = pltpu.roll(both[half], 1, 0) if b == 0 else ref[half, 8 * b - 1 : 8 * b + 7, :]
        down = pltpu.roll(both[half], 7, 0) if b == TILES + 1 else ref[half, 8 * b + 1 : 8 * b + 9, :]
        found.append((both[half], up, down, lefts[half], rights[half]))
    return found


def build_kernel(
    ints, flow, pressure, heat, friction, north, south, west, east,
    fields, coef, warm, mixed, thick, cols_s, rows_s,
):
    lane = lanes()

    def target(f):
        if f < 8:
            return fields.at[f]
        return warm.at[f - 8] if f < 10 else thick.at[f - 10]

    outer = (lane < HALO) | (lane >= CELLS - HALO)

    def load(first):
        for f in range(PLANES):
            lo = first + HALO * f
            rows_s[8 * f : 8 * f + HALO, :] = west[lo : lo + HALO, :]
            rows_s[8 * f + HALO : 8 * f + 8, :] = east[lo : lo + HALO, :]
        cols_s[...] = rows_s[...].T

    def place(f, b, block):
        target(f)[1, tile(b), :] = jnp.where(outer, turn(block, -8 * f - HALO), 0.0)

    rows_s[8 * PLANES : CELLS, :] = jnp.zeros((CELLS - 8 * PLANES, CELLS), F32)
    load(0)
    for f in range(PLANES):
        source = plane_of(flow, pressure, heat, friction, f)
        target(f)[0, tile(0), :] = north[f]
        target(f)[0, tile(TILES + 1), :] = south[f]
        for b in range(TILES):
            target(f)[0, tile(b + 1), :] = source[tile(b), :]
            place(f, b + 1, cols_s[tile(b), :])
    load(HALO * PLANES)
    for f in range(PLANES):
        place(f, 0, cols_s[tile(TILES - 1), :])
        place(f, TILES + 1, cols_s[tile(0), :])

    at_north, at_south = ints[NORTH] > 0, ints[SOUTH] > 0
    at_west, at_east = ints[WEST] > 0, ints[EAST] > 0
    for k in range(2):
        for half in range(2):
            first = jnp.broadcast_to(thick[k, half, 8:9, :], (8, CELLS))
            last = jnp.broadcast_to(thick[k, half, ROWS - 9 : ROWS - 8, :], (8, CELLS))
            for b, at_end, line in ((0, at_north, first), (TILES + 1, at_south, last)):
                thick[k, half, tile(b), :] = jnp.where(at_end, line, thick[k, half, tile(b), :])
        for b in range(TILES + 2):
            own, other = thick[k, 0, tile(b), :], thick[k, 1, tile(b), :]
            other = jnp.where((lane == CELLS - 1) & at_west, turn(own, -1), other)
            other = jnp.where((lane == 0) & at_east, turn(own, 1), other)
            thick[k, 1, tile(b), :] = jnp.where(other > 0.0, other, 1.0)

    for b in range(TILES + 2):
        found = [around(thick.at[k], b, 2) for k in range(2)]
        for half in range(2):
            between = 0.5 * (found[0][half][0] + found[1][half][0])
            for k in range(2):
                here, *others = found[k][half]
                faces = [0.5 * (here + other) for other in others]
                diagonal = (faces[0] + faces[1]) + (faces[2] + faces[3]) + (between + here)
                inverse = 0.8 / diagonal
                for n, face in enumerate(faces):
                    coef[n, k, half, tile(b), :] = inverse * face
                coef[4, k, half, tile(b), :] = inverse * between
                coef[5, k, half, tile(b), :] = 0.5 * inverse
                coef[6, k, half, tile(b), :] = inverse * warm[k, half, tile(b), :]
                coef[7, k, half, tile(b), :] = 0.125 * here

    mixed[...] = jnp.zeros((4, CELLS, CELLS), F32)
    for term in range(2):
        lo = pl.multiple_of(2 * HALO * PLANES + 8 * (ints[LAT_BASE] + term), 8)
        mixed[term, tile(TILES - 1), :] = west[pl.ds(lo, 8), :]
        mixed[term, tile(0), :] = east[pl.ds(lo, 8), :]
        mixed[2 + term, tile(TILES - 1), :] = north[8 + ints[LON_BASE] + term]
        mixed[2 + term, tile(0), :] = south[8 + ints[LON_BASE] + term]


def split(x):
    high = x.astype(jnp.bfloat16)
    return high, (x - high.astype(F32)).astype(jnp.bfloat16)


def blended(block, weights):
    dims = (((1,), (1,)), ((), ()))
    b_high, b_low = split(block)
    w_high, w_low = split(weights)
    out = lax.dot_general(b_high, w_low, dims, preferred_element_type=F32)
    out = out + lax.dot_general(b_low, w_high, dims, preferred_element_type=F32)
    return out + lax.dot_general(b_high, w_high, dims, preferred_element_type=F32)


def blend_sides(ints, arrived, weights, mixed, lat_ghost, lon_ghost):
    sides = (
        (lat_ghost, (ints[NORTH] + ints[SOUTH]) > 0, PLACES, ints[LAT_BASE], 0),
        (lon_ghost, (ints[WEST] + ints[EAST]) > 0, PLACES + 6, ints[LON_BASE], 2),
    )
    for ghost, active, places, base, near in sides:
        ghost[...] = jnp.zeros((8, LANES), F32)

        @pl.when(active)
        def _():
            own = jnp.zeros((8, CELLS), F32)
            ends = jnp.zeros((16, CELLS), F32)
            for term in range(2):
                own = own + blended(arrived[ints[places + term]], weights[base + term])
                low, high = arrived[ints[places + 2 + term]], arrived[ints[places + 4 + term]]
                ends = ends + blended(jnp.concatenate([low, high], axis=0), mixed[near + term])
            ghost[:, 0:CELLS] = own
            ghost[:, CELLS:LANES] = jnp.where(lanes() < CELLS // 2, ends[8:16], ends[0:8])


def blend_kernel(ints, fields, coef, arrived, weights, mixed, lat_ghost, lon_ghost, row, packed):
    blend_sides(ints, arrived, weights, mixed, lat_ghost, lon_ghost)
    at = ints[0] + 8
    lane, sub = lanes(), sublanes()
    for f in range(8):
        packed[0, f : f + 1, :] = fields[f, 0, pl.ds(at, 1), :]
        packed[1, f : f + 1, :] = fields[f, 1, pl.ds(at, 1), :]
        packed[2, f : f + 1, :] = fields[f, 0, pl.ds(at - 1, 1), :]
        packed[3, f : f + 1, :] = fields[f, 0, pl.ds(at + 1, 1), :]
    here, outside, up, down = packed[0], packed[1], packed[2], packed[3]
    up = jnp.where((ints[NORTH] > 0) & (at == 8), lat_ghost[:, 0:CELLS], up)
    down = jnp.where((ints[SOUTH] > 0) & (at == CELLS + 7), lat_ghost[:, 0:CELLS], down)
    beside = jnp.sum(jnp.where(lane == ints[0], lon_ghost[:, 0:CELLS], 0.0), axis=1, keepdims=True)
    on_side = ((lane == CELLS - 1) & (ints[WEST] > 0)) | ((lane == 0) & (ints[EAST] > 0))
    outside = jnp.where(on_side, beside, outside)
    lefts, rights = sideways(here, outside)
    left, right = lefts[0], rights[0]
    even = sub % 2 == 0

    def factor(n):
        return jnp.where(even, coef[n, 0, 0, pl.ds(at, 1), :], coef[n, 1, 0, pl.ds(at, 1), :])

    partner = jnp.where(even, pltpu.roll(here, 7, 0), pltpu.roll(here, 1, 0))
    value = 0.2 * here + factor(0) * up + factor(1) * down
    value = value + factor(2) * left + factor(3) * right + factor(4) * partner
    value = value + jnp.where(sub < 2, factor(6), 0.0)
    steps = (jnp.where(even, partner, -partner), down - up, right - left)
    slope = jnp.where(
        sub < 2,
        pltpu.roll(steps[0], 2, 0),
        jnp.where(sub < 4, pltpu.roll(steps[1], 4, 0), pltpu.roll(steps[2], 6, 0)),
    )
    value = value - factor(5) * slope
    divergence = (
        pltpu.roll(steps[0], 6, 0) + pltpu.roll(steps[1], 4, 0) + pltpu.roll(steps[2], 2, 0)
    )
    row[...] = jnp.where(sub < 6, value, here - factor(7) * divergence)


def with_ghosts(ints, count, fields, lat_ghost, lon_ghost, full, cols_s, ends_s, rows_s):
    lane, sub = lanes(), sublanes()
    rows_s[...] = jnp.zeros((CELLS, CELLS), F32)
    for cut, out in ((slice(0, CELLS), cols_s), (slice(CELLS, LANES), ends_s)):
        for f in range(count):
            rows_s[2 * f : 2 * f + 1, :] = lon_ghost[f : f + 1, cut]
            last = (2 * f - 1) % CELLS
            rows_s[last : last + 1, :] = lon_ghost[f : f + 1, cut]
        out[...] = rows_s[...].T
    at_north, at_south = ints[NORTH] > 0, ints[SOUTH] > 0
    on_side = ((lane == CELLS - 1) & (ints[WEST] > 0)) | ((lane == 0) & (ints[EAST] > 0))
    for b in range(TILES + 2):
        if b == 0:
            column = ends_s[tile(TILES - 1), :]
        elif b == TILES + 1:
            column = ends_s[tile(0), :]
        else:
            column = cols_s[tile(b - 1), :]
        for f in range(count):
            own, other = fields[f, 0, tile(b), :], fields[f, 1, tile(b), :]
            if b == 0 or b == TILES + 1:
                edge = (sub == 7) & at_north if b == 0 else (sub == 0) & at_south
                own = jnp.where(edge, lat_ghost[f : f + 1, 0:CELLS], own)
                other = jnp.where(edge, lat_ghost[f : f + 1, CELLS:LANES], other)
            full[f, 0, tile(b), :] = own
            full[f, 1, tile(b), :] = jnp.where(on_side, turn(column, -2 * f), other)


def relaxed(full, coef, b, halves):
    found = [around(full.at[f], b, halves) for f in range(8)]
    answers = []
    for half in range(halves):
        at = [found[f][half] for f in range(8)]

        def factor(n, k):
            return coef[n, k, half, tile(b), :]

        new = []
        for component in range(3):
            for k in range(2):
                here, up, down, left, right = at[2 * component + k]
                value = 0.2 * here + factor(0, k) * up + factor(1, k) * down
                value = value + factor(2, k) * left + factor(3, k) * right
                value = value + factor(4, k) * at[2 * component + 1 - k][0]
                if component == 0:
                    value = value + factor(6, k)
                    slope = at[7][0] if k == 0 else -at[6][0]
                elif component == 1:
                    slope = at[6 + k][2] - at[6 + k][1]
                else:
                    slope = at[6 + k][4] - at[6 + k][3]
                new.append(value - factor(5, k) * slope)
        for k in range(2):
            divergence = (at[2 + k][2] - at[2 + k][1]) + (at[4 + k][4] - at[4 + k][3])
            divergence = divergence + at[1][0] if k == 0 else divergence - at[0][0]
            new.append(at[6 + k][0] - factor(7, k) * divergence)
        answers.append(new)
    return answers


def sweep_kernel(ints, fields, coef, lat_ghost, lon_ghost, out, full, cols_s, ends_s, rows_s):
    with_ghosts(ints, 8, fields, lat_ghost, lon_ghost, full, cols_s, ends_s, rows_s)
    for b in range(TILES + 2):
        for half, new in enumerate(relaxed(full, coef, b, 2)):
            for f in range(8):
                out[f, half, tile(b), :] = new[f]


def relay_kernel(places, arrived, out):
    for n in range(8):
        out[2 * n : 2 * n + 2, :] = arrived[places[n], 0:2, :]


def heat_kernel(ints, warm, blocks, weights, out, lat_ghost, lon_ghost, cols_s, ends_s, rows_s):
    sides = (
        (lat_ghost, (ints[NORTH] + ints[SOUTH]) > 0, ints[LAT_BASE]),
        (lon_ghost, (ints[WEST] + ints[EAST]) > 0, ints[LON_BASE]),
    )
    for ghost, active, base in sides:
        ghost[...] = jnp.zeros((8, LANES), F32)

        @pl.when(active)
        def _():
            total = jnp.zeros((16, CELLS), F32)
            for term in range(2):
                total = total + blended(blocks[base + term], weights[base + term])
            ghost[:, 0:CELLS] = total[0:8]

    with_ghosts(ints, 2, warm, lat_ghost, lon_ghost, out, cols_s, ends_s, rows_s)


def final_kernel(
    ints, fields, coef, arrived, weights, mixed, warm,
    flow_out, pressure_out, heat_out, lat_ghost, lon_ghost, full, cols_s, ends_s, rows_s,
):
    blend_sides(ints, arrived, weights, mixed, lat_ghost, lon_ghost)
    with_ghosts(ints, 8, fields, lat_ghost, lon_ghost, full, cols_s, ends_s, rows_s)
    for b in range(TILES):
        (new,) = relaxed(full, coef, b + 1, 1)
        for f in range(6):
            flow_out[f, tile(b), :] = new[f]
        for k in range(2):
            pressure_out[k, tile(b), :] = new[6 + k]
        layers = [around(warm.at[k], b + 1, 1)[0] for k in range(2)]
        for k in range(2):
            here, up, down, left, right = layers[k]
            below = jnp.ones((8, CELLS), F32) if k == 0 else layers[0][0]
            above = layers[1][0] if k == 0 else jnp.zeros((8, CELLS), F32)
            advect = jnp.zeros((8, CELLS), F32)
            for component, minus, plus in ((0, below, above), (1, up, down), (2, left, right)):
                speed = new[2 * component + k]
                advect = advect + jnp.maximum(speed, 0.0) * (here - minus)
                advect = advect + jnp.minimum(speed, 0.0) * (plus - here)
            spread = (up + down) + (left + right) + (below + above) - 6.0 * here
            heat_out[k, tile(b), :] = here + 0.1 * (spread - advect)


def shape(*dims):
    return jax.ShapeDtypeStruct(dims, F32)


def scratch(*dims):
    return pltpu.VMEM(dims, F32)


def call(kernel, outs, ins, scratches, specs=None, aliases=None, name=None):
    return pl.pallas_call(
        kernel,
        out_shape=outs,
        in_specs=specs or [SMEM] + [VMEM] * (len(ins) - 1),
        out_specs=[VMEM] * len(outs),
        scratch_shapes=scratches,
        input_output_aliases=aliases or {},
        compiler_params=pltpu.CompilerParams(vmem_limit_bytes=32 * 1024 * 1024),
        name=name,
    )(*ins)


def shards(
    flow_vector,
    normal_stress,
    thermal_field,
    shear_resistance,
    departing_bands,
    receiving_processor,
    shift_filled_by_lane,
    blending_factors,
):
    flow = flow_vector.reshape(6, CELLS, CELLS)
    pressure = normal_stress[0]
    heat = thermal_field[0]
    friction = shear_resistance[0]
    weights = blending_factors.reshape(8, CELLS, CELLS)
    lat, lon = lax.axis_index("lat"), lax.axis_index("lon")
    n_lat, n_lon = lax.axis_size("lat"), lax.axis_size("lon")
    devices = n_lat * n_lon
    own_row = departing_bands.reshape(1)

    def swap(x):
        return lax.ppermute(x, "patch", [(0, 1), (1, 0)])

    def ring(x, axis, step):
        count = lax.axis_size(axis)
        pairs = [(i, i + step) for i in range(count) if 0 <= i + step < count]
        return lax.ppermute(x, axis, pairs)

    def to_relay(x):
        return lax.ppermute(x, "lon", [(i, i ^ 2) for i in range(n_lon)])

    def deliver(buffer):
        return lax.all_to_all(buffer, ("lat", "lon"), 0, 0, tiled=True)

    receiver = swap(receiving_processor.reshape(1).astype(F32)).astype(jnp.int32)
    receiver = jnp.maximum(receiver, 0)
    near = receiver + jnp.array([0, 1, -1, n_lon, -n_lon], jnp.int32)
    near = jnp.where((near >= 0) & (near < devices), near, receiver)
    chunks = jnp.concatenate([near, receiver ^ 2])

    row, top, bottom = call(
        start_kernel,
        [shape(16, CELLS), shape(17, 8, CELLS), shape(17, 8, CELLS)],
        (own_row, shift_filled_by_lane.reshape(1, CELLS), flow, pressure, heat, friction, weights),
        [scratch(10, 8, CELLS), pltpu.SemaphoreType.DMA((13,))],
        specs=[SMEM, VMEM] + [ANY] * 5,
        name="start",
    )
    (buffer,) = call(
        fill_kernel, [shape(devices, 8, CELLS)], (chunks, swap(row)), [], name="fill"
    )
    arrived = deliver(buffer)
    north, south = ring(bottom, "lat", 1), ring(top, "lat", -1)
    wide = shape(2 * HALO * PLANES + 32, CELLS)
    to_west, to_east = call(
        columns_kernel,
        [wide, wide],
        (flow, pressure, heat, friction, weights, north, south),
        [scratch(CELLS, CELLS)] * 2,
        specs=[VMEM] * 7,
        name="columns",
    )
    places = top[16]
    to_west = jnp.concatenate([to_west, places])
    to_east = jnp.concatenate([to_east, places])
    west, east = ring(to_east, "lon", 1), ring(to_west, "lon", -1)

    def numbers(block):
        return block[:, 0].astype(jnp.int32)

    on_edge = jnp.stack([lat == 0, lat == n_lat - 1, lon == 0, lon == n_lon - 1]).astype(jnp.int32)
    own = numbers(places)

    def side(block, base, last):
        return jnp.where(last, block[base + 2 : base + 4], block[base : base + 2])

    pick = [side(numbers(x), 0, lat > 0) for x in (places, west[-8:], east[-8:])]
    pick += [side(numbers(x), 4, lon > 0) for x in (places, north[16], south[16])]
    bases = jnp.stack([jnp.where(lat > 0, 2, 0), jnp.where(lon > 0, 6, 4)]).astype(jnp.int32)
    ints = jnp.concatenate([own_row, on_edge] + pick + [bases])

    fields, coef, warm, mixed = call(
        build_kernel,
        [
            shape(8, 2, ROWS, CELLS),
            shape(8, 2, 2, ROWS, CELLS),
            shape(2, 2, ROWS, CELLS),
            shape(4, CELLS, CELLS),
        ],
        (ints, flow, pressure, heat, friction, north, south, west, east),
        [scratch(2, 2, ROWS, CELLS)] + [scratch(CELLS, CELLS)] * 2,
        name="build",
    )
    relayed = numbers(to_relay(places))
    squares = [scratch(CELLS, CELLS)] * 3
    ghost = shape(8, LANES)
    first_arrived = arrived
    for sweep in range(SWEEPS - 1):
        lat_ghost, lon_ghost, row = call(
            blend_kernel,
            [ghost, ghost, shape(8, CELLS)],
            (ints, fields, coef, arrived, weights, mixed),
            [scratch(4, 8, CELLS)],
            name="blend",
        )
        (buffer,) = call(
            refill_kernel,
            [shape(devices, 8, CELLS)],
            (chunks, swap(row), buffer),
            [],
            aliases={2: 0},
            name="refill",
        )
        arrived = deliver(buffer)
        (fields,) = call(
            sweep_kernel,
            [shape(8, 2, ROWS, CELLS)],
            (ints, fields, coef, lat_ghost, lon_ghost),
            [scratch(8, 2, ROWS, CELLS)] + squares,
            name="sweep",
        )
        if sweep == 0:
            (blocks,) = call(
                relay_kernel, [shape(16, CELLS)], (relayed, first_arrived), [], name="relay"
            )
            blocks = to_relay(blocks).reshape(8, 2, CELLS)
            blocks = jnp.pad(blocks, ((0, 0), (0, 14), (0, 0)))
            (warm,) = call(
                heat_kernel,
                [shape(2, 2, ROWS, CELLS)],
                (ints, warm, blocks, weights),
                [scratch(8, LANES)] * 2 + squares,
                name="heat",
            )
    flow, pressure, heat = call(
        final_kernel,
        [shape(6, CELLS, CELLS), shape(2, CELLS, CELLS), shape(2, CELLS, CELLS)],
        (ints, fields, coef, arrived, weights, mixed, warm),
        [scratch(8, LANES)] * 2 + [scratch(8, 2, ROWS, CELLS)] + squares,
        name="final",
    )
    return flow.reshape(3, 1, 2, CELLS, CELLS), pressure[None], heat[None]


def solution(mesh):
    placed = (
        P(None, "patch", None, "lat", "lon"),
        P("patch", None, "lat", "lon"),
        P("patch", None, "lat", "lon"),
        P("patch", None, "lat", "lon"),
        P("patch", "lat", "lon", None),
        P("patch", "lat", "lon", None),
        P("patch", "lat", "lon", None),
        P("patch", "lat", "lon", None, None, None),
    )
    return jax.shard_map(
        shards,
        mesh=mesh,
        in_specs=placed,
        out_specs=(
            P(None, "patch", None, "lat", "lon"),
            P("patch", None, "lat", "lon"),
            P("patch", None, "lat", "lon"),
        ),
        check_vma=False,
    )
```

```python
import jax
import jax.numpy as jnp
from jax import lax
from jax.experimental import pallas as pl
from jax.experimental.pallas import tpu as pltpu
from jax.sharding import PartitionSpec as P

SWEEPS = 4
CELLS = 128
TILES = 16
ROWS = CELLS + 16
LANES = 2 * CELLS
HALO = 4
PLANES = 12
F32 = jnp.float32
VMEM = pl.BlockSpec(memory_space=pltpu.VMEM)
SMEM = pl.BlockSpec(memory_space=pltpu.SMEM)
HBM = pl.BlockSpec(memory_space=pltpu.HBM)
NORTH, SOUTH, WEST, EAST = 1, 2, 3, 4
PLACES = 5
LAT_BASE, LON_BASE = 17, 18


def lanes():
    return lax.broadcasted_iota(jnp.int32, (8, CELLS), 1)


def sublanes():
    return lax.broadcasted_iota(jnp.int32, (8, CELLS), 0)


def turn(x, shift):
    shift = shift % CELLS
    return x if shift == 0 else pltpu.roll(x, shift, 1)


def tile(b):
    return pl.ds(8 * b, 8)


class Copies:
    def __init__(self, sems):
        self.sems, self.going = sems, []

    def start(self, source, target):
        copy = pltpu.make_async_copy(source, target, self.sems.at[len(self.going)])
        copy.start()
        self.going.append(copy)

    def wait(self, first=0, last=None):
        for copy in self.going[first:last]:
            copy.wait()


def start_kernel(
    at, slots, flow, pressure, heat, friction, weights, row, top, bottom, places, near, named, sems
):
    start = pl.multiple_of((at[0] // 8) * 8, 8)
    copies = Copies(sems)
    copies.start(slots, named)
    copies.start(flow.at[:, pl.ds(start, 8), :], near.at[0:6])
    copies.start(pressure.at[:, pl.ds(start, 8), :], near.at[6:8])
    copies.start(heat.at[:, pl.ds(start, 8), :], near.at[8:10])
    for out, lo in ((top, 0), (bottom, CELLS - 8)):
        copies.start(flow.at[:, lo : lo + 8, :], out.at[0:6])
        copies.start(pressure.at[:, lo : lo + 8, :], out.at[6:8])
        copies.start(heat.at[:, lo : lo + 8, :], out.at[8:10])
        copies.start(friction.at[:, lo : lo + 8, :], out.at[10:12])
        copies.start(weights.at[4:8, lo : lo + 8, :], out.at[12:16])
    row[...] = jnp.zeros((16, CELLS), F32)
    copies.wait()
    own = jnp.broadcast_to(named[...], (8, CELLS)) == sublanes()
    place = jnp.sum(jnp.where(own, lanes(), 0).astype(F32), axis=1, keepdims=True)
    place = jnp.broadcast_to(place, (8, CELLS))
    for out in (top.at[16], bottom.at[16], places):
        out[...] = place
    inside = at[0] - start
    for f in range(10):
        row[f : f + 1, :] = near[f, pl.ds(inside, 1), :]


def fill_kernel(chunks, row, out):
    out[...] = jnp.zeros((CELLS, 8, CELLS), F32)
    for n in range(5):
        out[chunks[n]] = row[0:8, :]
    out[chunks[5]] = row[8:16, :]


def refill_kernel(chunks, row, old, out):
    del old
    for n in range(5):
        out[chunks[n]] = row[...]


def columns_kernel(
    flow, pressure, heat, friction, weights, north, south, places,
    to_west, to_east, own, cols_s, rows_s, sems,
):
    lane = lanes()
    copies = Copies(sems)
    copies.start(flow, own.at[0:6])
    copies.start(pressure, own.at[6:8])
    copies.start(heat, own.at[8:10])
    copies.start(friction, own.at[10:12])
    for n in range(4):
        lo = 2 * HALO * PLANES + 8 * n
        copies.start(weights.at[n, 0:8, :], to_west.at[lo : lo + 8, :])
        copies.start(weights.at[n, CELLS - 8 : CELLS, :], to_east.at[lo : lo + 8, :])
    for out in (to_west, to_east):
        out[2 * HALO * PLANES + 32 :, :] = places[...]

    def pack(block):
        gathered = jnp.zeros((8, CELLS), F32)
        for f in range(PLANES):
            gathered = jnp.where(lane // 8 == f, turn(block(f), 8 * f + HALO), gathered)
        return gathered

    def unload(first):
        rows_s[...] = cols_s[...].T
        for f in range(PLANES):
            lo = first + HALO * f
            to_east[lo : lo + HALO, :] = rows_s[8 * f : 8 * f + HALO, :]
            to_west[lo : lo + HALO, :] = rows_s[8 * f + HALO : 8 * f + 8, :]

    cols_s[...] = jnp.zeros((CELLS, CELLS), F32)
    cols_s[tile(TILES - 1), :] = pack(lambda f: north[f])
    cols_s[tile(0), :] = pack(lambda f: south[f])
    unload(HALO * PLANES)
    copies.wait()
    for b in range(TILES):
        cols_s[tile(b), :] = pack(lambda f: own[f, tile(b), :])
    unload(0)


def sideways(first, second):
    lane = lanes()
    f_up, s_up = pltpu.roll(first, 1, 1), pltpu.roll(second, 1, 1)
    f_down, s_down = pltpu.roll(first, CELLS - 1, 1), pltpu.roll(second, CELLS - 1, 1)
    lefts = (jnp.where(lane == 0, s_up, f_up), jnp.where(lane == 0, f_up, s_up))
    rights = (
        jnp.where(lane == CELLS - 1, s_down, f_down),
        jnp.where(lane == CELLS - 1, f_down, s_down),
    )
    return lefts, rights


def around(ref, b, halves):
    both = [ref[half, tile(b), :] for half in range(2)]
    lefts, rights = sideways(*both)
    found = []
    for half in range(halves):
        up = pltpu.roll(both[half], 1, 0) if b == 0 else ref[half, 8 * b - 1 : 8 * b + 7, :]
        down = pltpu.roll(both[half], 7, 0) if b == TILES + 1 else ref[half, 8 * b + 1 : 8 * b + 9, :]
        found.append((both[half], up, down, lefts[half], rights[half]))
    return found


def build_kernel(
    ints, flow, pressure, heat, friction, weights, north, south, west, east,
    fields_out, coef_out, warm_out, strip, factors, high, low,
    fields, coef, warm, thick, chosen, cols_s, rows_s, sems,
):
    lane = lanes()
    copies = Copies(sems)
    inner = pl.ds(8, CELLS)
    copies.start(friction, thick.at[:, 0, inner, :])
    copies.start(heat, warm.at[:, 0, inner, :])
    copies.start(flow, fields.at[0:6, 0, inner, :])
    copies.start(pressure, fields.at[6:8, 0, inner, :])
    copies.start(weights.at[pl.ds(ints[LAT_BASE], 2)], chosen.at[0:2])
    copies.start(weights.at[pl.ds(ints[LON_BASE], 2)], chosen.at[2:4])

    def target(f):
        if f < 8:
            return fields.at[f]
        return warm.at[f - 8] if f < 10 else thick.at[f - 10]

    outer = (lane < HALO) | (lane >= CELLS - HALO)

    def load(first):
        for f in range(PLANES):
            lo = first + HALO * f
            rows_s[8 * f : 8 * f + HALO, :] = west[lo : lo + HALO, :]
            rows_s[8 * f + HALO : 8 * f + 8, :] = east[lo : lo + HALO, :]
        cols_s[...] = rows_s[...].T

    def place(f, b, block):
        target(f)[1, tile(b), :] = jnp.where(outer, turn(block, -8 * f - HALO), 0.0)

    rows_s[8 * PLANES : CELLS, :] = jnp.zeros((CELLS - 8 * PLANES, CELLS), F32)
    load(0)
    for f in range(PLANES):
        target(f)[0, tile(0), :] = north[f]
        target(f)[0, tile(TILES + 1), :] = south[f]
        for b in range(TILES):
            place(f, b + 1, cols_s[tile(b), :])
    load(HALO * PLANES)
    for f in range(PLANES):
        place(f, 0, cols_s[tile(TILES - 1), :])
        place(f, TILES + 1, cols_s[tile(0), :])
    copies.wait()
    copies.start(fields, fields_out)
    copies.start(warm, warm_out)
    strip_of(ints, fields, strip)

    at_north, at_south = ints[NORTH] > 0, ints[SOUTH] > 0
    at_west, at_east = ints[WEST] > 0, ints[EAST] > 0
    for k in range(2):
        for half in range(2):
            first = jnp.broadcast_to(thick[k, half, 8:9, :], (8, CELLS))
            last = jnp.broadcast_to(thick[k, half, ROWS - 9 : ROWS - 8, :], (8, CELLS))
            for b, at_end, line in ((0, at_north, first), (TILES + 1, at_south, last)):
                thick[k, half, tile(b), :] = jnp.where(at_end, line, thick[k, half, tile(b), :])
        for b in range(TILES + 2):
            own, other = thick[k, 0, tile(b), :], thick[k, 1, tile(b), :]
            other = jnp.where((lane == CELLS - 1) & at_west, turn(own, -1), other)
            other = jnp.where((lane == 0) & at_east, turn(own, 1), other)
            thick[k, 1, tile(b), :] = jnp.where(other > 0.0, other, 1.0)

    for b in range(TILES + 2):
        found = [around(thick.at[k], b, 2) for k in range(2)]
        for half in range(2):
            between = 0.5 * (found[0][half][0] + found[1][half][0])
            for k in range(2):
                here, *others = found[k][half]
                faces = [0.5 * (here + other) for other in others]
                diagonal = (faces[0] + faces[1]) + (faces[2] + faces[3]) + (between + here)
                inverse = 0.8 / diagonal
                for n, face in enumerate(faces):
                    coef[n, k, half, tile(b), :] = inverse * face
                coef[4, k, half, tile(b), :] = inverse * between
                coef[5, k, half, tile(b), :] = 0.5 * inverse
                coef[6, k, half, tile(b), :] = inverse * warm[k, half, tile(b), :]
                coef[7, k, half, tile(b), :] = 0.125 * here
    copies.start(coef, coef_out)
    at = ints[0] + 8
    for n in range(8):
        for f in range(8):
            factors[n, f : f + 1, :] = coef[n, f % 2, 0, pl.ds(at, 1), :]

    blank = jnp.zeros((8, CELLS), F32)
    for side in range(2):
        for term in range(2):
            cut = slice(term * CELLS, (term + 1) * CELLS)
            if side == 0:
                lo = pl.multiple_of(2 * HALO * PLANES + 8 * (ints[LAT_BASE] + term), 8)
                before, after = west[pl.ds(lo, 8), :], east[pl.ds(lo, 8), :]
            else:
                before = north[8 + ints[LON_BASE] + term]
                after = south[8 + ints[LON_BASE] + term]
            ends = [jnp.concatenate([after, blank], axis=0)]
            ends += [jnp.zeros((16, CELLS), F32)] * 6
            ends += [jnp.concatenate([blank, before], axis=0)]
            for n in range(16):
                if n < 8:
                    block = chosen[2 * side + term, 16 * n : 16 * n + 16, :]
                else:
                    block = ends[n - 8]
                for out, part in zip((high, low), split(block)):
                    out[side, 16 * n : 16 * n + 16, cut] = part
    copies.wait(6)


def strip_of(ints, fields, strip):
    at = ints[0] + 8
    for f in range(8):
        strip[0, f : f + 1, :] = fields[f, 0, pl.ds(at, 1), :]
        strip[1, f : f + 1, :] = fields[f, 1, pl.ds(at, 1), :]
        strip[2, f : f + 1, :] = fields[f, 0, pl.ds(at - 1, 1), :]
        strip[3, f : f + 1, :] = fields[f, 0, pl.ds(at + 1, 1), :]


def split(x):
    high = x.astype(jnp.bfloat16)
    return high, (x - high.astype(F32)).astype(jnp.bfloat16)


def times(left, right):
    return lax.dot_general(left, right, (((1,), (1,)), ((), ())), preferred_element_type=F32)


def blend_sides(ints, arrived, high, low, lat_ghost, lon_ghost):
    sides = (
        (lat_ghost, (ints[NORTH] + ints[SOUTH]) > 0, PLACES),
        (lon_ghost, (ints[WEST] + ints[EAST]) > 0, PLACES + 6),
    )
    for n, (ghost, active, places) in enumerate(sides):
        ghost[...] = jnp.zeros((8, LANES), F32)

        @pl.when(active)
        def _():
            blocks = [
                jnp.concatenate([arrived[ints[places + 2 * who + t]] for t in range(2)], axis=1)
                for who in range(3)
            ]
            b_high, b_low = split(jnp.concatenate(blocks, axis=0))
            both = times(jnp.concatenate([b_high, b_low], axis=0), high[n])
            total = both[0:24] + both[24:48] + times(b_high, low[n])
            ghost[:, 0:CELLS] = total[0:8, 0:CELLS]
            ghost[:, CELLS:LANES] = jnp.where(
                lanes() < CELLS // 2, total[16:24, CELLS:LANES], total[8:16, CELLS:LANES]
            )


def blend_kernel(ints, strip, factors, arrived, high, low, lat_ghost, lon_ghost, row):
    blend_sides(ints, arrived, high, low, lat_ghost, lon_ghost)
    at = ints[0]
    lane, sub = lanes(), sublanes()
    here, outside, up, down = strip[0], strip[1], strip[2], strip[3]
    up = jnp.where((ints[NORTH] > 0) & (at == 0), lat_ghost[:, 0:CELLS], up)
    down = jnp.where((ints[SOUTH] > 0) & (at == CELLS - 1), lat_ghost[:, 0:CELLS], down)
    beside = jnp.sum(jnp.where(lane == at, lon_ghost[:, 0:CELLS], 0.0), axis=1, keepdims=True)
    on_side = ((lane == CELLS - 1) & (ints[WEST] > 0)) | ((lane == 0) & (ints[EAST] > 0))
    outside = jnp.where(on_side, beside, outside)
    lefts, rights = sideways(here, outside)
    left, right = lefts[0], rights[0]
    even = sub % 2 == 0
    partner = jnp.where(even, pltpu.roll(here, 7, 0), pltpu.roll(here, 1, 0))
    value = 0.2 * here + factors[0] * up + factors[1] * down
    value = value + factors[2] * left + factors[3] * right + factors[4] * partner
    value = value + jnp.where(sub < 2, factors[6], 0.0)
    steps = (jnp.where(even, partner, -partner), down - up, right - left)
    slope = jnp.where(
        sub < 2,
        pltpu.roll(steps[0], 2, 0),
        jnp.where(sub < 4, pltpu.roll(steps[1], 4, 0), pltpu.roll(steps[2], 6, 0)),
    )
    value = value - factors[5] * slope
    divergence = (
        pltpu.roll(steps[0], 6, 0) + pltpu.roll(steps[1], 4, 0) + pltpu.roll(steps[2], 2, 0)
    )
    row[...] = jnp.where(sub < 6, value, here - factors[7] * divergence)


def ghost_columns(count, lon_ghost, cut, rows_s, out):
    for f in range(count):
        for lane in (2 * f, (2 * f - 1) % CELLS):
            rows_s[lane : lane + 1, :] = lon_ghost[f : f + 1, cut]
    out[...] = rows_s[...].T


def put_ghosts(ints, count, lat_ghost, lon_ghost, full, cols_s, ends_s, rows_s):
    lane, sub = lanes(), sublanes()
    rows_s[...] = jnp.zeros((CELLS, CELLS), F32)
    ghost_columns(count, lon_ghost, slice(0, CELLS), rows_s, cols_s)
    ghost_columns(count, lon_ghost, slice(CELLS, LANES), rows_s, ends_s)
    on_side = ((lane == CELLS - 1) & (ints[WEST] > 0)) | ((lane == 0) & (ints[EAST] > 0))
    ends = ((0, (sub == 7) & (ints[NORTH] > 0)), (TILES + 1, (sub == 0) & (ints[SOUTH] > 0)))
    for b, edge in ends:
        for f in range(count):
            for half in range(2):
                line = lat_ghost[f : f + 1, half * CELLS : (half + 1) * CELLS]
                full[f, half, tile(b), :] = jnp.where(edge, line, full[f, half, tile(b), :])
    for b in range(TILES + 2):
        if b == 0:
            column = ends_s[tile(TILES - 1), :]
        elif b == TILES + 1:
            column = ends_s[tile(0), :]
        else:
            column = cols_s[tile(b - 1), :]
        for f in range(count):
            other = full[f, 1, tile(b), :]
            full[f, 1, tile(b), :] = jnp.where(on_side, turn(column, -2 * f), other)


def relaxed(full, coef, b, halves):
    found = [around(full.at[f], b, halves) for f in range(8)]
    answers = []
    for half in range(halves):
        at = [found[f][half] for f in range(8)]

        def factor(n, k):
            return coef[n, k, half, tile(b), :]

        new = []
        for component in range(3):
            for k in range(2):
                here, up, down, left, right = at[2 * component + k]
                value = 0.2 * here + factor(0, k) * up + factor(1, k) * down
                value = value + factor(2, k) * left + factor(3, k) * right
                value = value + factor(4, k) * at[2 * component + 1 - k][0]
                if component == 0:
                    value = value + factor(6, k)
                    slope = at[7][0] if k == 0 else -at[6][0]
                elif component == 1:
                    slope = at[6 + k][2] - at[6 + k][1]
                else:
                    slope = at[6 + k][4] - at[6 + k][3]
                new.append(value - factor(5, k) * slope)
        for k in range(2):
            divergence = (at[2 + k][2] - at[2 + k][1]) + (at[4 + k][4] - at[4 + k][3])
            divergence = divergence + at[1][0] if k == 0 else divergence - at[0][0]
            new.append(at[6 + k][0] - factor(7, k) * divergence)
        answers.append(new)
    return answers


def sweep_kernel(
    ints, fields, coef, lat_ghost, lon_ghost, out, strip,
    full, factor, new_full, cols_s, ends_s, rows_s, sems,
):
    copies = Copies(sems)
    copies.start(fields, full)
    copies.start(coef, factor)
    copies.wait(0, 1)
    put_ghosts(ints, 8, lat_ghost, lon_ghost, full, cols_s, ends_s, rows_s)
    copies.wait(1, 2)
    for b in range(TILES + 2):
        for half, new in enumerate(relaxed(full, factor, b, 2)):
            for f in range(8):
                new_full[f, half, tile(b), :] = new[f]
    copies.start(new_full, out)
    strip_of(ints, new_full, strip)
    copies.wait(2)


def relay_kernel(places, arrived, out):
    for n in range(8):
        out[2 * n : 2 * n + 2, :] = arrived[places[n], 0:2, :]


def heat_kernel(
    ints, warm, blocks, weights, out, chosen, lat_ghost, lon_ghost, cols_s, ends_s, rows_s, sems
):
    copies = Copies(sems)
    copies.start(warm, out)
    copies.start(weights.at[pl.ds(ints[LAT_BASE], 2)], chosen.at[0:2])
    copies.start(weights.at[pl.ds(ints[LON_BASE], 2)], chosen.at[2:4])
    copies.wait()
    sides = (
        (lat_ghost, (ints[NORTH] + ints[SOUTH]) > 0, LAT_BASE),
        (lon_ghost, (ints[WEST] + ints[EAST]) > 0, LON_BASE),
    )
    for n, (ghost, active, base) in enumerate(sides):
        ghost[...] = jnp.zeros((8, LANES), F32)

        @pl.when(active)
        def _():
            total = jnp.zeros((16, CELLS), F32)
            for term in range(2):
                b_high, b_low = split(blocks[ints[base] + term])
                w_high, w_low = split(chosen[2 * n + term])
                total = total + times(b_high, w_low) + times(b_low, w_high) + times(b_high, w_high)
            ghost[:, 0:CELLS] = total[0:8]

    put_ghosts(ints, 2, lat_ghost, lon_ghost, out, cols_s, ends_s, rows_s)


def ahead_kernel(ints, fields, coef, new, beside, above, full, factor, cols_s, ends_s, rows_s, blank, sems):
    copies = Copies(sems)
    copies.start(fields, full)
    copies.start(coef, factor)
    blank[...] = jnp.zeros((8, LANES), F32)
    copies.wait(0, 1)
    put_ghosts(ints, 8, blank, blank, full, cols_s, ends_s, rows_s)
    copies.wait(1, 2)
    lane, sub = lanes(), sublanes()
    first, last = (lane == 0) & (ints[WEST] > 0), (lane == CELLS - 1) & (ints[EAST] > 0)
    ends = ((1, 0, (sub == 0) & (ints[NORTH] > 0), 1.0), (TILES, 1, (sub == 7) & (ints[SOUTH] > 0), -1.0))
    for b in range(1, TILES + 1):
        (answer,) = relaxed(full, factor, b, 1)
        for f in range(8):
            new[f, tile(b - 1), :] = answer[f]
        for k in range(2):
            at = [factor[n, k, 0, tile(b), :] for n in (2, 3, 5, 7)]
            beside[0, k, tile(b - 1), :] = jnp.where(first, at[0], jnp.where(last, at[1], 0.0))
            for n in (1, 2):
                beside[n, k, tile(b - 1), :] = jnp.where(
                    first, at[n + 1], jnp.where(last, -at[n + 1], 0.0)
                )
    for end, (b, n, edge, sign) in enumerate(ends):
        for k in range(2):
            above[end, 0, k] = jnp.where(edge, factor[n, k, 0, tile(b), :], 0.0)
            above[end, 1, k] = jnp.where(edge, sign * factor[5, k, 0, tile(b), :], 0.0)
            above[end, 2, k] = jnp.where(edge, sign * factor[7, k, 0, tile(b), :], 0.0)


def corrected(new, ghost, parts, component):
    out = []
    for f in range(6):
        k = f % 2
        value = new[f] + parts[0][k] * ghost[f]
        if f // 2 == component:
            value = value + parts[1][k] * ghost[6 + k]
        out.append(value)
    for k in range(2):
        out.append(new[6 + k] + parts[2][k] * ghost[2 * component + k])
    return out


def final_kernel(
    ints, arrived, high, low, ready, beside, above, warm,
    flow_out, pressure_out, heat_out, lat_ghost, lon_ghost, cols_s, rows_s,
):
    blend_sides(ints, arrived, high, low, lat_ghost, lon_ghost)
    rows_s[...] = jnp.zeros((CELLS, CELLS), F32)
    ghost_columns(8, lon_ghost, slice(0, CELLS), rows_s, cols_s)
    for b in range(TILES):
        new = [ready[f, tile(b), :] for f in range(8)]
        if b == 0 or b == TILES - 1:
            end = 0 if b == 0 else 1
            ghost = [lat_ghost[f : f + 1, 0:CELLS] for f in range(8)]
            new = corrected(new, ghost, [[above[end, n, k] for k in range(2)] for n in range(3)], 1)
        column = cols_s[tile(b), :]
        ghost = [turn(column, -2 * f) for f in range(8)]
        parts = [[beside[n, k, tile(b), :] for k in range(2)] for n in range(3)]
        new = corrected(new, ghost, parts, 2)
        for f in range(6):
            flow_out[f, tile(b), :] = new[f]
        for k in range(2):
            pressure_out[k, tile(b), :] = new[6 + k]
        layers = [around(warm.at[k], b + 1, 1)[0] for k in range(2)]
        for k in range(2):
            here, up, down, left, right = layers[k]
            under = jnp.ones((8, CELLS), F32) if k == 0 else layers[0][0]
            over = layers[1][0] if k == 0 else jnp.zeros((8, CELLS), F32)
            advect = jnp.zeros((8, CELLS), F32)
            for component, minus, plus in ((0, under, over), (1, up, down), (2, left, right)):
                speed = new[2 * component + k]
                advect = advect + jnp.maximum(speed, 0.0) * (here - minus)
                advect = advect + jnp.minimum(speed, 0.0) * (plus - here)
            spread = (up + down) + (left + right) + (under + over) - 6.0 * here
            heat_out[k, tile(b), :] = here + 0.1 * (spread - advect)


def shape(*dims):
    return jax.ShapeDtypeStruct(dims, F32)


def scratch(*dims):
    return pltpu.VMEM(dims, F32)


def call(kernel, outs, ins, scratches, specs=None, out_specs=None, aliases=None, name=None, limit=16):
    return pl.pallas_call(
        kernel,
        out_shape=outs,
        in_specs=specs or [SMEM] + [VMEM] * (len(ins) - 1),
        out_specs=out_specs or [VMEM] * len(outs),
        scratch_shapes=scratches,
        input_output_aliases=aliases or {},
        compiler_params=pltpu.CompilerParams(vmem_limit_bytes=limit * 1024 * 1024),
        name=name,
    )(*ins)


def semaphores(count):
    return pltpu.SemaphoreType.DMA((count,))


def shards(
    flow_vector,
    normal_stress,
    thermal_field,
    shear_resistance,
    departing_bands,
    receiving_processor,
    shift_filled_by_lane,
    blending_factors,
):
    flow = flow_vector.reshape(6, CELLS, CELLS)
    pressure = normal_stress[0]
    heat = thermal_field[0]
    friction = shear_resistance[0]
    weights = blending_factors.reshape(8, CELLS, CELLS)
    lat, lon = lax.axis_index("lat"), lax.axis_index("lon")
    n_lat, n_lon = lax.axis_size("lat"), lax.axis_size("lon")
    devices = n_lat * n_lon
    own_row = departing_bands.reshape(1)

    def swap(x):
        return lax.ppermute(x, "patch", [(0, 1), (1, 0)])

    def ring(x, axis, step):
        count = lax.axis_size(axis)
        pairs = [(i, i + step) for i in range(count) if 0 <= i + step < count]
        return lax.ppermute(x, axis, pairs)

    def to_relay(x):
        return lax.ppermute(x, "lon", [(i, i ^ 2) for i in range(n_lon)])

    def deliver(buffer):
        return lax.all_to_all(buffer, ("lat", "lon"), 0, 0, tiled=True)

    receiver = swap(receiving_processor.reshape(1).astype(F32)).astype(jnp.int32)
    receiver = jnp.maximum(receiver, 0)
    near = receiver + jnp.array([0, 1, -1, n_lon, -n_lon], jnp.int32)
    near = jnp.where((near >= 0) & (near < devices), near, receiver)
    chunks = jnp.concatenate([near, receiver ^ 2])

    planes = (flow, pressure, heat, friction, weights)
    row, top, bottom, places = call(
        start_kernel,
        [shape(16, CELLS), shape(17, 8, CELLS), shape(17, 8, CELLS), shape(8, CELLS)],
        (own_row, shift_filled_by_lane.reshape(1, CELLS), *planes),
        [scratch(10, 8, CELLS), pltpu.VMEM((1, CELLS), jnp.int32), semaphores(14)],
        specs=[SMEM] + [HBM] * 6,
        name="start",
    )
    (buffer,) = call(
        fill_kernel, [shape(devices, 8, CELLS)], (chunks, swap(row)), [], name="fill", limit=4
    )
    arrived = deliver(buffer)
    north, south = ring(bottom, "lat", 1), ring(top, "lat", -1)
    wide = shape(2 * HALO * PLANES + 40, CELLS)
    square = scratch(CELLS, CELLS)
    to_west, to_east = call(
        columns_kernel,
        [wide, wide],
        (*planes, north, south, places),
        [scratch(PLANES, CELLS, CELLS), square, square, semaphores(12)],
        specs=[HBM] * 5 + [VMEM] * 3,
        name="columns",
    )
    west, east = ring(to_east, "lon", 1), ring(to_west, "lon", -1)

    def numbers(block):
        return block[:, 0].astype(jnp.int32)

    on_edge = jnp.stack([lat == 0, lat == n_lat - 1, lon == 0, lon == n_lon - 1]).astype(jnp.int32)
    own = numbers(places)

    def side(block, base, last):
        return jnp.where(last, block[base + 2 : base + 4], block[base : base + 2])

    pick = [side(x, 0, lat > 0) for x in (own, numbers(west[-8:]), numbers(east[-8:]))]
    pick += [side(x, 4, lon > 0) for x in (own, numbers(north[16]), numbers(south[16]))]
    bases = jnp.stack([jnp.where(lat > 0, 2, 0), jnp.where(lon > 0, 6, 4)]).astype(jnp.int32)
    ints = jnp.concatenate([own_row, on_edge] + pick + [bases])

    state = shape(8, 2, ROWS, CELLS)
    state_s = scratch(8, 2, ROWS, CELLS)
    coef_s = scratch(8, 2, 2, ROWS, CELLS)
    warm_s = scratch(2, 2, ROWS, CELLS)
    strips = shape(4, 8, CELLS)
    joined = jax.ShapeDtypeStruct((2, LANES, LANES), jnp.bfloat16)
    fields, coef, warm, strip, factors, high, low = call(
        build_kernel,
        [
            state,
            shape(8, 2, 2, ROWS, CELLS),
            shape(2, 2, ROWS, CELLS),
            strips,
            shape(8, 8, CELLS),
            joined,
            joined,
        ],
        (ints, *planes, north, south, west, east),
        [state_s, coef_s, warm_s, warm_s, scratch(4, CELLS, CELLS), square, square, semaphores(9)],
        specs=[SMEM] + [HBM] * 5 + [VMEM] * 4,
        out_specs=[HBM] * 3 + [VMEM] * 4,
        name="build",
    )
    relayed = numbers(to_relay(places))
    ghost = shape(8, LANES)
    ghost_s = scratch(8, LANES)
    first_arrived = arrived
    for sweep in range(SWEEPS - 1):
        lat_ghost, lon_ghost, row = call(
            blend_kernel,
            [ghost, ghost, shape(8, CELLS)],
            (ints, strip, factors, arrived, high, low),
            [],
            name="blend",
            limit=4,
        )
        (buffer,) = call(
            refill_kernel,
            [shape(devices, 8, CELLS)],
            (chunks, swap(row), buffer),
            [],
            aliases={2: 0},
            name="refill",
            limit=4,
        )
        arrived = deliver(buffer)
        fields, strip = call(
            sweep_kernel,
            [state, strips],
            (ints, fields, coef, lat_ghost, lon_ghost),
            [state_s, coef_s, state_s, square, square, square, semaphores(3)],
            specs=[SMEM, HBM, HBM, VMEM, VMEM],
            out_specs=[HBM, VMEM],
            name="sweep",
        )
        if sweep == 0:
            (blocks,) = call(
                relay_kernel,
                [shape(16, CELLS)],
                (relayed, first_arrived),
                [],
                name="relay",
                limit=4,
            )
            blocks = to_relay(blocks).reshape(8, 2, CELLS)
            blocks = jnp.pad(blocks, ((0, 0), (0, 14), (0, 0)))
            (warm,) = call(
                heat_kernel,
                [shape(2, 2, ROWS, CELLS)],
                (ints, warm, blocks, weights),
                [scratch(4, CELLS, CELLS), ghost_s, ghost_s, square, square, square, semaphores(3)],
                specs=[SMEM, HBM, VMEM, HBM],
                name="heat",
                limit=4,
            )
    ready, beside, above = call(
        ahead_kernel,
        [shape(8, CELLS, CELLS), shape(3, 2, CELLS, CELLS), shape(2, 3, 2, 8, CELLS)],
        (ints, fields, coef),
        [state_s, coef_s, square, square, square, ghost_s, semaphores(2)],
        specs=[SMEM, HBM, HBM],
        name="ahead",
    )
    flow, pressure, heat = call(
        final_kernel,
        [shape(6, CELLS, CELLS), shape(2, CELLS, CELLS), shape(2, CELLS, CELLS)],
        (ints, arrived, high, low, ready, beside, above, warm),
        [ghost_s, ghost_s, square, square],
        name="final",
        limit=8,
    )
    return flow.reshape(3, 1, 2, CELLS, CELLS), pressure[None], heat[None]


def solution(mesh):
    placed = (
        P(None, "patch", None, "lat", "lon"),
        P("patch", None, "lat", "lon"),
        P("patch", None, "lat", "lon"),
        P("patch", None, "lat", "lon"),
        P("patch", "lat", "lon", None),
        P("patch", "lat", "lon", None),
        P("patch", "lat", "lon", None),
        P("patch", "lat", "lon", None, None, None),
    )
    return jax.shard_map(
        shards,
        mesh=mesh,
        in_specs=placed,
        out_specs=(
            P(None, "patch", None, "lat", "lon"),
            P("patch", None, "lat", "lon"),
            P("patch", None, "lat", "lon"),
        ),
        check_vma=False,
    )
```

```python
import jax
import jax.numpy as jnp
from jax import lax
from jax.experimental import pallas as pl
from jax.experimental.pallas import tpu as pltpu
from jax.sharding import PartitionSpec as P

SWEEPS = 4
CELLS = 128
TILES = 16
ROWS = CELLS + 16
LANES = 2 * CELLS
HALO = 4
PLANES = 12
F32 = jnp.float32
VMEM = pl.BlockSpec(memory_space=pltpu.VMEM)
SMEM = pl.BlockSpec(memory_space=pltpu.SMEM)
HBM = pl.BlockSpec(memory_space=pltpu.HBM)
NORTH, SOUTH, WEST, EAST = 1, 2, 3, 4
PLACES = 5
LAT_BASE, LON_BASE = 17, 18


def lanes():
    return lax.broadcasted_iota(jnp.int32, (8, CELLS), 1)


def sublanes():
    return lax.broadcasted_iota(jnp.int32, (8, CELLS), 0)


def turn(x, shift):
    shift = shift % CELLS
    return x if shift == 0 else pltpu.roll(x, shift, 1)


def tile(b):
    return pl.ds(8 * b, 8)


class Copies:
    def __init__(self, sems):
        self.sems, self.going = sems, []

    def start(self, source, target):
        copy = pltpu.make_async_copy(source, target, self.sems.at[len(self.going)])
        copy.start()
        self.going.append(copy)

    def wait(self, first=0, last=None):
        for copy in self.going[first:last]:
            copy.wait()


def start_kernel(
    at, slots, flow, pressure, heat, friction, weights, row, top, bottom, places, near, named, sems
):
    start = pl.multiple_of((at[0] // 8) * 8, 8)
    copies = Copies(sems)
    copies.start(slots, named)
    copies.start(flow.at[:, pl.ds(start, 8), :], near.at[0:6])
    copies.start(pressure.at[:, pl.ds(start, 8), :], near.at[6:8])
    copies.start(heat.at[:, pl.ds(start, 8), :], near.at[8:10])
    for out, lo in ((top, 0), (bottom, CELLS - 8)):
        copies.start(flow.at[:, lo : lo + 8, :], out.at[0:6])
        copies.start(pressure.at[:, lo : lo + 8, :], out.at[6:8])
        copies.start(heat.at[:, lo : lo + 8, :], out.at[8:10])
        copies.start(friction.at[:, lo : lo + 8, :], out.at[10:12])
        copies.start(weights.at[4:8, lo : lo + 8, :], out.at[12:16])
    row[...] = jnp.zeros((16, CELLS), F32)
    copies.wait()
    own = jnp.broadcast_to(named[...], (8, CELLS)) == sublanes()
    place = jnp.sum(jnp.where(own, lanes(), 0).astype(F32), axis=1, keepdims=True)
    place = jnp.broadcast_to(place, (8, CELLS))
    for out in (top.at[16], bottom.at[16], places):
        out[...] = place
    inside = at[0] - start
    for f in range(10):
        row[f : f + 1, :] = near[f, pl.ds(inside, 1), :]


def fill_kernel(chunks, row, out):
    out[...] = jnp.zeros((CELLS, 8, CELLS), F32)
    for n in range(5):
        out[chunks[n]] = row[0:8, :]
    out[chunks[5]] = row[8:16, :]


def refill_kernel(chunks, row, old, out):
    del old
    for n in range(5):
        out[chunks[n]] = row[...]


def columns_kernel(
    flow, pressure, heat, friction, weights, north, south, places,
    to_west, to_east, own, cols_s, rows_s, sems,
):
    lane = lanes()
    copies = Copies(sems)
    copies.start(flow, own.at[0:6])
    copies.start(pressure, own.at[6:8])
    copies.start(heat, own.at[8:10])
    copies.start(friction, own.at[10:12])
    for n in range(4):
        lo = 2 * HALO * PLANES + 8 * n
        copies.start(weights.at[n, 0:8, :], to_west.at[lo : lo + 8, :])
        copies.start(weights.at[n, CELLS - 8 : CELLS, :], to_east.at[lo : lo + 8, :])
    for out in (to_west, to_east):
        out[2 * HALO * PLANES + 32 :, :] = places[...]

    def pack(block):
        gathered = jnp.zeros((8, CELLS), F32)
        for f in range(PLANES):
            gathered = jnp.where(lane // 8 == f, turn(block(f), 8 * f + HALO), gathered)
        return gathered

    def unload(first):
        rows_s[...] = cols_s[...].T
        for f in range(PLANES):
            lo = first + HALO * f
            to_east[lo : lo + HALO, :] = rows_s[8 * f : 8 * f + HALO, :]
            to_west[lo : lo + HALO, :] = rows_s[8 * f + HALO : 8 * f + 8, :]

    cols_s[...] = jnp.zeros((CELLS, CELLS), F32)
    cols_s[tile(TILES - 1), :] = pack(lambda f: north[f])
    cols_s[tile(0), :] = pack(lambda f: south[f])
    unload(HALO * PLANES)
    copies.wait()
    for b in range(TILES):
        cols_s[tile(b), :] = pack(lambda f: own[f, tile(b), :])
    unload(0)


def sideways(first, second):
    lane = lanes()
    f_up, s_up = pltpu.roll(first, 1, 1), pltpu.roll(second, 1, 1)
    f_down, s_down = pltpu.roll(first, CELLS - 1, 1), pltpu.roll(second, CELLS - 1, 1)
    lefts = (jnp.where(lane == 0, s_up, f_up), jnp.where(lane == 0, f_up, s_up))
    rights = (
        jnp.where(lane == CELLS - 1, s_down, f_down),
        jnp.where(lane == CELLS - 1, f_down, s_down),
    )
    return lefts, rights


def around(ref, b, halves):
    both = [ref[half, tile(b), :] for half in range(2)]
    lefts, rights = sideways(*both)
    found = []
    for half in range(halves):
        up = pltpu.roll(both[half], 1, 0) if b == 0 else ref[half, 8 * b - 1 : 8 * b + 7, :]
        down = pltpu.roll(both[half], 7, 0) if b == TILES + 1 else ref[half, 8 * b + 1 : 8 * b + 9, :]
        found.append((both[half], up, down, lefts[half], rights[half]))
    return found


def build_kernel(
    ints, flow, pressure, heat, friction, weights, north, south, west, east,
    fields_out, coef_out, warm_out, strip, factors, high, low,
    fields, coef, warm, thick, chosen, cols_s, rows_s, sems,
):
    lane = lanes()
    copies = Copies(sems)
    inner = pl.ds(8, CELLS)
    copies.start(friction, thick.at[:, 0, inner, :])
    copies.start(heat, warm.at[:, 0, inner, :])
    copies.start(flow, fields.at[0:6, 0, inner, :])
    copies.start(pressure, fields.at[6:8, 0, inner, :])
    copies.start(weights.at[pl.ds(ints[LAT_BASE], 2)], chosen.at[0:2])
    copies.start(weights.at[pl.ds(ints[LON_BASE], 2)], chosen.at[2:4])

    def target(f):
        if f < 8:
            return fields.at[f]
        return warm.at[f - 8] if f < 10 else thick.at[f - 10]

    outer = (lane < HALO) | (lane >= CELLS - HALO)

    def load(first):
        for f in range(PLANES):
            lo = first + HALO * f
            rows_s[8 * f : 8 * f + HALO, :] = west[lo : lo + HALO, :]
            rows_s[8 * f + HALO : 8 * f + 8, :] = east[lo : lo + HALO, :]
        cols_s[...] = rows_s[...].T

    def place(f, b, block):
        target(f)[1, tile(b), :] = jnp.where(outer, turn(block, -8 * f - HALO), 0.0)

    rows_s[8 * PLANES : CELLS, :] = jnp.zeros((CELLS - 8 * PLANES, CELLS), F32)
    load(0)
    for f in range(PLANES):
        target(f)[0, tile(0), :] = north[f]
        target(f)[0, tile(TILES + 1), :] = south[f]
        for b in range(TILES):
            place(f, b + 1, cols_s[tile(b), :])
    load(HALO * PLANES)
    for f in range(PLANES):
        place(f, 0, cols_s[tile(TILES - 1), :])
        place(f, TILES + 1, cols_s[tile(0), :])
    copies.wait()
    copies.start(fields, fields_out)
    copies.start(warm, warm_out)
    strip_of(ints, fields, strip)

    at_north, at_south = ints[NORTH] > 0, ints[SOUTH] > 0
    at_west, at_east = ints[WEST] > 0, ints[EAST] > 0
    for k in range(2):
        for half in range(2):
            first = jnp.broadcast_to(thick[k, half, 8:9, :], (8, CELLS))
            last = jnp.broadcast_to(thick[k, half, ROWS - 9 : ROWS - 8, :], (8, CELLS))
            for b, at_end, line in ((0, at_north, first), (TILES + 1, at_south, last)):
                thick[k, half, tile(b), :] = jnp.where(at_end, line, thick[k, half, tile(b), :])
        for b in range(TILES + 2):
            own, other = thick[k, 0, tile(b), :], thick[k, 1, tile(b), :]
            other = jnp.where((lane == CELLS - 1) & at_west, turn(own, -1), other)
            other = jnp.where((lane == 0) & at_east, turn(own, 1), other)
            thick[k, 1, tile(b), :] = jnp.where(other > 0.0, other, 1.0)

    for b in range(TILES + 2):
        found = [around(thick.at[k], b, 2) for k in range(2)]
        for half in range(2):
            between = 0.5 * (found[0][half][0] + found[1][half][0])
            for k in range(2):
                here, *others = found[k][half]
                faces = [0.5 * (here + other) for other in others]
                diagonal = (faces[0] + faces[1]) + (faces[2] + faces[3]) + (between + here)
                inverse = 0.8 / diagonal
                for n, face in enumerate(faces):
                    coef[n, k, half, tile(b), :] = inverse * face
                coef[4, k, half, tile(b), :] = inverse * between
                coef[5, k, half, tile(b), :] = 0.5 * inverse
                coef[6, k, half, tile(b), :] = inverse * warm[k, half, tile(b), :]
                coef[7, k, half, tile(b), :] = 0.125 * here
    copies.start(coef, coef_out)
    at = ints[0] + 8
    for n in range(8):
        for f in range(8):
            factors[n, f : f + 1, :] = coef[n, f % 2, 0, pl.ds(at, 1), :]

    blank = jnp.zeros((8, CELLS), F32)
    for side in range(2):
        for term in range(2):
            cut = slice(term * CELLS, (term + 1) * CELLS)
            if side == 0:
                lo = pl.multiple_of(2 * HALO * PLANES + 8 * (ints[LAT_BASE] + term), 8)
                before, after = west[pl.ds(lo, 8), :], east[pl.ds(lo, 8), :]
            else:
                before = north[8 + ints[LON_BASE] + term]
                after = south[8 + ints[LON_BASE] + term]
            ends = [jnp.concatenate([after, blank], axis=0)]
            ends += [jnp.zeros((16, CELLS), F32)] * 6
            ends += [jnp.concatenate([blank, before], axis=0)]
            for n in range(16):
                if n < 8:
                    block = chosen[2 * side + term, 16 * n : 16 * n + 16, :]
                else:
                    block = ends[n - 8]
                for out, part in zip((high, low), split(block)):
                    out[side, 16 * n : 16 * n + 16, cut] = part
    copies.wait(6)


def strip_of(ints, fields, strip):
    at = ints[0] + 8
    for f in range(8):
        strip[0, f : f + 1, :] = fields[f, 0, pl.ds(at, 1), :]
        strip[1, f : f + 1, :] = fields[f, 1, pl.ds(at, 1), :]
        strip[2, f : f + 1, :] = fields[f, 0, pl.ds(at - 1, 1), :]
        strip[3, f : f + 1, :] = fields[f, 0, pl.ds(at + 1, 1), :]


def split(x):
    high = x.astype(jnp.bfloat16)
    return high, (x - high.astype(F32)).astype(jnp.bfloat16)


def times(left, right):
    return lax.dot_general(left, right, (((1,), (1,)), ((), ())), preferred_element_type=F32)


def blend_sides(ints, arrived, high, low, lat_ghost, lon_ghost):
    sides = (
        (lat_ghost, (ints[NORTH] + ints[SOUTH]) > 0, PLACES),
        (lon_ghost, (ints[WEST] + ints[EAST]) > 0, PLACES + 6),
    )
    for n, (ghost, active, places) in enumerate(sides):
        ghost[...] = jnp.zeros((8, LANES), F32)

        @pl.when(active)
        def _():
            blocks = [
                jnp.concatenate([arrived[ints[places + 2 * who + t]] for t in range(2)], axis=1)
                for who in range(3)
            ]
            b_high, b_low = split(jnp.concatenate(blocks, axis=0))
            both = times(jnp.concatenate([b_high, b_low], axis=0), high[n])
            total = both[0:24] + both[24:48] + times(b_high, low[n])
            ghost[:, 0:CELLS] = total[0:8, 0:CELLS]
            ghost[:, CELLS:LANES] = jnp.where(
                lanes() < CELLS // 2, total[16:24, CELLS:LANES], total[8:16, CELLS:LANES]
            )


def blend_kernel(ints, strip, factors, arrived, high, low, lat_ghost, lon_ghost, row):
    blend_sides(ints, arrived, high, low, lat_ghost, lon_ghost)
    at = ints[0]
    lane, sub = lanes(), sublanes()
    here, outside, up, down = strip[0], strip[1], strip[2], strip[3]
    up = jnp.where((ints[NORTH] > 0) & (at == 0), lat_ghost[:, 0:CELLS], up)
    down = jnp.where((ints[SOUTH] > 0) & (at == CELLS - 1), lat_ghost[:, 0:CELLS], down)
    beside = jnp.sum(jnp.where(lane == at, lon_ghost[:, 0:CELLS], 0.0), axis=1, keepdims=True)
    on_side = ((lane == CELLS - 1) & (ints[WEST] > 0)) | ((lane == 0) & (ints[EAST] > 0))
    outside = jnp.where(on_side, beside, outside)
    lefts, rights = sideways(here, outside)
    left, right = lefts[0], rights[0]
    even = sub % 2 == 0
    partner = jnp.where(even, pltpu.roll(here, 7, 0), pltpu.roll(here, 1, 0))
    value = 0.2 * here + factors[0] * up + factors[1] * down
    value = value + factors[2] * left + factors[3] * right + factors[4] * partner
    value = value + jnp.where(sub < 2, factors[6], 0.0)
    steps = (jnp.where(even, partner, -partner), down - up, right - left)
    slope = jnp.where(
        sub < 2,
        pltpu.roll(steps[0], 2, 0),
        jnp.where(sub < 4, pltpu.roll(steps[1], 4, 0), pltpu.roll(steps[2], 6, 0)),
    )
    value = value - factors[5] * slope
    divergence = (
        pltpu.roll(steps[0], 6, 0) + pltpu.roll(steps[1], 4, 0) + pltpu.roll(steps[2], 2, 0)
    )
    row[...] = jnp.where(sub < 6, value, here - factors[7] * divergence)


def ghost_columns(count, lon_ghost, cut, rows_s, out):
    for f in range(count):
        for lane in (2 * f, (2 * f - 1) % CELLS):
            rows_s[lane : lane + 1, :] = lon_ghost[f : f + 1, cut]
    out[...] = rows_s[...].T


def put_ghosts(ints, count, lat_ghost, lon_ghost, full, cols_s, ends_s, rows_s):
    lane, sub = lanes(), sublanes()
    rows_s[...] = jnp.zeros((CELLS, CELLS), F32)
    ghost_columns(count, lon_ghost, slice(0, CELLS), rows_s, cols_s)
    ghost_columns(count, lon_ghost, slice(CELLS, LANES), rows_s, ends_s)
    on_side = ((lane == CELLS - 1) & (ints[WEST] > 0)) | ((lane == 0) & (ints[EAST] > 0))
    ends = ((0, (sub == 7) & (ints[NORTH] > 0)), (TILES + 1, (sub == 0) & (ints[SOUTH] > 0)))
    for b, edge in ends:
        for f in range(count):
            for half in range(2):
                line = lat_ghost[f : f + 1, half * CELLS : (half + 1) * CELLS]
                full[f, half, tile(b), :] = jnp.where(edge, line, full[f, half, tile(b), :])
    for b in range(TILES + 2):
        if b == 0:
            column = ends_s[tile(TILES - 1), :]
        elif b == TILES + 1:
            column = ends_s[tile(0), :]
        else:
            column = cols_s[tile(b - 1), :]
        for f in range(count):
            other = full[f, 1, tile(b), :]
            full[f, 1, tile(b), :] = jnp.where(on_side, turn(column, -2 * f), other)


def relaxed(full, coef, b, halves):
    found = [around(full.at[f], b, halves) for f in range(8)]
    answers = []
    for half in range(halves):
        at = [found[f][half] for f in range(8)]

        def factor(n, k):
            return coef[n, k, half, tile(b), :]

        new = []
        for component in range(3):
            for k in range(2):
                here, up, down, left, right = at[2 * component + k]
                value = 0.2 * here + factor(0, k) * up + factor(1, k) * down
                value = value + factor(2, k) * left + factor(3, k) * right
                value = value + factor(4, k) * at[2 * component + 1 - k][0]
                if component == 0:
                    value = value + factor(6, k)
                    slope = at[7][0] if k == 0 else -at[6][0]
                elif component == 1:
                    slope = at[6 + k][2] - at[6 + k][1]
                else:
                    slope = at[6 + k][4] - at[6 + k][3]
                new.append(value - factor(5, k) * slope)
        for k in range(2):
            divergence = (at[2 + k][2] - at[2 + k][1]) + (at[4 + k][4] - at[4 + k][3])
            divergence = divergence + at[1][0] if k == 0 else divergence - at[0][0]
            new.append(at[6 + k][0] - factor(7, k) * divergence)
        answers.append(new)
    return answers


def sweep_kernel(
    ints, fields, coef, lat_ghost, lon_ghost, out, strip,
    full, factor, new_full, cols_s, ends_s, rows_s, sems,
):
    copies = Copies(sems)
    copies.start(fields, full)
    copies.start(coef, factor)
    copies.wait(0, 1)
    put_ghosts(ints, 8, lat_ghost, lon_ghost, full, cols_s, ends_s, rows_s)
    copies.wait(1, 2)
    for b in range(TILES + 2):
        for half, new in enumerate(relaxed(full, factor, b, 2)):
            for f in range(8):
                new_full[f, half, tile(b), :] = new[f]
    copies.start(new_full, out)
    strip_of(ints, new_full, strip)
    copies.wait(2)


def relay_kernel(places, arrived, out):
    for n in range(8):
        out[2 * n : 2 * n + 2, :] = arrived[places[n], 0:2, :]


def heat_kernel(
    ints, warm, blocks, weights, out, chosen, lat_ghost, lon_ghost, cols_s, ends_s, rows_s, sems
):
    copies = Copies(sems)
    copies.start(warm, out)
    copies.start(weights.at[pl.ds(ints[LAT_BASE], 2)], chosen.at[0:2])
    copies.start(weights.at[pl.ds(ints[LON_BASE], 2)], chosen.at[2:4])
    copies.wait()
    sides = (
        (lat_ghost, (ints[NORTH] + ints[SOUTH]) > 0, LAT_BASE),
        (lon_ghost, (ints[WEST] + ints[EAST]) > 0, LON_BASE),
    )
    for n, (ghost, active, base) in enumerate(sides):
        ghost[...] = jnp.zeros((8, LANES), F32)

        @pl.when(active)
        def _():
            total = jnp.zeros((16, CELLS), F32)
            for term in range(2):
                b_high, b_low = split(blocks[ints[base] + term])
                w_high, w_low = split(chosen[2 * n + term])
                total = total + times(b_high, w_low) + times(b_low, w_high) + times(b_high, w_high)
            ghost[:, 0:CELLS] = total[0:8]

    put_ghosts(ints, 2, lat_ghost, lon_ghost, out, cols_s, ends_s, rows_s)


def ahead_kernel(ints, fields, coef, new, beside, above, full, factor, cols_s, ends_s, rows_s, blank, sems):
    copies = Copies(sems)
    copies.start(fields, full)
    copies.start(coef, factor)
    blank[...] = jnp.zeros((8, LANES), F32)
    copies.wait(0, 1)
    put_ghosts(ints, 8, blank, blank, full, cols_s, ends_s, rows_s)
    copies.wait(1, 2)
    lane, sub = lanes(), sublanes()
    first, last = (lane == 0) & (ints[WEST] > 0), (lane == CELLS - 1) & (ints[EAST] > 0)
    ends = ((1, 0, (sub == 0) & (ints[NORTH] > 0), 1.0), (TILES, 1, (sub == 7) & (ints[SOUTH] > 0), -1.0))
    for b in range(1, TILES + 1):
        (answer,) = relaxed(full, factor, b, 1)
        for f in range(8):
            new[f, tile(b - 1), :] = answer[f]
        for k in range(2):
            at = [factor[n, k, 0, tile(b), :] for n in (2, 3, 5, 7)]
            beside[0, k, tile(b - 1), :] = jnp.where(first, at[0], jnp.where(last, at[1], 0.0))
            for n in (1, 2):
                beside[n, k, tile(b - 1), :] = jnp.where(
                    first, at[n + 1], jnp.where(last, -at[n + 1], 0.0)
                )
    for end, (b, n, edge, sign) in enumerate(ends):
        for k in range(2):
            above[end, 0, k] = jnp.where(edge, factor[n, k, 0, tile(b), :], 0.0)
            above[end, 1, k] = jnp.where(edge, sign * factor[5, k, 0, tile(b), :], 0.0)
            above[end, 2, k] = jnp.where(edge, sign * factor[7, k, 0, tile(b), :], 0.0)


def corrected(new, ghost, parts, component):
    out = []
    for f in range(6):
        k = f % 2
        value = new[f] + parts[0][k] * ghost[f]
        if f // 2 == component:
            value = value + parts[1][k] * ghost[6 + k]
        out.append(value)
    for k in range(2):
        out.append(new[6 + k] + parts[2][k] * ghost[2 * component + k])
    return out


def final_kernel(
    ints, arrived, high, low, ready, beside, above, warm,
    flow_out, pressure_out, heat_out, lat_ghost, lon_ghost, cols_s, rows_s,
):
    blend_sides(ints, arrived, high, low, lat_ghost, lon_ghost)
    rows_s[...] = jnp.zeros((CELLS, CELLS), F32)
    ghost_columns(8, lon_ghost, slice(0, CELLS), rows_s, cols_s)
    for b in range(TILES):
        new = [ready[f, tile(b), :] for f in range(8)]
        if b == 0 or b == TILES - 1:
            end = 0 if b == 0 else 1
            ghost = [lat_ghost[f : f + 1, 0:CELLS] for f in range(8)]
            new = corrected(new, ghost, [[above[end, n, k] for k in range(2)] for n in range(3)], 1)
        column = cols_s[tile(b), :]
        ghost = [turn(column, -2 * f) for f in range(8)]
        parts = [[beside[n, k, tile(b), :] for k in range(2)] for n in range(3)]
        new = corrected(new, ghost, parts, 2)
        for f in range(6):
            flow_out[f, tile(b), :] = new[f]
        for k in range(2):
            pressure_out[k, tile(b), :] = new[6 + k]
        layers = [around(warm.at[k], b + 1, 1)[0] for k in range(2)]
        for k in range(2):
            here, up, down, left, right = layers[k]
            under = jnp.ones((8, CELLS), F32) if k == 0 else layers[0][0]
            over = layers[1][0] if k == 0 else jnp.zeros((8, CELLS), F32)
            advect = jnp.zeros((8, CELLS), F32)
            for component, minus, plus in ((0, under, over), (1, up, down), (2, left, right)):
                speed = new[2 * component + k]
                advect = advect + jnp.maximum(speed, 0.0) * (here - minus)
                advect = advect + jnp.minimum(speed, 0.0) * (plus - here)
            spread = (up + down) + (left + right) + (under + over) - 6.0 * here
            heat_out[k, tile(b), :] = here + 0.1 * (spread - advect)


def shape(*dims):
    return jax.ShapeDtypeStruct(dims, F32)


def scratch(*dims):
    return pltpu.VMEM(dims, F32)


def call(
    kernel, outs, ins, scratches, specs=None, out_specs=None, aliases=None, name=None, limit=16, keep=()
):
    specs = specs or [SMEM] + [VMEM] * (len(ins) - 1)
    out_specs = out_specs or [VMEM] * len(outs)
    placed = []
    for n, (x, spec) in enumerate(zip(ins, specs)):
        if spec is HBM or n in keep:
            x = pltpu.with_memory_space_constraint(x, spec.memory_space)
        placed.append(x)
    outs = [pltpu.HBM(x.shape, x.dtype) if spec is HBM else x for x, spec in zip(outs, out_specs)]
    return pl.pallas_call(
        kernel,
        out_shape=outs,
        in_specs=specs,
        out_specs=out_specs,
        scratch_shapes=scratches,
        input_output_aliases=aliases or {},
        compiler_params=pltpu.CompilerParams(vmem_limit_bytes=limit * 1024 * 1024),
        name=name,
    )(*placed)


def semaphores(count):
    return pltpu.SemaphoreType.DMA((count,))


def shards(
    flow_vector,
    normal_stress,
    thermal_field,
    shear_resistance,
    departing_bands,
    receiving_processor,
    shift_filled_by_lane,
    blending_factors,
):
    flow = flow_vector.reshape(6, CELLS, CELLS)
    pressure = normal_stress[0]
    heat = thermal_field[0]
    friction = shear_resistance[0]
    weights = blending_factors.reshape(8, CELLS, CELLS)
    lat, lon = lax.axis_index("lat"), lax.axis_index("lon")
    n_lat, n_lon = lax.axis_size("lat"), lax.axis_size("lon")
    devices = n_lat * n_lon
    own_row = departing_bands.reshape(1)

    def swap(x):
        return lax.ppermute(x, "patch", [(0, 1), (1, 0)])

    def ring(x, axis, step):
        count = lax.axis_size(axis)
        pairs = [(i, i + step) for i in range(count) if 0 <= i + step < count]
        return lax.ppermute(x, axis, pairs)

    def to_relay(x):
        return lax.ppermute(x, "lon", [(i, i ^ 2) for i in range(n_lon)])

    def deliver(buffer):
        return lax.all_to_all(buffer, ("lat", "lon"), 0, 0, tiled=True)

    receiver = swap(receiving_processor.reshape(1).astype(F32)).astype(jnp.int32)
    receiver = jnp.maximum(receiver, 0)
    near = receiver + jnp.array([0, 1, -1, n_lon, -n_lon], jnp.int32)
    near = jnp.where((near >= 0) & (near < devices), near, receiver)
    chunks = jnp.concatenate([near, receiver ^ 2])

    planes = (flow, pressure, heat, friction, weights)
    row, top, bottom, places = call(
        start_kernel,
        [shape(16, CELLS), shape(17, 8, CELLS), shape(17, 8, CELLS), shape(8, CELLS)],
        (own_row, shift_filled_by_lane.reshape(1, CELLS), *planes),
        [scratch(10, 8, CELLS), pltpu.VMEM((1, CELLS), jnp.int32), semaphores(14)],
        specs=[SMEM] + [HBM] * 6,
        name="start",
    )
    (buffer,) = call(
        fill_kernel, [shape(devices, 8, CELLS)], (chunks, swap(row)), [], name="fill", limit=4
    )
    arrived = deliver(buffer)
    north, south = ring(bottom, "lat", 1), ring(top, "lat", -1)
    wide = shape(2 * HALO * PLANES + 40, CELLS)
    square = scratch(CELLS, CELLS)
    to_west, to_east = call(
        columns_kernel,
        [wide, wide],
        (*planes, north, south, places),
        [scratch(PLANES, CELLS, CELLS), square, square, semaphores(12)],
        specs=[HBM] * 5 + [VMEM] * 3,
        name="columns",
    )
    west, east = ring(to_east, "lon", 1), ring(to_west, "lon", -1)

    def numbers(block):
        return block[:, 0].astype(jnp.int32)

    on_edge = jnp.stack([lat == 0, lat == n_lat - 1, lon == 0, lon == n_lon - 1]).astype(jnp.int32)
    own = numbers(places)

    def side(block, base, last):
        return jnp.where(last, block[base + 2 : base + 4], block[base : base + 2])

    pick = [side(x, 0, lat > 0) for x in (own, numbers(west[-8:]), numbers(east[-8:]))]
    pick += [side(x, 4, lon > 0) for x in (own, numbers(north[16]), numbers(south[16]))]
    bases = jnp.stack([jnp.where(lat > 0, 2, 0), jnp.where(lon > 0, 6, 4)]).astype(jnp.int32)
    ints = jnp.concatenate([own_row, on_edge] + pick + [bases])

    state = shape(8, 2, ROWS, CELLS)
    state_s = scratch(8, 2, ROWS, CELLS)
    coef_s = scratch(8, 2, 2, ROWS, CELLS)
    warm_s = scratch(2, 2, ROWS, CELLS)
    strips = shape(4, 8, CELLS)
    joined = jax.ShapeDtypeStruct((2, LANES, LANES), jnp.bfloat16)
    fields, coef, warm, strip, factors, high, low = call(
        build_kernel,
        [
            state,
            shape(8, 2, 2, ROWS, CELLS),
            shape(2, 2, ROWS, CELLS),
            strips,
            shape(8, 8, CELLS),
            joined,
            joined,
        ],
        (ints, *planes, north, south, west, east),
        [state_s, coef_s, warm_s, warm_s, scratch(4, CELLS, CELLS), square, square, semaphores(9)],
        specs=[SMEM] + [HBM] * 5 + [VMEM] * 4,
        out_specs=[HBM] * 3 + [VMEM] * 4,
        name="build",
    )
    relayed = numbers(to_relay(places))
    ghost = shape(8, LANES)
    ghost_s = scratch(8, LANES)
    first_arrived = arrived
    for sweep in range(SWEEPS - 1):
        lat_ghost, lon_ghost, row = call(
            blend_kernel,
            [ghost, ghost, shape(8, CELLS)],
            (ints, strip, factors, arrived, high, low),
            [],
            name="blend",
            limit=4,
            keep=(1, 2, 3, 4, 5),
        )
        (buffer,) = call(
            refill_kernel,
            [shape(devices, 8, CELLS)],
            (chunks, swap(row), buffer),
            [],
            aliases={2: 0},
            name="refill",
            limit=4,
            keep=(2,),
        )
        arrived = deliver(buffer)
        fields, strip = call(
            sweep_kernel,
            [state, strips],
            (ints, fields, coef, lat_ghost, lon_ghost),
            [state_s, coef_s, state_s, square, square, square, semaphores(3)],
            specs=[SMEM, HBM, HBM, VMEM, VMEM],
            out_specs=[HBM, VMEM],
            name="sweep",
        )
        if sweep == 0:
            (blocks,) = call(
                relay_kernel,
                [shape(16, CELLS)],
                (relayed, first_arrived),
                [],
                name="relay",
                limit=4,
            )
            blocks = to_relay(blocks).reshape(8, 2, CELLS)
            blocks = jnp.pad(blocks, ((0, 0), (0, 14), (0, 0)))
            (warm,) = call(
                heat_kernel,
                [shape(2, 2, ROWS, CELLS)],
                (ints, warm, blocks, weights),
                [scratch(4, CELLS, CELLS), ghost_s, ghost_s, square, square, square, semaphores(3)],
                specs=[SMEM, HBM, VMEM, HBM],
                name="heat",
                limit=4,
            )
    ready, beside, above = call(
        ahead_kernel,
        [shape(8, CELLS, CELLS), shape(3, 2, CELLS, CELLS), shape(2, 3, 2, 8, CELLS)],
        (ints, fields, coef),
        [state_s, coef_s, square, square, square, ghost_s, semaphores(2)],
        specs=[SMEM, HBM, HBM],
        name="ahead",
    )
    flow, pressure, heat = call(
        final_kernel,
        [shape(6, CELLS, CELLS), shape(2, CELLS, CELLS), shape(2, CELLS, CELLS)],
        (ints, arrived, high, low, ready, beside, above, warm),
        [ghost_s, ghost_s, square, square],
        name="final",
        limit=8,
        keep=(1, 2, 3),
    )
    return flow.reshape(3, 1, 2, CELLS, CELLS), pressure[None], heat[None]


def solution(mesh):
    placed = (
        P(None, "patch", None, "lat", "lon"),
        P("patch", None, "lat", "lon"),
        P("patch", None, "lat", "lon"),
        P("patch", None, "lat", "lon"),
        P("patch", "lat", "lon", None),
        P("patch", "lat", "lon", None),
        P("patch", "lat", "lon", None),
        P("patch", "lat", "lon", None, None, None),
    )
    return jax.shard_map(
        shards,
        mesh=mesh,
        in_specs=placed,
        out_specs=(
            P(None, "patch", None, "lat", "lon"),
            P("patch", None, "lat", "lon"),
            P("patch", None, "lat", "lon"),
        ),
        check_vma=False,
    )
```

```python
import jax
import jax.numpy as jnp
from jax import lax
from jax.experimental import pallas as pl
from jax.experimental.pallas import tpu as pltpu
from jax.sharding import PartitionSpec as P

SWEEPS = 4
CELLS = 128
TILES = 16
ROWS = CELLS + 16
LANES = 2 * CELLS
HALO = 4
PLANES = 12
F32 = jnp.float32
VMEM = pl.BlockSpec(memory_space=pltpu.VMEM)
SMEM = pl.BlockSpec(memory_space=pltpu.SMEM)
HBM = pl.BlockSpec(memory_space=pltpu.HBM)
NORTH, SOUTH, WEST, EAST = 1, 2, 3, 4
LAT_BASE, LON_BASE = 5, 6
CHUNKS = 7
PLACES = 10
WARM = 22
SLOTS = 8


def lanes():
    return lax.broadcasted_iota(jnp.int32, (8, CELLS), 1)


def sublanes():
    return lax.broadcasted_iota(jnp.int32, (8, CELLS), 0)


def turn(x, shift):
    shift = shift % CELLS
    return x if shift == 0 else pltpu.roll(x, shift, 1)


def tile(b):
    return pl.ds(8 * b, 8)


class Copies:
    def __init__(self, sems):
        self.sems, self.going = sems, []

    def start(self, source, target):
        copy = pltpu.make_async_copy(source, target, self.sems.at[len(self.going)])
        copy.start()
        self.going.append(copy)

    def wait(self, first=0, last=None):
        for copy in self.going[first:last]:
            copy.wait()


def start_kernel(
    at, slots, flow, pressure, heat, friction, weights, chunks, top, bottom, places, near, named, row, sems
):
    start = pl.multiple_of((at[0] // 8) * 8, 8)
    copies = Copies(sems)
    copies.start(slots, named)
    copies.start(flow.at[:, pl.ds(start, 8), :], near.at[0:6])
    copies.start(pressure.at[:, pl.ds(start, 8), :], near.at[6:8])
    copies.start(heat.at[:, pl.ds(start, 8), :], near.at[8:10])
    for out, lo in ((top, 0), (bottom, CELLS - 8)):
        copies.start(flow.at[:, lo : lo + 8, :], out.at[0:6])
        copies.start(pressure.at[:, lo : lo + 8, :], out.at[6:8])
        copies.start(heat.at[:, lo : lo + 8, :], out.at[8:10])
        copies.start(friction.at[:, lo : lo + 8, :], out.at[10:12])
        copies.start(weights.at[4:8, lo : lo + 8, :], out.at[12:16])
    row[8:16, :] = jnp.broadcast_to((at[4] + 1).astype(F32), (8, CELLS))
    chunks[...] = jnp.zeros(chunks.shape, F32)
    copies.wait()
    own = jnp.broadcast_to(named[...], (8, CELLS)) == sublanes()
    place = jnp.sum(jnp.where(own, lanes() + 1, 0).astype(F32), axis=1, keepdims=True)
    place = jnp.broadcast_to(place, (8, CELLS))
    for out in (top.at[16], bottom.at[16], places):
        out[...] = place
    inside = at[0] - start
    for f in range(10):
        to = f if f < 8 else f + 1
        row[to : to + 1, :] = near[f, pl.ds(inside, 1), :]
    for n in range(3):
        chunks[at[1 + n]] = row[...]


def pack_kernel(table, arrived, out):
    count = out.shape[1]
    for lat in range(out.shape[0]):
        for n in range(SLOTS):
            out[lat, n] = arrived[table[SLOTS * lat + n], 0:8, :]
        if count > SLOTS:
            for n in range(4):
                block = table[SLOTS * out.shape[0] + 4 * lat + n]
                out[lat, SLOTS, 2 * n : 2 * n + 2, :] = arrived[block, 9:11, :]


def columns_kernel(
    flow, pressure, heat, friction, weights, north, south, places,
    to_west, to_east, own, cols_s, rows_s, sems,
):
    lane = lanes()
    copies = Copies(sems)
    copies.start(flow, own.at[0:6])
    copies.start(pressure, own.at[6:8])
    copies.start(heat, own.at[8:10])
    copies.start(friction, own.at[10:12])
    for n in range(4):
        lo = 2 * HALO * PLANES + 8 * n
        copies.start(weights.at[n, 0:8, :], to_west.at[lo : lo + 8, :])
        copies.start(weights.at[n, CELLS - 8 : CELLS, :], to_east.at[lo : lo + 8, :])
    for out in (to_west, to_east):
        out[2 * HALO * PLANES + 32 :, :] = places[...]

    def pack(block):
        gathered = jnp.zeros((8, CELLS), F32)
        for f in range(PLANES):
            gathered = jnp.where(lane // 8 == f, turn(block(f), 8 * f + HALO), gathered)
        return gathered

    def unload(first):
        rows_s[...] = cols_s[...].T
        for f in range(PLANES):
            lo = first + HALO * f
            to_east[lo : lo + HALO, :] = rows_s[8 * f : 8 * f + HALO, :]
            to_west[lo : lo + HALO, :] = rows_s[8 * f + HALO : 8 * f + 8, :]

    cols_s[...] = jnp.zeros((CELLS, CELLS), F32)
    cols_s[tile(TILES - 1), :] = pack(lambda f: north[f])
    cols_s[tile(0), :] = pack(lambda f: south[f])
    unload(HALO * PLANES)
    copies.wait()
    for b in range(TILES):
        cols_s[tile(b), :] = pack(lambda f: own[f, tile(b), :])
    unload(0)


def sideways(first, second):
    lane = lanes()
    f_up, s_up = pltpu.roll(first, 1, 1), pltpu.roll(second, 1, 1)
    f_down, s_down = pltpu.roll(first, CELLS - 1, 1), pltpu.roll(second, CELLS - 1, 1)
    lefts = (jnp.where(lane == 0, s_up, f_up), jnp.where(lane == 0, f_up, s_up))
    rights = (
        jnp.where(lane == CELLS - 1, s_down, f_down),
        jnp.where(lane == CELLS - 1, f_down, s_down),
    )
    return lefts, rights


def around(ref, b, halves):
    both = [ref[half, tile(b), :] for half in range(2)]
    lefts, rights = sideways(*both)
    found = []
    for half in range(halves):
        up = pltpu.roll(both[half], 1, 0) if b == 0 else ref[half, 8 * b - 1 : 8 * b + 7, :]
        down = pltpu.roll(both[half], 7, 0) if b == TILES + 1 else ref[half, 8 * b + 1 : 8 * b + 9, :]
        found.append((both[half], up, down, lefts[half], rights[half]))
    return found


def build_kernel(
    ints, flow, pressure, heat, friction, weights, north, south, west, east,
    fields_out, coef_out, warm_out, strip, factors, high, low,
    fields, coef, warm, thick, chosen, cols_s, rows_s, sems,
):
    lane = lanes()
    copies = Copies(sems)
    inner = pl.ds(8, CELLS)
    copies.start(friction, thick.at[:, 0, inner, :])
    copies.start(heat, warm.at[:, 0, inner, :])
    copies.start(flow, fields.at[0:6, 0, inner, :])
    copies.start(pressure, fields.at[6:8, 0, inner, :])
    copies.start(weights.at[pl.ds(ints[LAT_BASE], 2)], chosen.at[0:2])
    copies.start(weights.at[pl.ds(ints[LON_BASE], 2)], chosen.at[2:4])

    def target(f):
        if f < 8:
            return fields.at[f]
        return warm.at[f - 8] if f < 10 else thick.at[f - 10]

    outer = (lane < HALO) | (lane >= CELLS - HALO)

    def load(first):
        for f in range(PLANES):
            lo = first + HALO * f
            rows_s[8 * f : 8 * f + HALO, :] = west[lo : lo + HALO, :]
            rows_s[8 * f + HALO : 8 * f + 8, :] = east[lo : lo + HALO, :]
        cols_s[...] = rows_s[...].T

    def place(f, b, block):
        target(f)[1, tile(b), :] = jnp.where(outer, turn(block, -8 * f - HALO), 0.0)

    rows_s[8 * PLANES : CELLS, :] = jnp.zeros((CELLS - 8 * PLANES, CELLS), F32)
    load(0)
    for f in range(PLANES):
        target(f)[0, tile(0), :] = north[f]
        target(f)[0, tile(TILES + 1), :] = south[f]
        for b in range(TILES):
            place(f, b + 1, cols_s[tile(b), :])
    load(HALO * PLANES)
    for f in range(PLANES):
        place(f, 0, cols_s[tile(TILES - 1), :])
        place(f, TILES + 1, cols_s[tile(0), :])
    copies.wait()
    copies.start(fields, fields_out)
    copies.start(warm, warm_out)
    strip_of(ints, fields, strip)

    at_north, at_south = ints[NORTH] > 0, ints[SOUTH] > 0
    at_west, at_east = ints[WEST] > 0, ints[EAST] > 0
    for k in range(2):
        for half in range(2):
            first = jnp.broadcast_to(thick[k, half, 8:9, :], (8, CELLS))
            last = jnp.broadcast_to(thick[k, half, ROWS - 9 : ROWS - 8, :], (8, CELLS))
            for b, at_end, line in ((0, at_north, first), (TILES + 1, at_south, last)):
                thick[k, half, tile(b), :] = jnp.where(at_end, line, thick[k, half, tile(b), :])
        for b in range(TILES + 2):
            own, other = thick[k, 0, tile(b), :], thick[k, 1, tile(b), :]
            other = jnp.where((lane == CELLS - 1) & at_west, turn(own, -1), other)
            other = jnp.where((lane == 0) & at_east, turn(own, 1), other)
            thick[k, 1, tile(b), :] = jnp.where(other > 0.0, other, 1.0)

    for b in range(TILES + 2):
        found = [around(thick.at[k], b, 2) for k in range(2)]
        for half in range(2):
            between = 0.5 * (found[0][half][0] + found[1][half][0])
            for k in range(2):
                here, *others = found[k][half]
                faces = [0.5 * (here + other) for other in others]
                diagonal = (faces[0] + faces[1]) + (faces[2] + faces[3]) + (between + here)
                inverse = 0.8 / diagonal
                for n, face in enumerate(faces):
                    coef[n, k, half, tile(b), :] = inverse * face
                coef[4, k, half, tile(b), :] = inverse * between
                coef[5, k, half, tile(b), :] = 0.5 * inverse
                coef[6, k, half, tile(b), :] = inverse * warm[k, half, tile(b), :]
                coef[7, k, half, tile(b), :] = 0.125 * here
    copies.start(coef, coef_out)
    at = ints[0] + 8
    for n in range(8):
        for f in range(8):
            factors[n, f : f + 1, :] = coef[n, f % 2, 0, pl.ds(at, 1), :]

    blank = jnp.zeros((8, CELLS), F32)
    for side in range(2):
        for term in range(2):
            cut = slice(term * CELLS, (term + 1) * CELLS)
            if side == 0:
                lo = pl.multiple_of(2 * HALO * PLANES + 8 * (ints[LAT_BASE] + term), 8)
                before, after = west[pl.ds(lo, 8), :], east[pl.ds(lo, 8), :]
            else:
                before = north[8 + ints[LON_BASE] + term]
                after = south[8 + ints[LON_BASE] + term]
            ends = [jnp.concatenate([after, blank], axis=0)]
            ends += [jnp.zeros((16, CELLS), F32)] * 6
            ends += [jnp.concatenate([blank, before], axis=0)]
            for n in range(16):
                if n < 8:
                    block = chosen[2 * side + term, 16 * n : 16 * n + 16, :]
                else:
                    block = ends[n - 8]
                for out, part in zip((high, low), split(block)):
                    out[side, 16 * n : 16 * n + 16, cut] = part
    copies.wait(6)


def strip_of(ints, fields, strip):
    at = ints[0] + 8
    for f in range(8):
        strip[0, f : f + 1, :] = fields[f, 0, pl.ds(at, 1), :]
        strip[1, f : f + 1, :] = fields[f, 1, pl.ds(at, 1), :]
        strip[2, f : f + 1, :] = fields[f, 0, pl.ds(at - 1, 1), :]
        strip[3, f : f + 1, :] = fields[f, 0, pl.ds(at + 1, 1), :]


def split(x):
    high = x.astype(jnp.bfloat16)
    return high, (x - high.astype(F32)).astype(jnp.bfloat16)


def times(left, right):
    return lax.dot_general(left, right, (((1,), (1,)), ((), ())), preferred_element_type=F32)


def blend_sides(ints, arrived, high, low, lat_ghost, lon_ghost):
    sides = (
        (lat_ghost, (ints[NORTH] + ints[SOUTH]) > 0, PLACES),
        (lon_ghost, (ints[WEST] + ints[EAST]) > 0, PLACES + 6),
    )
    for n, (ghost, active, places) in enumerate(sides):
        ghost[...] = jnp.zeros((8, LANES), F32)

        @pl.when(active)
        def _():
            blocks = [
                jnp.concatenate([arrived[ints[places + 2 * who + t]] for t in range(2)], axis=1)
                for who in range(3)
            ]
            b_high, b_low = split(jnp.concatenate(blocks, axis=0))
            both = times(jnp.concatenate([b_high, b_low], axis=0), high[n])
            total = both[0:24] + both[24:48] + times(b_high, low[n])
            ghost[:, 0:CELLS] = total[0:8, 0:CELLS]
            ghost[:, CELLS:LANES] = jnp.where(
                lanes() < CELLS // 2, total[16:24, CELLS:LANES], total[8:16, CELLS:LANES]
            )


def blend_kernel(ints, strip, factors, arrived, high, low, lat_ghost, lon_ghost, chunks):
    blend_sides(ints, arrived, high, low, lat_ghost, lon_ghost)
    at = ints[0]
    lane, sub = lanes(), sublanes()
    here, outside, up, down = strip[0], strip[1], strip[2], strip[3]
    up = jnp.where((ints[NORTH] > 0) & (at == 0), lat_ghost[:, 0:CELLS], up)
    down = jnp.where((ints[SOUTH] > 0) & (at == CELLS - 1), lat_ghost[:, 0:CELLS], down)
    beside = jnp.sum(jnp.where(lane == at, lon_ghost[:, 0:CELLS], 0.0), axis=1, keepdims=True)
    on_side = ((lane == CELLS - 1) & (ints[WEST] > 0)) | ((lane == 0) & (ints[EAST] > 0))
    outside = jnp.where(on_side, beside, outside)
    lefts, rights = sideways(here, outside)
    left, right = lefts[0], rights[0]
    even = sub % 2 == 0
    partner = jnp.where(even, pltpu.roll(here, 7, 0), pltpu.roll(here, 1, 0))
    value = 0.2 * here + factors[0] * up + factors[1] * down
    value = value + factors[2] * left + factors[3] * right + factors[4] * partner
    value = value + jnp.where(sub < 2, factors[6], 0.0)
    steps = (jnp.where(even, partner, -partner), down - up, right - left)
    slope = jnp.where(
        sub < 2,
        pltpu.roll(steps[0], 2, 0),
        jnp.where(sub < 4, pltpu.roll(steps[1], 4, 0), pltpu.roll(steps[2], 6, 0)),
    )
    value = value - factors[5] * slope
    divergence = (
        pltpu.roll(steps[0], 6, 0) + pltpu.roll(steps[1], 4, 0) + pltpu.roll(steps[2], 2, 0)
    )
    row = jnp.where(sub < 6, value, here - factors[7] * divergence)
    chunks[...] = jnp.zeros(chunks.shape, F32)
    for n in range(3):
        chunks[ints[CHUNKS + n]] = row


def ghost_columns(count, lon_ghost, cut, rows_s, out):
    for f in range(count):
        for lane in (2 * f, (2 * f - 1) % CELLS):
            rows_s[lane : lane + 1, :] = lon_ghost[f : f + 1, cut]
    out[...] = rows_s[...].T


def put_ghosts(ints, count, lat_ghost, lon_ghost, full, cols_s, ends_s, rows_s):
    lane, sub = lanes(), sublanes()
    rows_s[...] = jnp.zeros((CELLS, CELLS), F32)
    ghost_columns(count, lon_ghost, slice(0, CELLS), rows_s, cols_s)
    ghost_columns(count, lon_ghost, slice(CELLS, LANES), rows_s, ends_s)
    on_side = ((lane == CELLS - 1) & (ints[WEST] > 0)) | ((lane == 0) & (ints[EAST] > 0))
    ends = ((0, (sub == 7) & (ints[NORTH] > 0)), (TILES + 1, (sub == 0) & (ints[SOUTH] > 0)))
    for b, edge in ends:
        for f in range(count):
            for half in range(2):
                line = lat_ghost[f : f + 1, half * CELLS : (half + 1) * CELLS]
                full[f, half, tile(b), :] = jnp.where(edge, line, full[f, half, tile(b), :])
    for b in range(TILES + 2):
        if b == 0:
            column = ends_s[tile(TILES - 1), :]
        elif b == TILES + 1:
            column = ends_s[tile(0), :]
        else:
            column = cols_s[tile(b - 1), :]
        for f in range(count):
            other = full[f, 1, tile(b), :]
            full[f, 1, tile(b), :] = jnp.where(on_side, turn(column, -2 * f), other)


def relaxed(full, coef, b, halves):
    found = [around(full.at[f], b, halves) for f in range(8)]
    answers = []
    for half in range(halves):
        at = [found[f][half] for f in range(8)]

        def factor(n, k):
            return coef[n, k, half, tile(b), :]

        new = []
        for component in range(3):
            for k in range(2):
                here, up, down, left, right = at[2 * component + k]
                value = 0.2 * here + factor(0, k) * up + factor(1, k) * down
                value = value + factor(2, k) * left + factor(3, k) * right
                value = value + factor(4, k) * at[2 * component + 1 - k][0]
                if component == 0:
                    value = value + factor(6, k)
                    slope = at[7][0] if k == 0 else -at[6][0]
                elif component == 1:
                    slope = at[6 + k][2] - at[6 + k][1]
                else:
                    slope = at[6 + k][4] - at[6 + k][3]
                new.append(value - factor(5, k) * slope)
        for k in range(2):
            divergence = (at[2 + k][2] - at[2 + k][1]) + (at[4 + k][4] - at[4 + k][3])
            divergence = divergence + at[1][0] if k == 0 else divergence - at[0][0]
            new.append(at[6 + k][0] - factor(7, k) * divergence)
        answers.append(new)
    return answers


def sweep_kernel(
    ints, fields, coef, lat_ghost, lon_ghost, out, strip,
    full, factor, new_full, cols_s, ends_s, rows_s, sems,
):
    copies = Copies(sems)
    copies.start(fields, full)
    copies.start(coef, factor)
    copies.wait(0, 1)
    put_ghosts(ints, 8, lat_ghost, lon_ghost, full, cols_s, ends_s, rows_s)
    copies.wait(1, 2)
    for b in range(TILES + 2):
        for half, new in enumerate(relaxed(full, factor, b, 2)):
            for f in range(8):
                new_full[f, half, tile(b), :] = new[f]
    copies.start(new_full, out)
    strip_of(ints, new_full, strip)
    copies.wait(2)


def heat_kernel(
    ints, warm, arrived, weights, out, chosen, block, lat_ghost, lon_ghost, cols_s, ends_s, rows_s, sems
):
    copies = Copies(sems)
    copies.start(warm, out)
    copies.start(weights.at[pl.ds(ints[LAT_BASE], 2)], chosen.at[0:2])
    copies.start(weights.at[pl.ds(ints[LON_BASE], 2)], chosen.at[2:4])
    copies.wait()
    sides = (
        (lat_ghost, (ints[NORTH] + ints[SOUTH]) > 0),
        (lon_ghost, (ints[WEST] + ints[EAST]) > 0),
    )
    block[...] = jnp.zeros((16, CELLS), F32)
    for n, (ghost, active) in enumerate(sides):
        ghost[...] = jnp.zeros((8, LANES), F32)

        @pl.when(active)
        def _():
            total = jnp.zeros((16, CELLS), F32)
            for term in range(2):
                at = WARM + 2 * n + term
                for k in range(2):
                    block[k : k + 1, :] = arrived[ints[at], pl.ds(2 * ints[at + 4] + k, 1), :]
                b_high, b_low = split(block[...])
                w_high, w_low = split(chosen[2 * n + term])
                total = total + times(b_high, w_low) + times(b_low, w_high) + times(b_high, w_high)
            ghost[:, 0:CELLS] = total[0:8]

    put_ghosts(ints, 2, lat_ghost, lon_ghost, out, cols_s, ends_s, rows_s)


def ahead_kernel(ints, fields, coef, new, beside, above, full, factor, cols_s, ends_s, rows_s, blank, sems):
    copies = Copies(sems)
    copies.start(fields, full)
    copies.start(coef, factor)
    blank[...] = jnp.zeros((8, LANES), F32)
    copies.wait(0, 1)
    put_ghosts(ints, 8, blank, blank, full, cols_s, ends_s, rows_s)
    copies.wait(1, 2)
    lane, sub = lanes(), sublanes()
    first, last = (lane == 0) & (ints[WEST] > 0), (lane == CELLS - 1) & (ints[EAST] > 0)
    ends = ((1, 0, (sub == 0) & (ints[NORTH] > 0), 1.0), (TILES, 1, (sub == 7) & (ints[SOUTH] > 0), -1.0))
    for b in range(1, TILES + 1):
        (answer,) = relaxed(full, factor, b, 1)
        for f in range(8):
            new[f, tile(b - 1), :] = answer[f]
        for k in range(2):
            at = [factor[n, k, 0, tile(b), :] for n in (2, 3, 5, 7)]
            beside[0, k, tile(b - 1), :] = jnp.where(first, at[0], jnp.where(last, at[1], 0.0))
            for n in (1, 2):
                beside[n, k, tile(b - 1), :] = jnp.where(
                    first, at[n + 1], jnp.where(last, -at[n + 1], 0.0)
                )
    for end, (b, n, edge, sign) in enumerate(ends):
        for k in range(2):
            above[end, 0, k] = jnp.where(edge, factor[n, k, 0, tile(b), :], 0.0)
            above[end, 1, k] = jnp.where(edge, sign * factor[5, k, 0, tile(b), :], 0.0)
            above[end, 2, k] = jnp.where(edge, sign * factor[7, k, 0, tile(b), :], 0.0)


def corrected(new, ghost, parts, component):
    out = []
    for f in range(6):
        k = f % 2
        value = new[f] + parts[0][k] * ghost[f]
        if f // 2 == component:
            value = value + parts[1][k] * ghost[6 + k]
        out.append(value)
    for k in range(2):
        out.append(new[6 + k] + parts[2][k] * ghost[2 * component + k])
    return out


def final_kernel(
    ints, arrived, high, low, ready, beside, above, warm,
    flow_out, pressure_out, heat_out, lat_ghost, lon_ghost, cols_s, rows_s,
):
    blend_sides(ints, arrived, high, low, lat_ghost, lon_ghost)
    rows_s[...] = jnp.zeros((CELLS, CELLS), F32)
    ghost_columns(8, lon_ghost, slice(0, CELLS), rows_s, cols_s)
    for b in range(TILES):
        new = [ready[f, tile(b), :] for f in range(8)]
        if b == 0 or b == TILES - 1:
            end = 0 if b == 0 else 1
            ghost = [lat_ghost[f : f + 1, 0:CELLS] for f in range(8)]
            new = corrected(new, ghost, [[above[end, n, k] for k in range(2)] for n in range(3)], 1)
        column = cols_s[tile(b), :]
        ghost = [turn(column, -2 * f) for f in range(8)]
        parts = [[beside[n, k, tile(b), :] for k in range(2)] for n in range(3)]
        new = corrected(new, ghost, parts, 2)
        for f in range(6):
            flow_out[f, tile(b), :] = new[f]
        for k in range(2):
            pressure_out[k, tile(b), :] = new[6 + k]
        layers = [around(warm.at[k], b + 1, 1)[0] for k in range(2)]
        for k in range(2):
            here, up, down, left, right = layers[k]
            under = jnp.ones((8, CELLS), F32) if k == 0 else layers[0][0]
            over = layers[1][0] if k == 0 else jnp.zeros((8, CELLS), F32)
            advect = jnp.zeros((8, CELLS), F32)
            for component, minus, plus in ((0, under, over), (1, up, down), (2, left, right)):
                speed = new[2 * component + k]
                advect = advect + jnp.maximum(speed, 0.0) * (here - minus)
                advect = advect + jnp.minimum(speed, 0.0) * (plus - here)
            spread = (up + down) + (left + right) + (under + over) - 6.0 * here
            heat_out[k, tile(b), :] = here + 0.1 * (spread - advect)


def shape(*dims):
    return jax.ShapeDtypeStruct(dims, F32)


def scratch(*dims):
    return pltpu.VMEM(dims, F32)


def call(
    kernel, outs, ins, scratches, specs=None, out_specs=None, aliases=None, name=None, limit=16, keep=()
):
    specs = specs or [SMEM] + [VMEM] * (len(ins) - 1)
    out_specs = out_specs or [VMEM] * len(outs)
    placed = []
    for n, (x, spec) in enumerate(zip(ins, specs)):
        if spec is HBM or n in keep:
            x = pltpu.with_memory_space_constraint(x, spec.memory_space)
        placed.append(x)
    outs = [pltpu.HBM(x.shape, x.dtype) if spec is HBM else x for x, spec in zip(outs, out_specs)]
    return pl.pallas_call(
        kernel,
        out_shape=outs,
        in_specs=specs,
        out_specs=out_specs,
        scratch_shapes=scratches,
        input_output_aliases=aliases or {},
        compiler_params=pltpu.CompilerParams(vmem_limit_bytes=limit * 1024 * 1024),
        name=name,
    )(*placed)


def semaphores(count):
    return pltpu.SemaphoreType.DMA((count,))


def shards(
    flow_vector,
    normal_stress,
    thermal_field,
    shear_resistance,
    departing_bands,
    receiving_processor,
    shift_filled_by_lane,
    blending_factors,
):
    flow = flow_vector.reshape(6, CELLS, CELLS)
    pressure = normal_stress[0]
    heat = thermal_field[0]
    friction = shear_resistance[0]
    weights = blending_factors.reshape(8, CELLS, CELLS)
    lat, lon = lax.axis_index("lat"), lax.axis_index("lon")
    n_lat, n_lon = lax.axis_size("lat"), lax.axis_size("lon")
    devices = n_lat * n_lon
    own_row = departing_bands.reshape(1)

    def ring(x, axis, step):
        count = lax.axis_size(axis)
        pairs = [(i, i + step) for i in range(count) if 0 <= i + step < count]
        return lax.ppermute(x, axis, pairs)

    receiver = receiving_processor.reshape(1)
    other = (1 - lax.axis_index("patch")) * n_lon
    column = jnp.maximum(receiver, 0) % n_lon + jnp.array([0, -1, 1], jnp.int32)
    chunk = other + jnp.clip(column, 0, n_lon - 1)
    first = jnp.concatenate([own_row, chunk, receiver])

    planes = (flow, pressure, heat, friction, weights)
    chunks, top, bottom, places = call(
        start_kernel,
        [shape(2 * n_lon, 16, CELLS), shape(17, 8, CELLS), shape(17, 8, CELLS), shape(8, CELLS)],
        (first, shift_filled_by_lane.reshape(1, CELLS), *planes),
        [scratch(10, 8, CELLS), pltpu.VMEM((1, CELLS), jnp.int32), scratch(16, CELLS), semaphores(14)],
        specs=[SMEM] + [HBM] * 6,
        name="start",
    )

    def across(chunks):
        return lax.all_to_all(chunks, ("patch", "lon"), 0, 0, tiled=True)

    def along(table, blocks, slots):
        (packed,) = call(
            pack_kernel,
            [shape(n_lat, slots, 8, CELLS)],
            (table, blocks),
            [],
            name="pack",
            limit=4,
            keep=(1,),
        )
        return lax.all_to_all(packed, "lat", 0, 0, tiled=True).reshape(n_lat * slots, 8, CELLS)

    arrived = across(chunks)
    sent_to = lax.dynamic_slice(arrived, (other, 8, 0), (n_lon, 1, 1)).reshape(n_lon)
    sent_to = sent_to.astype(jnp.int32) - 1
    every_lat = jnp.arange(n_lat, dtype=jnp.int32)[:, None]
    to_lat, to_lon = (sent_to // n_lon)[None], (sent_to % n_lon)[None]
    exact = (sent_to >= 0)[None] & (to_lat == every_lat)
    close = (sent_to >= 0)[None] & (jnp.abs(to_lat - every_lat) == 1) & (to_lon == lon)

    def sorted_blocks(wanted, count):
        rank = jnp.sum(
            (wanted[:, None, :] & (jnp.arange(n_lon)[None, None, :] < jnp.arange(n_lon)[None, :, None]))
            .astype(jnp.int32),
            axis=2,
        )
        mine = wanted[:, None, :] & (rank[:, None, :] == jnp.arange(count)[None, :, None])
        found = jnp.sum(jnp.where(mine, jnp.arange(n_lon, dtype=jnp.int32)[None, None, :], 0), axis=2)
        return other + found.reshape(-1)

    table = jnp.concatenate(
        [sorted_blocks(exact | close, SLOTS), sorted_blocks(exact & (to_lon == lon), 4)]
    ).astype(jnp.int32)
    arrived = along(table, arrived, SLOTS + 1)
    north, south = ring(bottom, "lat", 1), ring(top, "lat", -1)
    wide = shape(2 * HALO * PLANES + 40, CELLS)
    square = scratch(CELLS, CELLS)
    to_west, to_east = call(
        columns_kernel,
        [wide, wide],
        (*planes, north, south, places),
        [scratch(PLANES, CELLS, CELLS), square, square, semaphores(12)],
        specs=[HBM] * 5 + [VMEM] * 3,
        name="columns",
    )
    west, east = ring(to_east, "lon", 1), ring(to_west, "lon", -1)

    def numbers(block):
        return block[:, 0].astype(jnp.int32) - 1

    on_edge = jnp.stack([lat == 0, lat == n_lat - 1, lon == 0, lon == n_lon - 1]).astype(jnp.int32)
    own, before, after = numbers(places), numbers(west[-8:]), numbers(east[-8:])
    above, below = numbers(north[16]), numbers(south[16])

    def side(block, base, last):
        return jnp.where(last, block[base + 2 : base + 4], block[base : base + 2])

    pick = [side(x, 0, lat > 0) for x in (own, before, after)]
    pick += [side(x, 4, lon > 0) for x in (own, above, below)]
    pick = jnp.concatenate(pick)

    def slot_of(chosen, listed, most):
        same = (listed >= 0)[None] & (listed[None] // n_lon == chosen[:, None] // n_lon)
        earlier = same & (listed[None] < chosen[:, None])
        return jnp.minimum(jnp.sum(earlier.astype(jnp.int32), axis=1), most)

    slot = slot_of(pick, jnp.concatenate([own, before, after, above, below]), SLOTS - 1)
    from_lat = jnp.maximum(pick, 0) // n_lon
    mine = jnp.concatenate([pick[0:2], pick[6:8]])
    mine_from = jnp.concatenate([from_lat[0:2], from_lat[6:8]])
    warm_at = [mine_from * (SLOTS + 1) + SLOTS, slot_of(mine, own, 3)]
    bases = jnp.stack([jnp.where(lat > 0, 2, 0), jnp.where(lon > 0, 6, 4)]).astype(jnp.int32)

    def integers(slots):
        return jnp.concatenate([own_row, on_edge, bases, chunk, from_lat * slots + slot, *warm_at])

    ints_first, ints = integers(SLOTS + 1), integers(SLOTS)

    state = shape(8, 2, ROWS, CELLS)
    state_s = scratch(8, 2, ROWS, CELLS)
    coef_s = scratch(8, 2, 2, ROWS, CELLS)
    warm_s = scratch(2, 2, ROWS, CELLS)
    strips = shape(4, 8, CELLS)
    joined = jax.ShapeDtypeStruct((2, LANES, LANES), jnp.bfloat16)
    fields, coef, warm, strip, factors, high, low = call(
        build_kernel,
        [
            state,
            shape(8, 2, 2, ROWS, CELLS),
            shape(2, 2, ROWS, CELLS),
            strips,
            shape(8, 8, CELLS),
            joined,
            joined,
        ],
        (ints, *planes, north, south, west, east),
        [state_s, coef_s, warm_s, warm_s, scratch(4, CELLS, CELLS), square, square, semaphores(9)],
        specs=[SMEM] + [HBM] * 5 + [VMEM] * 4,
        out_specs=[HBM] * 3 + [VMEM] * 4,
        name="build",
    )
    ghost = shape(8, LANES)
    ghost_s = scratch(8, LANES)
    for sweep in range(SWEEPS - 1):
        lat_ghost, lon_ghost, chunks = call(
            blend_kernel,
            [ghost, ghost, shape(2 * n_lon, 8, CELLS)],
            (ints_first if sweep == 0 else ints, strip, factors, arrived, high, low),
            [],
            name="blend",
            limit=4,
            keep=(1, 2, 3, 4, 5),
        )
        if sweep == 0:
            (warm,) = call(
                heat_kernel,
                [shape(2, 2, ROWS, CELLS)],
                (ints, warm, arrived, weights),
                [scratch(4, CELLS, CELLS), scratch(16, CELLS), ghost_s, ghost_s, square, square, square]
                + [semaphores(3)],
                specs=[SMEM, HBM, VMEM, HBM],
                name="heat",
                limit=4,
            )
        arrived = along(table[: n_lat * SLOTS], across(chunks), SLOTS)
        fields, strip = call(
            sweep_kernel,
            [state, strips],
            (ints, fields, coef, lat_ghost, lon_ghost),
            [state_s, coef_s, state_s, square, square, square, semaphores(3)],
            specs=[SMEM, HBM, HBM, VMEM, VMEM],
            out_specs=[HBM, VMEM],
            name="sweep",
        )
    ready, beside, above = call(
        ahead_kernel,
        [shape(8, CELLS, CELLS), shape(3, 2, CELLS, CELLS), shape(2, 3, 2, 8, CELLS)],
        (ints, fields, coef),
        [state_s, coef_s, square, square, square, ghost_s, semaphores(2)],
        specs=[SMEM, HBM, HBM],
        name="ahead",
    )
    flow, pressure, heat = call(
        final_kernel,
        [shape(6, CELLS, CELLS), shape(2, CELLS, CELLS), shape(2, CELLS, CELLS)],
        (ints, arrived, high, low, ready, beside, above, warm),
        [ghost_s, ghost_s, square, square],
        name="final",
        limit=8,
        keep=(1, 2, 3),
    )
    return flow.reshape(3, 1, 2, CELLS, CELLS), pressure[None], heat[None]


def solution(mesh):
    placed = (
        P(None, "patch", None, "lat", "lon"),
        P("patch", None, "lat", "lon"),
        P("patch", None, "lat", "lon"),
        P("patch", None, "lat", "lon"),
        P("patch", "lat", "lon", None),
        P("patch", "lat", "lon", None),
        P("patch", "lat", "lon", None),
        P("patch", "lat", "lon", None, None, None),
    )
    return jax.shard_map(
        shards,
        mesh=mesh,
        in_specs=placed,
        out_specs=(
            P(None, "patch", None, "lat", "lon"),
            P("patch", None, "lat", "lon"),
            P("patch", None, "lat", "lon"),
        ),
        check_vma=False,
    )
```

```python
import jax
import jax.numpy as jnp
from jax import lax
from jax.experimental import pallas as pl
from jax.experimental.pallas import tpu as pltpu
from jax.sharding import PartitionSpec as P

SWEEPS = 4
CELLS = 128
TILES = 16
PLANES = 12
SLOTS = 4
F32 = jnp.float32
VMEM = pl.BlockSpec(memory_space=pltpu.VMEM)
SMEM = pl.BlockSpec(memory_space=pltpu.SMEM)
HBM = pl.BlockSpec(memory_space=pltpu.HBM)
ROW, NORTH, SOUTH, WEST, EAST, LAT_BASE, LON_BASE = range(7)
CHUNK, TO_WEST, TO_EAST = 7, 8, 9
FROM_NORTH, FROM_SOUTH = 10, 11
BLOCKS, RANKS = 12, 16


def lanes():
    return lax.broadcasted_iota(jnp.int32, (8, CELLS), 1)


def sublanes():
    return lax.broadcasted_iota(jnp.int32, (8, CELLS), 0)


def turn(x, shift):
    shift = shift % CELLS
    return x if shift == 0 else pltpu.roll(x, shift, 1)


def tile(b):
    return pl.ds(8 * b, 8)


class Copies:
    def __init__(self, sems):
        self.sems, self.going = sems, []

    def start(self, source, target):
        copy = pltpu.make_async_copy(source, target, self.sems.at[len(self.going)])
        copy.start()
        self.going.append(copy)

    def wait(self, first=0, last=None):
        for copy in self.going[first:last]:
            copy.wait()


def own_lanes(f):
    return 2 * f, (2 * f - 1) % CELLS


def gather_edge(block, f, gathered):
    west, east = own_lanes(f)
    lane = lanes()
    return jnp.where((lane == west) | (lane == east), turn(block, 2 * f), gathered)


def ghost_columns(west, east, rows_s, cols_s):
    rows_s[...] = jnp.zeros((CELLS, CELLS), F32)
    for f, (w, e) in enumerate(zip(west, east)):
        to_w, to_e = own_lanes(f)
        rows_s[to_w : to_w + 1, :] = w
        rows_s[to_e : to_e + 1, :] = e
    cols_s[...] = rows_s[...].T


def around(ref, b, north, south, column, f):
    here = ref[tile(b), :]
    sub, lane = sublanes(), lanes()
    if b == 0:
        up = jnp.where(sub == 0, north, pltpu.roll(here, 1, 0))
    else:
        up = ref[8 * b - 1 : 8 * b + 7, :]
    if b == TILES - 1:
        down = jnp.where(sub == 7, south, pltpu.roll(here, 7, 0))
    else:
        down = ref[8 * b + 1 : 8 * b + 9, :]
    turned = turn(column, -2 * f)
    left = jnp.where(lane == 0, turned, pltpu.roll(here, 1, 1))
    right = jnp.where(lane == CELLS - 1, turned, pltpu.roll(here, CELLS - 1, 1))
    return here, up, down, left, right


def start_kernel(
    ints, slots, flow, pressure, heat, friction,
    chunks, north, south, places, own, named, row, cols_s, rows_s, sems,
):
    copies = Copies(sems)
    copies.start(slots, named)
    copies.start(flow, own.at[0:6])
    copies.start(pressure, own.at[6:8])
    copies.start(heat, own.at[8:10])
    copies.start(friction, own.at[10:12])
    row[8:16, :] = jnp.broadcast_to((ints[4] + 1).astype(F32), (8, CELLS))
    chunks[...] = jnp.zeros(chunks.shape, F32)
    north[...] = jnp.zeros(north.shape, F32)
    south[...] = jnp.zeros(south.shape, F32)
    copies.wait()
    mine = jnp.broadcast_to(named[...], (8, CELLS)) == sublanes()
    place = jnp.sum(jnp.where(mine, lanes() + 1, 0).astype(F32), axis=1, keepdims=True)
    places[...] = jnp.broadcast_to(place, (8, CELLS))
    for f in range(10):
        to = f if f < 8 else f + 1
        row[to : to + 1, :] = own[f, pl.ds(ints[0], 1), :]
    for b in range(TILES):
        gathered = jnp.zeros((8, CELLS), F32)
        for f in range(PLANES):
            gathered = gather_edge(own[f, tile(b), :], f, gathered)
        cols_s[tile(b), :] = gathered
    rows_s[...] = cols_s[...].T
    chunks[ints[1]] = row[...]
    for f in range(PLANES):
        west, east = own_lanes(f)
        chunks[ints[2], f : f + 1, :] = rows_s[west : west + 1, :]
        chunks[ints[3], f : f + 1, :] = rows_s[east : east + 1, :]
        n, at = divmod(f, 8)
        north[n, at : at + 1, :] = own[f, 0:1, :]
        south[n, at : at + 1, :] = own[f, CELLS - 1 : CELLS, :]


def pack_kernel(table, arrived, north, south, out):
    lats, count = out.shape[0], out.shape[1]
    halos = north.shape[0]
    for lat in range(lats):
        for n in range(SLOTS):
            block = table[2 + SLOTS * lat + n]
            out[lat, n] = arrived[block, 0:8, :]
            if count > SLOTS + 1:
                out[lat, count - 1, 2 * n : 2 * n + 2, :] = arrived[block, 9:11, :]
        for n in range(halos):
            out[lat, SLOTS + n] = jnp.zeros((8, CELLS), F32)
    for n in range(halos):
        out[table[0], SLOTS + n] = north[n]
        out[table[1], SLOTS + n] = south[n]


def split(x):
    high = x.astype(jnp.bfloat16)
    return high, (x - high.astype(F32)).astype(jnp.bfloat16)


def times(left, right):
    return lax.dot_general(left, right, (((1,), (1,)), ((), ())), preferred_element_type=F32)


def weights_kernel(ints, weights, high, low, chosen, sems):
    copies = Copies(sems)
    copies.start(weights.at[pl.ds(ints[LAT_BASE], 2)], chosen.at[0:2])
    copies.start(weights.at[pl.ds(ints[LON_BASE], 2)], chosen.at[2:4])
    copies.wait()
    for side in range(2):
        for term in range(2):
            cut = slice(term * CELLS, (term + 1) * CELLS)
            high[side, :, cut], low[side, :, cut] = split(chosen[2 * side + term])


def blend(ints, blocks_of, high, low, ghosts):
    for n, (first, last) in enumerate(((NORTH, SOUTH), (WEST, EAST))):
        ghosts[n] = jnp.zeros((8, CELLS), F32)

        @pl.when(ints[first] + ints[last] > 0)
        def _():
            block = jnp.concatenate([blocks_of(2 * n + t) for t in range(2)], axis=1)
            b_high, b_low = split(block)
            both = times(jnp.concatenate([b_high, b_low], axis=0), high[n])
            ghosts[n] = both[0:8] + both[8:16] + times(b_high, low[n])


def row_block(ints, arrived, slots):
    return lambda n: arrived[ints[BLOCKS + n], ints[RANKS + n]]


def edge_ghosts(ints, arrived, chunks, ghosts, slot, rows):
    halos = (
        arrived[ints[FROM_NORTH], slot],
        arrived[ints[FROM_SOUTH], slot],
        chunks[ints[TO_WEST], rows, :],
        chunks[ints[TO_EAST], rows, :],
    )
    flags = (ints[NORTH], ints[SOUTH], ints[WEST], ints[EAST])
    return [
        jnp.where(flag > 0, ghosts[n // 2], halo) for n, (flag, halo) in enumerate(zip(flags, halos))
    ]


def coefficient_kernel(ints, friction, heat, arrived, chunks, out, halos, cols_s, rows_s):
    slot = SLOTS + 1
    halos[0] = arrived[ints[FROM_NORTH], slot]
    halos[1] = arrived[ints[FROM_SOUTH], slot]
    lane, sub = lanes(), sublanes()
    west = [chunks[ints[TO_WEST], 10 + k : 11 + k, :] for k in range(2)]
    east = [chunks[ints[TO_EAST], 10 + k : 11 + k, :] for k in range(2)]
    ghost_columns(west, east, rows_s, cols_s)
    at_north, at_south = ints[NORTH] > 0, ints[SOUTH] > 0
    at_west, at_east = ints[WEST] > 0, ints[EAST] > 0
    for b in range(TILES):
        centre = [friction[k, tile(b), :] for k in range(2)]
        for k in range(2):
            north, south = halos[0, 2 + k : 3 + k, :], halos[1, 2 + k : 3 + k, :]
            here, up, down, left, right = around(
                friction.at[k], b, north, south, cols_s[tile(b), :], k
            )
            if b == 0:
                up = jnp.where((sub == 0) & at_north, here, up)
            if b == TILES - 1:
                down = jnp.where((sub == 7) & at_south, here, down)
            left = jnp.where((lane == 0) & at_west, here, left)
            right = jnp.where((lane == CELLS - 1) & at_east, here, right)
            faces = [0.5 * (here + other) for other in (up, down, left, right)]
            between = 0.5 * (centre[0] + centre[1])
            diagonal = (faces[0] + faces[1]) + (faces[2] + faces[3]) + (between + here)
            inverse = 0.8 / diagonal
            for n, face in enumerate(faces):
                out[n, k, tile(b), :] = inverse * face
            out[4, k, tile(b), :] = inverse * between
            out[5, k, tile(b), :] = 0.5 * inverse
            out[6, k, tile(b), :] = inverse * heat[k, tile(b), :]
            out[7, k, tile(b), :] = 0.125 * here


def relaxed(planes, coef, ghosts, column, b):
    at = [
        around(planes(f), b, ghosts[0, f : f + 1, :], ghosts[1, f : f + 1, :], column, f)
        for f in range(8)
    ]

    def factor(n, k):
        return coef[n, k, tile(b), :]

    new = []
    for component in range(3):
        for k in range(2):
            here, up, down, left, right = at[2 * component + k]
            value = 0.2 * here + factor(0, k) * up + factor(1, k) * down
            value = value + factor(2, k) * left + factor(3, k) * right
            value = value + factor(4, k) * at[2 * component + 1 - k][0]
            if component == 0:
                value = value + factor(6, k)
                slope = at[7][0] if k == 0 else -at[6][0]
            elif component == 1:
                slope = at[6 + k][2] - at[6 + k][1]
            else:
                slope = at[6 + k][4] - at[6 + k][3]
            new.append(value - factor(5, k) * slope)
    for k in range(2):
        divergence = (at[2 + k][2] - at[2 + k][1]) + (at[4 + k][4] - at[4 + k][3])
        divergence = divergence + at[1][0] if k == 0 else divergence - at[0][0]
        new.append(at[6 + k][0] - factor(7, k) * divergence)
    return new


def fill_ghosts(ints, arrived, chunks, high, low, sides, ghosts, cols_s, rows_s):
    blend(ints, row_block(ints, arrived, SLOTS), high, low, sides)
    found = edge_ghosts(ints, arrived, chunks, sides, SLOTS, slice(0, 8))
    for n in range(4):
        ghosts[n] = found[n]
    west = [ghosts[2, f : f + 1, :] for f in range(8)]
    east = [ghosts[3, f : f + 1, :] for f in range(8)]
    ghost_columns(west, east, rows_s, cols_s)


def sweep_kernel(
    ints, flow, pressure, coef, arrived, chunks_in, high, low,
    flow_out, pressure_out, chunks, north, south, sides, ghosts, cols_s, rows_s, edge_s,
):
    def planes(f):
        return flow.at[f] if f < 6 else pressure.at[f - 6]

    def planes_out(f):
        return flow_out.at[f] if f < 6 else pressure_out.at[f - 6]

    fill_ghosts(ints, arrived, chunks_in, high, low, sides, ghosts, cols_s, rows_s)
    chunks[...] = jnp.zeros(chunks.shape, F32)
    for b in range(TILES):
        new = relaxed(planes, coef, ghosts, cols_s[tile(b), :], b)
        gathered = jnp.zeros((8, CELLS), F32)
        for f in range(8):
            planes_out(f)[tile(b), :] = new[f]
            gathered = gather_edge(new[f], f, gathered)
            if b == 0:
                north[0, f : f + 1, :] = new[f][0:1, :]
            if b == TILES - 1:
                south[0, f : f + 1, :] = new[f][7:8, :]
        edge_s[tile(b), :] = gathered
    rows_s[...] = edge_s[...].T
    for f in range(8):
        west, east = own_lanes(f)
        chunks[ints[TO_WEST], f : f + 1, :] = rows_s[west : west + 1, :]
        chunks[ints[TO_EAST], f : f + 1, :] = rows_s[east : east + 1, :]
    for f in range(8):
        chunks[ints[CHUNK], f : f + 1, :] = planes_out(f)[pl.ds(ints[ROW], 1), :]


def heat_kernel(ints, heat, arrived, chunks, high, low, out, ghosts_out, block, sides):
    out[...] = heat[...]
    block[...] = jnp.zeros((4, 8, CELLS), F32)
    last = SLOTS + 2
    for n in range(4):
        for k in range(2):
            line = arrived[ints[BLOCKS + n], last, pl.ds(2 * ints[RANKS + n] + k, 1), :]
            block[n, k : k + 1, :] = line
    blend(ints, lambda n: block[n], high, low, sides)
    found = edge_ghosts(ints, arrived, chunks, sides, SLOTS + 1, slice(8, 16))
    for n in range(4):
        ghosts_out[n] = found[n]


def final_kernel(
    ints, flow, pressure, coef, arrived, chunks_in, high, low, heat, heat_ghosts,
    flow_out, pressure_out, heat_out, sides, ghosts, cols_s, rows_s, heat_cols_s,
):
    def planes(f):
        return flow.at[f] if f < 6 else pressure.at[f - 6]

    west = [heat_ghosts[2, k : k + 1, :] for k in range(2)]
    east = [heat_ghosts[3, k : k + 1, :] for k in range(2)]
    ghost_columns(west, east, rows_s, heat_cols_s)
    fill_ghosts(ints, arrived, chunks_in, high, low, sides, ghosts, cols_s, rows_s)
    for b in range(TILES):
        new = relaxed(planes, coef, ghosts, cols_s[tile(b), :], b)
        for f in range(6):
            flow_out[f, tile(b), :] = new[f]
        for k in range(2):
            pressure_out[k, tile(b), :] = new[6 + k]
        layers = [
            around(
                heat.at[k],
                b,
                heat_ghosts[0, k : k + 1, :],
                heat_ghosts[1, k : k + 1, :],
                heat_cols_s[tile(b), :],
                k,
            )
            for k in range(2)
        ]
        for k in range(2):
            here, up, down, left, right = layers[k]
            under = jnp.ones((8, CELLS), F32) if k == 0 else layers[0][0]
            over = layers[1][0] if k == 0 else jnp.zeros((8, CELLS), F32)
            advect = jnp.zeros((8, CELLS), F32)
            for component, minus, plus in ((0, under, over), (1, up, down), (2, left, right)):
                speed = new[2 * component + k]
                advect = advect + jnp.maximum(speed, 0.0) * (here - minus)
                advect = advect + jnp.minimum(speed, 0.0) * (plus - here)
            spread = (up + down) + (left + right) + (under + over) - 6.0 * here
            heat_out[k, tile(b), :] = here + 0.1 * (spread - advect)


def shape(*dims):
    return jax.ShapeDtypeStruct(dims, F32)


def scratch(*dims):
    return pltpu.VMEM(dims, F32)


def semaphores(count):
    return pltpu.SemaphoreType.DMA((count,))


def call(kernel, outs, ins, scratches, name, specs=None, limit=4, keep=()):
    specs = specs or [SMEM] + [VMEM] * (len(ins) - 1)
    placed = []
    for n, (x, spec) in enumerate(zip(ins, specs)):
        if spec is HBM or n in keep:
            x = pltpu.with_memory_space_constraint(x, spec.memory_space)
        placed.append(x)
    return pl.pallas_call(
        kernel,
        out_shape=outs,
        in_specs=specs,
        out_specs=[VMEM] * len(outs),
        scratch_shapes=scratches,
        compiler_params=pltpu.CompilerParams(vmem_limit_bytes=limit * 1024 * 1024),
        name=name,
    )(*placed)


def shards(
    flow_vector,
    normal_stress,
    thermal_field,
    shear_resistance,
    departing_bands,
    receiving_processor,
    shift_filled_by_lane,
    blending_factors,
):
    flow = flow_vector.reshape(6, CELLS, CELLS)
    pressure = normal_stress[0]
    heat = thermal_field[0]
    friction = shear_resistance[0]
    weights = blending_factors.reshape(8, CELLS, CELLS)
    lat, lon = lax.axis_index("lat"), lax.axis_index("lon")
    n_lat, n_lon = lax.axis_size("lat"), lax.axis_size("lon")
    patch = lax.axis_index("patch")
    own_row = departing_bands.reshape(1)
    receiver = receiving_processor.reshape(1)
    other = (1 - patch) * n_lon

    chunk = other + jnp.maximum(receiver, 0) % n_lon
    beside = patch * n_lon + jnp.clip(lon + jnp.array([-1, 1], jnp.int32), 0, n_lon - 1)
    beyond = jnp.clip(lat + jnp.array([-1, 1], jnp.int32), 0, n_lat - 1)
    first = jnp.concatenate([own_row, chunk, beside, receiver])

    square = scratch(CELLS, CELLS)
    tiles = 2 * n_lon
    chunks, north, south, places = call(
        start_kernel,
        [shape(tiles, 16, CELLS), shape(2, 8, CELLS), shape(2, 8, CELLS), shape(8, CELLS)],
        (first, shift_filled_by_lane.reshape(1, CELLS), flow, pressure, heat, friction),
        [scratch(PLANES, CELLS, CELLS), pltpu.VMEM((1, CELLS), jnp.int32), scratch(16, CELLS)]
        + [square, square, semaphores(5)],
        "start",
        specs=[SMEM] + [HBM] * 5,
    )

    def across(chunks):
        return lax.all_to_all(chunks, ("patch", "lon"), 0, 0, tiled=True)

    def along(table, blocks, north, south, count):
        (packed,) = call(
            pack_kernel,
            [shape(n_lat, count, 8, CELLS)],
            (table, blocks, north, south),
            [],
            "pack",
            keep=(1,),
        )
        return lax.all_to_all(packed, "lat", 0, 0, tiled=True)

    came = across(chunks)
    sent_to = lax.dynamic_slice(came, (other, 8, 0), (n_lon, 1, 1)).reshape(n_lon)
    sent_to = sent_to.astype(jnp.int32) - 1
    every_lat = jnp.arange(n_lat, dtype=jnp.int32)[:, None]
    wanted = sent_to[None] == every_lat * n_lon + lon
    order = jnp.arange(n_lon, dtype=jnp.int32)
    earlier = wanted[:, None, :] & (order[None, None, :] < order[None, :, None])
    rank = jnp.sum(earlier.astype(jnp.int32), axis=2)
    mine = wanted[:, None, :] & (rank[:, None, :] == jnp.arange(SLOTS)[None, :, None])
    found = jnp.sum(jnp.where(mine, order[None, None, :], 0), axis=2).reshape(-1)
    table = jnp.concatenate([beyond, other + found]).astype(jnp.int32)
    arrived = along(table, came, north, south, SLOTS + 3)

    on_edge = jnp.stack([lat == 0, lat == n_lat - 1, lon == 0, lon == n_lon - 1]).astype(jnp.int32)
    own = places[:, 0].astype(jnp.int32) - 1
    pick = jnp.concatenate(
        [jnp.where(lat > 0, own[2:4], own[0:2]), jnp.where(lon > 0, own[6:8], own[4:6])]
    )
    same = (own >= 0)[None] & (own[None] // n_lon == pick[:, None] // n_lon)
    slot = jnp.sum((same & (own[None] < pick[:, None])).astype(jnp.int32), axis=1)
    bases = jnp.stack([jnp.where(lat > 0, 2, 0), jnp.where(lon > 0, 6, 4)]).astype(jnp.int32)
    ints = [own_row, on_edge, bases, chunk, beside, beyond]
    ints += [jnp.maximum(pick, 0) // n_lon, jnp.minimum(slot, SLOTS - 1)]
    ints = jnp.concatenate(ints).astype(jnp.int32)

    joined = jax.ShapeDtypeStruct((2, CELLS, 2 * CELLS), jnp.bfloat16)
    high, low = call(
        weights_kernel,
        [joined, joined],
        (ints, weights),
        [scratch(4, CELLS, CELLS), semaphores(2)],
        "weights",
        specs=[SMEM, HBM],
    )
    (coef,) = call(
        coefficient_kernel,
        [shape(8, 2, CELLS, CELLS)],
        (ints, friction, heat, arrived, came),
        [scratch(2, 8, CELLS), square, square],
        "coefficients",
        keep=(3, 4),
    )
    sides, ghosts = scratch(2, 8, CELLS), scratch(4, 8, CELLS)
    state = [shape(6, CELLS, CELLS), shape(2, CELLS, CELLS)]
    for sweep in range(SWEEPS - 1):
        if sweep == 0:
            warm, warm_ghosts = call(
                heat_kernel,
                [shape(2, CELLS, CELLS), shape(4, 8, CELLS)],
                (ints, heat, arrived, came, high, low),
                [scratch(4, 8, CELLS), sides],
                "heat",
                keep=(2, 3, 4, 5),
            )
        flow, pressure, chunks, north, south = call(
            sweep_kernel,
            state + [shape(tiles, 8, CELLS), shape(1, 8, CELLS), shape(1, 8, CELLS)],
            (ints, flow, pressure, coef, arrived, came, high, low),
            [sides, ghosts, square, square, square],
            "sweep",
            limit=8,
            keep=(3, 4, 5, 6, 7),
        )
        came = across(chunks)
        arrived = along(table, came, north, south, SLOTS + 1)
    flow, pressure, heat = call(
        final_kernel,
        state + [shape(2, CELLS, CELLS)],
        (ints, flow, pressure, coef, arrived, came, high, low, warm, warm_ghosts),
        [sides, ghosts, square, square, square],
        "final",
        limit=8,
        keep=(1, 2, 3, 4, 5, 6, 7, 8, 9),
    )
    return flow.reshape(3, 1, 2, CELLS, CELLS), pressure[None], heat[None]


def solution(mesh):
    placed = (
        P(None, "patch", None, "lat", "lon"),
        P("patch", None, "lat", "lon"),
        P("patch", None, "lat", "lon"),
        P("patch", None, "lat", "lon"),
        P("patch", "lat", "lon", None),
        P("patch", "lat", "lon", None),
        P("patch", "lat", "lon", None),
        P("patch", "lat", "lon", None, None, None),
    )
    return jax.shard_map(
        shards,
        mesh=mesh,
        in_specs=placed,
        out_specs=(
            P(None, "patch", None, "lat", "lon"),
            P("patch", None, "lat", "lon"),
            P("patch", None, "lat", "lon"),
        ),
        check_vma=False,
    )
```

```python
import jax
import jax.numpy as jnp
from jax import lax
from jax.experimental import pallas as pl
from jax.experimental.pallas import tpu as pltpu
from jax.sharding import PartitionSpec as P

SWEEPS = 4
CELLS = 128
TILES = 16
PLANES = 12
SLOTS = 4
F32 = jnp.float32
VMEM = pl.BlockSpec(memory_space=pltpu.VMEM)
SMEM = pl.BlockSpec(memory_space=pltpu.SMEM)
HBM = pl.BlockSpec(memory_space=pltpu.HBM)
ROW, NORTH, SOUTH, WEST, EAST, LAT_BASE, LON_BASE = range(7)
CHUNK, TO_WEST, TO_EAST = 7, 8, 9
FROM_NORTH, FROM_SOUTH = 10, 11
BLOCKS, RANKS = 12, 16


def lanes():
    return lax.broadcasted_iota(jnp.int32, (8, CELLS), 1)


def sublanes():
    return lax.broadcasted_iota(jnp.int32, (8, CELLS), 0)


def turn(x, shift):
    shift = shift % CELLS
    return x if shift == 0 else pltpu.roll(x, shift, 1)


def tile(b):
    return pl.ds(8 * b, 8)


class Copies:
    def __init__(self, sems):
        self.sems, self.going = sems, []

    def start(self, source, target):
        copy = pltpu.make_async_copy(source, target, self.sems.at[len(self.going)])
        copy.start()
        self.going.append(copy)

    def wait(self, first=0, last=None):
        for copy in self.going[first:last]:
            copy.wait()


def own_lanes(f):
    return 2 * f, (2 * f - 1) % CELLS


def gather_edge(block, f, gathered):
    west, east = own_lanes(f)
    lane = lanes()
    return jnp.where((lane == west) | (lane == east), turn(block, 2 * f), gathered)


def ghost_columns(west, east, rows_s, cols_s):
    rows_s[...] = jnp.zeros((CELLS, CELLS), F32)
    for f, (w, e) in enumerate(zip(west, east)):
        to_w, to_e = own_lanes(f)
        rows_s[to_w : to_w + 1, :] = w
        rows_s[to_e : to_e + 1, :] = e
    cols_s[...] = rows_s[...].T


def around(ref, b, north, south, column, f):
    here = ref[tile(b), :]
    sub, lane = sublanes(), lanes()
    if b == 0:
        up = jnp.where(sub == 0, north, pltpu.roll(here, 1, 0))
    else:
        up = ref[8 * b - 1 : 8 * b + 7, :]
    if b == TILES - 1:
        down = jnp.where(sub == 7, south, pltpu.roll(here, 7, 0))
    else:
        down = ref[8 * b + 1 : 8 * b + 9, :]
    turned = turn(column, -2 * f)
    left = jnp.where(lane == 0, turned, pltpu.roll(here, 1, 1))
    right = jnp.where(lane == CELLS - 1, turned, pltpu.roll(here, CELLS - 1, 1))
    return here, up, down, left, right


def start_kernel(
    ints, slots, flow, pressure, heat, friction,
    chunks, north, south, places, own, named, row, cols_s, rows_s, sems,
):
    copies = Copies(sems)
    copies.start(slots, named)
    copies.start(flow, own.at[0:6])
    copies.start(pressure, own.at[6:8])
    copies.start(heat, own.at[8:10])
    copies.start(friction, own.at[10:12])
    row[8:16, :] = jnp.broadcast_to((ints[4] + 1).astype(F32), (8, CELLS))
    chunks[...] = jnp.zeros(chunks.shape, F32)
    north[...] = jnp.zeros(north.shape, F32)
    south[...] = jnp.zeros(south.shape, F32)
    copies.wait()
    mine = jnp.broadcast_to(named[...], (8, CELLS)) == sublanes()
    place = jnp.sum(jnp.where(mine, lanes() + 1, 0).astype(F32), axis=1, keepdims=True)
    places[...] = jnp.broadcast_to(place, (8, CELLS))
    for f in range(10):
        to = f if f < 8 else f + 1
        row[to : to + 1, :] = own[f, pl.ds(ints[0], 1), :]
    for b in range(TILES):
        gathered = jnp.zeros((8, CELLS), F32)
        for f in range(PLANES):
            gathered = gather_edge(own[f, tile(b), :], f, gathered)
        cols_s[tile(b), :] = gathered
    rows_s[...] = cols_s[...].T
    chunks[ints[1]] = row[...]
    for f in range(PLANES):
        west, east = own_lanes(f)
        chunks[ints[2], f : f + 1, :] = rows_s[west : west + 1, :]
        chunks[ints[3], f : f + 1, :] = rows_s[east : east + 1, :]
        n, at = divmod(f, 8)
        north[n, at : at + 1, :] = own[f, 0:1, :]
        south[n, at : at + 1, :] = own[f, CELLS - 1 : CELLS, :]


def pack_kernel(table, arrived, north, south, out):
    lats, count = out.shape[0], out.shape[1]
    halos = north.shape[0]
    for lat in range(lats):
        for n in range(SLOTS):
            block = table[2 + SLOTS * lat + n]
            out[lat, n] = arrived[block, 0:8, :]
            if count > SLOTS + 1:
                out[lat, count - 1, 2 * n : 2 * n + 2, :] = arrived[block, 9:11, :]
        for n in range(halos):
            out[lat, SLOTS + n] = jnp.zeros((8, CELLS), F32)
    for n in range(halos):
        out[table[0], SLOTS + n] = north[n]
        out[table[1], SLOTS + n] = south[n]


def split(x):
    high = x.astype(jnp.bfloat16)
    return high, (x - high.astype(F32)).astype(jnp.bfloat16)


def times(left, right):
    return lax.dot_general(left, right, (((1,), (1,)), ((), ())), preferred_element_type=F32)


def weights_kernel(ints, weights, high, low, chosen, sems):
    copies = Copies(sems)
    copies.start(weights.at[pl.ds(ints[LAT_BASE], 2)], chosen.at[0:2])
    copies.start(weights.at[pl.ds(ints[LON_BASE], 2)], chosen.at[2:4])
    copies.wait()
    for side in range(2):
        for term in range(2):
            cut = slice(term * CELLS, (term + 1) * CELLS)
            high[side, :, cut], low[side, :, cut] = split(chosen[2 * side + term])


def blend(ints, blocks_of, high, low, ghosts):
    for n, (first, last) in enumerate(((NORTH, SOUTH), (WEST, EAST))):
        count = ghosts.shape[1]
        ghosts[n] = jnp.zeros((count, CELLS), F32)

        @pl.when(ints[first] + ints[last] > 0)
        def _():
            block = jnp.concatenate([blocks_of(2 * n + t) for t in range(2)], axis=1)
            b_high, b_low = split(block)
            both = times(jnp.concatenate([b_high, b_low], axis=0), high[n])
            ghosts[n] = both[0:count] + both[count:] + times(b_high, low[n])


def edge_ghosts(ints, arrived, chunks, ghosts, slot, rows, of):
    halos = (
        arrived[ints[FROM_NORTH], slot],
        arrived[ints[FROM_SOUTH], slot],
        chunks[ints[TO_WEST], rows, :],
        chunks[ints[TO_EAST], rows, :],
    )
    flags = (ints[NORTH], ints[SOUTH], ints[WEST], ints[EAST])
    return [
        jnp.where(flag > 0, ghosts[n // 2, of, :], halo)
        for n, (flag, halo) in enumerate(zip(flags, halos))
    ]


def coefficients(ints, friction, heat, north, south, column, f, b, put):
    lane, sub = lanes(), sublanes()
    centre = [friction[k, tile(b), :] for k in range(2)]
    for k in range(2):
        here, up, down, left, right = around(
            friction.at[k], b, north[k], south[k], column, f + k
        )
        if b == 0:
            up = jnp.where((sub == 0) & (ints[NORTH] > 0), here, up)
        if b == TILES - 1:
            down = jnp.where((sub == 7) & (ints[SOUTH] > 0), here, down)
        left = jnp.where((lane == 0) & (ints[WEST] > 0), here, left)
        right = jnp.where((lane == CELLS - 1) & (ints[EAST] > 0), here, right)
        faces = [0.5 * (here + other) for other in (up, down, left, right)]
        between = 0.5 * (centre[0] + centre[1])
        diagonal = (faces[0] + faces[1]) + (faces[2] + faces[3]) + (between + here)
        inverse = 0.8 / diagonal
        for n, face in enumerate(faces):
            put(n, k, inverse * face)
        put(4, k, inverse * between)
        put(5, k, 0.5 * inverse)
        put(6, k, inverse * heat[k, tile(b), :])
        put(7, k, 0.125 * here)


def coefficient_kernel(ints, friction, heat, chunks, out, cols_s, rows_s):
    west = [chunks[ints[TO_WEST], 10 + k : 11 + k, :] for k in range(2)]
    east = [chunks[ints[TO_EAST], 10 + k : 11 + k, :] for k in range(2)]
    ghost_columns(west, east, rows_s, cols_s)
    for b in range(1, TILES - 1):

        def put(n, k, value):
            out[n, k, tile(b), :] = value

        coefficients(ints, friction, heat, (None, None), (None, None), cols_s[tile(b), :], 0, b, put)
    for b in (0, TILES - 1):
        for n in range(8):
            for k in range(2):
                out[n, k, tile(b), :] = jnp.zeros((8, CELLS), F32)


def relaxed(planes, coef, ends, ghosts, column, b):
    at = [
        around(planes(f), b, ghosts[0, f : f + 1, :], ghosts[1, f : f + 1, :], column, f)
        for f in range(8)
    ]

    def factor(n, k):
        if b == 0 or b == TILES - 1:
            return ends[n, k, tile(0 if b == 0 else 1), :]
        return coef[n, k, tile(b), :]

    new = []
    for component in range(3):
        for k in range(2):
            here, up, down, left, right = at[2 * component + k]
            value = 0.2 * here + factor(0, k) * up + factor(1, k) * down
            value = value + factor(2, k) * left + factor(3, k) * right
            value = value + factor(4, k) * at[2 * component + 1 - k][0]
            if component == 0:
                value = value + factor(6, k)
                slope = at[7][0] if k == 0 else -at[6][0]
            elif component == 1:
                slope = at[6 + k][2] - at[6 + k][1]
            else:
                slope = at[6 + k][4] - at[6 + k][3]
            new.append(value - factor(5, k) * slope)
    for k in range(2):
        divergence = (at[2 + k][2] - at[2 + k][1]) + (at[4 + k][4] - at[4 + k][3])
        divergence = divergence + at[1][0] if k == 0 else divergence - at[0][0]
        new.append(at[6 + k][0] - factor(7, k) * divergence)
    return new


def fill_ghosts(ints, arrived, chunks, high, low, sides, ghosts, cols_s, rows_s, others=()):
    count = sides.shape[1]

    def block(n):
        rows = arrived[ints[BLOCKS + n], ints[RANKS + n]]
        if count == 8:
            return rows
        warm = [
            arrived[ints[BLOCKS + n], SLOTS + 2, pl.ds(2 * ints[RANKS + n] + k, 1), :]
            for k in range(2)
        ]
        return jnp.concatenate([rows, *warm, jnp.zeros((6, CELLS), F32)], axis=0)

    blend(ints, block, high, low, sides)
    found = edge_ghosts(ints, arrived, chunks, sides, SLOTS, slice(0, 8), slice(0, 8))
    for n in range(4):
        ghosts[n] = found[n]
    west = [ghosts[2, f : f + 1, :] for f in range(8)]
    east = [ghosts[3, f : f + 1, :] for f in range(8)]
    ghost_columns(west + [w for w, _ in others], east + [e for _, e in others], rows_s, cols_s)


def first_kernel(
    ints, flow, pressure, coef, friction, heat, arrived, chunks_in, high, low,
    flow_out, pressure_out, chunks, north, south, ends, heat_ghosts,
    sides, ghosts, cols_s, rows_s, edge_s, halos,
):
    others = [
        [chunks_in[ints[at], 10 + k : 11 + k, :] for at in (TO_WEST, TO_EAST)] for k in range(2)
    ]
    fill_ghosts(ints, arrived, chunks_in, high, low, sides, ghosts, cols_s, rows_s, others)
    found = edge_ghosts(ints, arrived, chunks_in, sides, SLOTS + 1, slice(8, 16), slice(8, 16))
    for n in range(4):
        heat_ghosts[n] = found[n]
    halos[0] = arrived[ints[FROM_NORTH], SLOTS + 1]
    halos[1] = arrived[ints[FROM_SOUTH], SLOTS + 1]
    for end, b in enumerate((0, TILES - 1)):

        def put(n, k, value):
            ends[n, k, tile(end), :] = value

        lines = [[halos[side, 2 + k : 3 + k, :] for k in range(2)] for side in range(2)]
        coefficients(ints, friction, heat, *lines, cols_s[tile(b), :], 8, b, put)
    sweep(
        ints, flow, pressure, coef, ends, ghosts, cols_s, rows_s, edge_s,
        flow_out, pressure_out, chunks, north, south,
    )


def sweep_kernel(
    ints, flow, pressure, coef, ends, arrived, chunks_in, high, low,
    flow_out, pressure_out, chunks, north, south, sides, ghosts, cols_s, rows_s, edge_s,
):
    fill_ghosts(ints, arrived, chunks_in, high, low, sides, ghosts, cols_s, rows_s)
    sweep(
        ints, flow, pressure, coef, ends, ghosts, cols_s, rows_s, edge_s,
        flow_out, pressure_out, chunks, north, south,
    )


def sweep(
    ints, flow, pressure, coef, ends, ghosts, cols_s, rows_s, edge_s,
    flow_out, pressure_out, chunks, north, south,
):
    def planes(f):
        return flow.at[f] if f < 6 else pressure.at[f - 6]

    def planes_out(f):
        return flow_out.at[f] if f < 6 else pressure_out.at[f - 6]

    chunks[...] = jnp.zeros(chunks.shape, F32)
    for b in range(TILES):
        new = relaxed(planes, coef, ends, ghosts, cols_s[tile(b), :], b)
        gathered = jnp.zeros((8, CELLS), F32)
        for f in range(8):
            planes_out(f)[tile(b), :] = new[f]
            gathered = gather_edge(new[f], f, gathered)
            if b == 0:
                north[0, f : f + 1, :] = new[f][0:1, :]
            if b == TILES - 1:
                south[0, f : f + 1, :] = new[f][7:8, :]
        edge_s[tile(b), :] = gathered
    rows_s[...] = edge_s[...].T
    for f in range(8):
        west, east = own_lanes(f)
        chunks[ints[TO_WEST], f : f + 1, :] = rows_s[west : west + 1, :]
        chunks[ints[TO_EAST], f : f + 1, :] = rows_s[east : east + 1, :]
    for f in range(8):
        chunks[ints[CHUNK], f : f + 1, :] = planes_out(f)[pl.ds(ints[ROW], 1), :]


def final_kernel(
    ints, flow, pressure, coef, ends, arrived, chunks_in, high, low, heat, heat_ghosts,
    flow_out, pressure_out, heat_out, sides, ghosts, cols_s, rows_s, heat_cols_s,
):
    def planes(f):
        return flow.at[f] if f < 6 else pressure.at[f - 6]

    west = [heat_ghosts[2, k : k + 1, :] for k in range(2)]
    east = [heat_ghosts[3, k : k + 1, :] for k in range(2)]
    ghost_columns(west, east, rows_s, heat_cols_s)
    fill_ghosts(ints, arrived, chunks_in, high, low, sides, ghosts, cols_s, rows_s)
    for b in range(TILES):
        new = relaxed(planes, coef, ends, ghosts, cols_s[tile(b), :], b)
        for f in range(6):
            flow_out[f, tile(b), :] = new[f]
        for k in range(2):
            pressure_out[k, tile(b), :] = new[6 + k]
        layers = [
            around(
                heat.at[k],
                b,
                heat_ghosts[0, k : k + 1, :],
                heat_ghosts[1, k : k + 1, :],
                heat_cols_s[tile(b), :],
                k,
            )
            for k in range(2)
        ]
        for k in range(2):
            here, up, down, left, right = layers[k]
            under = jnp.ones((8, CELLS), F32) if k == 0 else layers[0][0]
            over = layers[1][0] if k == 0 else jnp.zeros((8, CELLS), F32)
            advect = jnp.zeros((8, CELLS), F32)
            for component, minus, plus in ((0, under, over), (1, up, down), (2, left, right)):
                speed = new[2 * component + k]
                advect = advect + jnp.maximum(speed, 0.0) * (here - minus)
                advect = advect + jnp.minimum(speed, 0.0) * (plus - here)
            spread = (up + down) + (left + right) + (under + over) - 6.0 * here
            heat_out[k, tile(b), :] = here + 0.1 * (spread - advect)


def shape(*dims):
    return jax.ShapeDtypeStruct(dims, F32)


def scratch(*dims):
    return pltpu.VMEM(dims, F32)


def semaphores(count):
    return pltpu.SemaphoreType.DMA((count,))


def call(kernel, outs, ins, scratches, name, specs=None, limit=4, keep=(), pin=()):
    specs = specs or [SMEM] + [VMEM] * (len(ins) - 1)
    placed = []
    for n, (x, spec) in enumerate(zip(ins, specs)):
        if spec is HBM or n in keep:
            x = pltpu.with_memory_space_constraint(x, spec.memory_space)
        placed.append(x)
    outs = [pltpu.VMEM(x.shape, x.dtype) if n in pin else x for n, x in enumerate(outs)]
    return pl.pallas_call(
        kernel,
        out_shape=outs,
        in_specs=specs,
        out_specs=[VMEM] * len(outs),
        scratch_shapes=scratches,
        compiler_params=pltpu.CompilerParams(vmem_limit_bytes=limit * 1024 * 1024),
        name=name,
    )(*placed)


def shards(
    flow_vector,
    normal_stress,
    thermal_field,
    shear_resistance,
    departing_bands,
    receiving_processor,
    shift_filled_by_lane,
    blending_factors,
):
    flow = flow_vector.reshape(6, CELLS, CELLS)
    pressure = normal_stress[0]
    heat = thermal_field[0]
    friction = shear_resistance[0]
    weights = blending_factors.reshape(8, CELLS, CELLS)
    lat, lon = lax.axis_index("lat"), lax.axis_index("lon")
    n_lat, n_lon = lax.axis_size("lat"), lax.axis_size("lon")
    patch = lax.axis_index("patch")
    own_row = departing_bands.reshape(1)
    receiver = receiving_processor.reshape(1)
    other = (1 - patch) * n_lon

    chunk = other + jnp.maximum(receiver, 0) % n_lon
    beside = jnp.stack([jnp.maximum(lon - 1, 0), jnp.minimum(lon + 1, n_lon - 1)])
    beside = (beside + patch * n_lon).astype(jnp.int32)
    beyond = jnp.stack([jnp.maximum(lat - 1, 0), jnp.minimum(lat + 1, n_lat - 1)])
    beyond = beyond.astype(jnp.int32)
    first = jnp.concatenate([own_row, chunk, beside, receiver])

    square = scratch(CELLS, CELLS)
    tiles = 2 * n_lon
    chunks, north, south, places = call(
        start_kernel,
        [shape(tiles, 16, CELLS), shape(2, 8, CELLS), shape(2, 8, CELLS), shape(8, CELLS)],
        (first, shift_filled_by_lane.reshape(1, CELLS), flow, pressure, heat, friction),
        [scratch(PLANES, CELLS, CELLS), pltpu.VMEM((1, CELLS), jnp.int32), scratch(16, CELLS)]
        + [square, square, semaphores(5)],
        "start",
        specs=[SMEM] + [HBM] * 5,
        pin=(0,),
    )

    def across(chunks):
        return lax.all_to_all(chunks, ("patch", "lon"), 0, 0, tiled=True)

    def along(table, blocks, north, south, count):
        (packed,) = call(
            pack_kernel,
            [shape(n_lat, count, 8, CELLS)],
            (table, blocks, north, south),
            [],
            "pack",
            keep=(1,),
            pin=(0,),
        )
        return lax.all_to_all(packed, "lat", 0, 0, tiled=True)

    came = across(chunks)
    sent_to = lax.dynamic_slice(came, (other, 8, 0), (n_lon, 1, 1)).reshape(n_lon)
    sent_to = sent_to.astype(jnp.int32) - 1
    every_lat = jnp.arange(n_lat, dtype=jnp.int32)[:, None]
    wanted = sent_to[None] == every_lat * n_lon + lon
    order = jnp.arange(n_lon, dtype=jnp.int32)
    earlier = wanted[:, None, :] & (order[None, None, :] < order[None, :, None])
    rank = jnp.sum(earlier.astype(jnp.int32), axis=2)
    mine = wanted[:, None, :] & (rank[:, None, :] == jnp.arange(SLOTS)[None, :, None])
    found = jnp.sum(jnp.where(mine, order[None, None, :], 0), axis=2).reshape(-1)
    table = jnp.concatenate([beyond, other + found]).astype(jnp.int32)
    arrived = along(table, came, north, south, SLOTS + 3)

    on_edge = jnp.stack([lat == 0, lat == n_lat - 1, lon == 0, lon == n_lon - 1]).astype(jnp.int32)
    own = places[:, 0].astype(jnp.int32) - 1
    pick = jnp.concatenate(
        [jnp.where(lat > 0, own[2:4], own[0:2]), jnp.where(lon > 0, own[6:8], own[4:6])]
    )
    same = (own >= 0)[None] & (own[None] // n_lon == pick[:, None] // n_lon)
    slot = jnp.sum((same & (own[None] < pick[:, None])).astype(jnp.int32), axis=1)
    bases = jnp.stack([jnp.where(lat > 0, 2, 0), jnp.where(lon > 0, 6, 4)]).astype(jnp.int32)
    ints = [own_row, on_edge, bases, chunk, beside, beyond]
    ints += [jnp.maximum(pick, 0) // n_lon, jnp.minimum(slot, SLOTS - 1)]
    ints = jnp.concatenate(ints).astype(jnp.int32)

    joined = jax.ShapeDtypeStruct((2, CELLS, 2 * CELLS), jnp.bfloat16)
    high, low = call(
        weights_kernel,
        [joined, joined],
        (ints, weights),
        [scratch(4, CELLS, CELLS), semaphores(2)],
        "weights",
        specs=[SMEM, HBM],
    )
    (coef,) = call(
        coefficient_kernel,
        [shape(8, 2, CELLS, CELLS)],
        (ints, friction, heat, came),
        [square, square],
        "coefficients",
        keep=(3,),
    )
    sides, ghosts = scratch(2, 8, CELLS), scratch(4, 8, CELLS)
    state = [shape(6, CELLS, CELLS), shape(2, CELLS, CELLS)]
    for sweep in range(SWEEPS - 1):
        outs = state + [shape(tiles, 8, CELLS), shape(1, 8, CELLS), shape(1, 8, CELLS)]
        if sweep == 0:
            flow, pressure, chunks, north, south, ends, heat_ghosts = call(
                first_kernel,
                outs + [shape(8, 2, 16, CELLS), shape(4, 8, CELLS)],
                (ints, flow, pressure, coef, friction, heat, arrived, came, high, low),
                [scratch(2, 16, CELLS), ghosts, square, square, square, scratch(2, 8, CELLS)],
                "first_sweep",
                limit=8,
                keep=(3, 6, 7, 8, 9),
                pin=(2,),
            )
        else:
            flow, pressure, chunks, north, south = call(
                sweep_kernel,
                outs,
                (ints, flow, pressure, coef, ends, arrived, came, high, low),
                [sides, ghosts, square, square, square],
                "sweep",
                limit=8,
                keep=(3, 4, 5, 6, 7, 8),
                pin=(2,),
            )
        came = across(chunks)
        arrived = along(table, came, north, south, SLOTS + 1)
    flow, pressure, heat = call(
        final_kernel,
        state + [shape(2, CELLS, CELLS)],
        (ints, flow, pressure, coef, ends, arrived, came, high, low, heat, heat_ghosts),
        [sides, ghosts, square, square, square],
        "final",
        limit=8,
        keep=(1, 2, 3, 4, 5, 6, 7, 8),
    )
    return flow.reshape(3, 1, 2, CELLS, CELLS), pressure[None], heat[None]


def solution(mesh):
    placed = (
        P(None, "patch", None, "lat", "lon"),
        P("patch", None, "lat", "lon"),
        P("patch", None, "lat", "lon"),
        P("patch", None, "lat", "lon"),
        P("patch", "lat", "lon", None),
        P("patch", "lat", "lon", None),
        P("patch", "lat", "lon", None),
        P("patch", "lat", "lon", None, None, None),
    )
    return jax.shard_map(
        shards,
        mesh=mesh,
        in_specs=placed,
        out_specs=(
            P(None, "patch", None, "lat", "lon"),
            P("patch", None, "lat", "lon"),
            P("patch", None, "lat", "lon"),
        ),
        check_vma=False,
    )
```

```python
import jax
import jax.numpy as jnp
from jax import lax
from jax.experimental import pallas as pl
from jax.experimental.pallas import tpu as pltpu
from jax.sharding import PartitionSpec as P

SWEEPS = 4
CELLS = 128
TILES = 16
PLANES = 12
SLOTS = 4
F32 = jnp.float32
VMEM = pl.BlockSpec(memory_space=pltpu.VMEM)
SMEM = pl.BlockSpec(memory_space=pltpu.SMEM)
HBM = pl.BlockSpec(memory_space=pltpu.HBM)
ROW, NORTH, SOUTH, WEST, EAST, LAT_BASE, LON_BASE = range(7)
CHUNK, TO_WEST, TO_EAST = 7, 8, 9
FROM_NORTH, FROM_SOUTH = 10, 11
OTHER, LON = 12, 13
BLOCKS, RANKS = 14, 18


def lanes():
    return lax.broadcasted_iota(jnp.int32, (8, CELLS), 1)


def sublanes():
    return lax.broadcasted_iota(jnp.int32, (8, CELLS), 0)


def turn(x, shift):
    shift = shift % CELLS
    return x if shift == 0 else pltpu.roll(x, shift, 1)


def tile(b):
    return pl.ds(8 * b, 8)


class Copies:
    def __init__(self, sems):
        self.sems, self.going = sems, []

    def start(self, source, target):
        copy = pltpu.make_async_copy(source, target, self.sems.at[len(self.going)])
        copy.start()
        self.going.append(copy)

    def wait(self, first=0, last=None):
        for copy in self.going[first:last]:
            copy.wait()


def gather_edge(block, f, gathered):
    lane = lanes()
    return jnp.where(lane // 2 == f, turn(block, 2 * f + 1), gathered)


def every_second(first, count=8):
    return pl.ds(first, count, stride=2)


def ghost_columns(west, east, rows_s, cols_s, first=0):
    rows_s[every_second(2 * first + 1), :] = west
    rows_s[every_second(2 * first), :] = east
    cols_s[...] = rows_s[...].T


def around(ref, b, north, south, column, f):
    here = ref[tile(b), :]
    sub, lane = sublanes(), lanes()
    if b == 0:
        up = jnp.where(sub == 0, north, pltpu.roll(here, 1, 0))
    else:
        up = ref[8 * b - 1 : 8 * b + 7, :]
    if b == TILES - 1:
        down = jnp.where(sub == 7, south, pltpu.roll(here, 7, 0))
    else:
        down = ref[8 * b + 1 : 8 * b + 9, :]
    turned = turn(column, -2 * f - 1)
    left = jnp.where(lane == 0, turned, pltpu.roll(here, 1, 1))
    right = jnp.where(lane == CELLS - 1, turned, pltpu.roll(here, CELLS - 1, 1))
    return here, up, down, left, right


def start_kernel(
    ints, slots, flow, pressure, heat, friction,
    chunks, north, south, places, own, named, row, cols_s, rows_s, sems,
):
    copies = Copies(sems)
    copies.start(slots, named)
    copies.start(flow, own.at[0:6])
    copies.start(pressure, own.at[6:8])
    copies.start(heat, own.at[8:10])
    copies.start(friction, own.at[10:12])
    row[8:16, :] = jnp.broadcast_to((ints[4] + 1).astype(F32), (8, CELLS))
    chunks[...] = jnp.zeros(chunks.shape, F32)
    north[...] = jnp.zeros(north.shape, F32)
    south[...] = jnp.zeros(south.shape, F32)
    copies.wait()
    mine = jnp.broadcast_to(named[...], (8, CELLS)) == sublanes()
    place = jnp.sum(jnp.where(mine, lanes() + 1, 0).astype(F32), axis=1, keepdims=True)
    places[...] = jnp.broadcast_to(place, (8, CELLS))
    for f in range(10):
        to = f if f < 8 else f + 1
        row[to : to + 1, :] = own[f, pl.ds(ints[0], 1), :]
    for b in range(TILES):
        gathered = jnp.zeros((8, CELLS), F32)
        for f in range(PLANES):
            gathered = gather_edge(own[f, tile(b), :], f, gathered)
        cols_s[tile(b), :] = gathered
    rows_s[...] = cols_s[...].T
    chunks[ints[1]] = row[...]
    chunks[ints[2]] = rows_s[every_second(1, 16), :]
    chunks[ints[3]] = rows_s[every_second(0, 16), :]
    for f in range(PLANES):
        n, at = divmod(f, 8)
        north[n, at : at + 1, :] = own[f, 0:1, :]
        south[n, at : at + 1, :] = own[f, CELLS - 1 : CELLS, :]


def pack_kernel(ints, sent_to, arrived, north, south, out, filled):
    lats, count = out.shape[0], out.shape[1]
    sources = sent_to.shape[0]
    halos = north.shape[0]
    out[...] = jnp.zeros(out.shape, F32)
    for lat in range(lats):
        filled[lat] = 0
    for n in range(sources):
        number = sent_to[n]
        lat = jnp.maximum(number, 0) // sources

        @pl.when((number >= 0) & (number == lat * sources + ints[LON]))
        def _():
            slot = filled[lat]
            filled[lat] = slot + 1
            block = ints[OTHER] + n
            out[lat, slot] = arrived[block, 0:8, :]
            if count > SLOTS + 1:
                for k in range(2):
                    to = pl.ds(2 * slot + k, 1)
                    out[lat, count - 1, to, :] = arrived[block, 9 + k : 10 + k, :]

    for n in range(halos):
        out[ints[FROM_NORTH], SLOTS + n] = north[n]
        out[ints[FROM_SOUTH], SLOTS + n] = south[n]


def split(x):
    high = x.astype(jnp.bfloat16)
    return high, (x - high.astype(F32)).astype(jnp.bfloat16)


def times(left, right):
    return lax.dot_general(left, right, (((1,), (1,)), ((), ())), preferred_element_type=F32)


def weights_kernel(ints, weights, high, low, chosen, sems):
    copies = Copies(sems)
    copies.start(weights.at[pl.ds(ints[LAT_BASE], 2)], chosen.at[0:2])
    copies.start(weights.at[pl.ds(ints[LON_BASE], 2)], chosen.at[2:4])
    copies.wait()
    for side in range(2):
        for term in range(2):
            cut = slice(term * CELLS, (term + 1) * CELLS)
            high[side, :, cut], low[side, :, cut] = split(chosen[2 * side + term])


def blend(ints, blocks_of, high, low, ghosts):
    for n, (first, last) in enumerate(((NORTH, SOUTH), (WEST, EAST))):
        count = ghosts.shape[1]
        ghosts[n] = jnp.zeros((count, CELLS), F32)

        @pl.when(ints[first] + ints[last] > 0)
        def _():
            block = jnp.concatenate([blocks_of(2 * n + t) for t in range(2)], axis=1)
            b_high, b_low = split(block)
            both = times(jnp.concatenate([b_high, b_low], axis=0), high[n])
            ghosts[n] = both[0:count] + both[count:] + times(b_high, low[n])


def edge_ghosts(ints, arrived, chunks, ghosts, slot, rows, of):
    halos = (
        arrived[ints[FROM_NORTH], slot],
        arrived[ints[FROM_SOUTH], slot],
        chunks[ints[TO_WEST], rows, :],
        chunks[ints[TO_EAST], rows, :],
    )
    flags = (ints[NORTH], ints[SOUTH], ints[WEST], ints[EAST])
    return [
        jnp.where(flag > 0, ghosts[n // 2, of, :], halo)
        for n, (flag, halo) in enumerate(zip(flags, halos))
    ]


def coefficients(ints, friction, heat, north, south, column, f, b, put):
    lane, sub = lanes(), sublanes()
    centre = [friction[k, tile(b), :] for k in range(2)]
    for k in range(2):
        here, up, down, left, right = around(
            friction.at[k], b, north[k], south[k], column, f + k
        )
        if b == 0:
            up = jnp.where((sub == 0) & (ints[NORTH] > 0), here, up)
        if b == TILES - 1:
            down = jnp.where((sub == 7) & (ints[SOUTH] > 0), here, down)
        left = jnp.where((lane == 0) & (ints[WEST] > 0), here, left)
        right = jnp.where((lane == CELLS - 1) & (ints[EAST] > 0), here, right)
        faces = [0.5 * (here + other) for other in (up, down, left, right)]
        between = 0.5 * (centre[0] + centre[1])
        diagonal = (faces[0] + faces[1]) + (faces[2] + faces[3]) + (between + here)
        inverse = 0.8 / diagonal
        for n, face in enumerate(faces):
            put(n, k, inverse * face)
        put(4, k, inverse * between)
        put(5, k, 0.5 * inverse)
        put(6, k, inverse * heat[k, tile(b), :])
        put(7, k, 0.125 * here)


def coefficient_kernel(ints, friction, heat, chunks, out, cols_s, rows_s):
    west, east = chunks[ints[TO_WEST], 8:16, :], chunks[ints[TO_EAST], 8:16, :]
    ghost_columns(west, east, rows_s, cols_s)
    for b in range(1, TILES - 1):

        def put(n, k, value):
            out[n, k, tile(b), :] = value

        coefficients(ints, friction, heat, (None, None), (None, None), cols_s[tile(b), :], 2, b, put)
    for b in (0, TILES - 1):
        for n in range(8):
            for k in range(2):
                out[n, k, tile(b), :] = jnp.zeros((8, CELLS), F32)


def relaxed(planes, coef, ends, ghosts, column, b):
    at = [
        around(planes(f), b, ghosts[0, f : f + 1, :], ghosts[1, f : f + 1, :], column, f)
        for f in range(8)
    ]

    def factor(n, k):
        if b == 0 or b == TILES - 1:
            return ends[n, k, tile(0 if b == 0 else 1), :]
        return coef[n, k, tile(b), :]

    new = []
    for component in range(3):
        for k in range(2):
            here, up, down, left, right = at[2 * component + k]
            value = 0.2 * here + factor(0, k) * up + factor(1, k) * down
            value = value + factor(2, k) * left + factor(3, k) * right
            value = value + factor(4, k) * at[2 * component + 1 - k][0]
            if component == 0:
                value = value + factor(6, k)
                slope = at[7][0] if k == 0 else -at[6][0]
            elif component == 1:
                slope = at[6 + k][2] - at[6 + k][1]
            else:
                slope = at[6 + k][4] - at[6 + k][3]
            new.append(value - factor(5, k) * slope)
    for k in range(2):
        divergence = (at[2 + k][2] - at[2 + k][1]) + (at[4 + k][4] - at[4 + k][3])
        divergence = divergence + at[1][0] if k == 0 else divergence - at[0][0]
        new.append(at[6 + k][0] - factor(7, k) * divergence)
    return new


def fill_ghosts(ints, arrived, chunks, high, low, sides, ghosts, cols_s, rows_s):
    count = sides.shape[1]

    def block(n):
        rows = arrived[ints[BLOCKS + n], ints[RANKS + n]]
        if count == 8:
            return rows
        warm = [
            arrived[ints[BLOCKS + n], SLOTS + 2, pl.ds(2 * ints[RANKS + n] + k, 1), :]
            for k in range(2)
        ]
        return jnp.concatenate([rows, *warm, jnp.zeros((6, CELLS), F32)], axis=0)

    blend(ints, block, high, low, sides)
    found = edge_ghosts(ints, arrived, chunks, sides, SLOTS, slice(0, 8), slice(0, 8))
    for n in range(4):
        ghosts[n] = found[n]
    ghost_columns(found[2], found[3], rows_s, cols_s)


def first_kernel(
    ints, flow, pressure, coef, friction, heat, arrived, chunks_in, high, low,
    flow_out, pressure_out, chunks, north, south, ends, heat_ghosts,
    sides, ghosts, cols_s, rows_s, edge_s, halos,
):
    rows_s[every_second(17), :] = chunks_in[ints[TO_WEST], 8:16, :]
    rows_s[every_second(16), :] = chunks_in[ints[TO_EAST], 8:16, :]
    fill_ghosts(ints, arrived, chunks_in, high, low, sides, ghosts, cols_s, rows_s)
    found = edge_ghosts(ints, arrived, chunks_in, sides, SLOTS + 1, slice(8, 16), slice(8, 16))
    for n in range(4):
        heat_ghosts[n] = found[n]
    halos[0] = arrived[ints[FROM_NORTH], SLOTS + 1]
    halos[1] = arrived[ints[FROM_SOUTH], SLOTS + 1]
    for end, b in enumerate((0, TILES - 1)):

        def put(n, k, value):
            ends[n, k, tile(end), :] = value

        lines = [[halos[side, 2 + k : 3 + k, :] for k in range(2)] for side in range(2)]
        coefficients(ints, friction, heat, *lines, cols_s[tile(b), :], 10, b, put)
    sweep(
        ints, flow, pressure, coef, ends, ghosts, cols_s, rows_s, edge_s,
        flow_out, pressure_out, chunks, north, south,
    )


def sweep_kernel(
    ints, flow, pressure, coef, ends, arrived, chunks_in, high, low,
    flow_out, pressure_out, chunks, north, south, sides, ghosts, cols_s, rows_s, edge_s,
):
    fill_ghosts(ints, arrived, chunks_in, high, low, sides, ghosts, cols_s, rows_s)
    sweep(
        ints, flow, pressure, coef, ends, ghosts, cols_s, rows_s, edge_s,
        flow_out, pressure_out, chunks, north, south,
    )


def sweep(
    ints, flow, pressure, coef, ends, ghosts, cols_s, rows_s, edge_s,
    flow_out, pressure_out, chunks, north, south,
):
    def planes(f):
        return flow.at[f] if f < 6 else pressure.at[f - 6]

    def planes_out(f):
        return flow_out.at[f] if f < 6 else pressure_out.at[f - 6]

    chunks[...] = jnp.zeros(chunks.shape, F32)
    for b in range(TILES):
        new = relaxed(planes, coef, ends, ghosts, cols_s[tile(b), :], b)
        gathered = jnp.zeros((8, CELLS), F32)
        for f in range(8):
            planes_out(f)[tile(b), :] = new[f]
            gathered = gather_edge(new[f], f, gathered)
            if b == 0:
                north[0, f : f + 1, :] = new[f][0:1, :]
            if b == TILES - 1:
                south[0, f : f + 1, :] = new[f][7:8, :]
        edge_s[tile(b), :] = gathered
    rows_s[...] = edge_s[...].T
    chunks[ints[TO_WEST]] = rows_s[every_second(1), :]
    chunks[ints[TO_EAST]] = rows_s[every_second(0), :]
    for f in range(8):
        edge_s[f : f + 1, :] = planes_out(f)[pl.ds(ints[ROW], 1), :]
    chunks[ints[CHUNK]] = edge_s[0:8, :]


def final_kernel(
    ints, flow, pressure, coef, ends, arrived, chunks_in, high, low, heat, heat_ghosts,
    flow_out, pressure_out, heat_out, sides, ghosts, cols_s, rows_s, heat_cols_s,
):
    def planes(f):
        return flow.at[f] if f < 6 else pressure.at[f - 6]

    ghost_columns(heat_ghosts[2], heat_ghosts[3], rows_s, heat_cols_s)
    fill_ghosts(ints, arrived, chunks_in, high, low, sides, ghosts, cols_s, rows_s)
    for b in range(TILES):
        new = relaxed(planes, coef, ends, ghosts, cols_s[tile(b), :], b)
        for f in range(6):
            flow_out[f, tile(b), :] = new[f]
        for k in range(2):
            pressure_out[k, tile(b), :] = new[6 + k]
        layers = [
            around(
                heat.at[k],
                b,
                heat_ghosts[0, k : k + 1, :],
                heat_ghosts[1, k : k + 1, :],
                heat_cols_s[tile(b), :],
                k,
            )
            for k in range(2)
        ]
        for k in range(2):
            here, up, down, left, right = layers[k]
            under = jnp.ones((8, CELLS), F32) if k == 0 else layers[0][0]
            over = layers[1][0] if k == 0 else jnp.zeros((8, CELLS), F32)
            advect = jnp.zeros((8, CELLS), F32)
            for component, minus, plus in ((0, under, over), (1, up, down), (2, left, right)):
                speed = new[2 * component + k]
                advect = advect + jnp.maximum(speed, 0.0) * (here - minus)
                advect = advect + jnp.minimum(speed, 0.0) * (plus - here)
            spread = (up + down) + (left + right) + (under + over) - 6.0 * here
            heat_out[k, tile(b), :] = here + 0.1 * (spread - advect)


def shape(*dims):
    return jax.ShapeDtypeStruct(dims, F32)


def scratch(*dims):
    return pltpu.VMEM(dims, F32)


def semaphores(count):
    return pltpu.SemaphoreType.DMA((count,))


def call(kernel, outs, ins, scratches, name, specs=None, limit=4, keep=(), pin=()):
    specs = specs or [SMEM] + [VMEM] * (len(ins) - 1)
    placed = []
    for n, (x, spec) in enumerate(zip(ins, specs)):
        if spec is HBM or n in keep:
            x = pltpu.with_memory_space_constraint(x, spec.memory_space)
        placed.append(x)
    outs = [pltpu.VMEM(x.shape, x.dtype) if n in pin else x for n, x in enumerate(outs)]
    return pl.pallas_call(
        kernel,
        out_shape=outs,
        in_specs=specs,
        out_specs=[VMEM] * len(outs),
        scratch_shapes=scratches,
        compiler_params=pltpu.CompilerParams(vmem_limit_bytes=limit * 1024 * 1024),
        name=name,
    )(*placed)


def shards(
    flow_vector,
    normal_stress,
    thermal_field,
    shear_resistance,
    departing_bands,
    receiving_processor,
    shift_filled_by_lane,
    blending_factors,
):
    flow = flow_vector.reshape(6, CELLS, CELLS)
    pressure = normal_stress[0]
    heat = thermal_field[0]
    friction = shear_resistance[0]
    weights = blending_factors.reshape(8, CELLS, CELLS)
    lat, lon = lax.axis_index("lat"), lax.axis_index("lon")
    n_lat, n_lon = lax.axis_size("lat"), lax.axis_size("lon")
    patch = lax.axis_index("patch")
    own_row = departing_bands.reshape(1)
    receiver = receiving_processor.reshape(1)
    other = (1 - patch) * n_lon

    chunk = other + jnp.maximum(receiver, 0) % n_lon
    beside = jnp.stack([jnp.maximum(lon - 1, 0), jnp.minimum(lon + 1, n_lon - 1)])
    beside = (beside + patch * n_lon).astype(jnp.int32)
    beyond = jnp.stack([jnp.maximum(lat - 1, 0), jnp.minimum(lat + 1, n_lat - 1)])
    beyond = beyond.astype(jnp.int32)
    first = jnp.concatenate([own_row, chunk, beside, receiver])
    on_edge = jnp.stack([lat == 0, lat == n_lat - 1, lon == 0, lon == n_lon - 1]).astype(jnp.int32)
    bases = jnp.stack([jnp.where(lat > 0, 2, 0), jnp.where(lon > 0, 6, 4)]).astype(jnp.int32)
    here = jnp.stack([other, lon]).astype(jnp.int32)
    places_of = jnp.concatenate([own_row, on_edge, bases, chunk, beside, beyond, here])

    square = scratch(CELLS, CELLS)
    tiles = 2 * n_lon
    chunks, north, south, places = call(
        start_kernel,
        [shape(tiles, 16, CELLS), shape(2, 8, CELLS), shape(2, 8, CELLS), shape(8, CELLS)],
        (first, shift_filled_by_lane.reshape(1, CELLS), flow, pressure, heat, friction),
        [scratch(PLANES, CELLS, CELLS), pltpu.VMEM((1, CELLS), jnp.int32), scratch(16, CELLS)]
        + [square, square, semaphores(5)],
        "start",
        specs=[SMEM] + [HBM] * 5,
        pin=(0,),
    )

    def across(chunks):
        return lax.all_to_all(chunks, ("patch", "lon"), 0, 0, tiled=True)

    def along(blocks, north, south, count):
        (packed,) = call(
            pack_kernel,
            [shape(n_lat, count, 8, CELLS)],
            (places_of, sent_to, blocks, north, south),
            [pltpu.SMEM((n_lat,), jnp.int32)],
            "pack",
            specs=[SMEM, SMEM, VMEM, VMEM, VMEM],
            keep=(2,),
            pin=(0,),
        )
        return lax.all_to_all(packed, "lat", 0, 0, tiled=True)

    came, places = lax.optimization_barrier((across(chunks), places))
    sent_to = lax.dynamic_slice(came, (other, 8, 0), (n_lon, 1, 1)).reshape(n_lon)
    sent_to = sent_to.astype(jnp.int32) - 1
    arrived = along(came, north, south, SLOTS + 3)

    own = places[:, 0].astype(jnp.int32) - 1
    pick = jnp.concatenate(
        [jnp.where(lat > 0, own[2:4], own[0:2]), jnp.where(lon > 0, own[6:8], own[4:6])]
    )
    same = (own >= 0)[None] & (own[None] // n_lon == pick[:, None] // n_lon)
    slot = jnp.sum((same & (own[None] < pick[:, None])).astype(jnp.int32), axis=1)
    ints = [places_of, jnp.maximum(pick, 0) // n_lon, jnp.minimum(slot, SLOTS - 1)]
    ints = jnp.concatenate(ints).astype(jnp.int32)

    joined = jax.ShapeDtypeStruct((2, CELLS, 2 * CELLS), jnp.bfloat16)
    high, low = call(
        weights_kernel,
        [joined, joined],
        (ints, weights),
        [scratch(4, CELLS, CELLS), semaphores(2)],
        "weights",
        specs=[SMEM, HBM],
    )
    (coef,) = call(
        coefficient_kernel,
        [shape(8, 2, CELLS, CELLS)],
        (ints, friction, heat, came),
        [square, square],
        "coefficients",
        keep=(3,),
    )
    sides, ghosts = scratch(2, 8, CELLS), scratch(4, 8, CELLS)
    state = [shape(6, CELLS, CELLS), shape(2, CELLS, CELLS)]
    for sweep in range(SWEEPS - 1):
        outs = state + [shape(tiles, 8, CELLS), shape(1, 8, CELLS), shape(1, 8, CELLS)]
        if sweep == 0:
            flow, pressure, chunks, north, south, ends, heat_ghosts = call(
                first_kernel,
                outs + [shape(8, 2, 16, CELLS), shape(4, 8, CELLS)],
                (ints, flow, pressure, coef, friction, heat, arrived, came, high, low),
                [scratch(2, 16, CELLS), ghosts, square, square, square, scratch(2, 8, CELLS)],
                "first_sweep",
                limit=8,
                keep=(3, 6, 7, 8, 9),
                pin=(2,),
            )
        else:
            flow, pressure, chunks, north, south = call(
                sweep_kernel,
                outs,
                (ints, flow, pressure, coef, ends, arrived, came, high, low),
                [sides, ghosts, square, square, square],
                "sweep",
                limit=8,
                keep=(3, 4, 5, 6, 7, 8),
                pin=(2,),
            )
        came = across(chunks)
        arrived = along(came, north, south, SLOTS + 1)
    flow, pressure, heat = call(
        final_kernel,
        state + [shape(2, CELLS, CELLS)],
        (ints, flow, pressure, coef, ends, arrived, came, high, low, heat, heat_ghosts),
        [sides, ghosts, square, square, square],
        "final",
        limit=8,
        keep=(1, 2, 3, 4, 5, 6, 7, 8),
    )
    return flow.reshape(3, 1, 2, CELLS, CELLS), pressure[None], heat[None]


def solution(mesh):
    placed = (
        P(None, "patch", None, "lat", "lon"),
        P("patch", None, "lat", "lon"),
        P("patch", None, "lat", "lon"),
        P("patch", None, "lat", "lon"),
        P("patch", "lat", "lon", None),
        P("patch", "lat", "lon", None),
        P("patch", "lat", "lon", None),
        P("patch", "lat", "lon", None, None, None),
    )
    return jax.shard_map(
        shards,
        mesh=mesh,
        in_specs=placed,
        out_specs=(
            P(None, "patch", None, "lat", "lon"),
            P("patch", None, "lat", "lon"),
            P("patch", None, "lat", "lon"),
        ),
        check_vma=False,
    )
```

```python
import jax
import jax.numpy as jnp
from jax import lax
from jax.experimental import pallas as pl
from jax.experimental.pallas import tpu as pltpu
from jax.sharding import PartitionSpec as P

SWEEPS = 4
CELLS = 128
TILES = 16
PLANES = 12
SLOTS = 4
F32 = jnp.float32
VMEM = pl.BlockSpec(memory_space=pltpu.VMEM)
SMEM = pl.BlockSpec(memory_space=pltpu.SMEM)
HBM = pl.BlockSpec(memory_space=pltpu.HBM)
ROW, NORTH, SOUTH, WEST, EAST, LAT_BASE, LON_BASE = range(7)
CHUNK, TO_WEST, TO_EAST = 7, 8, 9
FROM_NORTH, FROM_SOUTH = 10, 11
OTHER, LON, RECEIVER = 12, 13, 14
BLOCKS, RANKS = 15, 19


def lanes():
    return lax.broadcasted_iota(jnp.int32, (8, CELLS), 1)


def sublanes():
    return lax.broadcasted_iota(jnp.int32, (8, CELLS), 0)


def turn(x, shift):
    shift = shift % CELLS
    return x if shift == 0 else pltpu.roll(x, shift, 1)


def tile(b):
    return pl.ds(8 * b, 8)


class Copies:
    def __init__(self, sems):
        self.sems, self.going = sems, []

    def start(self, source, target):
        copy = pltpu.make_async_copy(source, target, self.sems.at[len(self.going)])
        copy.start()
        self.going.append(copy)

    def wait(self, first=0, last=None):
        for copy in self.going[first:last]:
            copy.wait()


def gather_edge(block, f, gathered):
    lane = lanes()
    return jnp.where(lane // 2 == f, turn(block, 2 * f + 1), gathered)


def every_second(first, count=8):
    return pl.ds(first, count, stride=2)


def ghost_columns(west, east, rows_s, cols_s, first=0):
    rows_s[every_second(2 * first + 1), :] = west
    rows_s[every_second(2 * first), :] = east
    cols_s[...] = rows_s[...].T


def around(ref, b, north, south, column, f):
    here = ref[tile(b), :]
    sub, lane = sublanes(), lanes()
    if b == 0:
        up = jnp.where(sub == 0, north, pltpu.roll(here, 1, 0))
    else:
        up = ref[8 * b - 1 : 8 * b + 7, :]
    if b == TILES - 1:
        down = jnp.where(sub == 7, south, pltpu.roll(here, 7, 0))
    else:
        down = ref[8 * b + 1 : 8 * b + 9, :]
    turned = turn(column, -2 * f - 1)
    left = jnp.where(lane == 0, turned, pltpu.roll(here, 1, 1))
    right = jnp.where(lane == CELLS - 1, turned, pltpu.roll(here, CELLS - 1, 1))
    return here, up, down, left, right


def start_kernel(
    ints, slots, flow, pressure, heat, friction,
    chunks, north, south, places, own, named, row, cols_s, rows_s, sems,
):
    copies = Copies(sems)
    copies.start(slots, named)
    copies.start(flow, own.at[0:6])
    copies.start(pressure, own.at[6:8])
    copies.start(heat, own.at[8:10])
    copies.start(friction, own.at[10:12])
    row[8:16, :] = jnp.broadcast_to((ints[RECEIVER] + 1).astype(F32), (8, CELLS))
    chunks[...] = jnp.zeros(chunks.shape, F32)
    north[...] = jnp.zeros(north.shape, F32)
    south[...] = jnp.zeros(south.shape, F32)
    copies.wait()
    mine = jnp.broadcast_to(named[...], (8, CELLS)) == sublanes()
    place = jnp.sum(jnp.where(mine, lanes() + 1, 0).astype(F32), axis=1, keepdims=True)
    places[...] = jnp.broadcast_to(place, (8, CELLS))
    for f in range(10):
        to = f if f < 8 else f + 1
        row[to : to + 1, :] = own[f, pl.ds(ints[ROW], 1), :]
    for b in range(TILES):
        gathered = jnp.zeros((8, CELLS), F32)
        for f in range(PLANES):
            gathered = gather_edge(own[f, tile(b), :], f, gathered)
        cols_s[tile(b), :] = gathered
    rows_s[...] = cols_s[...].T
    chunks[ints[CHUNK]] = row[...]
    chunks[ints[TO_WEST]] = rows_s[every_second(1, 16), :]
    chunks[ints[TO_EAST]] = rows_s[every_second(0, 16), :]
    for f in range(PLANES):
        n, at = divmod(f, 8)
        north[n, at : at + 1, :] = own[f, 0:1, :]
        south[n, at : at + 1, :] = own[f, CELLS - 1 : CELLS, :]


def pack_kernel(table, arrived, north, south, out):
    out[:, SLOTS] = jnp.zeros((out.shape[0], 8, CELLS), F32)
    for lat in range(out.shape[0]):
        for n in range(SLOTS):
            out[lat, n] = arrived[table[2 + SLOTS * lat + n]]
    out[table[0], SLOTS] = north[0]
    out[table[1], SLOTS] = south[0]


def sort_kernel(ints, sent_to, arrived, north, south, out, filled):
    lats, count = out.shape[0], out.shape[1]
    sources = sent_to.shape[0]
    halos = north.shape[0]
    out[...] = jnp.zeros(out.shape, F32)
    for lat in range(lats):
        filled[lat] = 0
    for n in range(sources):
        number = sent_to[n]
        lat = jnp.maximum(number, 0) // sources

        @pl.when((number >= 0) & (number == lat * sources + ints[LON]))
        def _():
            slot = filled[lat]
            filled[lat] = slot + 1
            block = ints[OTHER] + n
            out[lat, slot] = arrived[block, 0:8, :]
            for k in range(2):
                to = pl.ds(2 * slot + k, 1)
                out[lat, count - 1, to, :] = arrived[block, 9 + k : 10 + k, :]

    for n in range(halos):
        out[ints[FROM_NORTH], SLOTS + n] = north[n]
        out[ints[FROM_SOUTH], SLOTS + n] = south[n]


def split(x):
    high = x.astype(jnp.bfloat16)
    return high, (x - high.astype(F32)).astype(jnp.bfloat16)


def times(left, right):
    return lax.dot_general(left, right, (((1,), (1,)), ((), ())), preferred_element_type=F32)


def weights_kernel(ints, weights, high, low, chosen, sems):
    copies = Copies(sems)
    copies.start(weights.at[pl.ds(ints[LAT_BASE], 2)], chosen.at[0:2])
    copies.start(weights.at[pl.ds(ints[LON_BASE], 2)], chosen.at[2:4])
    copies.wait()
    for side in range(2):
        for term in range(2):
            cut = slice(term * CELLS, (term + 1) * CELLS)
            high[side, :, cut], low[side, :, cut] = split(chosen[2 * side + term])


def blend(ints, blocks_of, high, low, ghosts):
    for n, (first, last) in enumerate(((NORTH, SOUTH), (WEST, EAST))):
        count = ghosts.shape[1]
        ghosts[n] = jnp.zeros((count, CELLS), F32)

        @pl.when(ints[first] + ints[last] > 0)
        def _():
            block = jnp.concatenate([blocks_of(2 * n + t) for t in range(2)], axis=1)
            b_high, b_low = split(block)
            both = times(jnp.concatenate([b_high, b_low], axis=0), high[n])
            ghosts[n] = both[0:count] + both[count:] + times(b_high, low[n])


def edge_ghosts(ints, arrived, chunks, ghosts, slot, rows, of):
    halos = (
        arrived[ints[FROM_NORTH], slot],
        arrived[ints[FROM_SOUTH], slot],
        chunks[ints[TO_WEST], rows, :],
        chunks[ints[TO_EAST], rows, :],
    )
    flags = (ints[NORTH], ints[SOUTH], ints[WEST], ints[EAST])
    return [
        jnp.where(flag > 0, ghosts[n // 2, of, :], halo)
        for n, (flag, halo) in enumerate(zip(flags, halos))
    ]


def coefficients(ints, friction, heat, north, south, column, f, b, put):
    lane, sub = lanes(), sublanes()
    centre = [friction[k, tile(b), :] for k in range(2)]
    for k in range(2):
        here, up, down, left, right = around(
            friction.at[k], b, north[k], south[k], column, f + k
        )
        if b == 0:
            up = jnp.where((sub == 0) & (ints[NORTH] > 0), here, up)
        if b == TILES - 1:
            down = jnp.where((sub == 7) & (ints[SOUTH] > 0), here, down)
        left = jnp.where((lane == 0) & (ints[WEST] > 0), here, left)
        right = jnp.where((lane == CELLS - 1) & (ints[EAST] > 0), here, right)
        faces = [0.5 * (here + other) for other in (up, down, left, right)]
        between = 0.5 * (centre[0] + centre[1])
        diagonal = (faces[0] + faces[1]) + (faces[2] + faces[3]) + (between + here)
        inverse = 0.8 / diagonal
        for n, face in enumerate(faces):
            put(n, k, inverse * face)
        put(4, k, inverse * between)
        put(5, k, 0.5 * inverse)
        put(6, k, inverse * heat[k, tile(b), :])
        put(7, k, 0.125 * here)


def coefficient_kernel(ints, friction, heat, chunks, out, cols_s, rows_s):
    west, east = chunks[ints[TO_WEST], 8:16, :], chunks[ints[TO_EAST], 8:16, :]
    ghost_columns(west, east, rows_s, cols_s)
    for b in range(1, TILES - 1):

        def put(n, k, value):
            out[n, k, tile(b), :] = value

        coefficients(ints, friction, heat, (None, None), (None, None), cols_s[tile(b), :], 2, b, put)
    for b in (0, TILES - 1):
        for n in range(8):
            for k in range(2):
                out[n, k, tile(b), :] = jnp.zeros((8, CELLS), F32)


def relaxed(planes, coef, ends, ghosts, column, b):
    at = [
        around(planes(f), b, ghosts[0, f : f + 1, :], ghosts[1, f : f + 1, :], column, f)
        for f in range(8)
    ]

    def factor(n, k):
        if b == 0 or b == TILES - 1:
            return ends[n, k, tile(0 if b == 0 else 1), :]
        return coef[n, k, tile(b), :]

    new = []
    for component in range(3):
        for k in range(2):
            here, up, down, left, right = at[2 * component + k]
            value = 0.2 * here + factor(0, k) * up + factor(1, k) * down
            value = value + factor(2, k) * left + factor(3, k) * right
            value = value + factor(4, k) * at[2 * component + 1 - k][0]
            if component == 0:
                value = value + factor(6, k)
                slope = at[7][0] if k == 0 else -at[6][0]
            elif component == 1:
                slope = at[6 + k][2] - at[6 + k][1]
            else:
                slope = at[6 + k][4] - at[6 + k][3]
            new.append(value - factor(5, k) * slope)
    for k in range(2):
        divergence = (at[2 + k][2] - at[2 + k][1]) + (at[4 + k][4] - at[4 + k][3])
        divergence = divergence + at[1][0] if k == 0 else divergence - at[0][0]
        new.append(at[6 + k][0] - factor(7, k) * divergence)
    return new


def fill_ghosts(ints, arrived, chunks, high, low, sides, ghosts, cols_s, rows_s):
    count = sides.shape[1]

    def block(n):
        rows = arrived[ints[BLOCKS + n], ints[RANKS + n]]
        if count == 8:
            return rows
        warm = [
            arrived[ints[BLOCKS + n], SLOTS + 2, pl.ds(2 * ints[RANKS + n] + k, 1), :]
            for k in range(2)
        ]
        return jnp.concatenate([rows, *warm, jnp.zeros((6, CELLS), F32)], axis=0)

    blend(ints, block, high, low, sides)
    found = edge_ghosts(ints, arrived, chunks, sides, SLOTS, slice(0, 8), slice(0, 8))
    for n in range(4):
        ghosts[n] = found[n]
    ghost_columns(found[2], found[3], rows_s, cols_s)


def first_kernel(
    ints, flow, pressure, coef, friction, heat, arrived, chunks_in, high, low,
    flow_out, pressure_out, chunks, north, south, ends, heat_ghosts,
    sides, ghosts, cols_s, rows_s, edge_s, halos,
):
    rows_s[every_second(17), :] = chunks_in[ints[TO_WEST], 8:16, :]
    rows_s[every_second(16), :] = chunks_in[ints[TO_EAST], 8:16, :]
    fill_ghosts(ints, arrived, chunks_in, high, low, sides, ghosts, cols_s, rows_s)
    found = edge_ghosts(ints, arrived, chunks_in, sides, SLOTS + 1, slice(8, 16), slice(8, 16))
    for n in range(4):
        heat_ghosts[n] = found[n]
    halos[0] = arrived[ints[FROM_NORTH], SLOTS + 1]
    halos[1] = arrived[ints[FROM_SOUTH], SLOTS + 1]
    for end, b in enumerate((0, TILES - 1)):

        def put(n, k, value):
            ends[n, k, tile(end), :] = value

        lines = [[halos[side, 2 + k : 3 + k, :] for k in range(2)] for side in range(2)]
        coefficients(ints, friction, heat, *lines, cols_s[tile(b), :], 10, b, put)
    sweep(
        ints, flow, pressure, coef, ends, ghosts, cols_s, rows_s, edge_s,
        flow_out, pressure_out, chunks, north, south,
    )


def sweep_kernel(
    ints, flow, pressure, coef, ends, arrived, chunks_in, high, low,
    flow_out, pressure_out, chunks, north, south, sides, ghosts, cols_s, rows_s, edge_s,
):
    fill_ghosts(ints, arrived, chunks_in, high, low, sides, ghosts, cols_s, rows_s)
    sweep(
        ints, flow, pressure, coef, ends, ghosts, cols_s, rows_s, edge_s,
        flow_out, pressure_out, chunks, north, south,
    )


def sweep(
    ints, flow, pressure, coef, ends, ghosts, cols_s, rows_s, edge_s,
    flow_out, pressure_out, chunks, north, south,
):
    def planes(f):
        return flow.at[f] if f < 6 else pressure.at[f - 6]

    def planes_out(f):
        return flow_out.at[f] if f < 6 else pressure_out.at[f - 6]

    chunks[...] = jnp.zeros(chunks.shape, F32)
    for b in range(TILES):
        new = relaxed(planes, coef, ends, ghosts, cols_s[tile(b), :], b)
        for f in range(8):
            planes_out(f)[tile(b), :] = new[f]
    for b in range(TILES):
        gathered = jnp.zeros((8, CELLS), F32)
        for f in range(8):
            gathered = gather_edge(planes_out(f)[tile(b), :], f, gathered)
        edge_s[tile(b), :] = gathered
    for f in range(8):
        north[0, f : f + 1, :] = planes_out(f)[0:1, :]
        south[0, f : f + 1, :] = planes_out(f)[CELLS - 1 : CELLS, :]
    rows_s[...] = edge_s[...].T
    chunks[ints[TO_WEST]] = rows_s[every_second(1), :]
    chunks[ints[TO_EAST]] = rows_s[every_second(0), :]
    for f in range(8):
        edge_s[f : f + 1, :] = planes_out(f)[pl.ds(ints[ROW], 1), :]
    chunks[ints[CHUNK]] = edge_s[0:8, :]


def final_kernel(
    ints, flow, pressure, coef, ends, arrived, chunks_in, high, low, heat, heat_ghosts,
    flow_out, pressure_out, heat_out,
    sides, ghosts, cols_s, rows_s, heat_cols_s, answer, warm, sems,
):
    def planes(f):
        return flow.at[f] if f < 6 else pressure.at[f - 6]

    ghost_columns(heat_ghosts[2], heat_ghosts[3], rows_s, heat_cols_s)
    fill_ghosts(ints, arrived, chunks_in, high, low, sides, ghosts, cols_s, rows_s)
    for b in range(TILES):
        new = relaxed(planes, coef, ends, ghosts, cols_s[tile(b), :], b)
        for f in range(8):
            answer[f, tile(b), :] = new[f]
    copies = Copies(sems)
    copies.start(answer.at[0:6], flow_out)
    copies.start(answer.at[6:8], pressure_out)
    for b in range(TILES):
        layers = [
            around(
                heat.at[k],
                b,
                heat_ghosts[0, k : k + 1, :],
                heat_ghosts[1, k : k + 1, :],
                heat_cols_s[tile(b), :],
                k,
            )
            for k in range(2)
        ]
        for k in range(2):
            here, up, down, left, right = layers[k]
            under = jnp.ones((8, CELLS), F32) if k == 0 else layers[0][0]
            over = layers[1][0] if k == 0 else jnp.zeros((8, CELLS), F32)
            advect = jnp.zeros((8, CELLS), F32)
            for component, minus, plus in ((0, under, over), (1, up, down), (2, left, right)):
                speed = answer[2 * component + k, tile(b), :]
                advect = advect + jnp.maximum(speed, 0.0) * (here - minus)
                advect = advect + jnp.minimum(speed, 0.0) * (plus - here)
            spread = (up + down) + (left + right) + (under + over) - 6.0 * here
            warm[k, tile(b), :] = here + 0.1 * (spread - advect)
    copies.start(warm, heat_out)
    copies.wait()


def shape(*dims):
    return jax.ShapeDtypeStruct(dims, F32)


def scratch(*dims):
    return pltpu.VMEM(dims, F32)


def semaphores(count):
    return pltpu.SemaphoreType.DMA((count,))


def call(
    kernel, outs, ins, scratches, name, specs=None, out_specs=None, limit=4, keep=(), pin=()
):
    out_specs = out_specs or [VMEM] * len(outs)
    specs = specs or [SMEM] + [VMEM] * (len(ins) - 1)
    placed = []
    for n, (x, spec) in enumerate(zip(ins, specs)):
        if spec is HBM or n in keep:
            x = pltpu.with_memory_space_constraint(x, spec.memory_space)
        placed.append(x)
    outs = [
        pltpu.HBM(x.shape, x.dtype)
        if spec is HBM
        else pltpu.VMEM(x.shape, x.dtype)
        if n in pin
        else x
        for n, (x, spec) in enumerate(zip(outs, out_specs))
    ]
    return pl.pallas_call(
        kernel,
        out_shape=outs,
        in_specs=specs,
        out_specs=out_specs,
        scratch_shapes=scratches,
        compiler_params=pltpu.CompilerParams(vmem_limit_bytes=limit * 1024 * 1024),
        name=name,
    )(*placed)


def shards(
    flow_vector,
    normal_stress,
    thermal_field,
    shear_resistance,
    departing_bands,
    receiving_processor,
    shift_filled_by_lane,
    blending_factors,
):
    flow = flow_vector.reshape(6, CELLS, CELLS)
    pressure = normal_stress[0]
    heat = thermal_field[0]
    friction = shear_resistance[0]
    weights = blending_factors.reshape(8, CELLS, CELLS)
    lat, lon = lax.axis_index("lat"), lax.axis_index("lon")
    n_lat, n_lon = lax.axis_size("lat"), lax.axis_size("lon")
    patch = lax.axis_index("patch")
    own_row = departing_bands.reshape(1)
    receiver = receiving_processor.reshape(1)
    other = (1 - patch) * n_lon

    chunk = other + jnp.maximum(receiver, 0) % n_lon
    beside = jnp.stack([jnp.maximum(lon - 1, 0), jnp.minimum(lon + 1, n_lon - 1)])
    beside = (beside + patch * n_lon).astype(jnp.int32)
    beyond = jnp.stack([jnp.maximum(lat - 1, 0), jnp.minimum(lat + 1, n_lat - 1)])
    beyond = beyond.astype(jnp.int32)
    on_edge = jnp.stack([lat == 0, lat == n_lat - 1, lon == 0, lon == n_lon - 1]).astype(jnp.int32)
    bases = jnp.stack([jnp.where(lat > 0, 2, 0), jnp.where(lon > 0, 6, 4)]).astype(jnp.int32)
    here = jnp.stack([other, lon]).astype(jnp.int32)
    first = jnp.concatenate([own_row, on_edge, bases, chunk, beside, beyond, here, receiver])

    square = scratch(CELLS, CELLS)
    tiles = 2 * n_lon
    chunks, north, south, places = call(
        start_kernel,
        [shape(tiles, 16, CELLS), shape(2, 8, CELLS), shape(2, 8, CELLS), shape(8, CELLS)],
        (first, shift_filled_by_lane.reshape(1, CELLS), flow, pressure, heat, friction),
        [scratch(PLANES, CELLS, CELLS), pltpu.VMEM((1, CELLS), jnp.int32), scratch(16, CELLS)]
        + [square, square, semaphores(5)],
        "start",
        specs=[SMEM] + [HBM] * 5,
        pin=(0,),
    )

    def across(chunks):
        return lax.all_to_all(chunks, ("patch", "lon"), 0, 0, tiled=True)

    def along(packed):
        return lax.all_to_all(packed, "lat", 0, 0, tiled=True)

    came, places, lon, lat, other = lax.optimization_barrier(
        (across(chunks), places, lon, lat, other)
    )
    sent_to = lax.dynamic_slice(came, (other, 8, 0), (n_lon, 1, 1)).reshape(n_lon)
    sent_to = sent_to.astype(jnp.int32) - 1
    (packed,) = call(
        sort_kernel,
        [shape(n_lat, SLOTS + 3, 8, CELLS)],
        (first, sent_to, came, north, south),
        [pltpu.SMEM((n_lat,), jnp.int32)],
        "sort",
        specs=[SMEM, SMEM, VMEM, VMEM, VMEM],
        keep=(2,),
        pin=(0,),
    )
    arrived = along(packed)

    packed, sent_to = lax.optimization_barrier((packed, sent_to))
    every_lat = jnp.arange(n_lat, dtype=jnp.int32)[:, None]
    wanted = sent_to[None] == every_lat * n_lon + lon
    order = jnp.arange(n_lon, dtype=jnp.int32)
    earlier = wanted[:, None, :] & (order[None, None, :] < order[None, :, None])
    rank = jnp.sum(earlier.astype(jnp.int32), axis=2)
    mine = wanted[:, None, :] & (rank[:, None, :] == jnp.arange(SLOTS)[None, :, None])
    found = jnp.sum(jnp.where(mine, order[None, None, :], 0), axis=2).reshape(-1)
    table = jnp.concatenate([beyond, other + found]).astype(jnp.int32)

    own = places[:, 0].astype(jnp.int32) - 1
    pick = jnp.concatenate(
        [jnp.where(lat > 0, own[2:4], own[0:2]), jnp.where(lon > 0, own[6:8], own[4:6])]
    )
    same = (own >= 0)[None] & (own[None] // n_lon == pick[:, None] // n_lon)
    slot = jnp.sum((same & (own[None] < pick[:, None])).astype(jnp.int32), axis=1)
    ints = [first, jnp.maximum(pick, 0) // n_lon, jnp.minimum(slot, SLOTS - 1)]
    ints = jnp.concatenate(ints).astype(jnp.int32)

    joined = jax.ShapeDtypeStruct((2, CELLS, 2 * CELLS), jnp.bfloat16)
    high, low = call(
        weights_kernel,
        [joined, joined],
        (ints, weights),
        [scratch(4, CELLS, CELLS), semaphores(2)],
        "weights",
        specs=[SMEM, HBM],
    )
    (coef,) = call(
        coefficient_kernel,
        [shape(8, 2, CELLS, CELLS)],
        (ints, friction, heat, came),
        [square, square],
        "coefficients",
        keep=(3,),
    )
    sides, ghosts = scratch(2, 8, CELLS), scratch(4, 8, CELLS)
    state = [shape(6, CELLS, CELLS), shape(2, CELLS, CELLS)]
    for sweep in range(SWEEPS - 1):
        outs = state + [shape(tiles, 8, CELLS), shape(1, 8, CELLS), shape(1, 8, CELLS)]
        if sweep == 0:
            flow, pressure, chunks, north, south, ends, heat_ghosts = call(
                first_kernel,
                outs + [shape(8, 2, 16, CELLS), shape(4, 8, CELLS)],
                (ints, flow, pressure, coef, friction, heat, arrived, came, high, low),
                [scratch(2, 16, CELLS), ghosts, square, square, square, scratch(2, 8, CELLS)],
                "first_sweep",
                limit=8,
                keep=(3, 6, 7, 8, 9),
                pin=(2,),
            )
        else:
            flow, pressure, chunks, north, south = call(
                sweep_kernel,
                outs,
                (ints, flow, pressure, coef, ends, arrived, came, high, low),
                [sides, ghosts, square, square, square],
                "sweep",
                limit=8,
                keep=(3, 4, 5, 6, 7, 8),
                pin=(2,),
            )
        came = across(chunks)
        (packed,) = call(
            pack_kernel,
            [shape(n_lat, SLOTS + 1, 8, CELLS)],
            (table, came, north, south),
            [],
            "pack",
            keep=(1,),
            pin=(0,),
        )
        arrived = along(packed)
    flow, pressure, heat = call(
        final_kernel,
        state + [shape(2, CELLS, CELLS)],
        (ints, flow, pressure, coef, ends, arrived, came, high, low, heat, heat_ghosts),
        [sides, ghosts, square, square, square]
        + [scratch(8, CELLS, CELLS), scratch(2, CELLS, CELLS), semaphores(3)],
        "final",
        out_specs=[HBM] * 3,
        limit=8,
        keep=(1, 2, 3, 4, 5, 6, 7, 8),
    )
    return flow.reshape(3, 1, 2, CELLS, CELLS), pressure[None], heat[None]


def solution(mesh):
    placed = (
        P(None, "patch", None, "lat", "lon"),
        P("patch", None, "lat", "lon"),
        P("patch", None, "lat", "lon"),
        P("patch", None, "lat", "lon"),
        P("patch", "lat", "lon", None),
        P("patch", "lat", "lon", None),
        P("patch", "lat", "lon", None),
        P("patch", "lat", "lon", None, None, None),
    )
    return jax.shard_map(
        shards,
        mesh=mesh,
        in_specs=placed,
        out_specs=(
            P(None, "patch", None, "lat", "lon"),
            P("patch", None, "lat", "lon"),
            P("patch", None, "lat", "lon"),
        ),
        check_vma=False,
    )
```

```python
import jax
import jax.numpy as jnp
from jax import lax
from jax.experimental import pallas as pl
from jax.experimental.pallas import tpu as pltpu
from jax.sharding import PartitionSpec as P

SWEEPS = 4
CELLS = 128
TILES = 16
PLANES = 12
SLOTS = 4
F32 = jnp.float32
VMEM = pl.BlockSpec(memory_space=pltpu.VMEM)
SMEM = pl.BlockSpec(memory_space=pltpu.SMEM)
HBM = pl.BlockSpec(memory_space=pltpu.HBM)
ROW, NORTH, SOUTH, WEST, EAST, LAT_BASE, LON_BASE = range(7)
CHUNK, TO_WEST, TO_EAST = 7, 8, 9
FROM_NORTH, FROM_SOUTH = 10, 11
OTHER, LON, RECEIVER = 12, 13, 14
BLOCKS, RANKS = 15, 19


def lanes():
    return lax.broadcasted_iota(jnp.int32, (8, CELLS), 1)


def sublanes():
    return lax.broadcasted_iota(jnp.int32, (8, CELLS), 0)


def turn(x, shift):
    shift = shift % CELLS
    return x if shift == 0 else pltpu.roll(x, shift, 1)


def tile(b):
    return pl.ds(8 * b, 8)


class Copies:
    def __init__(self, sems):
        self.sems, self.going = sems, []

    def start(self, source, target):
        copy = pltpu.make_async_copy(source, target, self.sems.at[len(self.going)])
        copy.start()
        self.going.append(copy)

    def wait(self, first=0, last=None):
        for copy in self.going[first:last]:
            copy.wait()


def gather_edge(block, f, gathered):
    lane = lanes()
    return jnp.where(lane // 2 == f, turn(block, 2 * f + 1), gathered)


def every_second(first, count=8):
    return pl.ds(first, count, stride=2)


def ghost_columns(west, east, rows_s, cols_s, first=0):
    rows_s[every_second(2 * first + 1), :] = west
    rows_s[every_second(2 * first), :] = east
    cols_s[...] = rows_s[...].T


def around(ref, b, north, south, column, f):
    here = ref[tile(b), :]
    sub, lane = sublanes(), lanes()
    if b == 0:
        up = jnp.where(sub == 0, north, pltpu.roll(here, 1, 0))
    else:
        up = ref[8 * b - 1 : 8 * b + 7, :]
    if b == TILES - 1:
        down = jnp.where(sub == 7, south, pltpu.roll(here, 7, 0))
    else:
        down = ref[8 * b + 1 : 8 * b + 9, :]
    turned = turn(column, -2 * f - 1)
    left = jnp.where(lane == 0, turned, pltpu.roll(here, 1, 1))
    right = jnp.where(lane == CELLS - 1, turned, pltpu.roll(here, CELLS - 1, 1))
    return here, up, down, left, right


def start_kernel(
    ints, slots, flow, pressure, heat, friction,
    chunks, north, south, places, own, named, row, cols_s, rows_s, sems,
):
    copies = Copies(sems)
    copies.start(slots, named)
    copies.start(flow, own.at[0:6])
    copies.start(pressure, own.at[6:8])
    copies.start(heat, own.at[8:10])
    copies.start(friction, own.at[10:12])
    row[8:16, :] = jnp.broadcast_to((ints[RECEIVER] + 1).astype(F32), (8, CELLS))
    chunks[...] = jnp.zeros(chunks.shape, F32)
    north[...] = jnp.zeros(north.shape, F32)
    south[...] = jnp.zeros(south.shape, F32)
    copies.wait()
    mine = jnp.broadcast_to(named[...], (8, CELLS)) == sublanes()
    place = jnp.sum(jnp.where(mine, lanes() + 1, 0).astype(F32), axis=1, keepdims=True)
    places[...] = jnp.broadcast_to(place, (8, CELLS))
    for f in range(10):
        to = f if f < 8 else f + 1
        row[to : to + 1, :] = own[f, pl.ds(ints[ROW], 1), :]
    for b in range(TILES):
        gathered = jnp.zeros((8, CELLS), F32)
        for f in range(PLANES):
            gathered = gather_edge(own[f, tile(b), :], f, gathered)
        cols_s[tile(b), :] = gathered
    rows_s[...] = cols_s[...].T
    chunks[ints[CHUNK]] = row[...]
    chunks[ints[TO_WEST]] = rows_s[every_second(1, 16), :]
    chunks[ints[TO_EAST]] = rows_s[every_second(0, 16), :]
    for f in range(PLANES):
        n, at = divmod(f, 8)
        north[n, at : at + 1, :] = own[f, 0:1, :]
        south[n, at : at + 1, :] = own[f, CELLS - 1 : CELLS, :]


def pack_kernel(table, arrived, north, south, out):
    out[:, SLOTS] = jnp.zeros((out.shape[0], 8, CELLS), F32)
    for lat in range(out.shape[0]):
        for n in range(SLOTS):
            out[lat, n] = arrived[table[2 + SLOTS * lat + n]]
    out[table[0], SLOTS] = north[0]
    out[table[1], SLOTS] = south[0]


def for_each_block(ints, sent_to, filled, lats, act):
    sources = sent_to.shape[0]
    for lat in range(lats):
        filled[lat] = 0
    for n in range(sources):
        number = sent_to[n]
        lat = jnp.maximum(number, 0) // sources

        @pl.when((number >= 0) & (number == lat * sources + ints[LON]))
        def _():
            slot = filled[lat]
            filled[lat] = slot + 1
            act(lat, slot, ints[OTHER] + n)


def table_kernel(ints, sent_to, table, filled):
    table[0] = ints[FROM_NORTH]
    table[1] = ints[FROM_SOUTH]
    for n in range(2, table.shape[0]):
        table[n] = ints[OTHER]

    def act(lat, slot, block):
        table[2 + SLOTS * lat + slot] = block

    for_each_block(ints, sent_to, filled, (table.shape[0] - 2) // SLOTS, act)


def sort_kernel(ints, sent_to, arrived, north, south, out, filled):
    lats, count = out.shape[0], out.shape[1]
    out[...] = jnp.zeros(out.shape, F32)

    def act(lat, slot, block):
        out[lat, slot] = arrived[block, 0:8, :]
        for k in range(2):
            to = pl.ds(2 * slot + k, 1)
            out[lat, count - 1, to, :] = arrived[block, 9 + k : 10 + k, :]

    for_each_block(ints, sent_to, filled, lats, act)
    for n in range(north.shape[0]):
        out[ints[FROM_NORTH], SLOTS + n] = north[n]
        out[ints[FROM_SOUTH], SLOTS + n] = south[n]


def split(x):
    high = x.astype(jnp.bfloat16)
    return high, (x - high.astype(F32)).astype(jnp.bfloat16)


def times(left, right):
    return lax.dot_general(left, right, (((1,), (1,)), ((), ())), preferred_element_type=F32)


def weights_kernel(ints, weights, high, low, chosen, sems):
    copies = Copies(sems)
    copies.start(weights.at[pl.ds(ints[LAT_BASE], 2)], chosen.at[0:2])
    copies.start(weights.at[pl.ds(ints[LON_BASE], 2)], chosen.at[2:4])
    copies.wait()
    for side in range(2):
        for term in range(2):
            cut = slice(term * CELLS, (term + 1) * CELLS)
            high[side, :, cut], low[side, :, cut] = split(chosen[2 * side + term])


def blend(ints, blocks_of, high, low, ghosts):
    for n, (first, last) in enumerate(((NORTH, SOUTH), (WEST, EAST))):
        count = ghosts.shape[1]
        ghosts[n] = jnp.zeros((count, CELLS), F32)

        @pl.when(ints[first] + ints[last] > 0)
        def _():
            block = jnp.concatenate([blocks_of(2 * n + t) for t in range(2)], axis=1)
            b_high, b_low = split(block)
            both = times(jnp.concatenate([b_high, b_low], axis=0), high[n])
            ghosts[n] = both[0:count] + both[count:] + times(b_high, low[n])


def edge_ghosts(ints, arrived, chunks, ghosts, slot, rows, of):
    halos = (
        arrived[ints[FROM_NORTH], slot],
        arrived[ints[FROM_SOUTH], slot],
        chunks[ints[TO_WEST], rows, :],
        chunks[ints[TO_EAST], rows, :],
    )
    flags = (ints[NORTH], ints[SOUTH], ints[WEST], ints[EAST])
    return [
        jnp.where(flag > 0, ghosts[n // 2, of, :], halo)
        for n, (flag, halo) in enumerate(zip(flags, halos))
    ]


def coefficients(ints, friction, heat, north, south, column, f, b, put):
    lane, sub = lanes(), sublanes()
    centre = [friction[k, tile(b), :] for k in range(2)]
    for k in range(2):
        here, up, down, left, right = around(
            friction.at[k], b, north[k], south[k], column, f + k
        )
        if b == 0:
            up = jnp.where((sub == 0) & (ints[NORTH] > 0), here, up)
        if b == TILES - 1:
            down = jnp.where((sub == 7) & (ints[SOUTH] > 0), here, down)
        left = jnp.where((lane == 0) & (ints[WEST] > 0), here, left)
        right = jnp.where((lane == CELLS - 1) & (ints[EAST] > 0), here, right)
        faces = [0.5 * (here + other) for other in (up, down, left, right)]
        between = 0.5 * (centre[0] + centre[1])
        diagonal = (faces[0] + faces[1]) + (faces[2] + faces[3]) + (between + here)
        inverse = 0.8 / diagonal
        for n, face in enumerate(faces):
            put(n, k, inverse * face)
        put(4, k, inverse * between)
        put(5, k, 0.5 * inverse)
        put(6, k, inverse * heat[k, tile(b), :])
        put(7, k, 0.125 * here)


def coefficient_kernel(ints, friction, heat, chunks, out, cols_s, rows_s):
    west, east = chunks[ints[TO_WEST], 8:16, :], chunks[ints[TO_EAST], 8:16, :]
    ghost_columns(west, east, rows_s, cols_s)
    for b in range(1, TILES - 1):

        def put(n, k, value):
            out[n, k, tile(b), :] = value

        coefficients(ints, friction, heat, (None, None), (None, None), cols_s[tile(b), :], 2, b, put)
    for b in (0, TILES - 1):
        for n in range(8):
            for k in range(2):
                out[n, k, tile(b), :] = jnp.zeros((8, CELLS), F32)


def relaxed(planes, coef, ends, ghosts, column, b):
    at = [
        around(planes(f), b, ghosts[0, f : f + 1, :], ghosts[1, f : f + 1, :], column, f)
        for f in range(8)
    ]

    def factor(n, k):
        if b == 0 or b == TILES - 1:
            return ends[n, k, tile(0 if b == 0 else 1), :]
        return coef[n, k, tile(b), :]

    new = []
    for component in range(3):
        for k in range(2):
            here, up, down, left, right = at[2 * component + k]
            value = 0.2 * here + factor(0, k) * up + factor(1, k) * down
            value = value + factor(2, k) * left + factor(3, k) * right
            value = value + factor(4, k) * at[2 * component + 1 - k][0]
            if component == 0:
                value = value + factor(6, k)
                slope = at[7][0] if k == 0 else -at[6][0]
            elif component == 1:
                slope = at[6 + k][2] - at[6 + k][1]
            else:
                slope = at[6 + k][4] - at[6 + k][3]
            new.append(value - factor(5, k) * slope)
    for k in range(2):
        divergence = (at[2 + k][2] - at[2 + k][1]) + (at[4 + k][4] - at[4 + k][3])
        divergence = divergence + at[1][0] if k == 0 else divergence - at[0][0]
        new.append(at[6 + k][0] - factor(7, k) * divergence)
    return new


def fill_ghosts(ints, arrived, chunks, high, low, sides, ghosts, cols_s, rows_s):
    count = sides.shape[1]

    def block(n):
        rows = arrived[ints[BLOCKS + n], ints[RANKS + n]]
        if count == 8:
            return rows
        warm = [
            arrived[ints[BLOCKS + n], SLOTS + 2, pl.ds(2 * ints[RANKS + n] + k, 1), :]
            for k in range(2)
        ]
        return jnp.concatenate([rows, *warm, jnp.zeros((6, CELLS), F32)], axis=0)

    blend(ints, block, high, low, sides)
    found = edge_ghosts(ints, arrived, chunks, sides, SLOTS, slice(0, 8), slice(0, 8))
    for n in range(4):
        ghosts[n] = found[n]
    ghost_columns(found[2], found[3], rows_s, cols_s)


def first_kernel(
    ints, flow, pressure, coef, friction, heat, arrived, chunks_in, high, low,
    flow_out, pressure_out, chunks, north, south, ends, heat_ghosts,
    sides, ghosts, cols_s, rows_s, edge_s, halos,
):
    rows_s[every_second(17), :] = chunks_in[ints[TO_WEST], 8:16, :]
    rows_s[every_second(16), :] = chunks_in[ints[TO_EAST], 8:16, :]
    fill_ghosts(ints, arrived, chunks_in, high, low, sides, ghosts, cols_s, rows_s)
    found = edge_ghosts(ints, arrived, chunks_in, sides, SLOTS + 1, slice(8, 16), slice(8, 16))
    for n in range(4):
        heat_ghosts[n] = found[n]
    halos[0] = arrived[ints[FROM_NORTH], SLOTS + 1]
    halos[1] = arrived[ints[FROM_SOUTH], SLOTS + 1]
    for end, b in enumerate((0, TILES - 1)):

        def put(n, k, value):
            ends[n, k, tile(end), :] = value

        lines = [[halos[side, 2 + k : 3 + k, :] for k in range(2)] for side in range(2)]
        coefficients(ints, friction, heat, *lines, cols_s[tile(b), :], 10, b, put)
    sweep(
        ints, flow, pressure, coef, ends, ghosts, cols_s, rows_s, edge_s,
        flow_out, pressure_out, chunks, north, south,
    )


def sweep_kernel(
    ints, flow, pressure, coef, ends, arrived, chunks_in, high, low,
    flow_out, pressure_out, chunks, north, south, sides, ghosts, cols_s, rows_s, edge_s,
):
    fill_ghosts(ints, arrived, chunks_in, high, low, sides, ghosts, cols_s, rows_s)
    sweep(
        ints, flow, pressure, coef, ends, ghosts, cols_s, rows_s, edge_s,
        flow_out, pressure_out, chunks, north, south,
    )


def sweep(
    ints, flow, pressure, coef, ends, ghosts, cols_s, rows_s, edge_s,
    flow_out, pressure_out, chunks, north, south,
):
    def planes(f):
        return flow.at[f] if f < 6 else pressure.at[f - 6]

    def planes_out(f):
        return flow_out.at[f] if f < 6 else pressure_out.at[f - 6]

    chunks[...] = jnp.zeros(chunks.shape, F32)
    for b in range(TILES):
        new = relaxed(planes, coef, ends, ghosts, cols_s[tile(b), :], b)
        for f in range(8):
            planes_out(f)[tile(b), :] = new[f]
    for b in range(TILES):
        gathered = jnp.zeros((8, CELLS), F32)
        for f in range(8):
            gathered = gather_edge(planes_out(f)[tile(b), :], f, gathered)
        edge_s[tile(b), :] = gathered
    for f in range(8):
        north[0, f : f + 1, :] = planes_out(f)[0:1, :]
        south[0, f : f + 1, :] = planes_out(f)[CELLS - 1 : CELLS, :]
    rows_s[...] = edge_s[...].T
    chunks[ints[TO_WEST]] = rows_s[every_second(1), :]
    chunks[ints[TO_EAST]] = rows_s[every_second(0), :]
    for f in range(8):
        edge_s[f : f + 1, :] = planes_out(f)[pl.ds(ints[ROW], 1), :]
    chunks[ints[CHUNK]] = edge_s[0:8, :]


def final_kernel(
    ints, flow, pressure, coef, ends, arrived, chunks_in, high, low, heat, heat_ghosts,
    flow_out, pressure_out, heat_out,
    sides, ghosts, cols_s, rows_s, heat_cols_s, answer, warm, sems,
):
    def planes(f):
        return flow.at[f] if f < 6 else pressure.at[f - 6]

    ghost_columns(heat_ghosts[2], heat_ghosts[3], rows_s, heat_cols_s)
    fill_ghosts(ints, arrived, chunks_in, high, low, sides, ghosts, cols_s, rows_s)
    for b in range(TILES):
        new = relaxed(planes, coef, ends, ghosts, cols_s[tile(b), :], b)
        for f in range(8):
            answer[f, tile(b), :] = new[f]
    copies = Copies(sems)
    copies.start(answer.at[0:6], flow_out)
    copies.start(answer.at[6:8], pressure_out)
    for b in range(TILES):
        layers = [
            around(
                heat.at[k],
                b,
                heat_ghosts[0, k : k + 1, :],
                heat_ghosts[1, k : k + 1, :],
                heat_cols_s[tile(b), :],
                k,
            )
            for k in range(2)
        ]
        for k in range(2):
            here, up, down, left, right = layers[k]
            under = jnp.ones((8, CELLS), F32) if k == 0 else layers[0][0]
            over = layers[1][0] if k == 0 else jnp.zeros((8, CELLS), F32)
            advect = jnp.zeros((8, CELLS), F32)
            for component, minus, plus in ((0, under, over), (1, up, down), (2, left, right)):
                speed = answer[2 * component + k, tile(b), :]
                advect = advect + jnp.maximum(speed, 0.0) * (here - minus)
                advect = advect + jnp.minimum(speed, 0.0) * (plus - here)
            spread = (up + down) + (left + right) + (under + over) - 6.0 * here
            warm[k, tile(b), :] = here + 0.1 * (spread - advect)
    copies.start(warm, heat_out)
    copies.wait()


def shape(*dims):
    return jax.ShapeDtypeStruct(dims, F32)


def scratch(*dims):
    return pltpu.VMEM(dims, F32)


def semaphores(count):
    return pltpu.SemaphoreType.DMA((count,))


def call(
    kernel, outs, ins, scratches, name, specs=None, out_specs=None, limit=4, keep=(), pin=()
):
    out_specs = out_specs or [VMEM] * len(outs)
    specs = specs or [SMEM] + [VMEM] * (len(ins) - 1)
    placed = []
    for n, (x, spec) in enumerate(zip(ins, specs)):
        if spec is HBM or n in keep:
            x = pltpu.with_memory_space_constraint(x, spec.memory_space)
        placed.append(x)
    outs = [
        pltpu.HBM(x.shape, x.dtype)
        if spec is HBM
        else pltpu.VMEM(x.shape, x.dtype)
        if n in pin
        else x
        for n, (x, spec) in enumerate(zip(outs, out_specs))
    ]
    return pl.pallas_call(
        kernel,
        out_shape=outs,
        in_specs=specs,
        out_specs=out_specs,
        scratch_shapes=scratches,
        compiler_params=pltpu.CompilerParams(vmem_limit_bytes=limit * 1024 * 1024),
        name=name,
    )(*placed)


def shards(
    flow_vector,
    normal_stress,
    thermal_field,
    shear_resistance,
    departing_bands,
    receiving_processor,
    shift_filled_by_lane,
    blending_factors,
):
    flow = flow_vector.reshape(6, CELLS, CELLS)
    pressure = normal_stress[0]
    heat = thermal_field[0]
    friction = shear_resistance[0]
    weights = blending_factors.reshape(8, CELLS, CELLS)
    lat, lon = lax.axis_index("lat"), lax.axis_index("lon")
    n_lat, n_lon = lax.axis_size("lat"), lax.axis_size("lon")
    patch = lax.axis_index("patch")
    own_row = departing_bands.reshape(1)
    receiver = receiving_processor.reshape(1)
    other = (1 - patch) * n_lon

    chunk = other + jnp.maximum(receiver, 0) % n_lon
    beside = jnp.stack([jnp.maximum(lon - 1, 0), jnp.minimum(lon + 1, n_lon - 1)])
    beside = (beside + patch * n_lon).astype(jnp.int32)
    beyond = jnp.stack([jnp.maximum(lat - 1, 0), jnp.minimum(lat + 1, n_lat - 1)])
    beyond = beyond.astype(jnp.int32)
    on_edge = jnp.stack([lat == 0, lat == n_lat - 1, lon == 0, lon == n_lon - 1]).astype(jnp.int32)
    bases = jnp.stack([jnp.where(lat > 0, 2, 0), jnp.where(lon > 0, 6, 4)]).astype(jnp.int32)
    here = jnp.stack([other, lon]).astype(jnp.int32)
    first = jnp.concatenate([own_row, on_edge, bases, chunk, beside, beyond, here, receiver])

    square = scratch(CELLS, CELLS)
    tiles = 2 * n_lon
    chunks, north, south, places = call(
        start_kernel,
        [shape(tiles, 16, CELLS), shape(2, 8, CELLS), shape(2, 8, CELLS), shape(8, CELLS)],
        (first, shift_filled_by_lane.reshape(1, CELLS), flow, pressure, heat, friction),
        [scratch(PLANES, CELLS, CELLS), pltpu.VMEM((1, CELLS), jnp.int32), scratch(16, CELLS)]
        + [square, square, semaphores(5)],
        "start",
        specs=[SMEM] + [HBM] * 5,
        pin=(0,),
    )

    def across(chunks):
        return lax.all_to_all(chunks, ("patch", "lon"), 0, 0, tiled=True)

    def along(packed):
        return lax.all_to_all(packed, "lat", 0, 0, tiled=True)

    came, places, lon, lat, other = lax.optimization_barrier(
        (across(chunks), places, lon, lat, other)
    )
    sent_to = lax.dynamic_slice(came, (other, 8, 0), (n_lon, 1, 1)).reshape(n_lon)
    sent_to = sent_to.astype(jnp.int32) - 1
    (packed,) = call(
        sort_kernel,
        [shape(n_lat, SLOTS + 3, 8, CELLS)],
        (first, sent_to, came, north, south),
        [pltpu.SMEM((n_lat,), jnp.int32)],
        "sort",
        specs=[SMEM, SMEM, VMEM, VMEM, VMEM],
        keep=(2,),
        pin=(0,),
    )
    arrived = along(packed)

    (table,) = call(
        table_kernel,
        [jax.ShapeDtypeStruct((2 + n_lat * SLOTS,), jnp.int32)],
        lax.optimization_barrier((first, sent_to, packed))[:2],
        [pltpu.SMEM((n_lat,), jnp.int32)],
        "table",
        specs=[SMEM, SMEM],
        out_specs=[SMEM],
    )
    arrived, table = lax.optimization_barrier((arrived, table))

    own = places[:, 0].astype(jnp.int32) - 1
    pick = jnp.concatenate(
        [jnp.where(lat > 0, own[2:4], own[0:2]), jnp.where(lon > 0, own[6:8], own[4:6])]
    )
    same = (own >= 0)[None] & (own[None] // n_lon == pick[:, None] // n_lon)
    slot = jnp.sum((same & (own[None] < pick[:, None])).astype(jnp.int32), axis=1)
    ints = [first, jnp.maximum(pick, 0) // n_lon, jnp.minimum(slot, SLOTS - 1)]
    ints = jnp.concatenate(ints).astype(jnp.int32)

    joined = jax.ShapeDtypeStruct((2, CELLS, 2 * CELLS), jnp.bfloat16)
    high, low = call(
        weights_kernel,
        [joined, joined],
        (ints, weights),
        [scratch(4, CELLS, CELLS), semaphores(2)],
        "weights",
        specs=[SMEM, HBM],
    )
    (coef,) = call(
        coefficient_kernel,
        [shape(8, 2, CELLS, CELLS)],
        (ints, friction, heat, came),
        [square, square],
        "coefficients",
        keep=(3,),
    )
    sides, ghosts = scratch(2, 8, CELLS), scratch(4, 8, CELLS)
    state = [shape(6, CELLS, CELLS), shape(2, CELLS, CELLS)]
    for sweep in range(SWEEPS - 1):
        outs = state + [shape(tiles, 8, CELLS), shape(1, 8, CELLS), shape(1, 8, CELLS)]
        if sweep == 0:
            flow, pressure, chunks, north, south, ends, heat_ghosts = call(
                first_kernel,
                outs + [shape(8, 2, 16, CELLS), shape(4, 8, CELLS)],
                (ints, flow, pressure, coef, friction, heat, arrived, came, high, low),
                [scratch(2, 16, CELLS), ghosts, square, square, square, scratch(2, 8, CELLS)],
                "first_sweep",
                limit=8,
                keep=(3, 6, 7, 8, 9),
                pin=(2,),
            )
        else:
            flow, pressure, chunks, north, south = call(
                sweep_kernel,
                outs,
                (ints, flow, pressure, coef, ends, arrived, came, high, low),
                [sides, ghosts, square, square, square],
                "sweep",
                limit=8,
                keep=(3, 4, 5, 6, 7, 8),
                pin=(2,),
            )
        came = across(chunks)
        (packed,) = call(
            pack_kernel,
            [shape(n_lat, SLOTS + 1, 8, CELLS)],
            (table, came, north, south),
            [],
            "pack",
            keep=(1,),
            pin=(0,),
        )
        arrived = along(packed)
    flow, pressure, heat = call(
        final_kernel,
        state + [shape(2, CELLS, CELLS)],
        (ints, flow, pressure, coef, ends, arrived, came, high, low, heat, heat_ghosts),
        [sides, ghosts, square, square, square]
        + [scratch(8, CELLS, CELLS), scratch(2, CELLS, CELLS), semaphores(3)],
        "final",
        out_specs=[HBM] * 3,
        limit=8,
        keep=(1, 2, 3, 4, 5, 6, 7, 8),
    )
    return flow.reshape(3, 1, 2, CELLS, CELLS), pressure[None], heat[None]


def solution(mesh):
    placed = (
        P(None, "patch", None, "lat", "lon"),
        P("patch", None, "lat", "lon"),
        P("patch", None, "lat", "lon"),
        P("patch", None, "lat", "lon"),
        P("patch", "lat", "lon", None),
        P("patch", "lat", "lon", None),
        P("patch", "lat", "lon", None),
        P("patch", "lat", "lon", None, None, None),
    )
    return jax.shard_map(
        shards,
        mesh=mesh,
        in_specs=placed,
        out_specs=(
            P(None, "patch", None, "lat", "lon"),
            P("patch", None, "lat", "lon"),
            P("patch", None, "lat", "lon"),
        ),
        check_vma=False,
    )
```

```python
import jax
import jax.numpy as jnp
from jax import lax
from jax.experimental import pallas as pl
from jax.experimental.pallas import tpu as pltpu
from jax.sharding import PartitionSpec as P

SWEEPS = 4
CELLS = 128
TILES = 16
PLANES = 12
SLOTS = 4
F32 = jnp.float32
VMEM = pl.BlockSpec(memory_space=pltpu.VMEM)
SMEM = pl.BlockSpec(memory_space=pltpu.SMEM)
HBM = pl.BlockSpec(memory_space=pltpu.HBM)
ROW, NORTH, SOUTH, WEST, EAST, LAT_BASE, LON_BASE = range(7)
CHUNK, TO_WEST, TO_EAST = 7, 8, 9
FROM_NORTH, FROM_SOUTH = 10, 11
OTHER, LON, RECEIVER = 12, 13, 14
BLOCKS, RANKS = 15, 19


def lanes():
    return lax.broadcasted_iota(jnp.int32, (8, CELLS), 1)


def sublanes():
    return lax.broadcasted_iota(jnp.int32, (8, CELLS), 0)


def turn(x, shift):
    shift = shift % CELLS
    return x if shift == 0 else pltpu.roll(x, shift, 1)


def tile(b):
    return pl.ds(8 * b, 8)


class Copies:
    def __init__(self, sems):
        self.sems, self.going = sems, []

    def start(self, source, target):
        copy = pltpu.make_async_copy(source, target, self.sems.at[len(self.going)])
        copy.start()
        self.going.append(copy)

    def wait(self, first=0, last=None):
        for copy in self.going[first:last]:
            copy.wait()


def gather_edge(block, f, gathered):
    lane = lanes()
    return jnp.where(lane // 2 == f, turn(block, 2 * f + 1), gathered)


def every_second(first, count=8):
    return pl.ds(first, count, stride=2)


def ghost_columns(west, east, rows_s, cols_s, first=0):
    rows_s[every_second(2 * first + 1), :] = west
    rows_s[every_second(2 * first), :] = east
    cols_s[...] = rows_s[...].T


def around(ref, b, north, south, column, f):
    here = ref[tile(b), :]
    sub, lane = sublanes(), lanes()
    if b == 0:
        up = jnp.where(sub == 0, north, pltpu.roll(here, 1, 0))
    else:
        up = ref[8 * b - 1 : 8 * b + 7, :]
    if b == TILES - 1:
        down = jnp.where(sub == 7, south, pltpu.roll(here, 7, 0))
    else:
        down = ref[8 * b + 1 : 8 * b + 9, :]
    turned = turn(column, -2 * f - 1)
    left = jnp.where(lane == 0, turned, pltpu.roll(here, 1, 1))
    right = jnp.where(lane == CELLS - 1, turned, pltpu.roll(here, CELLS - 1, 1))
    return here, up, down, left, right


def start_kernel(
    ints, slots, flow, pressure, heat, friction,
    chunks, north, south, places, own, named, row, cols_s, rows_s, sems,
):
    copies = Copies(sems)
    copies.start(slots, named)
    copies.start(friction, own.at[10:12])
    copies.start(heat, own.at[8:10])
    copies.start(pressure, own.at[6:8])
    copies.start(flow, own.at[0:6])
    row[8:16, :] = jnp.broadcast_to((ints[RECEIVER] + 1).astype(F32), (8, CELLS))
    chunks[...] = jnp.zeros(chunks.shape, F32)
    north[...] = jnp.zeros(north.shape, F32)
    south[...] = jnp.zeros(south.shape, F32)
    copies.wait(0, 1)
    mine = jnp.broadcast_to(named[...], (8, CELLS)) == sublanes()
    place = jnp.sum(jnp.where(mine, lanes() + 1, 0).astype(F32), axis=1, keepdims=True)
    places[...] = jnp.broadcast_to(place, (8, CELLS))

    def collect(first, last):
        for b in range(TILES):
            gathered = jnp.zeros((8, CELLS), F32) if last == PLANES else cols_s[tile(b), :]
            for f in range(first, last):
                gathered = gather_edge(own[f, tile(b), :], f, gathered)
            cols_s[tile(b), :] = gathered
        for f in range(first, last):
            if f < 10:
                to = f if f < 8 else f + 1
                row[to : to + 1, :] = own[f, pl.ds(ints[ROW], 1), :]
            n, at = divmod(f, 8)
            north[n, at : at + 1, :] = own[f, 0:1, :]
            south[n, at : at + 1, :] = own[f, CELLS - 1 : CELLS, :]

    copies.wait(1, 4)
    collect(6, PLANES)
    copies.wait(4)
    collect(0, 6)
    rows_s[...] = cols_s[...].T
    chunks[ints[CHUNK]] = row[...]
    chunks[ints[TO_WEST]] = rows_s[every_second(1, 16), :]
    chunks[ints[TO_EAST]] = rows_s[every_second(0, 16), :]


def pack_kernel(table, arrived, north, south, out):
    out[:, SLOTS] = jnp.zeros((out.shape[0], 8, CELLS), F32)
    for lat in range(out.shape[0]):
        for n in range(SLOTS):
            out[lat, n] = arrived[table[2 + SLOTS * lat + n]]
    out[table[0], SLOTS] = north[0]
    out[table[1], SLOTS] = south[0]


def for_each_block(ints, sent_to, filled, lats, act):
    sources = sent_to.shape[0]
    for lat in range(lats):
        filled[lat] = 0
    for n in range(sources):
        number = sent_to[n]
        lat = jnp.maximum(number, 0) // sources

        @pl.when((number >= 0) & (number == lat * sources + ints[LON]))
        def _():
            slot = filled[lat]
            filled[lat] = slot + 1
            act(lat, slot, ints[OTHER] + n)


def table_kernel(ints, sent_to, table, filled):
    table[0] = ints[FROM_NORTH]
    table[1] = ints[FROM_SOUTH]
    for n in range(2, table.shape[0]):
        table[n] = ints[OTHER]

    def act(lat, slot, block):
        table[2 + SLOTS * lat + slot] = block

    for_each_block(ints, sent_to, filled, (table.shape[0] - 2) // SLOTS, act)


def sort_kernel(ints, sent_to, arrived, north, south, out, filled):
    lats, count = out.shape[0], out.shape[1]
    out[...] = jnp.zeros(out.shape, F32)

    def act(lat, slot, block):
        out[lat, slot] = arrived[block, 0:8, :]
        for k in range(2):
            to = pl.ds(2 * slot + k, 1)
            out[lat, count - 1, to, :] = arrived[block, 9 + k : 10 + k, :]

    for_each_block(ints, sent_to, filled, lats, act)
    for n in range(north.shape[0]):
        out[ints[FROM_NORTH], SLOTS + n] = north[n]
        out[ints[FROM_SOUTH], SLOTS + n] = south[n]


def split(x):
    high = x.astype(jnp.bfloat16)
    return high, (x - high.astype(F32)).astype(jnp.bfloat16)


def times(left, right):
    return lax.dot_general(left, right, (((1,), (1,)), ((), ())), preferred_element_type=F32)


def weights_kernel(ints, weights, high, low, chosen, sems):
    copies = Copies(sems)
    copies.start(weights.at[pl.ds(ints[LAT_BASE], 2)], chosen.at[0:2])
    copies.start(weights.at[pl.ds(ints[LON_BASE], 2)], chosen.at[2:4])
    copies.wait()
    for side in range(2):
        for term in range(2):
            cut = slice(term * CELLS, (term + 1) * CELLS)
            high[side, :, cut], low[side, :, cut] = split(chosen[2 * side + term])


def blend(blocks_of, high, low, ghosts):
    count = ghosts.shape[1]
    for n in range(2):
        block = jnp.concatenate([blocks_of(2 * n + t) for t in range(2)], axis=1)
        b_high, b_low = split(block)
        both = times(jnp.concatenate([b_high, b_low], axis=0), high[n])
        ghosts[n] = both[0:count] + both[count:] + times(b_high, low[n])


def edge_ghosts(ints, arrived, chunks, ghosts, slot, rows, of):
    halos = (
        arrived[ints[FROM_NORTH], slot],
        arrived[ints[FROM_SOUTH], slot],
        chunks[ints[TO_WEST], rows, :],
        chunks[ints[TO_EAST], rows, :],
    )
    flags = (ints[NORTH], ints[SOUTH], ints[WEST], ints[EAST])
    return [
        jnp.where(flag > 0, ghosts[n // 2, of, :], halo)
        for n, (flag, halo) in enumerate(zip(flags, halos))
    ]


def coefficients(ints, friction, heat, north, south, column, f, b, put):
    lane, sub = lanes(), sublanes()
    centre = [friction[k, tile(b), :] for k in range(2)]
    for k in range(2):
        here, up, down, left, right = around(
            friction.at[k], b, north[k], south[k], column, f + k
        )
        if b == 0:
            up = jnp.where((sub == 0) & (ints[NORTH] > 0), here, up)
        if b == TILES - 1:
            down = jnp.where((sub == 7) & (ints[SOUTH] > 0), here, down)
        left = jnp.where((lane == 0) & (ints[WEST] > 0), here, left)
        right = jnp.where((lane == CELLS - 1) & (ints[EAST] > 0), here, right)
        faces = [0.5 * (here + other) for other in (up, down, left, right)]
        between = 0.5 * (centre[0] + centre[1])
        diagonal = (faces[0] + faces[1]) + (faces[2] + faces[3]) + (between + here)
        inverse = 0.8 / diagonal
        for n, face in enumerate(faces):
            put(n, k, inverse * face)
        put(4, k, inverse * between)
        put(5, k, 0.5 * inverse)
        put(6, k, inverse * heat[k, tile(b), :])
        put(7, k, 0.125 * here)


def coefficient_kernel(ints, friction, heat, chunks, out, cols_s, rows_s):
    west, east = chunks[ints[TO_WEST], 8:16, :], chunks[ints[TO_EAST], 8:16, :]
    ghost_columns(west, east, rows_s, cols_s)
    for b in range(1, TILES - 1):

        def put(n, k, value):
            out[n, k, tile(b), :] = value

        coefficients(ints, friction, heat, (None, None), (None, None), cols_s[tile(b), :], 2, b, put)
    for b in (0, TILES - 1):
        for n in range(8):
            for k in range(2):
                out[n, k, tile(b), :] = jnp.zeros((8, CELLS), F32)


def relaxed(planes, coef, ends, ghosts, column, b):
    at = [
        around(planes(f), b, ghosts[0, f : f + 1, :], ghosts[1, f : f + 1, :], column, f)
        for f in range(8)
    ]

    def factor(n, k):
        if b == 0 or b == TILES - 1:
            return ends[n, k, tile(0 if b == 0 else 1), :]
        return coef[n, k, tile(b), :]

    new = []
    for component in range(3):
        for k in range(2):
            here, up, down, left, right = at[2 * component + k]
            value = 0.2 * here + factor(0, k) * up + factor(1, k) * down
            value = value + factor(2, k) * left + factor(3, k) * right
            value = value + factor(4, k) * at[2 * component + 1 - k][0]
            if component == 0:
                value = value + factor(6, k)
                slope = at[7][0] if k == 0 else -at[6][0]
            elif component == 1:
                slope = at[6 + k][2] - at[6 + k][1]
            else:
                slope = at[6 + k][4] - at[6 + k][3]
            new.append(value - factor(5, k) * slope)
    for k in range(2):
        divergence = (at[2 + k][2] - at[2 + k][1]) + (at[4 + k][4] - at[4 + k][3])
        divergence = divergence + at[1][0] if k == 0 else divergence - at[0][0]
        new.append(at[6 + k][0] - factor(7, k) * divergence)
    return new


def fill_ghosts(ints, arrived, chunks, high, low, sides, ghosts, cols_s, rows_s):
    count = sides.shape[1]

    def block(n):
        rows = arrived[ints[BLOCKS + n], ints[RANKS + n]]
        if count == 8:
            return rows
        warm = [
            arrived[ints[BLOCKS + n], SLOTS + 2, pl.ds(2 * ints[RANKS + n] + k, 1), :]
            for k in range(2)
        ]
        return jnp.concatenate([rows, *warm, jnp.zeros((6, CELLS), F32)], axis=0)

    blend(block, high, low, sides)
    found = edge_ghosts(ints, arrived, chunks, sides, SLOTS, slice(0, 8), slice(0, 8))
    for n in range(4):
        ghosts[n] = found[n]
    ghost_columns(found[2], found[3], rows_s, cols_s)


def first_kernel(
    ints, flow, pressure, coef, friction, heat, arrived, chunks_in, high, low,
    flow_out, pressure_out, chunks, north, south, ends, heat_ghosts,
    sides, ghosts, cols_s, rows_s, edge_s, halos,
):
    rows_s[every_second(17), :] = chunks_in[ints[TO_WEST], 8:16, :]
    rows_s[every_second(16), :] = chunks_in[ints[TO_EAST], 8:16, :]
    fill_ghosts(ints, arrived, chunks_in, high, low, sides, ghosts, cols_s, rows_s)
    found = edge_ghosts(ints, arrived, chunks_in, sides, SLOTS + 1, slice(8, 16), slice(8, 16))
    for n in range(4):
        heat_ghosts[n] = found[n]
    halos[0] = arrived[ints[FROM_NORTH], SLOTS + 1]
    halos[1] = arrived[ints[FROM_SOUTH], SLOTS + 1]
    for end, b in enumerate((0, TILES - 1)):

        def put(n, k, value):
            ends[n, k, tile(end), :] = value

        lines = [[halos[side, 2 + k : 3 + k, :] for k in range(2)] for side in range(2)]
        coefficients(ints, friction, heat, *lines, cols_s[tile(b), :], 10, b, put)
    sweep(
        ints, flow, pressure, coef, ends, ghosts, cols_s, rows_s, edge_s,
        flow_out, pressure_out, chunks, north, south,
    )


def sweep_kernel(
    ints, flow, pressure, coef, ends, arrived, chunks_in, high, low,
    flow_out, pressure_out, chunks, north, south, sides, ghosts, cols_s, rows_s, edge_s,
):
    fill_ghosts(ints, arrived, chunks_in, high, low, sides, ghosts, cols_s, rows_s)
    sweep(
        ints, flow, pressure, coef, ends, ghosts, cols_s, rows_s, edge_s,
        flow_out, pressure_out, chunks, north, south,
    )


def sweep(
    ints, flow, pressure, coef, ends, ghosts, cols_s, rows_s, edge_s,
    flow_out, pressure_out, chunks, north, south,
):
    def planes(f):
        return flow.at[f] if f < 6 else pressure.at[f - 6]

    def planes_out(f):
        return flow_out.at[f] if f < 6 else pressure_out.at[f - 6]

    chunks[...] = jnp.zeros(chunks.shape, F32)
    for b in range(TILES):
        new = relaxed(planes, coef, ends, ghosts, cols_s[tile(b), :], b)
        for f in range(8):
            planes_out(f)[tile(b), :] = new[f]
    for b in range(TILES):
        gathered = jnp.zeros((8, CELLS), F32)
        for f in range(8):
            gathered = gather_edge(planes_out(f)[tile(b), :], f, gathered)
        edge_s[tile(b), :] = gathered
    for f in range(8):
        north[0, f : f + 1, :] = planes_out(f)[0:1, :]
        south[0, f : f + 1, :] = planes_out(f)[CELLS - 1 : CELLS, :]
    rows_s[...] = edge_s[...].T
    chunks[ints[TO_WEST]] = rows_s[every_second(1), :]
    chunks[ints[TO_EAST]] = rows_s[every_second(0), :]
    for f in range(8):
        edge_s[f : f + 1, :] = planes_out(f)[pl.ds(ints[ROW], 1), :]
    chunks[ints[CHUNK]] = edge_s[0:8, :]


def final_kernel(
    ints, flow, pressure, coef, ends, arrived, chunks_in, high, low, heat, heat_ghosts,
    flow_out, pressure_out, heat_out,
    sides, ghosts, cols_s, rows_s, heat_cols_s, answer, warm, sems,
):
    def planes(f):
        return flow.at[f] if f < 6 else pressure.at[f - 6]

    ghost_columns(heat_ghosts[2], heat_ghosts[3], rows_s, heat_cols_s)
    fill_ghosts(ints, arrived, chunks_in, high, low, sides, ghosts, cols_s, rows_s)
    for b in range(TILES):
        new = relaxed(planes, coef, ends, ghosts, cols_s[tile(b), :], b)
        for f in range(8):
            answer[f, tile(b), :] = new[f]
    copies = Copies(sems)
    copies.start(answer.at[0:6], flow_out)
    copies.start(answer.at[6:8], pressure_out)
    for b in range(TILES):
        layers = [
            around(
                heat.at[k],
                b,
                heat_ghosts[0, k : k + 1, :],
                heat_ghosts[1, k : k + 1, :],
                heat_cols_s[tile(b), :],
                k,
            )
            for k in range(2)
        ]
        for k in range(2):
            here, up, down, left, right = layers[k]
            under = jnp.ones((8, CELLS), F32) if k == 0 else layers[0][0]
            over = layers[1][0] if k == 0 else jnp.zeros((8, CELLS), F32)
            advect = jnp.zeros((8, CELLS), F32)
            for component, minus, plus in ((0, under, over), (1, up, down), (2, left, right)):
                speed = answer[2 * component + k, tile(b), :]
                advect = advect + jnp.maximum(speed, 0.0) * (here - minus)
                advect = advect + jnp.minimum(speed, 0.0) * (plus - here)
            spread = (up + down) + (left + right) + (under + over) - 6.0 * here
            warm[k, tile(b), :] = here + 0.1 * (spread - advect)
    copies.start(warm, heat_out)
    copies.wait()


def shape(*dims):
    return jax.ShapeDtypeStruct(dims, F32)


def scratch(*dims):
    return pltpu.VMEM(dims, F32)


def semaphores(count):
    return pltpu.SemaphoreType.DMA((count,))


def call(
    kernel, outs, ins, scratches, name, specs=None, out_specs=None, limit=4, keep=(), pin=()
):
    out_specs = out_specs or [VMEM] * len(outs)
    specs = specs or [SMEM] + [VMEM] * (len(ins) - 1)
    placed = []
    for n, (x, spec) in enumerate(zip(ins, specs)):
        if spec is HBM or n in keep:
            x = pltpu.with_memory_space_constraint(x, spec.memory_space)
        placed.append(x)
    outs = [
        pltpu.HBM(x.shape, x.dtype)
        if spec is HBM
        else pltpu.VMEM(x.shape, x.dtype)
        if n in pin
        else x
        for n, (x, spec) in enumerate(zip(outs, out_specs))
    ]
    return pl.pallas_call(
        kernel,
        out_shape=outs,
        in_specs=specs,
        out_specs=out_specs,
        scratch_shapes=scratches,
        compiler_params=pltpu.CompilerParams(vmem_limit_bytes=limit * 1024 * 1024),
        name=name,
    )(*placed)


def shards(
    flow_vector,
    normal_stress,
    thermal_field,
    shear_resistance,
    departing_bands,
    receiving_processor,
    shift_filled_by_lane,
    blending_factors,
):
    flow = flow_vector.reshape(6, CELLS, CELLS)
    pressure = normal_stress[0]
    heat = thermal_field[0]
    friction = shear_resistance[0]
    weights = blending_factors.reshape(8, CELLS, CELLS)
    lat, lon = lax.axis_index("lat"), lax.axis_index("lon")
    n_lat, n_lon = lax.axis_size("lat"), lax.axis_size("lon")
    patch = lax.axis_index("patch")
    own_row = departing_bands.reshape(1)
    receiver = receiving_processor.reshape(1)
    other = (1 - patch) * n_lon

    chunk = other + jnp.maximum(receiver, 0) % n_lon
    beside = jnp.stack([jnp.maximum(lon - 1, 0), jnp.minimum(lon + 1, n_lon - 1)])
    beside = (beside + patch * n_lon).astype(jnp.int32)
    beyond = jnp.stack([jnp.maximum(lat - 1, 0), jnp.minimum(lat + 1, n_lat - 1)])
    beyond = beyond.astype(jnp.int32)
    on_edge = jnp.stack([lat == 0, lat == n_lat - 1, lon == 0, lon == n_lon - 1]).astype(jnp.int32)
    bases = jnp.stack([jnp.where(lat > 0, 2, 0), jnp.where(lon > 0, 6, 4)]).astype(jnp.int32)
    here = jnp.stack([other, lon]).astype(jnp.int32)
    first = jnp.concatenate([own_row, on_edge, bases, chunk, beside, beyond, here, receiver])

    square = scratch(CELLS, CELLS)
    tiles = 2 * n_lon
    chunks, north, south, places = call(
        start_kernel,
        [shape(tiles, 16, CELLS), shape(2, 8, CELLS), shape(2, 8, CELLS), shape(8, CELLS)],
        (first, shift_filled_by_lane.reshape(1, CELLS), flow, pressure, heat, friction),
        [scratch(PLANES, CELLS, CELLS), pltpu.VMEM((1, CELLS), jnp.int32), scratch(16, CELLS)]
        + [square, square, semaphores(5)],
        "start",
        specs=[SMEM] + [HBM] * 5,
        pin=(0,),
    )

    def across(chunks):
        return lax.all_to_all(chunks, ("patch", "lon"), 0, 0, tiled=True)

    def along(packed):
        return lax.all_to_all(packed, "lat", 0, 0, tiled=True)

    came, places, lon, lat, other = lax.optimization_barrier(
        (across(chunks), places, lon, lat, other)
    )
    sent_to = lax.dynamic_slice(came, (other, 8, 0), (n_lon, 1, 1)).reshape(n_lon)
    sent_to = sent_to.astype(jnp.int32) - 1
    (packed,) = call(
        sort_kernel,
        [shape(n_lat, SLOTS + 3, 8, CELLS)],
        (first, sent_to, came, north, south),
        [pltpu.SMEM((n_lat,), jnp.int32)],
        "sort",
        specs=[SMEM, SMEM, VMEM, VMEM, VMEM],
        keep=(2,),
        pin=(0,),
    )
    packed, places = lax.optimization_barrier((packed, places))
    arrived = along(packed)

    (table,) = call(
        table_kernel,
        [jax.ShapeDtypeStruct((2 + n_lat * SLOTS,), jnp.int32)],
        lax.optimization_barrier((first, sent_to, packed))[:2],
        [pltpu.SMEM((n_lat,), jnp.int32)],
        "table",
        specs=[SMEM, SMEM],
        out_specs=[SMEM],
    )
    arrived, table = lax.optimization_barrier((arrived, table))

    own = places[:, 0].astype(jnp.int32) - 1
    pick = jnp.concatenate(
        [jnp.where(lat > 0, own[2:4], own[0:2]), jnp.where(lon > 0, own[6:8], own[4:6])]
    )
    same = (own >= 0)[None] & (own[None] // n_lon == pick[:, None] // n_lon)
    slot = jnp.sum((same & (own[None] < pick[:, None])).astype(jnp.int32), axis=1)
    ints = [first, jnp.maximum(pick, 0) // n_lon, jnp.minimum(slot, SLOTS - 1)]
    ints = jnp.concatenate(ints).astype(jnp.int32)

    joined = jax.ShapeDtypeStruct((2, CELLS, 2 * CELLS), jnp.bfloat16)
    high, low = call(
        weights_kernel,
        [joined, joined],
        (ints, weights),
        [scratch(4, CELLS, CELLS), semaphores(2)],
        "weights",
        specs=[SMEM, HBM],
    )
    (coef,) = call(
        coefficient_kernel,
        [shape(8, 2, CELLS, CELLS)],
        (ints, friction, heat, came),
        [square, square],
        "coefficients",
        keep=(3,),
    )
    sides, ghosts = scratch(2, 8, CELLS), scratch(4, 8, CELLS)
    state = [shape(6, CELLS, CELLS), shape(2, CELLS, CELLS)]
    for sweep in range(SWEEPS - 1):
        outs = state + [shape(tiles, 8, CELLS), shape(1, 8, CELLS), shape(1, 8, CELLS)]
        if sweep == 0:
            flow, pressure, chunks, north, south, ends, heat_ghosts = call(
                first_kernel,
                outs + [shape(8, 2, 16, CELLS), shape(4, 8, CELLS)],
                (ints, flow, pressure, coef, friction, heat, arrived, came, high, low),
                [scratch(2, 16, CELLS), ghosts, square, square, square, scratch(2, 8, CELLS)],
                "first_sweep",
                limit=8,
                keep=(3, 6, 7, 8, 9),
                pin=(2,),
            )
        else:
            flow, pressure, chunks, north, south = call(
                sweep_kernel,
                outs,
                (ints, flow, pressure, coef, ends, arrived, came, high, low),
                [sides, ghosts, square, square, square],
                "sweep",
                limit=8,
                keep=(3, 4, 5, 6, 7, 8),
                pin=(2,),
            )
        came = across(chunks)
        (packed,) = call(
            pack_kernel,
            [shape(n_lat, SLOTS + 1, 8, CELLS)],
            (table, came, north, south),
            [],
            "pack",
            keep=(1,),
            pin=(0,),
        )
        arrived = along(packed)
    flow, pressure, heat = call(
        final_kernel,
        state + [shape(2, CELLS, CELLS)],
        (ints, flow, pressure, coef, ends, arrived, came, high, low, heat, heat_ghosts),
        [sides, ghosts, square, square, square]
        + [scratch(8, CELLS, CELLS), scratch(2, CELLS, CELLS), semaphores(3)],
        "final",
        out_specs=[HBM] * 3,
        limit=8,
        keep=(1, 2, 3, 4, 5, 6, 7, 8),
    )
    return flow.reshape(3, 1, 2, CELLS, CELLS), pressure[None], heat[None]


def solution(mesh):
    placed = (
        P(None, "patch", None, "lat", "lon"),
        P("patch", None, "lat", "lon"),
        P("patch", None, "lat", "lon"),
        P("patch", None, "lat", "lon"),
        P("patch", "lat", "lon", None),
        P("patch", "lat", "lon", None),
        P("patch", "lat", "lon", None),
        P("patch", "lat", "lon", None, None, None),
    )
    return jax.shard_map(
        shards,
        mesh=mesh,
        in_specs=placed,
        out_specs=(
            P(None, "patch", None, "lat", "lon"),
            P("patch", None, "lat", "lon"),
            P("patch", None, "lat", "lon"),
        ),
        check_vma=False,
    )
```

```python
import jax
import jax.numpy as jnp
from jax import lax
from jax.experimental import pallas as pl
from jax.experimental.pallas import tpu as pltpu
from jax.sharding import PartitionSpec as P

SWEEPS = 4
CELLS = 128
TILES = 16
PLANES = 12
SLOTS = 4
F32 = jnp.float32
VMEM = pl.BlockSpec(memory_space=pltpu.VMEM)
SMEM = pl.BlockSpec(memory_space=pltpu.SMEM)
HBM = pl.BlockSpec(memory_space=pltpu.HBM)
ROW, NORTH, SOUTH, WEST, EAST, LAT_BASE, LON_BASE = range(7)
CHUNK, TO_WEST, TO_EAST = 7, 8, 9
FROM_NORTH, FROM_SOUTH = 10, 11
OTHER, LON, RECEIVER = 12, 13, 14
BLOCKS, RANKS = 15, 19


def lanes():
    return lax.broadcasted_iota(jnp.int32, (8, CELLS), 1)


def sublanes():
    return lax.broadcasted_iota(jnp.int32, (8, CELLS), 0)


def turn(x, shift):
    shift = shift % CELLS
    return x if shift == 0 else pltpu.roll(x, shift, 1)


def tile(b):
    return pl.ds(8 * b, 8)


class Copies:
    def __init__(self, sems):
        self.sems, self.going = sems, []

    def start(self, source, target):
        copy = pltpu.make_async_copy(source, target, self.sems.at[len(self.going)])
        copy.start()
        self.going.append(copy)

    def wait(self, first=0, last=None):
        for copy in self.going[first:last]:
            copy.wait()


def gather_edge(block, f, gathered):
    lane = lanes()
    return jnp.where(lane // 2 == f, turn(block, 2 * f + 1), gathered)


def every_second(first, count=8):
    return pl.ds(first, count, stride=2)


def ghost_columns(west, east, rows_s, cols_s, first=0):
    rows_s[every_second(2 * first + 1), :] = west
    rows_s[every_second(2 * first), :] = east
    cols_s[...] = rows_s[...].T


def around(ref, b, north, south, column, f):
    here = ref[tile(b), :]
    sub, lane = sublanes(), lanes()
    if b == 0:
        up = jnp.where(sub == 0, north, pltpu.roll(here, 1, 0))
    else:
        up = ref[8 * b - 1 : 8 * b + 7, :]
    if b == TILES - 1:
        down = jnp.where(sub == 7, south, pltpu.roll(here, 7, 0))
    else:
        down = ref[8 * b + 1 : 8 * b + 9, :]
    turned = turn(column, -2 * f - 1)
    left = jnp.where(lane == 0, turned, pltpu.roll(here, 1, 1))
    right = jnp.where(lane == CELLS - 1, turned, pltpu.roll(here, CELLS - 1, 1))
    return here, up, down, left, right


def start_kernel(
    ints, slots, flow, pressure, heat, friction,
    chunks, north, south, places, own, named, row, cols_s, rows_s, sems,
):
    copies = Copies(sems)
    copies.start(slots, named)
    for n, source in ((10, friction), (8, heat), (6, pressure)):
        for k in range(2):
            copies.start(source.at[k], own.at[n + k])
    for n in range(6):
        copies.start(flow.at[n], own.at[n])
    row[8:16, :] = jnp.broadcast_to((ints[RECEIVER] + 1).astype(F32), (8, CELLS))
    chunks[...] = jnp.zeros(chunks.shape, F32)
    north[...] = jnp.zeros(north.shape, F32)
    south[...] = jnp.zeros(south.shape, F32)
    copies.wait(0, 1)
    mine = jnp.broadcast_to(named[...], (8, CELLS)) == sublanes()
    place = jnp.sum(jnp.where(mine, lanes() + 1, 0).astype(F32), axis=1, keepdims=True)
    places[...] = jnp.broadcast_to(place, (8, CELLS))

    def collect(first, last):
        for b in range(TILES):
            gathered = jnp.zeros((8, CELLS), F32) if last == PLANES else cols_s[tile(b), :]
            for f in range(first, last):
                gathered = gather_edge(own[f, tile(b), :], f, gathered)
            cols_s[tile(b), :] = gathered
        for f in range(first, last):
            if f < 10:
                to = f if f < 8 else f + 1
                row[to : to + 1, :] = own[f, pl.ds(ints[ROW], 1), :]
            n, at = divmod(f, 8)
            north[n, at : at + 1, :] = own[f, 0:1, :]
            south[n, at : at + 1, :] = own[f, CELLS - 1 : CELLS, :]

    copies.wait(1, 7)
    collect(6, PLANES)
    copies.wait(7)
    collect(0, 6)
    rows_s[...] = cols_s[...].T
    chunks[ints[CHUNK]] = row[...]
    chunks[ints[TO_WEST]] = rows_s[every_second(1, 16), :]
    chunks[ints[TO_EAST]] = rows_s[every_second(0, 16), :]


def pack_kernel(table, arrived, north, south, out):
    out[:, SLOTS] = jnp.zeros((out.shape[0], 8, CELLS), F32)
    for lat in range(out.shape[0]):
        for n in range(SLOTS):
            out[lat, n] = arrived[table[2 + SLOTS * lat + n]]
    out[table[0], SLOTS] = north[0]
    out[table[1], SLOTS] = south[0]


def for_each_block(ints, sent_to, filled, lats, act):
    sources = sent_to.shape[0]
    for lat in range(lats):
        filled[lat] = 0
    for n in range(sources):
        number = sent_to[n]
        lat = jnp.maximum(number, 0) // sources

        @pl.when((number >= 0) & (number == lat * sources + ints[LON]))
        def _():
            slot = filled[lat]
            filled[lat] = slot + 1
            act(lat, slot, ints[OTHER] + n)


def table_kernel(ints, sent_to, table, filled):
    table[0] = ints[FROM_NORTH]
    table[1] = ints[FROM_SOUTH]
    for n in range(2, table.shape[0]):
        table[n] = ints[OTHER]

    def act(lat, slot, block):
        table[2 + SLOTS * lat + slot] = block

    for_each_block(ints, sent_to, filled, (table.shape[0] - 2) // SLOTS, act)


def sort_kernel(ints, sent_to, arrived, north, south, out, filled):
    lats, count = out.shape[0], out.shape[1]
    out[...] = jnp.zeros(out.shape, F32)

    def act(lat, slot, block):
        out[lat, slot] = arrived[block, 0:8, :]
        for k in range(2):
            to = pl.ds(2 * slot + k, 1)
            out[lat, count - 1, to, :] = arrived[block, 9 + k : 10 + k, :]

    for_each_block(ints, sent_to, filled, lats, act)
    for n in range(north.shape[0]):
        out[ints[FROM_NORTH], SLOTS + n] = north[n]
        out[ints[FROM_SOUTH], SLOTS + n] = south[n]


def split(x):
    high = x.astype(jnp.bfloat16)
    return high, (x - high.astype(F32)).astype(jnp.bfloat16)


def times(left, right):
    return lax.dot_general(left, right, (((1,), (1,)), ((), ())), preferred_element_type=F32)


def weights_kernel(ints, weights, high, low, chosen, sems):
    copies = Copies(sems)
    copies.start(weights.at[pl.ds(ints[LAT_BASE], 2)], chosen.at[0:2])
    copies.start(weights.at[pl.ds(ints[LON_BASE], 2)], chosen.at[2:4])
    copies.wait()
    for side in range(2):
        for term in range(2):
            cut = slice(term * CELLS, (term + 1) * CELLS)
            high[side, :, cut], low[side, :, cut] = split(chosen[2 * side + term])


def blend(blocks_of, high, low, ghosts):
    count = ghosts.shape[1]
    for n in range(2):
        block = jnp.concatenate([blocks_of(2 * n + t) for t in range(2)], axis=1)
        b_high, b_low = split(block)
        both = times(jnp.concatenate([b_high, b_low], axis=0), high[n])
        ghosts[n] = both[0:count] + both[count:] + times(b_high, low[n])


def edge_ghosts(ints, arrived, chunks, ghosts, slot, rows, of):
    halos = (
        arrived[ints[FROM_NORTH], slot],
        arrived[ints[FROM_SOUTH], slot],
        chunks[ints[TO_WEST], rows, :],
        chunks[ints[TO_EAST], rows, :],
    )
    flags = (ints[NORTH], ints[SOUTH], ints[WEST], ints[EAST])
    return [
        jnp.where(flag > 0, ghosts[n // 2, of, :], halo)
        for n, (flag, halo) in enumerate(zip(flags, halos))
    ]


def coefficients(ints, friction, heat, north, south, column, f, b, put):
    lane, sub = lanes(), sublanes()
    centre = [friction[k, tile(b), :] for k in range(2)]
    for k in range(2):
        here, up, down, left, right = around(
            friction.at[k], b, north[k], south[k], column, f + k
        )
        if b == 0:
            up = jnp.where((sub == 0) & (ints[NORTH] > 0), here, up)
        if b == TILES - 1:
            down = jnp.where((sub == 7) & (ints[SOUTH] > 0), here, down)
        left = jnp.where((lane == 0) & (ints[WEST] > 0), here, left)
        right = jnp.where((lane == CELLS - 1) & (ints[EAST] > 0), here, right)
        faces = [0.5 * (here + other) for other in (up, down, left, right)]
        between = 0.5 * (centre[0] + centre[1])
        diagonal = (faces[0] + faces[1]) + (faces[2] + faces[3]) + (between + here)
        inverse = 0.8 / diagonal
        for n, face in enumerate(faces):
            put(n, k, inverse * face)
        put(4, k, inverse * between)
        put(5, k, 0.5 * inverse)
        put(6, k, inverse * heat[k, tile(b), :])
        put(7, k, 0.125 * here)


def coefficient_kernel(ints, friction, heat, chunks, out, cols_s, rows_s):
    west, east = chunks[ints[TO_WEST], 8:16, :], chunks[ints[TO_EAST], 8:16, :]
    ghost_columns(west, east, rows_s, cols_s)
    for b in range(1, TILES - 1):

        def put(n, k, value):
            out[n, k, tile(b), :] = value

        coefficients(ints, friction, heat, (None, None), (None, None), cols_s[tile(b), :], 2, b, put)
    for b in (0, TILES - 1):
        for n in range(8):
            for k in range(2):
                out[n, k, tile(b), :] = jnp.zeros((8, CELLS), F32)


def relaxed(planes, coef, ends, ghosts, column, b):
    at = [
        around(planes(f), b, ghosts[0, f : f + 1, :], ghosts[1, f : f + 1, :], column, f)
        for f in range(8)
    ]

    def factor(n, k):
        if b == 0 or b == TILES - 1:
            return ends[n, k, tile(0 if b == 0 else 1), :]
        return coef[n, k, tile(b), :]

    new = []
    for component in range(3):
        for k in range(2):
            here, up, down, left, right = at[2 * component + k]
            value = 0.2 * here + factor(0, k) * up + factor(1, k) * down
            value = value + factor(2, k) * left + factor(3, k) * right
            value = value + factor(4, k) * at[2 * component + 1 - k][0]
            if component == 0:
                value = value + factor(6, k)
                slope = at[7][0] if k == 0 else -at[6][0]
            elif component == 1:
                slope = at[6 + k][2] - at[6 + k][1]
            else:
                slope = at[6 + k][4] - at[6 + k][3]
            new.append(value - factor(5, k) * slope)
    for k in range(2):
        divergence = (at[2 + k][2] - at[2 + k][1]) + (at[4 + k][4] - at[4 + k][3])
        divergence = divergence + at[1][0] if k == 0 else divergence - at[0][0]
        new.append(at[6 + k][0] - factor(7, k) * divergence)
    return new


def fill_ghosts(ints, arrived, chunks, high, low, sides, ghosts, cols_s, rows_s):
    count = sides.shape[1]

    def block(n):
        rows = arrived[ints[BLOCKS + n], ints[RANKS + n]]
        if count == 8:
            return rows
        warm = [
            arrived[ints[BLOCKS + n], SLOTS + 2, pl.ds(2 * ints[RANKS + n] + k, 1), :]
            for k in range(2)
        ]
        return jnp.concatenate([rows, *warm, jnp.zeros((6, CELLS), F32)], axis=0)

    blend(block, high, low, sides)
    found = edge_ghosts(ints, arrived, chunks, sides, SLOTS, slice(0, 8), slice(0, 8))
    for n in range(4):
        ghosts[n] = found[n]
    ghost_columns(found[2], found[3], rows_s, cols_s)


def first_kernel(
    ints, flow, pressure, coef, friction, heat, arrived, chunks_in, high, low,
    flow_out, pressure_out, chunks, north, south, ends, heat_ghosts,
    sides, ghosts, cols_s, rows_s, edge_s, halos,
):
    rows_s[every_second(17), :] = chunks_in[ints[TO_WEST], 8:16, :]
    rows_s[every_second(16), :] = chunks_in[ints[TO_EAST], 8:16, :]
    fill_ghosts(ints, arrived, chunks_in, high, low, sides, ghosts, cols_s, rows_s)
    found = edge_ghosts(ints, arrived, chunks_in, sides, SLOTS + 1, slice(8, 16), slice(8, 16))
    for n in range(4):
        heat_ghosts[n] = found[n]
    halos[0] = arrived[ints[FROM_NORTH], SLOTS + 1]
    halos[1] = arrived[ints[FROM_SOUTH], SLOTS + 1]
    for end, b in enumerate((0, TILES - 1)):

        def put(n, k, value):
            ends[n, k, tile(end), :] = value

        lines = [[halos[side, 2 + k : 3 + k, :] for k in range(2)] for side in range(2)]
        coefficients(ints, friction, heat, *lines, cols_s[tile(b), :], 10, b, put)
    sweep(
        ints, flow, pressure, coef, ends, ghosts, cols_s, rows_s, edge_s,
        flow_out, pressure_out, chunks, north, south,
    )


def sweep_kernel(
    ints, flow, pressure, coef, ends, arrived, chunks_in, high, low,
    flow_out, pressure_out, chunks, north, south, sides, ghosts, cols_s, rows_s, edge_s,
):
    fill_ghosts(ints, arrived, chunks_in, high, low, sides, ghosts, cols_s, rows_s)
    sweep(
        ints, flow, pressure, coef, ends, ghosts, cols_s, rows_s, edge_s,
        flow_out, pressure_out, chunks, north, south,
    )


def sweep(
    ints, flow, pressure, coef, ends, ghosts, cols_s, rows_s, edge_s,
    flow_out, pressure_out, chunks, north, south,
):
    def planes(f):
        return flow.at[f] if f < 6 else pressure.at[f - 6]

    def planes_out(f):
        return flow_out.at[f] if f < 6 else pressure_out.at[f - 6]

    chunks[...] = jnp.zeros(chunks.shape, F32)
    for b in range(TILES):
        new = relaxed(planes, coef, ends, ghosts, cols_s[tile(b), :], b)
        for f in range(8):
            planes_out(f)[tile(b), :] = new[f]
    for b in range(TILES):
        gathered = jnp.zeros((8, CELLS), F32)
        for f in range(8):
            gathered = gather_edge(planes_out(f)[tile(b), :], f, gathered)
        edge_s[tile(b), :] = gathered
    for f in range(8):
        north[0, f : f + 1, :] = planes_out(f)[0:1, :]
        south[0, f : f + 1, :] = planes_out(f)[CELLS - 1 : CELLS, :]
    rows_s[...] = edge_s[...].T
    chunks[ints[TO_WEST]] = rows_s[every_second(1), :]
    chunks[ints[TO_EAST]] = rows_s[every_second(0), :]
    for f in range(8):
        edge_s[f : f + 1, :] = planes_out(f)[pl.ds(ints[ROW], 1), :]
    chunks[ints[CHUNK]] = edge_s[0:8, :]


def final_kernel(
    ints, flow, pressure, coef, ends, arrived, chunks_in, high, low, heat, heat_ghosts,
    flow_out, pressure_out, heat_out,
    sides, ghosts, cols_s, rows_s, heat_cols_s, answer, warm, sems,
):
    def planes(f):
        return flow.at[f] if f < 6 else pressure.at[f - 6]

    ghost_columns(heat_ghosts[2], heat_ghosts[3], rows_s, heat_cols_s)
    fill_ghosts(ints, arrived, chunks_in, high, low, sides, ghosts, cols_s, rows_s)
    copies = Copies(sems)
    for b in range(TILES):
        new = relaxed(planes, coef, ends, ghosts, cols_s[tile(b), :], b)
        for f in range(8):
            answer[f, tile(b), :] = new[f]
        if b % 4 == 3:
            part = pl.ds(8 * (b - 3), 32)
            copies.start(answer.at[0:6, part, :], flow_out.at[:, part, :])
            copies.start(answer.at[6:8, part, :], pressure_out.at[:, part, :])
    for b in range(TILES):
        layers = [
            around(
                heat.at[k],
                b,
                heat_ghosts[0, k : k + 1, :],
                heat_ghosts[1, k : k + 1, :],
                heat_cols_s[tile(b), :],
                k,
            )
            for k in range(2)
        ]
        for k in range(2):
            here, up, down, left, right = layers[k]
            under = jnp.ones((8, CELLS), F32) if k == 0 else layers[0][0]
            over = layers[1][0] if k == 0 else jnp.zeros((8, CELLS), F32)
            advect = jnp.zeros((8, CELLS), F32)
            for component, minus, plus in ((0, under, over), (1, up, down), (2, left, right)):
                speed = answer[2 * component + k, tile(b), :]
                advect = advect + jnp.maximum(speed, 0.0) * (here - minus)
                advect = advect + jnp.minimum(speed, 0.0) * (plus - here)
            spread = (up + down) + (left + right) + (under + over) - 6.0 * here
            warm[k, tile(b), :] = here + 0.1 * (spread - advect)
        if b % 8 == 7:
            part = pl.ds(8 * (b - 7), 64)
            copies.start(warm.at[:, part, :], heat_out.at[:, part, :])
    copies.wait()


def shape(*dims):
    return jax.ShapeDtypeStruct(dims, F32)


def scratch(*dims):
    return pltpu.VMEM(dims, F32)


def semaphores(count):
    return pltpu.SemaphoreType.DMA((count,))


def call(
    kernel, outs, ins, scratches, name, specs=None, out_specs=None, limit=4, keep=(), pin=()
):
    out_specs = out_specs or [VMEM] * len(outs)
    specs = specs or [SMEM] + [VMEM] * (len(ins) - 1)
    placed = []
    for n, (x, spec) in enumerate(zip(ins, specs)):
        if spec is HBM or n in keep:
            x = pltpu.with_memory_space_constraint(x, spec.memory_space)
        placed.append(x)
    outs = [
        pltpu.HBM(x.shape, x.dtype)
        if spec is HBM
        else pltpu.VMEM(x.shape, x.dtype)
        if n in pin
        else x
        for n, (x, spec) in enumerate(zip(outs, out_specs))
    ]
    return pl.pallas_call(
        kernel,
        out_shape=outs,
        in_specs=specs,
        out_specs=out_specs,
        scratch_shapes=scratches,
        compiler_params=pltpu.CompilerParams(vmem_limit_bytes=limit * 1024 * 1024),
        name=name,
    )(*placed)


def shards(
    flow_vector,
    normal_stress,
    thermal_field,
    shear_resistance,
    departing_bands,
    receiving_processor,
    shift_filled_by_lane,
    blending_factors,
):
    flow = flow_vector.reshape(6, CELLS, CELLS)
    pressure = normal_stress[0]
    heat = thermal_field[0]
    friction = shear_resistance[0]
    weights = blending_factors.reshape(8, CELLS, CELLS)
    lat, lon = lax.axis_index("lat"), lax.axis_index("lon")
    n_lat, n_lon = lax.axis_size("lat"), lax.axis_size("lon")
    patch = lax.axis_index("patch")
    own_row = departing_bands.reshape(1)
    receiver = receiving_processor.reshape(1)
    other = (1 - patch) * n_lon

    chunk = other + jnp.maximum(receiver, 0) % n_lon
    beside = jnp.stack([jnp.maximum(lon - 1, 0), jnp.minimum(lon + 1, n_lon - 1)])
    beside = (beside + patch * n_lon).astype(jnp.int32)
    beyond = jnp.stack([jnp.maximum(lat - 1, 0), jnp.minimum(lat + 1, n_lat - 1)])
    beyond = beyond.astype(jnp.int32)
    on_edge = jnp.stack([lat == 0, lat == n_lat - 1, lon == 0, lon == n_lon - 1]).astype(jnp.int32)
    bases = jnp.stack([jnp.where(lat > 0, 2, 0), jnp.where(lon > 0, 6, 4)]).astype(jnp.int32)
    here = jnp.stack([other, lon]).astype(jnp.int32)
    first = jnp.concatenate([own_row, on_edge, bases, chunk, beside, beyond, here, receiver])

    square = scratch(CELLS, CELLS)
    tiles = 2 * n_lon
    chunks, north, south, places = call(
        start_kernel,
        [shape(tiles, 16, CELLS), shape(2, 8, CELLS), shape(2, 8, CELLS), shape(8, CELLS)],
        (first, shift_filled_by_lane.reshape(1, CELLS), flow, pressure, heat, friction),
        [scratch(PLANES, CELLS, CELLS), pltpu.VMEM((1, CELLS), jnp.int32), scratch(16, CELLS)]
        + [square, square, semaphores(13)],
        "start",
        specs=[SMEM] + [HBM] * 5,
        pin=(0,),
    )

    def across(chunks):
        return lax.all_to_all(chunks, ("patch", "lon"), 0, 0, tiled=True)

    def along(packed):
        return lax.all_to_all(packed, "lat", 0, 0, tiled=True)

    came, places, lon, lat, other = lax.optimization_barrier(
        (across(chunks), places, lon, lat, other)
    )
    sent_to = lax.dynamic_slice(came, (other, 8, 0), (n_lon, 1, 1)).reshape(n_lon)
    sent_to = sent_to.astype(jnp.int32) - 1
    (packed,) = call(
        sort_kernel,
        [shape(n_lat, SLOTS + 3, 8, CELLS)],
        (first, sent_to, came, north, south),
        [pltpu.SMEM((n_lat,), jnp.int32)],
        "sort",
        specs=[SMEM, SMEM, VMEM, VMEM, VMEM],
        keep=(2,),
        pin=(0,),
    )
    arrived = along(packed)

    (table,) = call(
        table_kernel,
        [jax.ShapeDtypeStruct((2 + n_lat * SLOTS,), jnp.int32)],
        lax.optimization_barrier((first, sent_to, packed))[:2],
        [pltpu.SMEM((n_lat,), jnp.int32)],
        "table",
        specs=[SMEM, SMEM],
        out_specs=[SMEM],
    )
    table, places = lax.optimization_barrier((table, places))
    own = places[:, 0].astype(jnp.int32) - 1
    pick = jnp.concatenate(
        [jnp.where(lat > 0, own[2:4], own[0:2]), jnp.where(lon > 0, own[6:8], own[4:6])]
    )
    same = (own >= 0)[None] & (own[None] // n_lon == pick[:, None] // n_lon)
    slot = jnp.sum((same & (own[None] < pick[:, None])).astype(jnp.int32), axis=1)
    ints = [first, jnp.maximum(pick, 0) // n_lon, jnp.minimum(slot, SLOTS - 1)]
    ints = jnp.concatenate(ints).astype(jnp.int32)
    arrived, table, ints = lax.optimization_barrier((arrived, table, ints))

    joined = jax.ShapeDtypeStruct((2, CELLS, 2 * CELLS), jnp.bfloat16)
    high, low = call(
        weights_kernel,
        [joined, joined],
        (ints, weights),
        [scratch(4, CELLS, CELLS), semaphores(2)],
        "weights",
        specs=[SMEM, HBM],
    )
    (coef,) = call(
        coefficient_kernel,
        [shape(8, 2, CELLS, CELLS)],
        (ints, friction, heat, came),
        [square, square],
        "coefficients",
        keep=(3,),
    )
    sides, ghosts = scratch(2, 8, CELLS), scratch(4, 8, CELLS)
    state = [shape(6, CELLS, CELLS), shape(2, CELLS, CELLS)]
    for sweep in range(SWEEPS - 1):
        outs = state + [shape(tiles, 8, CELLS), shape(1, 8, CELLS), shape(1, 8, CELLS)]
        if sweep == 0:
            flow, pressure, chunks, north, south, ends, heat_ghosts = call(
                first_kernel,
                outs + [shape(8, 2, 16, CELLS), shape(4, 8, CELLS)],
                (ints, flow, pressure, coef, friction, heat, arrived, came, high, low),
                [scratch(2, 16, CELLS), ghosts, square, square, square, scratch(2, 8, CELLS)],
                "first_sweep",
                limit=8,
                keep=(3, 6, 7, 8, 9),
                pin=(2,),
            )
        else:
            flow, pressure, chunks, north, south = call(
                sweep_kernel,
                outs,
                (ints, flow, pressure, coef, ends, arrived, came, high, low),
                [sides, ghosts, square, square, square],
                "sweep",
                limit=8,
                keep=(3, 4, 5, 6, 7, 8),
                pin=(2,),
            )
        came = across(chunks)
        (packed,) = call(
            pack_kernel,
            [shape(n_lat, SLOTS + 1, 8, CELLS)],
            (table, came, north, south),
            [],
            "pack",
            keep=(1,),
            pin=(0,),
        )
        arrived = along(packed)
    flow, pressure, heat = call(
        final_kernel,
        state + [shape(2, CELLS, CELLS)],
        (ints, flow, pressure, coef, ends, arrived, came, high, low, heat, heat_ghosts),
        [sides, ghosts, square, square, square]
        + [scratch(8, CELLS, CELLS), scratch(2, CELLS, CELLS), semaphores(10)],
        "final",
        out_specs=[HBM] * 3,
        limit=8,
        keep=(1, 2, 3, 4, 5, 6, 7, 8),
    )
    return flow.reshape(3, 1, 2, CELLS, CELLS), pressure[None], heat[None]


def solution(mesh):
    placed = (
        P(None, "patch", None, "lat", "lon"),
        P("patch", None, "lat", "lon"),
        P("patch", None, "lat", "lon"),
        P("patch", None, "lat", "lon"),
        P("patch", "lat", "lon", None),
        P("patch", "lat", "lon", None),
        P("patch", "lat", "lon", None),
        P("patch", "lat", "lon", None, None, None),
    )
    return jax.shard_map(
        shards,
        mesh=mesh,
        in_specs=placed,
        out_specs=(
            P(None, "patch", None, "lat", "lon"),
            P("patch", None, "lat", "lon"),
            P("patch", None, "lat", "lon"),
        ),
        check_vma=False,
    )
```

```python
import jax
import jax.numpy as jnp
from jax import lax
from jax.experimental import pallas as pl
from jax.experimental.pallas import tpu as pltpu
from jax.sharding import PartitionSpec as P

SWEEPS = 4
CELLS = 128
TILES = 16
PLANES = 12
SLOTS = 4
F32 = jnp.float32
VMEM = pl.BlockSpec(memory_space=pltpu.VMEM)
SMEM = pl.BlockSpec(memory_space=pltpu.SMEM)
HBM = pl.BlockSpec(memory_space=pltpu.HBM)
ROW, NORTH, SOUTH, WEST, EAST, LAT_BASE, LON_BASE = range(7)
CHUNK, TO_WEST, TO_EAST = 7, 8, 9
FROM_NORTH, FROM_SOUTH = 10, 11
OTHER, LON, RECEIVER = 12, 13, 14
BLOCKS, RANKS = 15, 19


def lanes():
    return lax.broadcasted_iota(jnp.int32, (8, CELLS), 1)


def sublanes():
    return lax.broadcasted_iota(jnp.int32, (8, CELLS), 0)


def turn(x, shift):
    shift = shift % CELLS
    return x if shift == 0 else pltpu.roll(x, shift, 1)


def tile(b):
    return pl.ds(8 * b, 8)


class Copies:
    def __init__(self, sems):
        self.sems, self.going = sems, []

    def start(self, source, target):
        copy = pltpu.make_async_copy(source, target, self.sems.at[len(self.going)])
        copy.start()
        self.going.append(copy)

    def wait(self, first=0, last=None):
        for copy in self.going[first:last]:
            copy.wait()


def gather_edge(block, f, gathered):
    lane = lanes()
    return jnp.where(lane // 2 == f, turn(block, 2 * f + 1), gathered)


def every_second(first, count=8):
    return pl.ds(first, count, stride=2)


def ghost_columns(west, east, rows_s, cols_s, first=0):
    rows_s[every_second(2 * first + 1), :] = west
    rows_s[every_second(2 * first), :] = east
    cols_s[...] = rows_s[...].T


def around(ref, b, north, south, column, f):
    here = ref[tile(b), :]
    sub, lane = sublanes(), lanes()
    if b == 0:
        up = jnp.where(sub == 0, north, pltpu.roll(here, 1, 0))
    else:
        up = ref[8 * b - 1 : 8 * b + 7, :]
    if b == TILES - 1:
        down = jnp.where(sub == 7, south, pltpu.roll(here, 7, 0))
    else:
        down = ref[8 * b + 1 : 8 * b + 9, :]
    turned = turn(column, -2 * f - 1)
    left = jnp.where(lane == 0, turned, pltpu.roll(here, 1, 1))
    right = jnp.where(lane == CELLS - 1, turned, pltpu.roll(here, CELLS - 1, 1))
    return here, up, down, left, right


def start_kernel(
    ints, slots, flow, pressure, heat, friction,
    chunks, north, south, places, own, named, row, cols_s, rows_s, sems,
):
    copies = Copies(sems)
    copies.start(slots, named)
    copies.start(friction, own.at[10:12])
    copies.start(heat, own.at[8:10])
    copies.start(pressure, own.at[6:8])
    copies.start(flow, own.at[0:6])
    row[8:16, :] = jnp.broadcast_to((ints[RECEIVER] + 1).astype(F32), (8, CELLS))
    chunks[...] = jnp.zeros(chunks.shape, F32)
    north[...] = jnp.zeros(north.shape, F32)
    south[...] = jnp.zeros(south.shape, F32)
    copies.wait(0, 1)
    mine = jnp.broadcast_to(named[...], (8, CELLS)) == sublanes()
    place = jnp.sum(jnp.where(mine, lanes() + 1, 0).astype(F32), axis=1, keepdims=True)
    places[...] = jnp.broadcast_to(place, (8, CELLS))

    def collect(first, last):
        for b in range(TILES):
            gathered = jnp.zeros((8, CELLS), F32) if last == PLANES else cols_s[tile(b), :]
            for f in range(first, last):
                gathered = gather_edge(own[f, tile(b), :], f, gathered)
            cols_s[tile(b), :] = gathered
        for f in range(first, last):
            if f < 10:
                to = f if f < 8 else f + 1
                row[to : to + 1, :] = own[f, pl.ds(ints[ROW], 1), :]
            n, at = divmod(f, 8)
            north[n, at : at + 1, :] = own[f, 0:1, :]
            south[n, at : at + 1, :] = own[f, CELLS - 1 : CELLS, :]

    copies.wait(1, 4)
    collect(6, PLANES)
    copies.wait(4)
    collect(0, 6)
    rows_s[...] = cols_s[...].T
    chunks[ints[CHUNK]] = row[...]
    chunks[ints[TO_WEST]] = rows_s[every_second(1, 16), :]
    chunks[ints[TO_EAST]] = rows_s[every_second(0, 16), :]


def pack_kernel(table, arrived, north, south, out):
    out[:, SLOTS] = jnp.zeros((out.shape[0], 8, CELLS), F32)
    for lat in range(out.shape[0]):
        for n in range(SLOTS):
            out[lat, n] = arrived[table[2 + SLOTS * lat + n]]
    out[table[0], SLOTS] = north[0]
    out[table[1], SLOTS] = south[0]


def for_each_block(ints, sent_to, filled, lats, act):
    sources = sent_to.shape[0]
    for lat in range(lats):
        filled[lat] = 0
    for n in range(sources):
        number = sent_to[n]
        lat = jnp.maximum(number, 0) // sources

        @pl.when((number >= 0) & (number == lat * sources + ints[LON]))
        def _():
            slot = filled[lat]
            filled[lat] = slot + 1
            act(lat, slot, ints[OTHER] + n)


def table_kernel(ints, sent_to, table, filled):
    table[0] = ints[FROM_NORTH]
    table[1] = ints[FROM_SOUTH]
    for n in range(2, table.shape[0]):
        table[n] = ints[OTHER]

    def act(lat, slot, block):
        table[2 + SLOTS * lat + slot] = block

    for_each_block(ints, sent_to, filled, (table.shape[0] - 2) // SLOTS, act)


def sort_kernel(ints, sent_to, arrived, north, south, out, filled):
    lats, count = out.shape[0], out.shape[1]
    out[...] = jnp.zeros(out.shape, F32)

    def act(lat, slot, block):
        out[lat, slot] = arrived[block, 0:8, :]
        for k in range(2):
            to = pl.ds(2 * slot + k, 1)
            out[lat, count - 1, to, :] = arrived[block, 9 + k : 10 + k, :]

    for_each_block(ints, sent_to, filled, lats, act)
    for n in range(north.shape[0]):
        out[ints[FROM_NORTH], SLOTS + n] = north[n]
        out[ints[FROM_SOUTH], SLOTS + n] = south[n]


def split(x):
    high = x.astype(jnp.bfloat16)
    return high, (x - high.astype(F32)).astype(jnp.bfloat16)


def times(left, right):
    return lax.dot_general(left, right, (((1,), (1,)), ((), ())), preferred_element_type=F32)


def weights_kernel(ints, weights, high, low, chosen, sems):
    copies = Copies(sems)
    copies.start(weights.at[pl.ds(ints[LAT_BASE], 2)], chosen.at[0:2])
    copies.start(weights.at[pl.ds(ints[LON_BASE], 2)], chosen.at[2:4])
    copies.wait()
    for side in range(2):
        for term in range(2):
            cut = slice(term * CELLS, (term + 1) * CELLS)
            high[side, :, cut], low[side, :, cut] = split(chosen[2 * side + term])


def blend(blocks_of, high, low, ghosts):
    count = ghosts.shape[1]
    for n in range(2):
        block = jnp.concatenate([blocks_of(2 * n + t) for t in range(2)], axis=1)
        b_high, b_low = split(block)
        both = times(jnp.concatenate([b_high, b_low], axis=0), high[n])
        ghosts[n] = both[0:count] + both[count:] + times(b_high, low[n])


def edge_ghosts(ints, arrived, chunks, ghosts, slot, rows, of):
    halos = (
        arrived[ints[FROM_NORTH], slot],
        arrived[ints[FROM_SOUTH], slot],
        chunks[ints[TO_WEST], rows, :],
        chunks[ints[TO_EAST], rows, :],
    )
    flags = (ints[NORTH], ints[SOUTH], ints[WEST], ints[EAST])
    return [
        jnp.where(flag > 0, ghosts[n // 2, of, :], halo)
        for n, (flag, halo) in enumerate(zip(flags, halos))
    ]


def coefficients(ints, friction, heat, north, south, column, f, b, put):
    lane, sub = lanes(), sublanes()
    centre = [friction[k, tile(b), :] for k in range(2)]
    for k in range(2):
        here, up, down, left, right = around(
            friction.at[k], b, north[k], south[k], column, f + k
        )
        if b == 0:
            up = jnp.where((sub == 0) & (ints[NORTH] > 0), here, up)
        if b == TILES - 1:
            down = jnp.where((sub == 7) & (ints[SOUTH] > 0), here, down)
        left = jnp.where((lane == 0) & (ints[WEST] > 0), here, left)
        right = jnp.where((lane == CELLS - 1) & (ints[EAST] > 0), here, right)
        faces = [0.5 * (here + other) for other in (up, down, left, right)]
        between = 0.5 * (centre[0] + centre[1])
        diagonal = (faces[0] + faces[1]) + (faces[2] + faces[3]) + (between + here)
        inverse = 0.8 / diagonal
        for n, face in enumerate(faces):
            put(n, k, inverse * face)
        put(4, k, inverse * between)
        put(5, k, 0.5 * inverse)
        put(6, k, inverse * heat[k, tile(b), :])
        put(7, k, 0.125 * here)


def coefficient_kernel(ints, friction, heat, chunks, out, cols_s, rows_s):
    west, east = chunks[ints[TO_WEST], 8:16, :], chunks[ints[TO_EAST], 8:16, :]
    ghost_columns(west, east, rows_s, cols_s)
    for b in range(1, TILES - 1):

        def put(n, k, value):
            out[n, k, tile(b), :] = value

        coefficients(ints, friction, heat, (None, None), (None, None), cols_s[tile(b), :], 2, b, put)
    for b in (0, TILES - 1):
        for n in range(8):
            for k in range(2):
                out[n, k, tile(b), :] = jnp.zeros((8, CELLS), F32)


def relaxed(planes, coef, ends, ghosts, column, b):
    def at(f):
        return around(planes(f), b, ghosts[0, f : f + 1, :], ghosts[1, f : f + 1, :], column, f)

    def factor(n, k):
        if b == 0 or b == TILES - 1:
            return ends[n, k, tile(0 if b == 0 else 1), :]
        return coef[n, k, tile(b), :]

    stress = [at(6 + k) for k in range(2)]
    centre = [stress[k][0] for k in range(2)]
    slopes = [[centre[1], -centre[0]]]
    slopes += [[stress[k][n + 1] - stress[k][n] for k in range(2)] for n in (1, 3)]
    new = []
    divergence = []
    for component in range(3):
        cells = [at(2 * component + k) for k in range(2)]
        for k in range(2):
            here, up, down, left, right = cells[k]
            value = 0.2 * here + factor(0, k) * up + factor(1, k) * down
            value = value + factor(2, k) * left + factor(3, k) * right
            value = value + factor(4, k) * cells[1 - k][0]
            if component == 0:
                value = value + factor(6, k)
                divergence.append(cells[1][0] if k == 0 else -cells[0][0])
            else:
                divergence[k] = divergence[k] + (down - up if component == 1 else right - left)
            new.append(value - factor(5, k) * slopes[component][k])
    for k in range(2):
        new.append(centre[k] - factor(7, k) * divergence[k])
    return new


def fill_ghosts(ints, arrived, chunks, high, low, sides, ghosts, cols_s, rows_s):
    count = sides.shape[1]

    def block(n):
        rows = arrived[ints[BLOCKS + n], ints[RANKS + n]]
        if count == 8:
            return rows
        warm = [
            arrived[ints[BLOCKS + n], SLOTS + 2, pl.ds(2 * ints[RANKS + n] + k, 1), :]
            for k in range(2)
        ]
        return jnp.concatenate([rows, *warm, jnp.zeros((6, CELLS), F32)], axis=0)

    blend(block, high, low, sides)
    found = edge_ghosts(ints, arrived, chunks, sides, SLOTS, slice(0, 8), slice(0, 8))
    for n in range(4):
        ghosts[n] = found[n]
    ghost_columns(found[2], found[3], rows_s, cols_s)


def first_kernel(
    ints, flow, pressure, coef, friction, heat, arrived, chunks_in, high, low,
    flow_out, pressure_out, chunks, north, south, ends, heat_ghosts,
    sides, ghosts, cols_s, rows_s, edge_s, halos,
):
    rows_s[every_second(17), :] = chunks_in[ints[TO_WEST], 8:16, :]
    rows_s[every_second(16), :] = chunks_in[ints[TO_EAST], 8:16, :]
    fill_ghosts(ints, arrived, chunks_in, high, low, sides, ghosts, cols_s, rows_s)
    found = edge_ghosts(ints, arrived, chunks_in, sides, SLOTS + 1, slice(8, 16), slice(8, 16))
    for n in range(4):
        heat_ghosts[n] = found[n]
    halos[0] = arrived[ints[FROM_NORTH], SLOTS + 1]
    halos[1] = arrived[ints[FROM_SOUTH], SLOTS + 1]
    for end, b in enumerate((0, TILES - 1)):

        def put(n, k, value):
            ends[n, k, tile(end), :] = value

        lines = [[halos[side, 2 + k : 3 + k, :] for k in range(2)] for side in range(2)]
        coefficients(ints, friction, heat, *lines, cols_s[tile(b), :], 10, b, put)
    sweep(
        ints, flow, pressure, coef, ends, ghosts, cols_s, rows_s, edge_s,
        flow_out, pressure_out, chunks, north, south,
    )


def sweep_kernel(
    ints, flow, pressure, coef, ends, arrived, chunks_in, high, low,
    flow_out, pressure_out, chunks, north, south, sides, ghosts, cols_s, rows_s, edge_s,
):
    fill_ghosts(ints, arrived, chunks_in, high, low, sides, ghosts, cols_s, rows_s)
    sweep(
        ints, flow, pressure, coef, ends, ghosts, cols_s, rows_s, edge_s,
        flow_out, pressure_out, chunks, north, south,
    )


def sweep(
    ints, flow, pressure, coef, ends, ghosts, cols_s, rows_s, edge_s,
    flow_out, pressure_out, chunks, north, south,
):
    def planes(f):
        return flow.at[f] if f < 6 else pressure.at[f - 6]

    def planes_out(f):
        return flow_out.at[f] if f < 6 else pressure_out.at[f - 6]

    chunks[...] = jnp.zeros(chunks.shape, F32)
    for b in range(TILES):
        new = relaxed(planes, coef, ends, ghosts, cols_s[tile(b), :], b)
        for f in range(8):
            planes_out(f)[tile(b), :] = new[f]
    for b in range(TILES):
        gathered = jnp.zeros((8, CELLS), F32)
        for f in range(8):
            gathered = gather_edge(planes_out(f)[tile(b), :], f, gathered)
        edge_s[tile(b), :] = gathered
    for f in range(8):
        north[0, f : f + 1, :] = planes_out(f)[0:1, :]
        south[0, f : f + 1, :] = planes_out(f)[CELLS - 1 : CELLS, :]
    rows_s[...] = edge_s[...].T
    chunks[ints[TO_WEST]] = rows_s[every_second(1), :]
    chunks[ints[TO_EAST]] = rows_s[every_second(0), :]
    for f in range(8):
        edge_s[f : f + 1, :] = planes_out(f)[pl.ds(ints[ROW], 1), :]
    chunks[ints[CHUNK]] = edge_s[0:8, :]


def final_kernel(
    ints, flow, pressure, coef, ends, arrived, chunks_in, high, low, heat, heat_ghosts,
    flow_out, pressure_out, heat_out,
    sides, ghosts, cols_s, rows_s, heat_cols_s, answer, warm, sems,
):
    def planes(f):
        return flow.at[f] if f < 6 else pressure.at[f - 6]

    ghost_columns(heat_ghosts[2], heat_ghosts[3], rows_s, heat_cols_s)
    fill_ghosts(ints, arrived, chunks_in, high, low, sides, ghosts, cols_s, rows_s)
    for b in range(TILES):
        new = relaxed(planes, coef, ends, ghosts, cols_s[tile(b), :], b)
        for f in range(8):
            answer[f, tile(b), :] = new[f]
    copies = Copies(sems)
    copies.start(answer.at[0:6], flow_out)
    copies.start(answer.at[6:8], pressure_out)
    for b in range(TILES):
        layers = [
            around(
                heat.at[k],
                b,
                heat_ghosts[0, k : k + 1, :],
                heat_ghosts[1, k : k + 1, :],
                heat_cols_s[tile(b), :],
                k,
            )
            for k in range(2)
        ]
        for k in range(2):
            here, up, down, left, right = layers[k]
            under = jnp.ones((8, CELLS), F32) if k == 0 else layers[0][0]
            over = layers[1][0] if k == 0 else jnp.zeros((8, CELLS), F32)
            advect = jnp.zeros((8, CELLS), F32)
            for component, minus, plus in ((0, under, over), (1, up, down), (2, left, right)):
                speed = answer[2 * component + k, tile(b), :]
                advect = advect + jnp.maximum(speed, 0.0) * (here - minus)
                advect = advect + jnp.minimum(speed, 0.0) * (plus - here)
            spread = (up + down) + (left + right) + (under + over) - 6.0 * here
            warm[k, tile(b), :] = here + 0.1 * (spread - advect)
    copies.start(warm, heat_out)
    copies.wait()


def shape(*dims):
    return jax.ShapeDtypeStruct(dims, F32)


def scratch(*dims):
    return pltpu.VMEM(dims, F32)


def semaphores(count):
    return pltpu.SemaphoreType.DMA((count,))


def call(
    kernel, outs, ins, scratches, name, specs=None, out_specs=None, limit=4, keep=(), pin=()
):
    out_specs = out_specs or [VMEM] * len(outs)
    specs = specs or [SMEM] + [VMEM] * (len(ins) - 1)
    placed = []
    for n, (x, spec) in enumerate(zip(ins, specs)):
        if spec is HBM or n in keep:
            x = pltpu.with_memory_space_constraint(x, spec.memory_space)
        placed.append(x)
    outs = [
        pltpu.HBM(x.shape, x.dtype)
        if spec is HBM
        else pltpu.VMEM(x.shape, x.dtype)
        if n in pin
        else x
        for n, (x, spec) in enumerate(zip(outs, out_specs))
    ]
    return pl.pallas_call(
        kernel,
        out_shape=outs,
        in_specs=specs,
        out_specs=out_specs,
        scratch_shapes=scratches,
        compiler_params=pltpu.CompilerParams(vmem_limit_bytes=limit * 1024 * 1024),
        name=name,
    )(*placed)


def shards(
    flow_vector,
    normal_stress,
    thermal_field,
    shear_resistance,
    departing_bands,
    receiving_processor,
    shift_filled_by_lane,
    blending_factors,
):
    flow = flow_vector.reshape(6, CELLS, CELLS)
    pressure = normal_stress[0]
    heat = thermal_field[0]
    friction = shear_resistance[0]
    weights = blending_factors.reshape(8, CELLS, CELLS)
    lat, lon = lax.axis_index("lat"), lax.axis_index("lon")
    n_lat, n_lon = lax.axis_size("lat"), lax.axis_size("lon")
    patch = lax.axis_index("patch")
    own_row = departing_bands.reshape(1)
    receiver = receiving_processor.reshape(1)
    other = (1 - patch) * n_lon

    chunk = other + jnp.maximum(receiver, 0) % n_lon
    beside = jnp.stack([jnp.maximum(lon - 1, 0), jnp.minimum(lon + 1, n_lon - 1)])
    beside = (beside + patch * n_lon).astype(jnp.int32)
    beyond = jnp.stack([jnp.maximum(lat - 1, 0), jnp.minimum(lat + 1, n_lat - 1)])
    beyond = beyond.astype(jnp.int32)
    on_edge = jnp.stack([lat == 0, lat == n_lat - 1, lon == 0, lon == n_lon - 1]).astype(jnp.int32)
    bases = jnp.stack([jnp.where(lat > 0, 2, 0), jnp.where(lon > 0, 6, 4)]).astype(jnp.int32)
    here = jnp.stack([other, lon]).astype(jnp.int32)
    first = jnp.concatenate([own_row, on_edge, bases, chunk, beside, beyond, here, receiver])

    square = scratch(CELLS, CELLS)
    tiles = 2 * n_lon
    chunks, north, south, places = call(
        start_kernel,
        [shape(tiles, 16, CELLS), shape(2, 8, CELLS), shape(2, 8, CELLS), shape(8, CELLS)],
        (first, shift_filled_by_lane.reshape(1, CELLS), flow, pressure, heat, friction),
        [scratch(PLANES, CELLS, CELLS), pltpu.VMEM((1, CELLS), jnp.int32), scratch(16, CELLS)]
        + [square, square, semaphores(5)],
        "start",
        specs=[SMEM] + [HBM] * 5,
        pin=(0,),
    )

    def across(chunks):
        return lax.all_to_all(chunks, ("patch", "lon"), 0, 0, tiled=True)

    def along(packed):
        return lax.all_to_all(packed, "lat", 0, 0, tiled=True)

    came, places, lon, lat, other = lax.optimization_barrier(
        (across(chunks), places, lon, lat, other)
    )
    sent_to = lax.dynamic_slice(came, (other, 8, 0), (n_lon, 1, 1)).reshape(n_lon)
    sent_to = sent_to.astype(jnp.int32) - 1
    (packed,) = call(
        sort_kernel,
        [shape(n_lat, SLOTS + 3, 8, CELLS)],
        (first, sent_to, came, north, south),
        [pltpu.SMEM((n_lat,), jnp.int32)],
        "sort",
        specs=[SMEM, SMEM, VMEM, VMEM, VMEM],
        keep=(2,),
        pin=(0,),
    )
    packed, places = lax.optimization_barrier((packed, places))
    arrived = along(packed)

    (table,) = call(
        table_kernel,
        [jax.ShapeDtypeStruct((2 + n_lat * SLOTS,), jnp.int32)],
        lax.optimization_barrier((first, sent_to, packed))[:2],
        [pltpu.SMEM((n_lat,), jnp.int32)],
        "table",
        specs=[SMEM, SMEM],
        out_specs=[SMEM],
    )
    arrived, table = lax.optimization_barrier((arrived, table))

    own = places[:, 0].astype(jnp.int32) - 1
    pick = jnp.concatenate(
        [jnp.where(lat > 0, own[2:4], own[0:2]), jnp.where(lon > 0, own[6:8], own[4:6])]
    )
    same = (own >= 0)[None] & (own[None] // n_lon == pick[:, None] // n_lon)
    slot = jnp.sum((same & (own[None] < pick[:, None])).astype(jnp.int32), axis=1)
    ints = [first, jnp.maximum(pick, 0) // n_lon, jnp.minimum(slot, SLOTS - 1)]
    ints = jnp.concatenate(ints).astype(jnp.int32)

    joined = jax.ShapeDtypeStruct((2, CELLS, 2 * CELLS), jnp.bfloat16)
    high, low = call(
        weights_kernel,
        [joined, joined],
        (ints, weights),
        [scratch(4, CELLS, CELLS), semaphores(2)],
        "weights",
        specs=[SMEM, HBM],
    )
    (coef,) = call(
        coefficient_kernel,
        [shape(8, 2, CELLS, CELLS)],
        (ints, friction, heat, came),
        [square, square],
        "coefficients",
        keep=(3,),
    )
    sides, ghosts = scratch(2, 8, CELLS), scratch(4, 8, CELLS)
    state = [shape(6, CELLS, CELLS), shape(2, CELLS, CELLS)]
    for sweep in range(SWEEPS - 1):
        outs = state + [shape(tiles, 8, CELLS), shape(1, 8, CELLS), shape(1, 8, CELLS)]
        if sweep == 0:
            flow, pressure, chunks, north, south, ends, heat_ghosts = call(
                first_kernel,
                outs + [shape(8, 2, 16, CELLS), shape(4, 8, CELLS)],
                (ints, flow, pressure, coef, friction, heat, arrived, came, high, low),
                [scratch(2, 16, CELLS), ghosts, square, square, square, scratch(2, 8, CELLS)],
                "first_sweep",
                limit=8,
                keep=(3, 6, 7, 8, 9),
                pin=(2,),
            )
        else:
            flow, pressure, chunks, north, south = call(
                sweep_kernel,
                outs,
                (ints, flow, pressure, coef, ends, arrived, came, high, low),
                [sides, ghosts, square, square, square],
                "sweep",
                limit=8,
                keep=(3, 4, 5, 6, 7, 8),
                pin=(2,),
            )
        came = across(chunks)
        (packed,) = call(
            pack_kernel,
            [shape(n_lat, SLOTS + 1, 8, CELLS)],
            (table, came, north, south),
            [],
            "pack",
            keep=(1,),
            pin=(0,),
        )
        arrived = along(packed)
    flow, pressure, heat = call(
        final_kernel,
        state + [shape(2, CELLS, CELLS)],
        (ints, flow, pressure, coef, ends, arrived, came, high, low, heat, heat_ghosts),
        [sides, ghosts, square, square, square]
        + [scratch(8, CELLS, CELLS), scratch(2, CELLS, CELLS), semaphores(3)],
        "final",
        out_specs=[HBM] * 3,
        limit=8,
        keep=(1, 2, 3, 4, 5, 6, 7, 8),
    )
    return flow.reshape(3, 1, 2, CELLS, CELLS), pressure[None], heat[None]


def solution(mesh):
    placed = (
        P(None, "patch", None, "lat", "lon"),
        P("patch", None, "lat", "lon"),
        P("patch", None, "lat", "lon"),
        P("patch", None, "lat", "lon"),
        P("patch", "lat", "lon", None),
        P("patch", "lat", "lon", None),
        P("patch", "lat", "lon", None),
        P("patch", "lat", "lon", None, None, None),
    )
    return jax.shard_map(
        shards,
        mesh=mesh,
        in_specs=placed,
        out_specs=(
            P(None, "patch", None, "lat", "lon"),
            P("patch", None, "lat", "lon"),
            P("patch", None, "lat", "lon"),
        ),
        check_vma=False,
    )
```

```python
import jax
import jax.numpy as jnp
from jax import lax
from jax.experimental import pallas as pl
from jax.experimental.pallas import tpu as pltpu
from jax.sharding import PartitionSpec as P

SWEEPS = 4
CELLS = 128
TILES = 16
PLANES = 12
SLOTS = 4
F32 = jnp.float32
VMEM = pl.BlockSpec(memory_space=pltpu.VMEM)
SMEM = pl.BlockSpec(memory_space=pltpu.SMEM)
HBM = pl.BlockSpec(memory_space=pltpu.HBM)
ROW, NORTH, SOUTH, WEST, EAST, LAT_BASE, LON_BASE = range(7)
CHUNK, TO_WEST, TO_EAST = 7, 8, 9
FROM_NORTH, FROM_SOUTH = 10, 11
OTHER, LON, RECEIVER = 12, 13, 14
BLOCKS, RANKS = 15, 19


def lanes():
    return lax.broadcasted_iota(jnp.int32, (8, CELLS), 1)


def sublanes():
    return lax.broadcasted_iota(jnp.int32, (8, CELLS), 0)


def turn(x, shift):
    shift = shift % CELLS
    return x if shift == 0 else pltpu.roll(x, shift, 1)


def tile(b):
    return pl.ds(8 * b, 8)


class Copies:
    def __init__(self, sems):
        self.sems, self.going = sems, []

    def start(self, source, target):
        copy = pltpu.make_async_copy(source, target, self.sems.at[len(self.going)])
        copy.start()
        self.going.append(copy)

    def wait(self, first=0, last=None):
        for copy in self.going[first:last]:
            copy.wait()


def gather_edge(block, f, gathered):
    lane = lanes()
    return jnp.where(lane // 2 == f, turn(block, 2 * f + 1), gathered)


def every_second(first, count=8):
    return pl.ds(first, count, stride=2)


def ghost_columns(west, east, rows_s, cols_s, first=0):
    rows_s[every_second(2 * first + 1), :] = west
    rows_s[every_second(2 * first), :] = east
    cols_s[...] = rows_s[...].T


def around(ref, b, north, south, column, f):
    here = ref[tile(b), :]
    sub, lane = sublanes(), lanes()
    if b == 0:
        up = jnp.where(sub == 0, north, pltpu.roll(here, 1, 0))
    else:
        up = ref[8 * b - 1 : 8 * b + 7, :]
    if b == TILES - 1:
        down = jnp.where(sub == 7, south, pltpu.roll(here, 7, 0))
    else:
        down = ref[8 * b + 1 : 8 * b + 9, :]
    turned = turn(column, -2 * f - 1)
    left = jnp.where(lane == 0, turned, pltpu.roll(here, 1, 1))
    right = jnp.where(lane == CELLS - 1, turned, pltpu.roll(here, CELLS - 1, 1))
    return here, up, down, left, right


def start_kernel(
    ints, slots, flow, pressure, heat, friction, weights,
    chunks, north, south, places, high, low, own, named, row, chosen, cols_s, rows_s, sems,
):
    copies = Copies(sems)
    copies.start(slots, named)
    copies.start(friction, own.at[10:12])
    copies.start(heat, own.at[8:10])
    copies.start(pressure, own.at[6:8])
    copies.start(flow, own.at[0:6])
    copies.start(weights.at[pl.ds(ints[LAT_BASE], 2)], chosen.at[0:2])
    copies.start(weights.at[pl.ds(ints[LON_BASE], 2)], chosen.at[2:4])
    row[8:16, :] = jnp.broadcast_to((ints[RECEIVER] + 1).astype(F32), (8, CELLS))
    chunks[...] = jnp.zeros(chunks.shape, F32)
    north[...] = jnp.zeros(north.shape, F32)
    south[...] = jnp.zeros(south.shape, F32)
    copies.wait(0, 1)
    mine = jnp.broadcast_to(named[...], (8, CELLS)) == sublanes()
    place = jnp.sum(jnp.where(mine, lanes() + 1, 0).astype(F32), axis=1, keepdims=True)
    places[...] = jnp.broadcast_to(place, (8, CELLS))

    def collect(first, last):
        for b in range(TILES):
            gathered = jnp.zeros((8, CELLS), F32) if last == PLANES else cols_s[tile(b), :]
            for f in range(first, last):
                gathered = gather_edge(own[f, tile(b), :], f, gathered)
            cols_s[tile(b), :] = gathered
        for f in range(first, last):
            if f < 10:
                to = f if f < 8 else f + 1
                row[to : to + 1, :] = own[f, pl.ds(ints[ROW], 1), :]
            n, at = divmod(f, 8)
            north[n, at : at + 1, :] = own[f, 0:1, :]
            south[n, at : at + 1, :] = own[f, CELLS - 1 : CELLS, :]

    copies.wait(1, 4)
    collect(6, PLANES)
    copies.wait(4, 5)
    collect(0, 6)
    rows_s[...] = cols_s[...].T
    chunks[ints[CHUNK]] = row[...]
    chunks[ints[TO_WEST]] = rows_s[every_second(1, 16), :]
    chunks[ints[TO_EAST]] = rows_s[every_second(0, 16), :]
    copies.wait(5)
    for side in range(2):
        for term in range(2):
            cut = slice(term * CELLS, (term + 1) * CELLS)
            high[side, :, cut], low[side, :, cut] = split(chosen[2 * side + term])


def pack_kernel(table, arrived, north, south, out):
    out[:, SLOTS] = jnp.zeros((out.shape[0], 8, CELLS), F32)
    for lat in range(out.shape[0]):
        for n in range(SLOTS):
            out[lat, n] = arrived[table[2 + SLOTS * lat + n]]
    out[table[0], SLOTS] = north[0]
    out[table[1], SLOTS] = south[0]


def for_each_block(ints, sent_to, filled, lats, act):
    sources = sent_to.shape[0]
    for lat in range(lats):
        filled[lat] = 0
    for n in range(sources):
        number = sent_to[n]
        lat = jnp.maximum(number, 0) // sources

        @pl.when((number >= 0) & (number == lat * sources + ints[LON]))
        def _():
            slot = filled[lat]
            filled[lat] = slot + 1
            act(lat, slot, ints[OTHER] + n)


def sort_kernel(ints, sent_to, arrived, north, south, out, table, filled):
    lats, count = out.shape[0], out.shape[1]
    out[...] = jnp.zeros(out.shape, F32)
    table[0] = ints[FROM_NORTH]
    table[1] = ints[FROM_SOUTH]
    for n in range(2, table.shape[0]):
        table[n] = ints[OTHER]

    def act(lat, slot, block):
        table[2 + SLOTS * lat + slot] = block
        out[lat, slot] = arrived[block, 0:8, :]
        for k in range(2):
            to = pl.ds(2 * slot + k, 1)
            out[lat, count - 1, to, :] = arrived[block, 9 + k : 10 + k, :]

    for_each_block(ints, sent_to, filled, lats, act)
    for n in range(north.shape[0]):
        out[ints[FROM_NORTH], SLOTS + n] = north[n]
        out[ints[FROM_SOUTH], SLOTS + n] = south[n]


def split(x):
    high = x.astype(jnp.bfloat16)
    return high, (x - high.astype(F32)).astype(jnp.bfloat16)


def times(left, right):
    return lax.dot_general(left, right, (((1,), (1,)), ((), ())), preferred_element_type=F32)


def blend(blocks_of, high, low, ghosts):
    count = ghosts.shape[1]
    for n in range(2):
        block = jnp.concatenate([blocks_of(2 * n + t) for t in range(2)], axis=1)
        b_high, b_low = split(block)
        both = times(jnp.concatenate([b_high, b_low], axis=0), high[n])
        ghosts[n] = both[0:count] + both[count:] + times(b_high, low[n])


def edge_ghosts(ints, arrived, chunks, ghosts, slot, rows, of):
    halos = (
        arrived[ints[FROM_NORTH], slot],
        arrived[ints[FROM_SOUTH], slot],
        chunks[ints[TO_WEST], rows, :],
        chunks[ints[TO_EAST], rows, :],
    )
    flags = (ints[NORTH], ints[SOUTH], ints[WEST], ints[EAST])
    return [
        jnp.where(flag > 0, ghosts[n // 2, of, :], halo)
        for n, (flag, halo) in enumerate(zip(flags, halos))
    ]


def coefficients(ints, friction, heat, north, south, column, f, b, put):
    lane, sub = lanes(), sublanes()
    centre = [friction[k, tile(b), :] for k in range(2)]
    for k in range(2):
        here, up, down, left, right = around(
            friction.at[k], b, north[k], south[k], column, f + k
        )
        if b == 0:
            up = jnp.where((sub == 0) & (ints[NORTH] > 0), here, up)
        if b == TILES - 1:
            down = jnp.where((sub == 7) & (ints[SOUTH] > 0), here, down)
        left = jnp.where((lane == 0) & (ints[WEST] > 0), here, left)
        right = jnp.where((lane == CELLS - 1) & (ints[EAST] > 0), here, right)
        faces = [0.5 * (here + other) for other in (up, down, left, right)]
        between = 0.5 * (centre[0] + centre[1])
        diagonal = (faces[0] + faces[1]) + (faces[2] + faces[3]) + (between + here)
        inverse = 0.8 / diagonal
        for n, face in enumerate(faces):
            put(n, k, inverse * face)
        put(4, k, inverse * between)
        put(5, k, 0.5 * inverse)
        put(6, k, inverse * heat[k, tile(b), :])
        put(7, k, 0.125 * here)


def relaxed(planes, coef, ghosts, column, b):
    at = [
        around(planes(f), b, ghosts[0, f : f + 1, :], ghosts[1, f : f + 1, :], column, f)
        for f in range(8)
    ]

    def factor(n, k):
        return coef[n, k, tile(b), :]

    new = []
    for component in range(3):
        for k in range(2):
            here, up, down, left, right = at[2 * component + k]
            value = 0.2 * here + factor(0, k) * up + factor(1, k) * down
            value = value + factor(2, k) * left + factor(3, k) * right
            value = value + factor(4, k) * at[2 * component + 1 - k][0]
            if component == 0:
                value = value + factor(6, k)
                slope = at[7][0] if k == 0 else -at[6][0]
            elif component == 1:
                slope = at[6 + k][2] - at[6 + k][1]
            else:
                slope = at[6 + k][4] - at[6 + k][3]
            new.append(value - factor(5, k) * slope)
    for k in range(2):
        divergence = (at[2 + k][2] - at[2 + k][1]) + (at[4 + k][4] - at[4 + k][3])
        divergence = divergence + at[1][0] if k == 0 else divergence - at[0][0]
        new.append(at[6 + k][0] - factor(7, k) * divergence)
    return new


def fill_ghosts(ints, arrived, chunks, high, low, sides, ghosts, cols_s, rows_s):
    count = sides.shape[1]

    def block(n):
        rows = arrived[ints[BLOCKS + n], ints[RANKS + n]]
        if count == 8:
            return rows
        warm = [
            arrived[ints[BLOCKS + n], SLOTS + 2, pl.ds(2 * ints[RANKS + n] + k, 1), :]
            for k in range(2)
        ]
        return jnp.concatenate([rows, *warm, jnp.zeros((6, CELLS), F32)], axis=0)

    blend(block, high, low, sides)
    found = edge_ghosts(ints, arrived, chunks, sides, SLOTS, slice(0, 8), slice(0, 8))
    for n in range(4):
        ghosts[n] = found[n]
    ghost_columns(found[2], found[3], rows_s, cols_s)


def first_kernel(
    ints, flow, pressure, friction, heat, arrived, chunks_in, high, low,
    flow_out, pressure_out, chunks, north, south, coef, heat_ghosts,
    sides, ghosts, cols_s, rows_s, edge_s, halos,
):
    rows_s[every_second(17), :] = chunks_in[ints[TO_WEST], 8:16, :]
    rows_s[every_second(16), :] = chunks_in[ints[TO_EAST], 8:16, :]
    fill_ghosts(ints, arrived, chunks_in, high, low, sides, ghosts, cols_s, rows_s)
    found = edge_ghosts(ints, arrived, chunks_in, sides, SLOTS + 1, slice(8, 16), slice(8, 16))
    for n in range(4):
        heat_ghosts[n] = found[n]
    halos[0] = arrived[ints[FROM_NORTH], SLOTS + 1]
    halos[1] = arrived[ints[FROM_SOUTH], SLOTS + 1]
    lines = [[halos[side, 2 + k : 3 + k, :] for k in range(2)] for side in range(2)]
    for b in range(TILES):

        def put(n, k, value):
            coef[n, k, tile(b), :] = value

        coefficients(ints, friction, heat, *lines, cols_s[tile(b), :], 10, b, put)
    sweep(
        ints, flow, pressure, coef, ghosts, cols_s, rows_s, edge_s,
        flow_out, pressure_out, chunks, north, south,
    )


def sweep_kernel(
    ints, flow, pressure, coef, arrived, chunks_in, high, low,
    flow_out, pressure_out, chunks, north, south, sides, ghosts, cols_s, rows_s, edge_s,
):
    fill_ghosts(ints, arrived, chunks_in, high, low, sides, ghosts, cols_s, rows_s)
    sweep(
        ints, flow, pressure, coef, ghosts, cols_s, rows_s, edge_s,
        flow_out, pressure_out, chunks, north, south,
    )


def sweep(
    ints, flow, pressure, coef, ghosts, cols_s, rows_s, edge_s,
    flow_out, pressure_out, chunks, north, south,
):
    def planes(f):
        return flow.at[f] if f < 6 else pressure.at[f - 6]

    def planes_out(f):
        return flow_out.at[f] if f < 6 else pressure_out.at[f - 6]

    chunks[...] = jnp.zeros(chunks.shape, F32)
    for b in range(TILES):
        new = relaxed(planes, coef, ghosts, cols_s[tile(b), :], b)
        for f in range(8):
            planes_out(f)[tile(b), :] = new[f]
    for b in range(TILES):
        gathered = jnp.zeros((8, CELLS), F32)
        for f in range(8):
            gathered = gather_edge(planes_out(f)[tile(b), :], f, gathered)
        edge_s[tile(b), :] = gathered
    for f in range(8):
        north[0, f : f + 1, :] = planes_out(f)[0:1, :]
        south[0, f : f + 1, :] = planes_out(f)[CELLS - 1 : CELLS, :]
    rows_s[...] = edge_s[...].T
    chunks[ints[TO_WEST]] = rows_s[every_second(1), :]
    chunks[ints[TO_EAST]] = rows_s[every_second(0), :]
    for f in range(8):
        edge_s[f : f + 1, :] = planes_out(f)[pl.ds(ints[ROW], 1), :]
    chunks[ints[CHUNK]] = edge_s[0:8, :]


def final_kernel(
    ints, flow, pressure, coef, arrived, chunks_in, high, low, heat, heat_ghosts,
    flow_out, pressure_out, heat_out,
    sides, ghosts, cols_s, rows_s, heat_cols_s, answer, warm, sems,
):
    def planes(f):
        return flow.at[f] if f < 6 else pressure.at[f - 6]

    ghost_columns(heat_ghosts[2], heat_ghosts[3], rows_s, heat_cols_s)
    fill_ghosts(ints, arrived, chunks_in, high, low, sides, ghosts, cols_s, rows_s)
    for b in range(TILES):
        new = relaxed(planes, coef, ghosts, cols_s[tile(b), :], b)
        for f in range(8):
            answer[f, tile(b), :] = new[f]
    copies = Copies(sems)
    copies.start(answer.at[0:6], flow_out)
    copies.start(answer.at[6:8], pressure_out)
    for b in range(TILES):
        layers = [
            around(
                heat.at[k],
                b,
                heat_ghosts[0, k : k + 1, :],
                heat_ghosts[1, k : k + 1, :],
                heat_cols_s[tile(b), :],
                k,
            )
            for k in range(2)
        ]
        for k in range(2):
            here, up, down, left, right = layers[k]
            under = jnp.ones((8, CELLS), F32) if k == 0 else layers[0][0]
            over = layers[1][0] if k == 0 else jnp.zeros((8, CELLS), F32)
            advect = jnp.zeros((8, CELLS), F32)
            for component, minus, plus in ((0, under, over), (1, up, down), (2, left, right)):
                speed = answer[2 * component + k, tile(b), :]
                advect = advect + jnp.maximum(speed, 0.0) * (here - minus)
                advect = advect + jnp.minimum(speed, 0.0) * (plus - here)
            spread = (up + down) + (left + right) + (under + over) - 6.0 * here
            warm[k, tile(b), :] = here + 0.1 * (spread - advect)
    copies.start(warm, heat_out)
    copies.wait()


def shape(*dims):
    return jax.ShapeDtypeStruct(dims, F32)


def scratch(*dims):
    return pltpu.VMEM(dims, F32)


def semaphores(count):
    return pltpu.SemaphoreType.DMA((count,))


def call(
    kernel, outs, ins, scratches, name, specs=None, out_specs=None, limit=4, keep=(), pin=()
):
    out_specs = out_specs or [VMEM] * len(outs)
    specs = specs or [SMEM] + [VMEM] * (len(ins) - 1)
    placed = []
    for n, (x, spec) in enumerate(zip(ins, specs)):
        if spec is HBM or n in keep:
            x = pltpu.with_memory_space_constraint(x, spec.memory_space)
        placed.append(x)
    outs = [
        pltpu.HBM(x.shape, x.dtype)
        if spec is HBM
        else pltpu.VMEM(x.shape, x.dtype)
        if n in pin
        else x
        for n, (x, spec) in enumerate(zip(outs, out_specs))
    ]
    return pl.pallas_call(
        kernel,
        out_shape=outs,
        in_specs=specs,
        out_specs=out_specs,
        scratch_shapes=scratches,
        compiler_params=pltpu.CompilerParams(vmem_limit_bytes=limit * 1024 * 1024),
        name=name,
    )(*placed)


def shards(
    flow_vector,
    normal_stress,
    thermal_field,
    shear_resistance,
    departing_bands,
    receiving_processor,
    shift_filled_by_lane,
    blending_factors,
):
    flow = flow_vector.reshape(6, CELLS, CELLS)
    pressure = normal_stress[0]
    heat = thermal_field[0]
    friction = shear_resistance[0]
    weights = blending_factors.reshape(8, CELLS, CELLS)
    lat, lon = lax.axis_index("lat"), lax.axis_index("lon")
    n_lat, n_lon = lax.axis_size("lat"), lax.axis_size("lon")
    patch = lax.axis_index("patch")
    own_row = departing_bands.reshape(1)
    receiver = receiving_processor.reshape(1)
    other = (1 - patch) * n_lon

    chunk = other + jnp.maximum(receiver, 0) % n_lon
    beside = jnp.stack([jnp.maximum(lon - 1, 0), jnp.minimum(lon + 1, n_lon - 1)])
    beside = (beside + patch * n_lon).astype(jnp.int32)
    beyond = jnp.stack([jnp.maximum(lat - 1, 0), jnp.minimum(lat + 1, n_lat - 1)])
    beyond = beyond.astype(jnp.int32)
    on_edge = jnp.stack([lat == 0, lat == n_lat - 1, lon == 0, lon == n_lon - 1]).astype(jnp.int32)
    bases = jnp.stack([jnp.where(lat > 0, 2, 0), jnp.where(lon > 0, 6, 4)]).astype(jnp.int32)
    here = jnp.stack([other, lon]).astype(jnp.int32)
    first = jnp.concatenate([own_row, on_edge, bases, chunk, beside, beyond, here, receiver])

    square = scratch(CELLS, CELLS)
    tiles = 2 * n_lon
    joined = jax.ShapeDtypeStruct((2, CELLS, 2 * CELLS), jnp.bfloat16)
    chunks, north, south, places, high, low = call(
        start_kernel,
        [shape(tiles, 16, CELLS), shape(2, 8, CELLS), shape(2, 8, CELLS), shape(8, CELLS)]
        + [joined, joined],
        (first, shift_filled_by_lane.reshape(1, CELLS), flow, pressure, heat, friction, weights),
        [scratch(PLANES, CELLS, CELLS), pltpu.VMEM((1, CELLS), jnp.int32), scratch(16, CELLS)]
        + [scratch(4, CELLS, CELLS), square, square, semaphores(7)],
        "start",
        specs=[SMEM] + [HBM] * 6,
        pin=(0,),
    )

    def across(chunks):
        return lax.all_to_all(chunks, ("patch", "lon"), 0, 0, tiled=True)

    def along(packed):
        return lax.all_to_all(packed, "lat", 0, 0, tiled=True)

    came, places, lon, lat, other = lax.optimization_barrier(
        (across(chunks), places, lon, lat, other)
    )
    sent_to = lax.dynamic_slice(came, (other, 8, 0), (n_lon, 1, 1)).reshape(n_lon)
    sent_to = sent_to.astype(jnp.int32) - 1
    own = places[:, 0].astype(jnp.int32) - 1
    pick = jnp.concatenate(
        [jnp.where(lat > 0, own[2:4], own[0:2]), jnp.where(lon > 0, own[6:8], own[4:6])]
    )
    same = (own >= 0)[None] & (own[None] // n_lon == pick[:, None] // n_lon)
    slot = jnp.sum((same & (own[None] < pick[:, None])).astype(jnp.int32), axis=1)
    ints = [first, jnp.maximum(pick, 0) // n_lon, jnp.minimum(slot, SLOTS - 1)]
    ints = jnp.concatenate(ints).astype(jnp.int32)

    packed, table = call(
        sort_kernel,
        [
            shape(n_lat, SLOTS + 3, 8, CELLS),
            jax.ShapeDtypeStruct((2 + n_lat * SLOTS,), jnp.int32),
        ],
        (ints, sent_to, came, north, south),
        [pltpu.SMEM((n_lat,), jnp.int32)],
        "sort",
        specs=[SMEM, SMEM, VMEM, VMEM, VMEM],
        out_specs=[VMEM, SMEM],
        keep=(2,),
        pin=(0,),
    )
    arrived = along(packed)

    sides, ghosts = scratch(2, 8, CELLS), scratch(4, 8, CELLS)
    state = [shape(6, CELLS, CELLS), shape(2, CELLS, CELLS)]
    for sweep in range(SWEEPS - 1):
        outs = state + [shape(tiles, 8, CELLS), shape(1, 8, CELLS), shape(1, 8, CELLS)]
        if sweep == 0:
            flow, pressure, chunks, north, south, coef, heat_ghosts = call(
                first_kernel,
                outs + [shape(8, 2, CELLS, CELLS), shape(4, 8, CELLS)],
                (ints, flow, pressure, friction, heat, arrived, came, high, low),
                [scratch(2, 16, CELLS), ghosts, square, square, square, scratch(2, 8, CELLS)],
                "first_sweep",
                limit=8,
                keep=(5, 6, 7, 8),
                pin=(2,),
            )
        else:
            flow, pressure, chunks, north, south = call(
                sweep_kernel,
                outs,
                (ints, flow, pressure, coef, arrived, came, high, low),
                [sides, ghosts, square, square, square],
                "sweep",
                limit=8,
                keep=(3, 4, 5, 6, 7),
                pin=(2,),
            )
        came = across(chunks)
        (packed,) = call(
            pack_kernel,
            [shape(n_lat, SLOTS + 1, 8, CELLS)],
            (table, came, north, south),
            [],
            "pack",
            keep=(1,),
            pin=(0,),
        )
        arrived = along(packed)
    flow, pressure, heat = call(
        final_kernel,
        state + [shape(2, CELLS, CELLS)],
        (ints, flow, pressure, coef, arrived, came, high, low, heat, heat_ghosts),
        [sides, ghosts, square, square, square]
        + [scratch(8, CELLS, CELLS), scratch(2, CELLS, CELLS), semaphores(3)],
        "final",
        out_specs=[HBM] * 3,
        limit=8,
        keep=(1, 2, 3, 4, 5, 6, 7),
    )
    return flow.reshape(3, 1, 2, CELLS, CELLS), pressure[None], heat[None]


def solution(mesh):
    placed = (
        P(None, "patch", None, "lat", "lon"),
        P("patch", None, "lat", "lon"),
        P("patch", None, "lat", "lon"),
        P("patch", None, "lat", "lon"),
        P("patch", "lat", "lon", None),
        P("patch", "lat", "lon", None),
        P("patch", "lat", "lon", None),
        P("patch", "lat", "lon", None, None, None),
    )
    return jax.shard_map(
        shards,
        mesh=mesh,
        in_specs=placed,
        out_specs=(
            P(None, "patch", None, "lat", "lon"),
            P("patch", None, "lat", "lon"),
            P("patch", None, "lat", "lon"),
        ),
        check_vma=False,
    )
```

```python
import jax
import jax.numpy as jnp
from jax import lax
from jax.experimental import pallas as pl
from jax.experimental.pallas import tpu as pltpu
from jax.sharding import PartitionSpec as P

SWEEPS = 4
CELLS = 128
TILES = 16
PLANES = 12
SLOTS = 4
F32 = jnp.float32
VMEM = pl.BlockSpec(memory_space=pltpu.VMEM)
SMEM = pl.BlockSpec(memory_space=pltpu.SMEM)
HBM = pl.BlockSpec(memory_space=pltpu.HBM)
ROW, NORTH, SOUTH, WEST, EAST, LAT_BASE, LON_BASE = range(7)
CHUNK, TO_WEST, TO_EAST = 7, 8, 9
FROM_NORTH, FROM_SOUTH = 10, 11
OTHER, LON, RECEIVER = 12, 13, 14
BLOCKS, RANKS = 15, 19


def lanes():
    return lax.broadcasted_iota(jnp.int32, (8, CELLS), 1)


def sublanes():
    return lax.broadcasted_iota(jnp.int32, (8, CELLS), 0)


def turn(x, shift):
    shift = shift % CELLS
    return x if shift == 0 else pltpu.roll(x, shift, 1)


def tile(b):
    return pl.ds(8 * b, 8)


class Copies:
    def __init__(self, sems):
        self.sems, self.going = sems, []

    def start(self, source, target):
        copy = pltpu.make_async_copy(source, target, self.sems.at[len(self.going)])
        copy.start()
        self.going.append(copy)

    def wait(self, first=0, last=None):
        for copy in self.going[first:last]:
            copy.wait()


def gather_edge(block, f, gathered):
    lane = lanes()
    return jnp.where(lane // 2 == f, turn(block, 2 * f + 1), gathered)


def every_second(first, count=8):
    return pl.ds(first, count, stride=2)


def ghost_columns(west, east, rows_s, cols_s, first=0):
    rows_s[every_second(2 * first + 1), :] = west
    rows_s[every_second(2 * first), :] = east
    cols_s[...] = rows_s[...].T


def around(ref, b, north, south, column, f):
    here = ref[tile(b), :]
    sub, lane = sublanes(), lanes()
    if b == 0:
        up = jnp.where(sub == 0, north, pltpu.roll(here, 1, 0))
    else:
        up = ref[8 * b - 1 : 8 * b + 7, :]
    if b == TILES - 1:
        down = jnp.where(sub == 7, south, pltpu.roll(here, 7, 0))
    else:
        down = ref[8 * b + 1 : 8 * b + 9, :]
    turned = turn(column, -2 * f - 1)
    left = jnp.where(lane == 0, turned, pltpu.roll(here, 1, 1))
    right = jnp.where(lane == CELLS - 1, turned, pltpu.roll(here, CELLS - 1, 1))
    return here, up, down, left, right


def start_kernel(
    ints, slots, flow, pressure, heat, friction,
    chunks, north, south, places, own, named, row, cols_s, rows_s, sems,
):
    copies = Copies(sems)
    copies.start(slots, named)
    copies.start(friction, own.at[10:12])
    copies.start(heat, own.at[8:10])
    copies.start(pressure, own.at[6:8])
    copies.start(flow, own.at[0:6])
    row[8:16, :] = jnp.broadcast_to((ints[RECEIVER] + 1).astype(F32), (8, CELLS))
    chunks[...] = jnp.zeros(chunks.shape, F32)
    north[...] = jnp.zeros(north.shape, F32)
    south[...] = jnp.zeros(south.shape, F32)
    copies.wait(0, 1)
    mine = jnp.broadcast_to(named[...], (8, CELLS)) == sublanes()
    place = jnp.sum(jnp.where(mine, lanes() + 1, 0).astype(F32), axis=1, keepdims=True)
    places[...] = jnp.broadcast_to(place, (8, CELLS))

    def collect(first, last):
        for b in range(TILES):
            gathered = jnp.zeros((8, CELLS), F32) if last == PLANES else cols_s[tile(b), :]
            for f in range(first, last):
                gathered = gather_edge(own[f, tile(b), :], f, gathered)
            cols_s[tile(b), :] = gathered
        for f in range(first, last):
            if f < 10:
                to = f if f < 8 else f + 1
                row[to : to + 1, :] = own[f, pl.ds(ints[ROW], 1), :]
            n, at = divmod(f, 8)
            north[n, at : at + 1, :] = own[f, 0:1, :]
            south[n, at : at + 1, :] = own[f, CELLS - 1 : CELLS, :]

    copies.wait(1, 4)
    collect(6, PLANES)
    copies.wait(4)
    collect(0, 6)
    rows_s[...] = cols_s[...].T
    chunks[ints[CHUNK]] = row[...]
    chunks[ints[TO_WEST]] = rows_s[every_second(1, 16), :]
    chunks[ints[TO_EAST]] = rows_s[every_second(0, 16), :]


def pack_kernel(table, arrived, north, south, out):
    out[:, SLOTS] = jnp.zeros((out.shape[0], 8, CELLS), F32)
    for lat in range(out.shape[0]):
        for n in range(SLOTS):
            out[lat, n] = arrived[table[2 + SLOTS * lat + n]]
    out[table[0], SLOTS] = north[0]
    out[table[1], SLOTS] = south[0]


def for_each_block(ints, sent_to, filled, lats, act):
    sources = sent_to.shape[0]
    for lat in range(lats):
        filled[lat] = 0
    for n in range(sources):
        number = sent_to[n]
        lat = jnp.maximum(number, 0) // sources

        @pl.when((number >= 0) & (number == lat * sources + ints[LON]))
        def _():
            slot = filled[lat]
            filled[lat] = slot + 1
            act(lat, slot, ints[OTHER] + n)


def table_kernel(ints, sent_to, table, filled):
    table[0] = ints[FROM_NORTH]
    table[1] = ints[FROM_SOUTH]
    for n in range(2, table.shape[0]):
        table[n] = ints[OTHER]

    def act(lat, slot, block):
        table[2 + SLOTS * lat + slot] = block

    for_each_block(ints, sent_to, filled, (table.shape[0] - 2) // SLOTS, act)


def sort_kernel(ints, sent_to, arrived, north, south, out, filled):
    lats, count = out.shape[0], out.shape[1]
    out[...] = jnp.zeros(out.shape, F32)

    sources = sent_to.shape[0]
    for lat in range(lats):
        filled[lat] = 0
    for n in range(sources):
        number = sent_to[n]
        lat = jnp.maximum(number, 0) // sources
        here = (number >= 0) & (number == lat * sources + ints[LON])
        slot = filled[lat]
        filled[lat] = slot + here.astype(jnp.int32)
        block = ints[OTHER] + n
        out[lat, jnp.where(here, slot, SLOTS)] = arrived[block, 0:8, :]
        warm = jnp.where(here, count - 1, SLOTS + 1)
        row = jnp.where(here, 2 * slot, 0)
        for k in range(2):
            out[lat, warm, pl.ds(row + k, 1), :] = arrived[block, 9 + k : 10 + k, :]

    for n in range(north.shape[0]):
        out[ints[FROM_NORTH], SLOTS + n] = north[n]
        out[ints[FROM_SOUTH], SLOTS + n] = south[n]


def split(x):
    high = x.astype(jnp.bfloat16)
    return high, (x - high.astype(F32)).astype(jnp.bfloat16)


def times(left, right):
    return lax.dot_general(left, right, (((1,), (1,)), ((), ())), preferred_element_type=F32)


def weights_kernel(ints, weights, high, low, chosen, sems):
    copies = Copies(sems)
    copies.start(weights.at[pl.ds(ints[LAT_BASE], 2)], chosen.at[0:2])
    copies.start(weights.at[pl.ds(ints[LON_BASE], 2)], chosen.at[2:4])
    copies.wait()
    for side in range(2):
        for term in range(2):
            cut = slice(term * CELLS, (term + 1) * CELLS)
            high[side, :, cut], low[side, :, cut] = split(chosen[2 * side + term])


def blend(blocks_of, high, low, ghosts):
    count = ghosts.shape[1]
    for n in range(2):
        block = jnp.concatenate([blocks_of(2 * n + t) for t in range(2)], axis=1)
        b_high, b_low = split(block)
        both = times(jnp.concatenate([b_high, b_low], axis=0), high[n])
        ghosts[n] = both[0:count] + both[count:] + times(b_high, low[n])


def edge_ghosts(ints, arrived, chunks, ghosts, slot, rows, of):
    halos = (
        arrived[ints[FROM_NORTH], slot],
        arrived[ints[FROM_SOUTH], slot],
        chunks[ints[TO_WEST], rows, :],
        chunks[ints[TO_EAST], rows, :],
    )
    flags = (ints[NORTH], ints[SOUTH], ints[WEST], ints[EAST])
    return [
        jnp.where(flag > 0, ghosts[n // 2, of, :], halo)
        for n, (flag, halo) in enumerate(zip(flags, halos))
    ]


def coefficients(ints, friction, heat, north, south, column, f, b, put):
    lane, sub = lanes(), sublanes()
    centre = [friction[k, tile(b), :] for k in range(2)]
    for k in range(2):
        here, up, down, left, right = around(
            friction.at[k], b, north[k], south[k], column, f + k
        )
        if b == 0:
            up = jnp.where((sub == 0) & (ints[NORTH] > 0), here, up)
        if b == TILES - 1:
            down = jnp.where((sub == 7) & (ints[SOUTH] > 0), here, down)
        left = jnp.where((lane == 0) & (ints[WEST] > 0), here, left)
        right = jnp.where((lane == CELLS - 1) & (ints[EAST] > 0), here, right)
        faces = [0.5 * (here + other) for other in (up, down, left, right)]
        between = 0.5 * (centre[0] + centre[1])
        diagonal = (faces[0] + faces[1]) + (faces[2] + faces[3]) + (between + here)
        inverse = 0.8 / diagonal
        for n, face in enumerate(faces):
            put(n, k, inverse * face)
        put(4, k, inverse * between)
        put(5, k, 0.5 * inverse)
        put(6, k, inverse * heat[k, tile(b), :])
        put(7, k, 0.125 * here)


def coefficient_kernel(ints, friction, heat, chunks, out, cols_s, rows_s):
    west, east = chunks[ints[TO_WEST], 8:16, :], chunks[ints[TO_EAST], 8:16, :]
    ghost_columns(west, east, rows_s, cols_s)
    for b in range(1, TILES - 1):

        def put(n, k, value):
            out[n, k, tile(b), :] = value

        coefficients(ints, friction, heat, (None, None), (None, None), cols_s[tile(b), :], 2, b, put)
    for b in (0, TILES - 1):
        for n in range(8):
            for k in range(2):
                out[n, k, tile(b), :] = jnp.zeros((8, CELLS), F32)


def relaxed(planes, coef, ends, ghosts, column, b):
    at = [
        around(planes(f), b, ghosts[0, f : f + 1, :], ghosts[1, f : f + 1, :], column, f)
        for f in range(8)
    ]

    def factor(n, k):
        if b == 0 or b == TILES - 1:
            return ends[n, k, tile(0 if b == 0 else 1), :]
        return coef[n, k, tile(b), :]

    new = []
    for component in range(3):
        for k in range(2):
            here, up, down, left, right = at[2 * component + k]
            value = 0.2 * here + factor(0, k) * up + factor(1, k) * down
            value = value + factor(2, k) * left + factor(3, k) * right
            value = value + factor(4, k) * at[2 * component + 1 - k][0]
            if component == 0:
                value = value + factor(6, k)
                slope = at[7][0] if k == 0 else -at[6][0]
            elif component == 1:
                slope = at[6 + k][2] - at[6 + k][1]
            else:
                slope = at[6 + k][4] - at[6 + k][3]
            new.append(value - factor(5, k) * slope)
    for k in range(2):
        divergence = (at[2 + k][2] - at[2 + k][1]) + (at[4 + k][4] - at[4 + k][3])
        divergence = divergence + at[1][0] if k == 0 else divergence - at[0][0]
        new.append(at[6 + k][0] - factor(7, k) * divergence)
    return new


def fill_ghosts(ints, arrived, chunks, high, low, sides, ghosts, cols_s, rows_s):
    count = sides.shape[1]

    def block(n):
        rows = arrived[ints[BLOCKS + n], ints[RANKS + n]]
        if count == 8:
            return rows
        warm = [
            arrived[ints[BLOCKS + n], SLOTS + 2, pl.ds(2 * ints[RANKS + n] + k, 1), :]
            for k in range(2)
        ]
        return jnp.concatenate([rows, *warm, jnp.zeros((6, CELLS), F32)], axis=0)

    blend(block, high, low, sides)
    found = edge_ghosts(ints, arrived, chunks, sides, SLOTS, slice(0, 8), slice(0, 8))
    for n in range(4):
        ghosts[n] = found[n]
    ghost_columns(found[2], found[3], rows_s, cols_s)


def first_kernel(
    ints, flow, pressure, coef, friction, heat, arrived, chunks_in, high, low,
    flow_out, pressure_out, chunks, north, south, ends, heat_ghosts,
    sides, ghosts, cols_s, rows_s, edge_s, halos,
):
    rows_s[every_second(17), :] = chunks_in[ints[TO_WEST], 8:16, :]
    rows_s[every_second(16), :] = chunks_in[ints[TO_EAST], 8:16, :]
    fill_ghosts(ints, arrived, chunks_in, high, low, sides, ghosts, cols_s, rows_s)
    found = edge_ghosts(ints, arrived, chunks_in, sides, SLOTS + 1, slice(8, 16), slice(8, 16))
    for n in range(4):
        heat_ghosts[n] = found[n]
    halos[0] = arrived[ints[FROM_NORTH], SLOTS + 1]
    halos[1] = arrived[ints[FROM_SOUTH], SLOTS + 1]
    for end, b in enumerate((0, TILES - 1)):

        def put(n, k, value):
            ends[n, k, tile(end), :] = value

        lines = [[halos[side, 2 + k : 3 + k, :] for k in range(2)] for side in range(2)]
        coefficients(ints, friction, heat, *lines, cols_s[tile(b), :], 10, b, put)
    sweep(
        ints, flow, pressure, coef, ends, ghosts, cols_s, rows_s, edge_s,
        flow_out, pressure_out, chunks, north, south,
    )


def sweep_kernel(
    ints, flow, pressure, coef, ends, arrived, chunks_in, high, low,
    flow_out, pressure_out, chunks, north, south, sides, ghosts, cols_s, rows_s, edge_s,
):
    fill_ghosts(ints, arrived, chunks_in, high, low, sides, ghosts, cols_s, rows_s)
    sweep(
        ints, flow, pressure, coef, ends, ghosts, cols_s, rows_s, edge_s,
        flow_out, pressure_out, chunks, north, south,
    )


def sweep(
    ints, flow, pressure, coef, ends, ghosts, cols_s, rows_s, edge_s,
    flow_out, pressure_out, chunks, north, south,
):
    def planes(f):
        return flow.at[f] if f < 6 else pressure.at[f - 6]

    def planes_out(f):
        return flow_out.at[f] if f < 6 else pressure_out.at[f - 6]

    chunks[...] = jnp.zeros(chunks.shape, F32)
    for b in range(TILES):
        new = relaxed(planes, coef, ends, ghosts, cols_s[tile(b), :], b)
        for f in range(8):
            planes_out(f)[tile(b), :] = new[f]
    for b in range(TILES):
        gathered = jnp.zeros((8, CELLS), F32)
        for f in range(8):
            gathered = gather_edge(planes_out(f)[tile(b), :], f, gathered)
        edge_s[tile(b), :] = gathered
    for f in range(8):
        north[0, f : f + 1, :] = planes_out(f)[0:1, :]
        south[0, f : f + 1, :] = planes_out(f)[CELLS - 1 : CELLS, :]
    rows_s[...] = edge_s[...].T
    chunks[ints[TO_WEST]] = rows_s[every_second(1), :]
    chunks[ints[TO_EAST]] = rows_s[every_second(0), :]
    for f in range(8):
        edge_s[f : f + 1, :] = planes_out(f)[pl.ds(ints[ROW], 1), :]
    chunks[ints[CHUNK]] = edge_s[0:8, :]


def final_kernel(
    ints, flow, pressure, coef, ends, arrived, chunks_in, high, low, heat, heat_ghosts,
    flow_out, pressure_out, heat_out,
    sides, ghosts, cols_s, rows_s, heat_cols_s, answer, warm, sems,
):
    def planes(f):
        return flow.at[f] if f < 6 else pressure.at[f - 6]

    ghost_columns(heat_ghosts[2], heat_ghosts[3], rows_s, heat_cols_s)
    fill_ghosts(ints, arrived, chunks_in, high, low, sides, ghosts, cols_s, rows_s)
    for b in range(TILES):
        new = relaxed(planes, coef, ends, ghosts, cols_s[tile(b), :], b)
        for f in range(8):
            answer[f, tile(b), :] = new[f]
    copies = Copies(sems)
    copies.start(answer.at[0:6], flow_out)
    copies.start(answer.at[6:8], pressure_out)
    for b in range(TILES):
        layers = [
            around(
                heat.at[k],
                b,
                heat_ghosts[0, k : k + 1, :],
                heat_ghosts[1, k : k + 1, :],
                heat_cols_s[tile(b), :],
                k,
            )
            for k in range(2)
        ]
        for k in range(2):
            here, up, down, left, right = layers[k]
            under = jnp.ones((8, CELLS), F32) if k == 0 else layers[0][0]
            over = layers[1][0] if k == 0 else jnp.zeros((8, CELLS), F32)
            advect = jnp.zeros((8, CELLS), F32)
            for component, minus, plus in ((0, under, over), (1, up, down), (2, left, right)):
                speed = answer[2 * component + k, tile(b), :]
                advect = advect + jnp.maximum(speed, 0.0) * (here - minus)
                advect = advect + jnp.minimum(speed, 0.0) * (plus - here)
            spread = (up + down) + (left + right) + (under + over) - 6.0 * here
            warm[k, tile(b), :] = here + 0.1 * (spread - advect)
    copies.start(warm, heat_out)
    copies.wait()


def shape(*dims):
    return jax.ShapeDtypeStruct(dims, F32)


def scratch(*dims):
    return pltpu.VMEM(dims, F32)


def semaphores(count):
    return pltpu.SemaphoreType.DMA((count,))


def call(
    kernel, outs, ins, scratches, name, specs=None, out_specs=None, limit=4, keep=(), pin=()
):
    out_specs = out_specs or [VMEM] * len(outs)
    specs = specs or [SMEM] + [VMEM] * (len(ins) - 1)
    placed = []
    for n, (x, spec) in enumerate(zip(ins, specs)):
        if spec is HBM or n in keep:
            x = pltpu.with_memory_space_constraint(x, spec.memory_space)
        placed.append(x)
    outs = [
        pltpu.HBM(x.shape, x.dtype)
        if spec is HBM
        else pltpu.VMEM(x.shape, x.dtype)
        if n in pin
        else x
        for n, (x, spec) in enumerate(zip(outs, out_specs))
    ]
    return pl.pallas_call(
        kernel,
        out_shape=outs,
        in_specs=specs,
        out_specs=out_specs,
        scratch_shapes=scratches,
        compiler_params=pltpu.CompilerParams(vmem_limit_bytes=limit * 1024 * 1024),
        name=name,
    )(*placed)


def shards(
    flow_vector,
    normal_stress,
    thermal_field,
    shear_resistance,
    departing_bands,
    receiving_processor,
    shift_filled_by_lane,
    blending_factors,
):
    flow = flow_vector.reshape(6, CELLS, CELLS)
    pressure = normal_stress[0]
    heat = thermal_field[0]
    friction = shear_resistance[0]
    weights = blending_factors.reshape(8, CELLS, CELLS)
    lat, lon = lax.axis_index("lat"), lax.axis_index("lon")
    n_lat, n_lon = lax.axis_size("lat"), lax.axis_size("lon")
    patch = lax.axis_index("patch")
    own_row = departing_bands.reshape(1)
    receiver = receiving_processor.reshape(1)
    other = (1 - patch) * n_lon

    chunk = other + jnp.maximum(receiver, 0) % n_lon
    beside = jnp.stack([jnp.maximum(lon - 1, 0), jnp.minimum(lon + 1, n_lon - 1)])
    beside = (beside + patch * n_lon).astype(jnp.int32)
    beyond = jnp.stack([jnp.maximum(lat - 1, 0), jnp.minimum(lat + 1, n_lat - 1)])
    beyond = beyond.astype(jnp.int32)
    on_edge = jnp.stack([lat == 0, lat == n_lat - 1, lon == 0, lon == n_lon - 1]).astype(jnp.int32)
    bases = jnp.stack([jnp.where(lat > 0, 2, 0), jnp.where(lon > 0, 6, 4)]).astype(jnp.int32)
    here = jnp.stack([other, lon]).astype(jnp.int32)
    first = jnp.concatenate([own_row, on_edge, bases, chunk, beside, beyond, here, receiver])

    square = scratch(CELLS, CELLS)
    tiles = 2 * n_lon
    chunks, north, south, places = call(
        start_kernel,
        [shape(tiles, 16, CELLS), shape(2, 8, CELLS), shape(2, 8, CELLS), shape(8, CELLS)],
        (first, shift_filled_by_lane.reshape(1, CELLS), flow, pressure, heat, friction),
        [scratch(PLANES, CELLS, CELLS), pltpu.VMEM((1, CELLS), jnp.int32), scratch(16, CELLS)]
        + [square, square, semaphores(5)],
        "start",
        specs=[SMEM] + [HBM] * 5,
        pin=(0,),
    )

    def across(chunks):
        return lax.all_to_all(chunks, ("patch", "lon"), 0, 0, tiled=True)

    def along(packed):
        return lax.all_to_all(packed, "lat", 0, 0, tiled=True)

    came, places, lon, lat, other = lax.optimization_barrier(
        (across(chunks), places, lon, lat, other)
    )
    sent_to = lax.dynamic_slice(came, (other, 8, 0), (n_lon, 1, 1)).reshape(n_lon)
    sent_to = sent_to.astype(jnp.int32) - 1
    (packed,) = call(
        sort_kernel,
        [shape(n_lat, SLOTS + 3, 8, CELLS)],
        (first, sent_to, came, north, south),
        [pltpu.SMEM((n_lat,), jnp.int32)],
        "sort",
        specs=[SMEM, SMEM, VMEM, VMEM, VMEM],
        keep=(2,),
        pin=(0,),
    )
    packed, places = lax.optimization_barrier((packed, places))
    arrived = along(packed)

    (table,) = call(
        table_kernel,
        [jax.ShapeDtypeStruct((2 + n_lat * SLOTS,), jnp.int32)],
        lax.optimization_barrier((first, sent_to, packed))[:2],
        [pltpu.SMEM((n_lat,), jnp.int32)],
        "table",
        specs=[SMEM, SMEM],
        out_specs=[SMEM],
    )
    arrived, table = lax.optimization_barrier((arrived, table))

    own = places[:, 0].astype(jnp.int32) - 1
    pick = jnp.concatenate(
        [jnp.where(lat > 0, own[2:4], own[0:2]), jnp.where(lon > 0, own[6:8], own[4:6])]
    )
    same = (own >= 0)[None] & (own[None] // n_lon == pick[:, None] // n_lon)
    slot = jnp.sum((same & (own[None] < pick[:, None])).astype(jnp.int32), axis=1)
    ints = [first, jnp.maximum(pick, 0) // n_lon, jnp.minimum(slot, SLOTS - 1)]
    ints = jnp.concatenate(ints).astype(jnp.int32)

    joined = jax.ShapeDtypeStruct((2, CELLS, 2 * CELLS), jnp.bfloat16)
    high, low = call(
        weights_kernel,
        [joined, joined],
        (ints, weights),
        [scratch(4, CELLS, CELLS), semaphores(2)],
        "weights",
        specs=[SMEM, HBM],
    )
    (coef,) = call(
        coefficient_kernel,
        [shape(8, 2, CELLS, CELLS)],
        (ints, friction, heat, came),
        [square, square],
        "coefficients",
        keep=(3,),
    )
    sides, ghosts = scratch(2, 8, CELLS), scratch(4, 8, CELLS)
    state = [shape(6, CELLS, CELLS), shape(2, CELLS, CELLS)]
    for sweep in range(SWEEPS - 1):
        outs = state + [shape(tiles, 8, CELLS), shape(1, 8, CELLS), shape(1, 8, CELLS)]
        if sweep == 0:
            flow, pressure, chunks, north, south, ends, heat_ghosts = call(
                first_kernel,
                outs + [shape(8, 2, 16, CELLS), shape(4, 8, CELLS)],
                (ints, flow, pressure, coef, friction, heat, arrived, came, high, low),
                [scratch(2, 16, CELLS), ghosts, square, square, square, scratch(2, 8, CELLS)],
                "first_sweep",
                limit=8,
                keep=(3, 6, 7, 8, 9),
                pin=(2,),
            )
        else:
            flow, pressure, chunks, north, south = call(
                sweep_kernel,
                outs,
                (ints, flow, pressure, coef, ends, arrived, came, high, low),
                [sides, ghosts, square, square, square],
                "sweep",
                limit=8,
                keep=(3, 4, 5, 6, 7, 8),
                pin=(2,),
            )
        came = across(chunks)
        (packed,) = call(
            pack_kernel,
            [shape(n_lat, SLOTS + 1, 8, CELLS)],
            (table, came, north, south),
            [],
            "pack",
            keep=(1,),
            pin=(0,),
        )
        arrived = along(packed)
    flow, pressure, heat = call(
        final_kernel,
        state + [shape(2, CELLS, CELLS)],
        (ints, flow, pressure, coef, ends, arrived, came, high, low, heat, heat_ghosts),
        [sides, ghosts, square, square, square]
        + [scratch(8, CELLS, CELLS), scratch(2, CELLS, CELLS), semaphores(3)],
        "final",
        out_specs=[HBM] * 3,
        limit=8,
        keep=(1, 2, 3, 4, 5, 6, 7, 8),
    )
    return flow.reshape(3, 1, 2, CELLS, CELLS), pressure[None], heat[None]


def solution(mesh):
    placed = (
        P(None, "patch", None, "lat", "lon"),
        P("patch", None, "lat", "lon"),
        P("patch", None, "lat", "lon"),
        P("patch", None, "lat", "lon"),
        P("patch", "lat", "lon", None),
        P("patch", "lat", "lon", None),
        P("patch", "lat", "lon", None),
        P("patch", "lat", "lon", None, None, None),
    )
    return jax.shard_map(
        shards,
        mesh=mesh,
        in_specs=placed,
        out_specs=(
            P(None, "patch", None, "lat", "lon"),
            P("patch", None, "lat", "lon"),
            P("patch", None, "lat", "lon"),
        ),
        check_vma=False,
    )
```
